128 devices in a mesh: group: 4 (over y), dp: 32 (over z, x, core).
Axes of the slice: x: 4, y: 4, z: 4, core: 2. Of those that a mesh axis runs over, the one named last changes fastest.
Arguments:
- tokens: bfloat16 [32768, 1152], P(('group', 'dp')), may hold values from -6 to 6
- out_grad: bfloat16 [32768, 1152], P(('group', 'dp')), may hold values from -24 to 24
- timesteps: int32 [8], P('group'), may hold values from 0 to 999
- labels: int32 [8], P('group'), may hold values from 0 to 100
- grid_ids: int32 [8], P('group'), may hold values from 0 to 2, as said below
- w_qkv: bfloat16 [1152, 3456], replicated, may hold values from -0.1875 to 0.1875
- b_qv: float32 [2304], replicated, may hold values from -3 to 3
- w_proj: bfloat16 [1152, 1152], replicated, may hold values from -0.75 to 0.75
- b_proj: float32 [1152], replicated, may hold values from -3 to 3
- w_fc1: bfloat16 [1152, 4608], replicated, may hold values from -0.1875 to 0.1875
- b_fc1: float32 [4608], replicated, may hold values from -3 to 3
- w_fc2: bfloat16 [4608, 1152], replicated, may hold values from -0.09375 to 0.09375
- b_fc2: float32 [1152], replicated, may hold values from -3 to 3
- w_ada: bfloat16 [1152, 6912], P(None, 'dp'), may hold values from -0.125 to 0.125
- b_ada: float32 [6912], P('dp'), may hold values from -3 to 3
- w_t1: bfloat16 [256, 1152], replicated, may hold values from -0.375 to 0.375
- b_t1: float32 [1152], replicated, may hold values from -3 to 3
- w_t2: bfloat16 [1152, 1152], replicated, may hold values from -0.1875 to 0.1875
- b_t2: float32 [1152], replicated, may hold values from -3 to 3
- table: float32 [101, 1152], replicated, may hold values from -5 to 5
Outputs:
- block_out: bfloat16 [32768, 1152], P(('group', 'dp'))
- input_grad: bfloat16 [32768, 1152], P(('group', 'dp'))
- d_w_qkv: float32 [1152, 3456], P('dp')
- d_b_qv: float32 [2304], P('dp')
- d_w_proj: float32 [1152, 1152], P('dp')
- d_b_proj: float32 [1152], P('dp')
- d_w_fc1: float32 [1152, 4608], P('dp')
- d_b_fc1: float32 [4608], P('dp')
- d_w_fc2: float32 [4608, 1152], P('dp')
- d_b_fc2: float32 [1152], P('dp')
- d_w_ada: float32 [1152, 6912], P(None, 'dp')
- d_b_ada: float32 [6912], P('dp')
- d_w_t1: float32 [256, 1152], P('dp')
- d_b_t1: float32 [1152], P('dp')
- d_w_t2: float32 [1152, 1152], P('dp')
- d_b_t2: float32 [1152], P('dp')
- d_table: float32 [101, 1152], replicated
The draws below stay inside these ranges and needn't reach their ends.
Inputs may be any that keep to these rules, and one draw needn't show every extreme that they name: `grid_ids`: all 2 items of one group share one grid id; 0 is the 16 x 16 grid, 1 the 12 x 20 grid, 2 the 20 x 12 grid.
All inputs are finite; a program needn't handle non-finite values.
Results may differ from the reference program's by a relative error of at most 0.014.
Values sent between devices are 32-bit elements; how exact they have to be, the bound alone decides.
A program may use at most 256 MiB of HBM per device.

```python
import math
import jax
import jax.numpy as jnp
from jax import lax

D = 1152
HEADS = 16
HD = 72
FF = 4608
FREQ = 256
NCLS = 101
SLOTS = 256
ITEM_FRAMES = 16
ITEMS_GRP = 2
ITEMS = 8
TOKENS = 32768


def draw_grid_ids(key, part):
    key = jax.random.fold_in(key, 11)
    group_count = ITEMS // ITEMS_GRP
    per_group = jax.random.randint(jax.random.fold_in(key, 5), (group_count,), 0, 3).astype(jnp.int32)
    return jnp.repeat(per_group, ITEMS_GRP, total_repeat_length=ITEMS).astype(jnp.int32)


def plant(drawn, key, smallest, largest):
    longest = drawn.shape.index(max(drawn.shape))
    spots = []
    for shift in (0, 1):
        where = [jax.random.randint(jax.random.fold_in(key, axis), (), 0, length) for axis, length in enumerate(drawn.shape)]
        where[longest] = (where[longest] + shift) % drawn.shape[longest]
        spots.append(tuple(where))
    return drawn.at[spots[0]].set(smallest).at[spots[1]].set(largest)


def spiked(drawn, stream_key, source, target, blocks, factor):
    owner, partner = [(jnp.arange(drawn.shape[position]) // (drawn.shape[position] // blocks)).reshape([-1 if axis == position else 1 for axis in range(drawn.ndim)]) for position in (source, target)]
    chosen = jax.random.permutation(stream_key, blocks)[partner]
    strong = (owner == chosen) | (owner == (partner + blocks // 2) % blocks)
    return jnp.where(strong, factor * drawn, drawn)


def block_scale(key, shape, pieces, smallest, high):
    gain = 1.0
    for axis_at, blocks in pieces:
        heights = jax.random.uniform(jax.random.fold_in(jax.random.fold_in(key, 6), axis_at), (blocks,), jnp.float32, smallest / len(pieces), high / len(pieces))
        gain = gain * jnp.repeat(jnp.exp(heights), shape[axis_at] // blocks).reshape((-1,) + (1,) * (len(shape) - 1 - axis_at))
    return gain


def scatter_about(rng, dims, scale, limit, shards=(), kind=jnp.bfloat16):
    array = scale * jax.random.normal(rng, dims, jnp.float32)
    if shards:
        array = array * block_scale(rng, dims, shards, -0.22, 0.18)
    return jnp.clip(array, -limit, limit).astype(kind)


def noise_with(rng, shape, spread, reach, shards, heavy, kind=jnp.bfloat16):
    values = spread * jax.random.normal(rng, shape, jnp.float32)
    if shards:
        values = values * block_scale(rng, shape, shards, -0.22, 0.18)
    return jnp.clip(spiked(values, jax.random.fold_in(rng, 3), *heavy), -reach, reach).astype(kind)


def setup_inputs(seed: int = 0) -> dict:
    arg_keys = jax.random.split(jax.random.key(seed), 21)
    tokens = scatter_about(arg_keys[0], (TOKENS, D), 1.0, 6.0, ((0, 128),))
    out_grad = noise_with(arg_keys[1], (TOKENS, D), 1.0, 24.0, ((0, 128),), (0, 1, 128, 5.5))
    timesteps = plant(jax.random.randint(arg_keys[2], (ITEMS,), 0, 1000), jax.random.fold_in(arg_keys[2], 1), 0, 999).astype(jnp.int32)
    labels = plant(jax.random.randint(arg_keys[3], (ITEMS,), 0, NCLS), jax.random.fold_in(arg_keys[3], 1), 0, NCLS - 1).astype(jnp.int32)
    grid_ids = draw_grid_ids(jax.random.fold_in(arg_keys[20], 71), 0)
    w_qkv = scatter_about(arg_keys[5], (D, 3 * D), D ** -0.5, 0.1875)
    b_qv = scatter_about(arg_keys[6], (2 * D,), 0.5, 3.0, (), jnp.float32)
    w_proj = scatter_about(arg_keys[7], (D, D), (D // 16) ** -0.5, 0.75)
    b_proj = scatter_about(arg_keys[8], (D,), 0.5, 3.0, (), jnp.float32)
    w_fc1 = scatter_about(arg_keys[9], (D, FF), D ** -0.5, 0.1875)
    b_fc1 = scatter_about(arg_keys[10], (FF,), 0.5, 3.0, (), jnp.float32)
    w_fc2 = scatter_about(arg_keys[11], (FF, D), FF ** -0.5, 0.09375)
    b_fc2 = scatter_about(arg_keys[12], (D,), 0.5, 3.0, (), jnp.float32)
    w_ada = scatter_about(arg_keys[13], (D, 6 * D), (2 * D) ** -0.5, 0.125, ((1, 32),))
    b_ada = scatter_about(arg_keys[14], (6 * D,), 0.5, 3.0, ((0, 32),), jnp.float32)
    w_t1 = scatter_about(arg_keys[15], (FREQ, D), FREQ ** -0.5, 0.375)
    b_t1 = scatter_about(arg_keys[16], (D,), 0.5, 3.0, (), jnp.float32)
    w_t2 = scatter_about(arg_keys[17], (D, D), D ** -0.5, 0.1875)
    b_t2 = scatter_about(arg_keys[18], (D,), 0.5, 3.0, (), jnp.float32)
    table = scatter_about(arg_keys[19], (NCLS, D), 1.0, 5.0, (), jnp.float32)
    return {"tokens": tokens, "out_grad": out_grad, "timesteps": timesteps, "labels": labels, "grid_ids": grid_ids, "w_qkv": w_qkv, "b_qv": b_qv, "w_proj": w_proj, "b_proj": b_proj, "w_fc1": w_fc1, "b_fc1": b_fc1, "w_fc2": w_fc2, "b_fc2": b_fc2, "w_ada": w_ada, "b_ada": b_ada, "w_t1": w_t1, "b_t1": b_t1, "w_t2": w_t2, "b_t2": b_t2, "table": table}


EPS = 1e-06
NEG = -1e+30

@jax.custom_vjp
def low(v):
    return lax.optimization_barrier(v.astype(jnp.bfloat16)).astype(jnp.float32)

@jax.custom_vjp
def low_back(v):
    return v

def low_keep(v):
    return (low(v), None)

def low_pass(kept, grad):
    return (grad,)

def back_keep(v):
    return (v, None)

def back_low(kept, grad):
    return (low(grad),)
low.defvjp(low_keep, low_pass)
low_back.defvjp(back_keep, back_low)

def hdot(left_op, right_op):
    return jnp.dot(left_op, right_op, precision=lax.Precision.HIGHEST, preferred_element_type=jnp.float32)

def norm_rows(matrix):
    row_mean = lax.optimization_barrier(jnp.mean(matrix, axis=-1, keepdims=True))
    centered = matrix - row_mean
    variance = lax.optimization_barrier(jnp.mean(centered * centered, axis=-1, keepdims=True))
    return centered * lax.rsqrt(variance + EPS)

def time_embed(step_ids, width_half):
    frequency = jnp.exp(jnp.arange(width_half, dtype=jnp.float32) * (-math.log(10000.0) / width_half))
    angles = step_ids.astype(jnp.float32)[:, None] * frequency[None, :]
    return jnp.concatenate([jnp.cos(angles), jnp.sin(angles)], axis=1)

def reference(tokens, out_grad, timesteps, labels, grid_ids, w_qkv, b_qv, w_proj, b_proj, w_fc1, b_fc1, w_fc2, b_fc2, w_ada, b_ada, w_t1, b_t1, w_t2, b_t2, table):
    first_live = jnp.where(grid_ids == 2, SLOTS // 16, 0).astype(jnp.int32)
    end_live = jnp.where(grid_ids == 1, SLOTS - SLOTS // 16, SLOTS).astype(jnp.int32)
    slot_pos = jnp.arange(SLOTS, dtype=jnp.int32)
    item_valid = (slot_pos[None, :] >= first_live[:, None]) & (slot_pos[None, :] < end_live[:, None])
    live_mask = jnp.broadcast_to(item_valid[:, None, :], (ITEMS, ITEM_FRAMES, SLOTS)).reshape(TOKENS, 1).astype(jnp.float32)
    time_feats = time_embed(timesteps, FREQ // 2)
    onehot = (labels[:, None] == jnp.arange(NCLS, dtype=jnp.int32)[None, :]).astype(jnp.float32)
    score_scale = 1.0 / math.sqrt(HD)
    frame_shape = (ITEM_FRAMES, SLOTS, HEADS, HD)

    def forward(token_vals, m_qkv, v_qv, m_proj, v_proj, m_fc1, v_fc1, m_fc2, v_fc2, m_ada, v_ada, m_t1, v_t1, m_t2, v_t2, m_table):
        pre_time = hdot(time_feats, m_t1) + v_t1
        condition = hdot(jax.nn.silu(pre_time), m_t2) + v_t2 + hdot(onehot, m_table)
        modulation = hdot(jax.nn.silu(condition), m_ada) + v_ada

        @jax.checkpoint
        def one_item(item_args):
            item_rows, item_mod, valid_keys = item_args
            shift_attn, scale_attn, gate_attn, shift_mlp, scale_mlp, gate_mlp = jnp.split(item_mod, 6)
            attn_in = low(norm_rows(item_rows) * (1.0 + scale_attn) + shift_attn)
            qkv_rows = hdot(attn_in, m_qkv)
            queries = low_back(low(qkv_rows[:, :D] + v_qv[:D]))
            key_rows = low_back(low(qkv_rows[:, D:2 * D]))
            values = low_back(low(qkv_rows[:, 2 * D:] + v_qv[D:]))
            scores = jnp.einsum('fqhd,fkhd->fhqk', queries.reshape(frame_shape), key_rows.reshape(frame_shape), precision=lax.Precision.HIGHEST) * score_scale
            scores = jnp.where(valid_keys[None, None, None, :], low_back(scores), NEG)
            row_max = lax.optimization_barrier(jnp.max(scores, axis=-1, keepdims=True))
            shifted = jnp.exp(scores - row_max)
            attn_weights = shifted / lax.optimization_barrier(jnp.sum(shifted, axis=-1, keepdims=True))
            mixed_rows = jnp.einsum('fhqk,fkhd->fqhd', low(attn_weights), values.reshape(frame_shape), precision=lax.Precision.HIGHEST)
            mixed_rows = low_back(low(mixed_rows.reshape(ITEM_FRAMES * SLOTS, D)))
            attn_out = low_back(hdot(mixed_rows, m_proj) + v_proj)
            resid_one = item_rows + gate_attn * attn_out
            mlp_in = low(norm_rows(resid_one) * (1.0 + scale_mlp) + shift_mlp)
            hidden = low_back(hdot(mlp_in, m_fc1) + v_fc1)
            activated = low(jax.nn.gelu(hidden, approximate=True))
            branch = low_back(hdot(activated, m_fc2) + v_fc2)
            return resid_one + gate_mlp * branch
        outputs = lax.map(one_item, (token_vals.reshape(ITEMS, ITEM_FRAMES * SLOTS, D), modulation, item_valid))
        return outputs.reshape(TOKENS, D)
    weight_list = (w_qkv, b_qv, w_proj, b_proj, w_fc1, b_fc1, w_fc2, b_fc2, w_ada, b_ada, w_t1, b_t1, w_t2, b_t2, table)
    weight_list = tuple((weight_arr.astype(jnp.float32) for weight_arr in weight_list))
    result, pullback = jax.vjp(forward, tokens.astype(jnp.float32), *weight_list)
    gradients = pullback(out_grad.astype(jnp.float32) * live_mask)
    return (result.astype(jnp.bfloat16), gradients[0].astype(jnp.bfloat16), gradients[1], gradients[2], gradients[3], gradients[4], gradients[5], gradients[6], gradients[7], gradients[8], gradients[9], gradients[10], gradients[11], gradients[12], gradients[13], gradients[14], gradients[15])
```

```python
import functools
import math

import jax
import jax.numpy as jnp
from jax import lax
from jax.experimental import pallas as pl
from jax.experimental.pallas import tpu as pltpu
from jax.sharding import PartitionSpec as P

HEADS = 16
SLOTS = 256
ITEM_FRAMES = 16


EPS = 1e-06
NEG = -1e30


def hdot(left_op, right_op):
    return jnp.dot(
        left_op, right_op, precision=lax.Precision.HIGHEST, preferred_element_type=jnp.float32
    )


def hdot_t(left_op, right_op):
    return lax.dot_general(
        left_op,
        right_op,
        (((0,), (0,)), ((), ())),
        precision=lax.Precision.HIGHEST,
        preferred_element_type=jnp.float32,
    )


def weight_term(left_op, right_op):
    return lax.dot_general(
        left_op, right_op, (((0,), (0,)), ((), ())), preferred_element_type=jnp.float32
    )


def norm_rows(matrix):
    row_mean = jnp.mean(matrix, axis=-1, keepdims=True)
    centered = matrix - row_mean
    inv_std = lax.rsqrt(jnp.mean(centered * centered, axis=-1, keepdims=True) + EPS)
    return (centered * inv_std, inv_std)


def norm_back(grad_in, normed, inv_std):
    return inv_std * (
        grad_in
        - jnp.mean(grad_in, axis=-1, keepdims=True)
        - normed * jnp.mean(grad_in * normed, axis=-1, keepdims=True)
    )


def silu_back(pre_vals, grad_in):
    sigmoid = jax.nn.sigmoid(pre_vals)
    return grad_in * sigmoid * (1.0 + pre_vals * (1.0 - sigmoid))


def time_embed(step_ids, width_half):
    frequency = jnp.exp(
        jnp.arange(width_half, dtype=jnp.float32) * (-math.log(10000.0) / width_half)
    )
    angles = step_ids.astype(jnp.float32)[:, None] * frequency[None, :]
    return jnp.concatenate([jnp.cos(angles), jnp.sin(angles)], axis=1)


def own_block(vector, dp_place, dp_count):
    block_rows = vector.shape[0] // dp_count
    return lax.dynamic_slice_in_dim(vector, dp_place * block_rows, block_rows, 0)


MESH = pl.DeviceIdType.MESH
ORDERS = (("y", "z", "x"), ("z", "x", "y"), ("x", "y", "z"))
STREAMS = tuple((order, pairing) for pairing in (0, 1) for order in ORDERS)
BLOCKS = (32, 16, 8, 4, 2, 1)
LANDS_AT = (0, 32, 48, 56, 60, 62)
PIECE = 56
OWN = 72


def coords():
    place = lax.axis_index("dp")
    return {
        "y": lax.axis_index("group"),
        "z": lax.div(place, 8),
        "x": lax.rem(lax.div(place, 2), 4),
        "core": lax.rem(place, 2),
    }


def device_at(at):
    return (at["y"], (at["z"] * 4 + at["x"]) * 2 + at["core"])


def sibling_of(at):
    return device_at({**at, "core": 1 - at["core"]})


def partner_of(at, axis, pairing):
    here = at[axis]
    if pairing == 0:
        there = here + 1 - 2 * lax.rem(here, 2)
    else:
        there = lax.rem(here + 3 + 2 * lax.rem(here, 2), 4)
    return device_at({**at, axis: there})


def slot_of(pairing, value):
    if pairing == 1:
        return value
    if isinstance(value, int):
        return (0, 2, 3, 1)[value]
    return lax.rem(value + lax.div(value + 1, 2), 4)


def grad_kernel(
    act_own,
    act_wide,
    gbr_own,
    gbr_wide,
    mlp_own,
    mlp_wide,
    ghid_own,
    ghid_wide,
    two_own,
    two_wide,
    gqkv_own,
    gqkv_wide,
    out_qkv,
    out_proj,
    out_fc1,
    out_fc2,
    parts,
    landed,
    lhs,
    rhs,
    stage_lhs,
    stage_rhs,
    final,
    other,
    send_sem,
    recv_sem,
    credit,
    swap_send,
    swap_recv,
    swap_credit,
    own_sem,
    ring_send,
    ring_recv,
    pair_send,
    pair_recv,
):
    at = coords()
    core = at["core"]
    sibling = sibling_of(at)
    barrier = pltpu.get_barrier_semaphore()
    peers = [partner_of(at, axis, pairing) for axis in "xyz" for pairing in (0, 1)]
    peers.append(device_at({**at, "y": lax.rem(at["y"] + 2, 4)}))
    peers.append(sibling)
    for peer in peers:
        pl.semaphore_signal(barrier, inc=1, device_id=peer, device_id_type=MESH)
    pl.semaphore_wait(barrier, len(peers))

    def swap(phase):
        if phase == 0:
            pairs = [(act_wide.at[1 - core], stage_lhs), (gbr_wide, stage_rhs.at[:, 0:1152])]
        elif phase == 1:
            pairs = [(mlp_wide, stage_lhs.at[0:8]), (ghid_wide.at[1 - core], stage_rhs)]
        else:
            pairs = [(two_wide, stage_lhs), (gqkv_wide.at[1 - core], stage_rhs)]
        return [
            pltpu.make_async_remote_copy(
                src_ref=source,
                dst_ref=target,
                send_sem=swap_send.at[place],
                recv_sem=swap_recv.at[place],
                device_id=sibling,
                device_id_type=MESH,
            )
            for place, (source, target) in enumerate(pairs)
        ]

    def own_loads(phase):
        if phase == 0:
            pairs = [
                (act_own.at[core], lhs.at[:, :, 0:256]),
                (gbr_own, rhs.at[0:256, 0:1152]),
            ]
        elif phase == 1:
            pairs = [
                (mlp_own, lhs.at[0:8, :, 0:256]),
                (ghid_own.at[core], rhs.at[0:256]),
            ]
        else:
            pairs = [
                (two_own, lhs.at[:, :, 0:256]),
                (gqkv_own.at[core], rhs.at[0:256]),
            ]
        return [
            pltpu.make_async_copy(source, target, own_sem.at[place])
            for place, (source, target) in enumerate(pairs)
        ]

    def swap_start(phase):
        if phase:
            pl.semaphore_wait(swap_credit, 1)
        for copy in swap(phase):
            copy.start()

    def swap_finish(phase):
        for copy in own_loads(phase):
            copy.start()
        for copy in swap(phase):
            copy.wait()

        def narrow_lhs(step, _):
            lhs[step, :, 256:512] = stage_lhs[step].astype(jnp.bfloat16)
            return _

        lax.fori_loop(0, 8 if phase == 1 else 16, narrow_lhs, 0)
        wide = 1152 if phase == 0 else 2304

        def narrow_rhs(step, _):
            rows = pl.ds(pl.multiple_of(step * 32, 32), 32)
            into = pl.ds(pl.multiple_of(256 + step * 32, 32), 32)
            rhs[into, 0:wide] = stage_rhs[rows, 0:wide].astype(jnp.bfloat16)
            return _

        lax.fori_loop(0, 8, narrow_rhs, 0)
        if phase < 2:
            pl.semaphore_signal(swap_credit, inc=1, device_id=sibling, device_id_type=MESH)
        for copy in own_loads(phase):
            copy.wait()

    def base_of(stream, z_place, x_place, y_slot):
        order, pairing = STREAMS[stream]
        slots = {"y": y_slot, "z": slot_of(pairing, z_place), "x": slot_of(pairing, x_place)}
        return (slots[order[0]] * 4 + slots[order[1]]) * 4 + slots[order[2]]

    def keep(half, stream, chip, rows):
        z_place, x_place = lax.div(chip, 4), lax.rem(chip, 4)
        for y_slot in range(4):
            block = base_of(stream, z_place, x_place, y_slot)
            first = y_slot * PIECE
            for unit in range(3):
                low, high = max(first, OWN * unit), min(first + PIECE, OWN * unit + OWN)
                if low < high:
                    parts[half, stream, block, low - first : high - first, :] = rows[
                        low - OWN * unit : high - OWN * unit, unit * 128 : unit * 128 + 128
                    ]

    def halving(phase, stream, step):
        order, pairing = STREAMS[stream]
        axis = order[step // 2]
        slots = [slot_of(pairing, at[name]) for name in order]
        base = 0
        for level in range(step // 2):
            base = base + slots[level] * (64 // 4 ** (level + 1))
        slot = slots[step // 2]
        side = lax.div(slot, 2) if step % 2 == 0 else slot
        away = 1 - side if step % 2 == 0 else slot + 1 - 2 * lax.rem(slot, 2)
        count = BLOCKS[step]
        kept, sent = base + side * count, base + away * count
        partner = partner_of(at, axis, pairing if step % 2 == 0 else 1 - pairing)
        copy = pltpu.make_async_remote_copy(
            src_ref=parts.at[phase % 2, stream, pl.ds(sent, count)],
            dst_ref=landed.at[stream, pl.ds(LANDS_AT[step], count)],
            send_sem=send_sem.at[stream, step],
            recv_sem=recv_sem.at[stream, step],
            device_id=partner,
            device_id_type=MESH,
        )
        return copy, kept, partner

    def send(phase, stream, step):
        copy, _, _ = halving(phase, stream, step)
        if phase:
            pl.semaphore_wait(credit.at[stream, step], 1)
        copy.start()

    def receive(phase, step):
        for stream in range(6):
            copy, kept, partner = halving(phase, stream, step)
            copy.wait()
            half = phase % 2
            count = BLOCKS[step]
            if step < 5:

                def add(block, _):
                    parts[half, stream, kept + block] += landed[stream, LANDS_AT[step] + block]
                    return _

                lax.fori_loop(0, count, add, 0, unroll=min(count, 4))
            else:
                final[phase, at["y"], stream] = (
                    parts[half, stream, kept] + landed[stream, LANDS_AT[step]]
                )
            if phase < 2:
                pl.semaphore_signal(
                    credit.at[stream, step], inc=1, device_id=partner, device_id_type=MESH
                )
            if step < 5:
                send(phase, stream, step + 1)

    def products(phase):
        half = phase % 2
        if phase == 0:
            for third in range(3):

                def pair(chip, _):
                    rows = jnp.dot(
                        lhs[chip],
                        rhs[:, third * 384 : third * 384 + 384],
                        preferred_element_type=jnp.float32,
                    )
                    keep(half, third, chip, rows[0:72])
                    keep(half, third + 3, chip, rows[72:144])
                    return _

                lax.fori_loop(0, 16, pair, 0)
                send(phase, third, 0)
                send(phase, third + 3, 0)
            return
        for stream in range(6):
            shift = core * 8 if phase == 2 and stream >= 3 else 0

            def duo(pair_at, _):
                rows = jnp.dot(
                    lhs[pair_at + shift],
                    rhs[:, stream * 384 : stream * 384 + 384],
                    preferred_element_type=jnp.float32,
                )
                keep(half, stream, pair_at * 2, rows[0:72])
                keep(half, stream, pair_at * 2 + 1, rows[72:144])
                return _

            lax.fori_loop(0, 8, duo, 0)
            send(phase, stream, 0)

    def ring(phase):
        return [
            pltpu.make_async_remote_copy(
                src_ref=final.at[phase, at["y"]],
                dst_ref=final.at[phase, at["y"]],
                send_sem=ring_send.at[phase, hop - 1],
                recv_sem=ring_recv.at[phase, hop - 1],
                device_id=device_at({**at, "y": lax.rem(at["y"] + hop, 4)}),
                device_id_type=MESH,
            )
            for hop in (1, 2, 3)
        ]

    def across(phase):
        return pltpu.make_async_remote_copy(
            src_ref=final.at[phase],
            dst_ref=other.at[phase - 1],
            send_sem=pair_send.at[phase - 1],
            recv_sem=pair_recv.at[phase - 1],
            device_id=sibling,
            device_id_type=MESH,
        )

    def whole(get, stream):
        pairing = STREAMS[stream][1]
        order = sorted(range(4), key=lambda y_place: slot_of(pairing, y_place))
        return jnp.concatenate([get(y_place, stream) for y_place in order], axis=0)

    def write_rows(phase, low):
        for side in range(2):
            mine = side == (0 if low == 0 else 1)
            for stream in range(6):
                if mine:
                    rows = whole(lambda y_place, stream: final[phase, y_place, stream], stream)
                else:
                    rows = whole(lambda y_place, stream: other[phase - 1, y_place, stream], stream)
                for unit in range(3):
                    block = rows[OWN * unit + low : OWN * unit + low + 36]
                    column = side * 18 + stream * 3 + unit
                    if phase == 1:
                        out_fc1[:, column * 128 : column * 128 + 128] = block
                    elif column < 27:
                        out_qkv[:, column * 128 : column * 128 + 128] = block
                    else:
                        out_proj[:, (column - 27) * 128 : (column - 27) * 128 + 128] = block

    def write(phase):
        if phase == 0:
            for stream in range(6):
                rows = whole(lambda y_place, stream: final[0, y_place, stream], stream)
                half, third = stream // 3, stream % 3
                for unit in range(3):
                    column = third * 3 + unit
                    out_fc2[half * 72 : half * 72 + 72, column * 128 : column * 128 + 128] = rows[
                        OWN * unit : OWN * unit + 72
                    ]
            return

        @pl.when(core == 0)
        def _():
            write_rows(phase, 0)

        @pl.when(core == 1)
        def _():
            write_rows(phase, 36)

    def ring_start(phase):
        for copy in ring(phase):
            copy.start()

    def ring_finish(phase):
        for copy in ring(phase):
            copy.wait()
        if phase:
            across(phase).start()

    def clear(block, _):
        for half in range(2):
            for stream in range(6):
                z_place, x_place = lax.div(block, 4), lax.rem(block, 4)
                parts[half, stream, base_of(stream, z_place, x_place, 3), 48:56, :] = jnp.zeros(
                    (8, 128), jnp.float32
                )
        return _

    swap_start(0)
    lax.fori_loop(0, 16, clear, 0)
    swap_finish(0)
    products(0)
    swap_start(1)
    swap_finish(1)
    receive(0, 0)
    products(1)
    swap_start(2)
    swap_finish(2)
    receive(0, 1)
    receive(0, 2)
    receive(0, 3)
    receive(1, 0)
    receive(0, 4)
    receive(0, 5)
    ring_start(0)
    products(2)
    receive(1, 1)
    receive(1, 2)
    ring_finish(0)
    write(0)
    receive(1, 3)
    receive(1, 4)
    receive(2, 0)
    receive(1, 5)
    ring_start(1)
    receive(2, 1)
    ring_finish(1)
    receive(2, 2)
    receive(2, 3)
    across(1).wait()
    write(1)
    receive(2, 4)
    receive(2, 5)
    ring_start(2)
    ring_finish(2)
    across(2).wait()
    write(2)


def reduce_grads(operands):
    dma = pltpu.SemaphoreType.DMA
    regular = pltpu.SemaphoreType.REGULAR
    vmem = pl.BlockSpec(memory_space=pltpu.VMEM)
    return pl.pallas_call(
        grad_kernel,
        out_shape=(
            jax.ShapeDtypeStruct((36, 3456), jnp.float32),
            jax.ShapeDtypeStruct((36, 1152), jnp.float32),
            jax.ShapeDtypeStruct((36, 4608), jnp.float32),
            jax.ShapeDtypeStruct((144, 1152), jnp.float32),
        ),
        in_specs=[pl.BlockSpec(memory_space=pl.ANY)] * 12,
        out_specs=(vmem, vmem, vmem, vmem),
        scratch_shapes=[
            pltpu.VMEM((2, 6, 64, PIECE, 128), jnp.float32),
            pltpu.VMEM((6, 63, PIECE, 128), jnp.float32),
            pltpu.VMEM((16, 144, 512), jnp.bfloat16),
            pltpu.VMEM((512, 2304), jnp.bfloat16),
            pltpu.VMEM((16, 144, 256), jnp.float32),
            pltpu.VMEM((256, 2304), jnp.float32),
            pltpu.VMEM((3, 4, 6, PIECE, 128), jnp.float32),
            pltpu.VMEM((2, 4, 6, PIECE, 128), jnp.float32),
            dma((6, 6)),
            dma((6, 6)),
            regular((6, 6)),
            dma((2,)),
            dma((2,)),
            regular,
            dma((2,)),
            dma((3, 3)),
            dma((3, 3)),
            dma((2,)),
            dma((2,)),
        ],
        compiler_params=pltpu.CompilerParams(
            collective_id=1, has_side_effects=True, vmem_limit_bytes=60 * 2**20
        ),
    )(*operands)


def on_device(
    tokens,
    out_grad,
    timesteps,
    labels,
    grid_ids,
    w_qkv,
    b_qv,
    w_proj,
    b_proj,
    w_fc1,
    b_fc1,
    w_fc2,
    b_fc2,
    w_ada,
    b_ada,
    w_t1,
    b_t1,
    w_t2,
    b_t2,
    table,
):
    dp_count = lax.axis_size("dp")
    dp_place = lax.axis_index("dp")
    row_count, model_width = tokens.shape
    frame_count = row_count // SLOTS
    head_count = HEADS
    head_dim = model_width // head_count
    score_scale = 1.0 / math.sqrt(head_dim)
    frame_shape = (frame_count, SLOTS, head_count, head_dim)
    item_count = timesteps.shape[0]
    time_feats = time_embed(timesteps, w_t1.shape[0] // 2)
    onehot = (labels[:, None] == jnp.arange(table.shape[0], dtype=jnp.int32)[None, :]).astype(
        jnp.float32
    )
    pre_time = hdot(time_feats, w_t1.astype(jnp.float32)) + b_t1
    act_time = jax.nn.silu(pre_time)
    condition = hdot(act_time, w_t2.astype(jnp.float32)) + b_t2 + hdot(onehot, table)
    act_cond = jax.nn.silu(condition)
    ada_cols = w_ada.astype(jnp.float32)
    mod_part = hdot(act_cond, ada_cols) + b_ada
    mod_all = lax.all_gather(mod_part, "dp", axis=1, tiled=True)
    own_item = dp_place * frame_count // ITEM_FRAMES
    item_mod = lax.dynamic_index_in_dim(mod_all, own_item, 0, keepdims=False)
    shift_attn, scale_attn, gate_attn, shift_mlp, scale_mlp, gate_mlp = jnp.split(item_mod, 6)
    grid_value = lax.dynamic_index_in_dim(grid_ids, own_item, 0, keepdims=False)
    first_live = jnp.where(grid_value == 2, SLOTS // 16, 0)
    end_live = jnp.where(grid_value == 1, SLOTS - SLOTS // 16, SLOTS)
    slot_pos = jnp.arange(SLOTS, dtype=jnp.int32)
    valid_keys = (slot_pos >= first_live) & (slot_pos < end_live)
    live_rows = jnp.tile(valid_keys, frame_count).astype(jnp.float32)[:, None]
    token_vals = tokens.astype(jnp.float32)
    normed_one, inv_one = norm_rows(token_vals)
    attn_in = (normed_one * (1.0 + scale_attn) + shift_attn).astype(jnp.bfloat16)
    qkv_rows = jnp.dot(attn_in, w_qkv, preferred_element_type=jnp.float32)
    queries = (
        (qkv_rows[:, :model_width] + b_qv[:model_width]).astype(jnp.bfloat16).reshape(frame_shape)
    )
    key_rows = qkv_rows[:, model_width : 2 * model_width].astype(jnp.bfloat16).reshape(frame_shape)
    values = (
        (qkv_rows[:, 2 * model_width :] + b_qv[model_width:])
        .astype(jnp.bfloat16)
        .reshape(frame_shape)
    )

    def masked_scores():
        raw = (
            jnp.einsum("fqhd,fkhd->fhqk", queries, key_rows, preferred_element_type=jnp.float32)
            * score_scale
        )
        return jnp.where(valid_keys[None, None, None, :], raw, NEG)

    scores = masked_scores()
    row_max = jnp.max(scores, axis=-1, keepdims=True)
    shifted = jnp.exp(scores - row_max)
    row_total = jnp.sum(shifted, axis=-1, keepdims=True)
    log_total = row_max + jnp.log(row_total)
    attn_weights = (shifted / row_total).astype(jnp.bfloat16)
    mixed = jnp.einsum("fhqk,fkhd->fqhd", attn_weights, values, preferred_element_type=jnp.float32)
    mixed_rows = mixed.reshape(row_count, model_width).astype(jnp.bfloat16)
    attn_out = jnp.dot(mixed_rows, w_proj, preferred_element_type=jnp.float32) + b_proj
    resid_one = token_vals + gate_attn * attn_out
    normed_two, inv_two = norm_rows(resid_one)
    mlp_in = (normed_two * (1.0 + scale_mlp) + shift_mlp).astype(jnp.bfloat16)
    hidden = jnp.dot(mlp_in, w_fc1, preferred_element_type=jnp.float32) + b_fc1
    gelu_vals, gelu_pull = jax.vjp(functools.partial(jax.nn.gelu, approximate=True), hidden)
    activated = gelu_vals.astype(jnp.bfloat16)
    branch = jnp.dot(activated, w_fc2, preferred_element_type=jnp.float32) + b_fc2
    block_out = (resid_one + gate_mlp * branch).astype(jnp.bfloat16)
    cotangent = out_grad.astype(jnp.float32) * live_rows
    d_gate_mlp = jnp.sum(cotangent * branch, axis=0)
    grad_branch = (cotangent * gate_mlp).astype(jnp.bfloat16)
    grad_act = jnp.dot(grad_branch, w_fc2.T, preferred_element_type=jnp.float32)
    grad_hidden = gelu_pull(grad_act)[0].astype(jnp.bfloat16)
    grad_mlp_in = jnp.dot(grad_hidden, w_fc1.T, preferred_element_type=jnp.float32)
    d_shift_mlp = jnp.sum(grad_mlp_in, axis=0)
    d_scale_mlp = jnp.sum(grad_mlp_in * normed_two, axis=0)
    grad_resid = cotangent + norm_back(grad_mlp_in * (1.0 + scale_mlp), normed_two, inv_two)
    d_gate_attn = jnp.sum(grad_resid * attn_out, axis=0)
    grad_attn = (grad_resid * gate_attn).astype(jnp.bfloat16)
    grad_mixed = (
        jnp.dot(grad_attn, w_proj.T, preferred_element_type=jnp.float32)
        .astype(jnp.bfloat16)
        .reshape(frame_shape)
    )
    probs_again = jnp.exp(masked_scores() - log_total)
    grad_weights = jnp.einsum(
        "fqhd,fkhd->fhqk", grad_mixed, values, preferred_element_type=jnp.float32
    )
    row_dot = jnp.sum(probs_again * grad_weights, axis=-1, keepdims=True)
    grad_scores = (probs_again * (grad_weights - row_dot)).astype(jnp.bfloat16)
    grad_query = (
        jnp.einsum("fhqk,fkhd->fqhd", grad_scores, key_rows, preferred_element_type=jnp.float32)
        * score_scale
    )
    grad_key = (
        jnp.einsum("fhqk,fqhd->fkhd", grad_scores, queries, preferred_element_type=jnp.float32)
        * score_scale
    )
    grad_value = jnp.einsum(
        "fhqk,fqhd->fkhd",
        probs_again.astype(jnp.bfloat16),
        grad_mixed,
        preferred_element_type=jnp.float32,
    )
    grad_qkv = jnp.concatenate(
        [
            grad_query.reshape(row_count, model_width),
            grad_key.reshape(row_count, model_width),
            grad_value.reshape(row_count, model_width),
        ],
        axis=1,
    ).astype(jnp.bfloat16)
    grad_attn_in = jnp.dot(grad_qkv, w_qkv.T, preferred_element_type=jnp.float32)
    d_shift_attn = jnp.sum(grad_attn_in, axis=0)
    d_scale_attn = jnp.sum(grad_attn_in * normed_one, axis=0)
    input_grad = (
        grad_resid + norm_back(grad_attn_in * (1.0 + scale_attn), normed_one, inv_one)
    ).astype(jnp.bfloat16)
    bias_qv = jnp.concatenate(
        [
            jnp.sum(grad_qkv[:, :model_width], axis=0, dtype=jnp.float32),
            jnp.sum(grad_qkv[:, 2 * model_width :], axis=0, dtype=jnp.float32),
        ]
    )
    bias_proj = jnp.sum(grad_attn, axis=0, dtype=jnp.float32)
    bias_fc1 = jnp.sum(grad_hidden, axis=0, dtype=jnp.float32)
    bias_fc2 = jnp.sum(grad_branch, axis=0, dtype=jnp.float32)
    d_mod_item = jnp.concatenate(
        [d_shift_attn, d_scale_attn, d_gate_attn, d_shift_mlp, d_scale_mlp, d_gate_mlp]
    )
    d_mod_all = lax.dynamic_update_index_in_dim(
        jnp.zeros((item_count, 6 * model_width), jnp.float32), d_mod_item, own_item, 0
    )
    d_mod_cols = lax.psum_scatter(d_mod_all, "dp", scatter_dimension=1, tiled=True)
    grad_w_ada = hdot_t(act_cond, d_mod_cols)
    grad_b_ada = jnp.sum(d_mod_cols, axis=0)
    cond_part = hdot(d_mod_cols, ada_cols.T)
    grad_act_cond, bias_qv, bias_proj, bias_fc1, bias_fc2 = lax.psum(
        (cond_part, bias_qv, bias_proj, bias_fc1, bias_fc2), "dp"
    )
    grad_cond = silu_back(condition, grad_act_cond)
    grad_table = hdot_t(onehot, grad_cond)
    grad_w_t2 = hdot_t(act_time, grad_cond)
    grad_b_t2 = jnp.sum(grad_cond, axis=0)
    grad_pre = silu_back(pre_time, hdot(grad_cond, w_t2.astype(jnp.float32).T))
    grad_w_t1 = hdot_t(time_feats, grad_pre)
    grad_b_t1 = jnp.sum(grad_pre, axis=0)
    slice_qv = own_block(bias_qv, dp_place, dp_count)
    slice_proj = own_block(bias_proj, dp_place, dp_count)
    slice_fc1 = own_block(bias_fc1, dp_place, dp_count)
    slice_fc2 = own_block(bias_fc2, dp_place, dp_count)
    slice_w_t1 = own_block(grad_w_t1, dp_place, dp_count)
    slice_b_t1 = own_block(grad_b_t1, dp_place, dp_count)
    slice_w_t2 = own_block(grad_w_t2, dp_place, dp_count)
    slice_b_t2 = own_block(grad_b_t2, dp_place, dp_count)
    wide = lambda array: array.astype(jnp.float32)
    act_own = activated.T.reshape(16, 2, 144, row_count).transpose(1, 0, 2, 3)
    mlp_own = mlp_in.T.reshape(8, 144, row_count)
    ghid_own = grad_hidden.reshape(row_count, 2, 2304).transpose(1, 0, 2)
    two_own = jnp.stack([attn_in.T, mixed_rows.T]).reshape(16, 144, row_count)
    gqkv_own = jnp.stack(
        [grad_qkv[:, :2304], jnp.concatenate([grad_qkv[:, 2304:], grad_attn], axis=1)]
    )
    operands = []
    for array in (act_own, grad_branch, mlp_own, ghid_own, two_own, gqkv_own):
        operands += [array, wide(array)]
    sum_qkv, sum_proj, sum_fc1, sum_fc2 = reduce_grads(operands)
    totals = lax.psum(
        (
            slice_qv,
            slice_proj,
            slice_fc1,
            slice_fc2,
            grad_w_ada,
            grad_b_ada,
            slice_w_t1,
            slice_b_t1,
            slice_w_t2,
            slice_b_t2,
            grad_table,
        ),
        "group",
    )
    rest = totals
    return (
        block_out,
        input_grad,
        sum_qkv,
        rest[0],
        sum_proj,
        rest[1],
        sum_fc1,
        rest[2],
        sum_fc2,
        rest[3],
        rest[4],
        rest[5],
        rest[6],
        rest[7],
        rest[8],
        rest[9],
        rest[10],
    )


def solution(mesh):
    placed = (
        P(("group", "dp"), None),
        P(("group", "dp"), None),
        P("group"),
        P("group"),
        P("group"),
        P(),
        P(),
        P(),
        P(),
        P(),
        P(),
        P(),
        P(),
        P(None, "dp"),
        P("dp"),
        P(),
        P(),
        P(),
        P(),
        P(),
    )
    return jax.shard_map(
        on_device,
        mesh=mesh,
        in_specs=placed,
        out_specs=(
            P(("group", "dp"), None),
            P(("group", "dp"), None),
            P("dp", None),
            P("dp"),
            P("dp", None),
            P("dp"),
            P("dp", None),
            P("dp"),
            P("dp", None),
            P("dp"),
            P(None, "dp"),
            P("dp"),
            P("dp", None),
            P("dp"),
            P("dp", None),
            P("dp"),
            P(),
        ),
        check_vma=False,
    )
```

```python
import functools
import math

import jax
import jax.numpy as jnp
from jax import lax
from jax.experimental import pallas as pl
from jax.experimental.pallas import tpu as pltpu
from jax.sharding import PartitionSpec as P

HEADS = 16
SLOTS = 256
ITEM_FRAMES = 16


EPS = 1e-06
NEG = -1e30


def hdot(left_op, right_op):
    return jnp.dot(
        left_op, right_op, precision=lax.Precision.HIGHEST, preferred_element_type=jnp.float32
    )


def hdot_t(left_op, right_op):
    return lax.dot_general(
        left_op,
        right_op,
        (((0,), (0,)), ((), ())),
        precision=lax.Precision.HIGHEST,
        preferred_element_type=jnp.float32,
    )


def weight_term(left_op, right_op):
    return lax.dot_general(
        left_op, right_op, (((0,), (0,)), ((), ())), preferred_element_type=jnp.float32
    )


def norm_rows(matrix):
    row_mean = jnp.mean(matrix, axis=-1, keepdims=True)
    centered = matrix - row_mean
    inv_std = lax.rsqrt(jnp.mean(centered * centered, axis=-1, keepdims=True) + EPS)
    return (centered * inv_std, inv_std)


def norm_back(grad_in, normed, inv_std):
    return inv_std * (
        grad_in
        - jnp.mean(grad_in, axis=-1, keepdims=True)
        - normed * jnp.mean(grad_in * normed, axis=-1, keepdims=True)
    )


def silu_back(pre_vals, grad_in):
    sigmoid = jax.nn.sigmoid(pre_vals)
    return grad_in * sigmoid * (1.0 + pre_vals * (1.0 - sigmoid))


def time_embed(step_ids, width_half):
    frequency = jnp.exp(
        jnp.arange(width_half, dtype=jnp.float32) * (-math.log(10000.0) / width_half)
    )
    angles = step_ids.astype(jnp.float32)[:, None] * frequency[None, :]
    return jnp.concatenate([jnp.cos(angles), jnp.sin(angles)], axis=1)


def own_block(vector, dp_place, dp_count):
    block_rows = vector.shape[0] // dp_count
    return lax.dynamic_slice_in_dim(vector, dp_place * block_rows, block_rows, 0)


MESH = pl.DeviceIdType.MESH
ORDERS = (("y", "z", "x"), ("z", "x", "y"), ("x", "y", "z"))
STREAMS = tuple((order, pairing) for pairing in (0, 1) for order in ORDERS)
BLOCKS = (32, 16, 8, 4, 2, 1)
LANDS_AT = (0, 32, 48, 56, 60, 62)
PIECE = 56
OWN = 72


def coords():
    place = lax.axis_index("dp")
    return {
        "y": lax.axis_index("group"),
        "z": lax.div(place, 8),
        "x": lax.rem(lax.div(place, 2), 4),
        "core": lax.rem(place, 2),
    }


def device_at(at):
    return (at["y"], (at["z"] * 4 + at["x"]) * 2 + at["core"])


def sibling_of(at):
    return device_at({**at, "core": 1 - at["core"]})


def partner_of(at, axis, pairing):
    here = at[axis]
    if pairing == 0:
        there = here + 1 - 2 * lax.rem(here, 2)
    else:
        there = lax.rem(here + 3 + 2 * lax.rem(here, 2), 4)
    return device_at({**at, axis: there})


def slot_of(pairing, value):
    if pairing == 1:
        return value
    if isinstance(value, int):
        return (0, 2, 3, 1)[value]
    return lax.rem(value + lax.div(value + 1, 2), 4)


def grad_kernel(
    act_own,
    act_wide,
    gbr_own,
    gbr_wide,
    mlp_own,
    mlp_wide,
    ghid_own,
    ghid_wide,
    two_own,
    two_wide,
    gqkv_own,
    gqkv_wide,
    out_qkv,
    out_proj,
    out_fc1,
    out_fc2,
    parts,
    landed,
    lhs,
    rhs,
    stage_lhs,
    stage_rhs,
    final,
    other,
    send_sem,
    recv_sem,
    credit,
    swap_send,
    swap_recv,
    swap_credit,
    own_sem,
    ring_send,
    ring_recv,
    pair_send,
    pair_recv,
):
    at = coords()
    core = at["core"]
    sibling = sibling_of(at)
    barrier = pltpu.get_barrier_semaphore()
    peers = [partner_of(at, axis, pairing) for axis in "xyz" for pairing in (0, 1)]
    peers.append(device_at({**at, "y": lax.rem(at["y"] + 2, 4)}))
    peers.append(sibling)
    for peer in peers:
        pl.semaphore_signal(barrier, inc=1, device_id=peer, device_id_type=MESH)
    pl.semaphore_wait(barrier, len(peers))

    def swap(phase):
        if phase == 0:
            pairs = [(act_wide.at[1 - core], stage_lhs), (gbr_wide, stage_rhs.at[:, 0:1152])]
        elif phase == 1:
            pairs = [(mlp_wide, stage_lhs.at[0:8]), (ghid_wide.at[1 - core], stage_rhs)]
        else:
            pairs = [(two_wide, stage_lhs), (gqkv_wide.at[1 - core], stage_rhs)]
        return [
            pltpu.make_async_remote_copy(
                src_ref=source,
                dst_ref=target,
                send_sem=swap_send.at[place],
                recv_sem=swap_recv.at[place],
                device_id=sibling,
                device_id_type=MESH,
            )
            for place, (source, target) in enumerate(pairs)
        ]

    def own_loads(phase):
        if phase == 0:
            pairs = [
                (act_own.at[core], lhs.at[:, :, 0:256]),
                (gbr_own, rhs.at[0:256, 0:1152]),
            ]
        elif phase == 1:
            pairs = [
                (mlp_own, lhs.at[0:8, :, 0:256]),
                (ghid_own.at[core], rhs.at[0:256]),
            ]
        else:
            pairs = [
                (two_own, lhs.at[:, :, 0:256]),
                (gqkv_own.at[core], rhs.at[0:256]),
            ]
        return [
            pltpu.make_async_copy(source, target, own_sem.at[place])
            for place, (source, target) in enumerate(pairs)
        ]

    def swap_start(phase):
        if phase:
            pl.semaphore_wait(swap_credit, 1)
        for copy in swap(phase):
            copy.start()

    def swap_finish(phase):
        for copy in own_loads(phase):
            copy.start()
        for copy in swap(phase):
            copy.wait()

        def narrow_lhs(step, _):
            lhs[step, :, 256:512] = stage_lhs[step].astype(jnp.bfloat16)
            return _

        lax.fori_loop(0, 8 if phase == 1 else 16, narrow_lhs, 0)
        wide = 1152 if phase == 0 else 2304

        def narrow_rhs(step, _):
            rows = pl.ds(pl.multiple_of(step * 32, 32), 32)
            into = pl.ds(pl.multiple_of(256 + step * 32, 32), 32)
            rhs[into, 0:wide] = stage_rhs[rows, 0:wide].astype(jnp.bfloat16)
            return _

        lax.fori_loop(0, 8, narrow_rhs, 0)
        if phase < 2:
            pl.semaphore_signal(swap_credit, inc=1, device_id=sibling, device_id_type=MESH)
        for copy in own_loads(phase):
            copy.wait()

    def base_of(stream, z_place, x_place, y_slot):
        order, pairing = STREAMS[stream]
        slots = {"y": y_slot, "z": slot_of(pairing, z_place), "x": slot_of(pairing, x_place)}
        return (slots[order[0]] * 4 + slots[order[1]]) * 4 + slots[order[2]]

    def keep(half, stream, chip, rows):
        z_place, x_place = lax.div(chip, 4), lax.rem(chip, 4)
        for y_slot in range(4):
            block = base_of(stream, z_place, x_place, y_slot)
            first = y_slot * PIECE
            for unit in range(3):
                low, high = max(first, OWN * unit), min(first + PIECE, OWN * unit + OWN)
                if low < high:
                    parts[half, stream, block, low - first : high - first, :] = rows[
                        low - OWN * unit : high - OWN * unit, unit * 128 : unit * 128 + 128
                    ]

    def halving(phase, stream, step):
        order, pairing = STREAMS[stream]
        axis = order[step // 2]
        slots = [slot_of(pairing, at[name]) for name in order]
        base = 0
        for level in range(step // 2):
            base = base + slots[level] * (64 // 4 ** (level + 1))
        slot = slots[step // 2]
        side = lax.div(slot, 2) if step % 2 == 0 else slot
        away = 1 - side if step % 2 == 0 else slot + 1 - 2 * lax.rem(slot, 2)
        count = BLOCKS[step]
        kept, sent = base + side * count, base + away * count
        partner = partner_of(at, axis, pairing if step % 2 == 0 else 1 - pairing)
        copy = pltpu.make_async_remote_copy(
            src_ref=parts.at[phase % 2, stream, pl.ds(sent, count)],
            dst_ref=landed.at[stream, pl.ds(LANDS_AT[step], count)],
            send_sem=send_sem.at[stream, step],
            recv_sem=recv_sem.at[stream, step],
            device_id=partner,
            device_id_type=MESH,
        )
        return copy, kept, partner

    def send(phase, stream, step):
        copy, _, _ = halving(phase, stream, step)
        if phase:
            pl.semaphore_wait(credit.at[stream, step], 1)
        copy.start()

    def receive(phase, step):
        for stream in range(6):
            copy, kept, partner = halving(phase, stream, step)
            copy.wait()
            half = phase % 2
            count = BLOCKS[step]
            if step < 5:

                def add(block, _):
                    parts[half, stream, kept + block] += landed[stream, LANDS_AT[step] + block]
                    return _

                lax.fori_loop(0, count, add, 0, unroll=min(count, 4))
            else:
                final[phase, at["y"], stream] = (
                    parts[half, stream, kept] + landed[stream, LANDS_AT[step]]
                )
            if phase < 2:
                pl.semaphore_signal(
                    credit.at[stream, step], inc=1, device_id=partner, device_id_type=MESH
                )
            if step < 5:
                send(phase, stream, step + 1)

    def products(phase):
        half = phase % 2
        if phase == 0:
            for third in range(3):

                def pair(chip, _):
                    rows = jnp.dot(
                        lhs[chip],
                        rhs[:, third * 384 : third * 384 + 384],
                        preferred_element_type=jnp.float32,
                    )
                    keep(half, third, chip, rows[0:72])
                    keep(half, third + 3, chip, rows[72:144])
                    return _

                lax.fori_loop(0, 16, pair, 0)
                send(phase, third, 0)
                send(phase, third + 3, 0)
            return
        for stream in range(6):
            shift = core * 8 if phase == 2 and stream >= 3 else 0

            def duo(pair_at, _):
                rows = jnp.dot(
                    lhs[pair_at + shift],
                    rhs[:, stream * 384 : stream * 384 + 384],
                    preferred_element_type=jnp.float32,
                )
                keep(half, stream, pair_at * 2, rows[0:72])
                keep(half, stream, pair_at * 2 + 1, rows[72:144])
                return _

            lax.fori_loop(0, 8, duo, 0)
            send(phase, stream, 0)

    def ring(phase):
        return [
            pltpu.make_async_remote_copy(
                src_ref=final.at[phase, at["y"]],
                dst_ref=final.at[phase, at["y"]],
                send_sem=ring_send.at[phase, hop - 1],
                recv_sem=ring_recv.at[phase, hop - 1],
                device_id=device_at({**at, "y": lax.rem(at["y"] + hop, 4)}),
                device_id_type=MESH,
            )
            for hop in (1, 2, 3)
        ]

    def across(phase):
        return pltpu.make_async_remote_copy(
            src_ref=final.at[phase],
            dst_ref=other.at[phase - 1],
            send_sem=pair_send.at[phase - 1],
            recv_sem=pair_recv.at[phase - 1],
            device_id=sibling,
            device_id_type=MESH,
        )

    def whole(get, stream):
        pairing = STREAMS[stream][1]
        order = sorted(range(4), key=lambda y_place: slot_of(pairing, y_place))
        return jnp.concatenate([get(y_place, stream) for y_place in order], axis=0)

    def write_rows(phase, low):
        for side in range(2):
            mine = side == (0 if low == 0 else 1)
            for stream in range(6):
                if mine:
                    rows = whole(lambda y_place, stream: final[phase, y_place, stream], stream)
                else:
                    rows = whole(lambda y_place, stream: other[phase - 1, y_place, stream], stream)
                for unit in range(3):
                    block = rows[OWN * unit + low : OWN * unit + low + 36]
                    column = side * 18 + stream * 3 + unit
                    if phase == 1:
                        out_fc1[:, column * 128 : column * 128 + 128] = block
                    elif column < 27:
                        out_qkv[:, column * 128 : column * 128 + 128] = block
                    else:
                        out_proj[:, (column - 27) * 128 : (column - 27) * 128 + 128] = block

    def write(phase):
        if phase == 0:
            for stream in range(6):
                rows = whole(lambda y_place, stream: final[0, y_place, stream], stream)
                half, third = stream // 3, stream % 3
                for unit in range(3):
                    column = third * 3 + unit
                    out_fc2[half * 72 : half * 72 + 72, column * 128 : column * 128 + 128] = rows[
                        OWN * unit : OWN * unit + 72
                    ]
            return

        @pl.when(core == 0)
        def _():
            write_rows(phase, 0)

        @pl.when(core == 1)
        def _():
            write_rows(phase, 36)

    def ring_start(phase):
        for copy in ring(phase):
            copy.start()

    def ring_finish(phase):
        for copy in ring(phase):
            copy.wait()
        if phase:
            across(phase).start()

    def clear(block, _):
        for half in range(2):
            for stream in range(6):
                z_place, x_place = lax.div(block, 4), lax.rem(block, 4)
                parts[half, stream, base_of(stream, z_place, x_place, 3), 48:56, :] = jnp.zeros(
                    (8, 128), jnp.float32
                )
        return _

    swap_start(0)
    lax.fori_loop(0, 16, clear, 0)
    swap_finish(0)
    products(0)
    swap_start(1)
    swap_finish(1)
    receive(0, 0)
    products(1)
    swap_start(2)
    swap_finish(2)
    receive(0, 1)
    receive(0, 2)
    receive(0, 3)
    receive(1, 0)
    receive(0, 4)
    receive(0, 5)
    ring_start(0)
    products(2)
    receive(1, 1)
    receive(1, 2)
    ring_finish(0)
    write(0)
    receive(1, 3)
    receive(1, 4)
    receive(2, 0)
    receive(1, 5)
    ring_start(1)
    receive(2, 1)
    ring_finish(1)
    receive(2, 2)
    receive(2, 3)
    across(1).wait()
    write(1)
    receive(2, 4)
    receive(2, 5)
    ring_start(2)
    ring_finish(2)
    across(2).wait()
    write(2)


def reduce_grads(operands):
    dma = pltpu.SemaphoreType.DMA
    regular = pltpu.SemaphoreType.REGULAR
    vmem = pl.BlockSpec(memory_space=pltpu.VMEM)
    return pl.pallas_call(
        grad_kernel,
        out_shape=(
            jax.ShapeDtypeStruct((36, 3456), jnp.float32),
            jax.ShapeDtypeStruct((36, 1152), jnp.float32),
            jax.ShapeDtypeStruct((36, 4608), jnp.float32),
            jax.ShapeDtypeStruct((144, 1152), jnp.float32),
        ),
        in_specs=[pl.BlockSpec(memory_space=pl.ANY)] * 12,
        out_specs=(vmem, vmem, vmem, vmem),
        scratch_shapes=[
            pltpu.VMEM((2, 6, 64, PIECE, 128), jnp.float32),
            pltpu.VMEM((6, 63, PIECE, 128), jnp.float32),
            pltpu.VMEM((16, 144, 512), jnp.bfloat16),
            pltpu.VMEM((512, 2304), jnp.bfloat16),
            pltpu.VMEM((16, 144, 256), jnp.float32),
            pltpu.VMEM((256, 2304), jnp.float32),
            pltpu.VMEM((3, 4, 6, PIECE, 128), jnp.float32),
            pltpu.VMEM((2, 4, 6, PIECE, 128), jnp.float32),
            dma((6, 6)),
            dma((6, 6)),
            regular((6, 6)),
            dma((2,)),
            dma((2,)),
            regular,
            dma((2,)),
            dma((3, 3)),
            dma((3, 3)),
            dma((2,)),
            dma((2,)),
        ],
        compiler_params=pltpu.CompilerParams(
            collective_id=1, has_side_effects=True, vmem_limit_bytes=60 * 2**20
        ),
    )(*operands)


def split_three(values):
    high = values.astype(jnp.bfloat16)
    rest = values - high.astype(jnp.float32)
    middle = rest.astype(jnp.bfloat16)
    low = (rest - middle.astype(jnp.float32)).astype(jnp.bfloat16)
    return jnp.concatenate([high, middle, low], axis=0)


def exact_dot(values, weights, contract=0):
    rows = values.shape[0]
    thrice = lax.dot_general(
        split_three(values),
        weights,
        (((1,), (contract,)), ((), ())),
        preferred_element_type=jnp.float32,
    )
    return thrice[0:rows] + thrice[rows : 2 * rows] + thrice[2 * rows : 3 * rows]


def silu(values):
    return values / (1.0 + jnp.exp(-values))


def greet(peers):
    barrier = pltpu.get_barrier_semaphore()
    for peer in peers:
        pl.semaphore_signal(barrier, inc=1, device_id=peer, device_id_type=MESH)
    pl.semaphore_wait(barrier, len(peers))


def dp_peer(hop):
    return (lax.axis_index("group"), lax.rem(lax.axis_index("dp") + hop, 32))


def front_kernel(
    feats, w_t1, b_t1, w_t2, b_t2, rows_table, w_ada, b_ada, pre_out, cond_out, mods, mine, send, recv
):
    place = lax.axis_index("dp")
    barrier = pltpu.get_barrier_semaphore()

    def hello(hop, _):
        pl.semaphore_signal(barrier, inc=1, device_id=dp_peer(hop), device_id_type=MESH)
        return _

    lax.fori_loop(1, 32, hello, 0)
    pre_time = exact_dot(feats[...], w_t1[...]) + b_t1[...]
    condition = exact_dot(silu(pre_time), w_t2[...]) + b_t2[...] + rows_table[...]
    mod_part = exact_dot(silu(condition), w_ada[...]) + b_ada[...]
    pre_out[...] = pre_time
    cond_out[...] = condition
    for item in range(2):
        mine[item, :, 0:216] = mod_part[item : item + 1]
        mine[item, :, 216:256] = jnp.zeros((1, 40), jnp.float32)
    mods[place] = mine[lax.div(place, 16)]
    pl.semaphore_wait(barrier, 31)

    def copy_to(hop):
        target = lax.rem(place + hop, 32)
        return pltpu.make_async_remote_copy(
            src_ref=mine.at[lax.div(target, 16)],
            dst_ref=mods.at[place],
            send_sem=send.at[hop],
            recv_sem=recv.at[hop],
            device_id=dp_peer(hop),
            device_id_type=MESH,
        )

    def begin(hop, _):
        copy_to(hop).start()
        return _

    def finish(hop, _):
        copy_to(hop).wait()
        return _

    lax.fori_loop(1, 32, begin, 0)
    lax.fori_loop(1, 32, finish, 0)


def front(feats, w_t1, b_t1, w_t2, b_t2, rows_table, w_ada, b_ada):
    vmem = pl.BlockSpec(memory_space=pltpu.VMEM)
    width = w_t2.shape[0]
    return pl.pallas_call(
        front_kernel,
        out_shape=(
            jax.ShapeDtypeStruct((2, width), jnp.float32),
            jax.ShapeDtypeStruct((2, width), jnp.float32),
            jax.ShapeDtypeStruct((32, 1, 256), jnp.float32),
        ),
        in_specs=[vmem] * 8,
        out_specs=(vmem, vmem, vmem),
        scratch_shapes=[
            pltpu.VMEM((2, 1, 256), jnp.float32),
            pltpu.SemaphoreType.DMA((32,)),
            pltpu.SemaphoreType.DMA((32,)),
        ],
        compiler_params=pltpu.CompilerParams(
            collective_id=2, has_side_effects=True, vmem_limit_bytes=32 * 2**20
        ),
    )(feats, w_t1, b_t1[None], w_t2, b_t2[None], rows_table, w_ada, b_ada[None])


PACK = 4 * 1152 + 2 * 256 + 128


def tail_kernel(
    shares,
    w_ada,
    w_t2,
    pre_in,
    cond_in,
    feats,
    onehot,
    packs,
    sums,
    got,
    conds,
    packed,
    sums_all,
    send,
    recv,
    cond_send,
    cond_recv,
    group_send,
    group_recv,
):
    place = lax.axis_index("dp")
    group = lax.axis_index("group")
    barrier = pltpu.get_barrier_semaphore()

    def group_peer(hop):
        return (lax.rem(group + hop, 4), place)

    def hello(hop, _):
        pl.semaphore_signal(barrier, inc=1, device_id=dp_peer(hop), device_id_type=MESH)
        return _

    lax.fori_loop(1, 32, hello, 0)
    for hop in (1, 2, 3):
        pl.semaphore_signal(barrier, inc=1, device_id=group_peer(hop), device_id_type=MESH)
    got[place] = shares[place]
    pl.semaphore_wait(barrier, 34)

    def share_to(hop):
        return pltpu.make_async_remote_copy(
            src_ref=shares.at[lax.rem(place + hop, 32)],
            dst_ref=got.at[place],
            send_sem=send.at[hop],
            recv_sem=recv.at[hop],
            device_id=dp_peer(hop),
            device_id_type=MESH,
        )

    def cond_to(hop):
        return pltpu.make_async_remote_copy(
            src_ref=conds.at[place],
            dst_ref=conds.at[place],
            send_sem=cond_send.at[hop],
            recv_sem=cond_recv.at[hop],
            device_id=dp_peer(hop),
            device_id_type=MESH,
        )

    def each(make, act):
        def one(hop, _):
            act(make(hop))
            return _

        lax.fori_loop(1, 32, one, 0)

    each(share_to, lambda copy: copy.start())
    each(share_to, lambda copy: copy.wait())
    first, second = got[0], got[16]
    for source in range(1, 16):
        first = first + got[source]
        second = second + got[16 + source]
    d_mod = jnp.concatenate(
        [
            jnp.concatenate([first[0:1], first[1:2]], axis=1),
            jnp.concatenate([second[0:1], second[1:2]], axis=1),
        ],
        axis=0,
    )
    conds[place] = exact_dot(d_mod[:, 0:216], w_ada[...], 1)
    each(cond_to, lambda copy: copy.start())
    pre_time, condition = pre_in[...], cond_in[...]
    packed[group, :, 2304:3456] = silu(condition)
    packed[group, :, 3456:4608] = silu(pre_time)
    packed[group, :, 4608:4864] = d_mod
    packed[group, :, 4864:5120] = feats[...]
    packed[group, :, 5120:5248] = onehot[...]
    sums_all[group] = first + second
    each(cond_to, lambda copy: copy.wait())
    total = conds[0]
    for source in range(1, 32):
        total = total + conds[source]
    grad_cond = silu_back(condition, total)
    packed[group, :, 0:1152] = grad_cond
    packed[group, :, 1152:2304] = silu_back(pre_time, exact_dot(grad_cond, w_t2[...], 1))

    def group_copies(hop):
        return [
            pltpu.make_async_remote_copy(
                src_ref=buffer.at[group],
                dst_ref=buffer.at[group],
                send_sem=group_send.at[side, hop],
                recv_sem=group_recv.at[side, hop],
                device_id=group_peer(hop),
                device_id_type=MESH,
            )
            for side, buffer in enumerate((packed, sums_all))
        ]

    for hop in (1, 2, 3):
        for copy in group_copies(hop):
            copy.start()
    for hop in (1, 2, 3):
        for copy in group_copies(hop):
            copy.wait()
    packs[...] = packed[...]
    sums[...] = sums_all[0] + sums_all[1] + sums_all[2] + sums_all[3]


def tail(shares, w_ada, w_t2, pre_time, condition, feats, onehot):
    vmem = pl.BlockSpec(memory_space=pltpu.VMEM)
    dma = pltpu.SemaphoreType.DMA
    return pl.pallas_call(
        tail_kernel,
        out_shape=(
            jax.ShapeDtypeStruct((4, 2, PACK), jnp.float32),
            jax.ShapeDtypeStruct((8, 128), jnp.float32),
        ),
        in_specs=[vmem] * 7,
        out_specs=(vmem, vmem),
        scratch_shapes=[
            pltpu.VMEM((32, 8, 128), jnp.float32),
            pltpu.VMEM((32, 2, 1152), jnp.float32),
            pltpu.VMEM((4, 2, PACK), jnp.float32),
            pltpu.VMEM((4, 8, 128), jnp.float32),
            dma((32,)),
            dma((32,)),
            dma((32,)),
            dma((32,)),
            dma((2, 4)),
            dma((2, 4)),
        ],
        compiler_params=pltpu.CompilerParams(
            collective_id=3, has_side_effects=True, vmem_limit_bytes=32 * 2**20
        ),
    )(shares, w_ada, w_t2, pre_time, condition, feats, onehot)


def on_device(
    tokens,
    out_grad,
    timesteps,
    labels,
    grid_ids,
    w_qkv,
    b_qv,
    w_proj,
    b_proj,
    w_fc1,
    b_fc1,
    w_fc2,
    b_fc2,
    w_ada,
    b_ada,
    w_t1,
    b_t1,
    w_t2,
    b_t2,
    table,
):
    dp_count = lax.axis_size("dp")
    dp_place = lax.axis_index("dp")
    row_count, model_width = tokens.shape
    frame_count = row_count // SLOTS
    head_count = HEADS
    head_dim = model_width // head_count
    score_scale = 1.0 / math.sqrt(head_dim)
    frame_shape = (frame_count, SLOTS, head_count, head_dim)
    time_feats = time_embed(timesteps, w_t1.shape[0] // 2)
    onehot = (labels[:, None] == jnp.arange(128, dtype=jnp.int32)[None, :]).astype(jnp.float32)
    pre_time, condition, mods = front(
        time_feats, w_t1, b_t1, w_t2, b_t2, table[labels], w_ada, b_ada
    )
    item_mod = mods.reshape(32, 256)[:, :216].reshape(6 * model_width)
    own_item = dp_place * frame_count // ITEM_FRAMES
    shift_attn, scale_attn, gate_attn, shift_mlp, scale_mlp, gate_mlp = jnp.split(item_mod, 6)
    grid_value = lax.dynamic_index_in_dim(grid_ids, own_item, 0, keepdims=False)
    first_live = jnp.where(grid_value == 2, SLOTS // 16, 0)
    end_live = jnp.where(grid_value == 1, SLOTS - SLOTS // 16, SLOTS)
    slot_pos = jnp.arange(SLOTS, dtype=jnp.int32)
    valid_keys = (slot_pos >= first_live) & (slot_pos < end_live)
    live_rows = jnp.tile(valid_keys, frame_count).astype(jnp.float32)[:, None]
    token_vals = tokens.astype(jnp.float32)
    normed_one, inv_one = norm_rows(token_vals)
    attn_in = (normed_one * (1.0 + scale_attn) + shift_attn).astype(jnp.bfloat16)
    qkv_rows = jnp.dot(attn_in, w_qkv, preferred_element_type=jnp.float32)
    queries = (
        (qkv_rows[:, :model_width] + b_qv[:model_width]).astype(jnp.bfloat16).reshape(frame_shape)
    )
    key_rows = qkv_rows[:, model_width : 2 * model_width].astype(jnp.bfloat16).reshape(frame_shape)
    values = (
        (qkv_rows[:, 2 * model_width :] + b_qv[model_width:])
        .astype(jnp.bfloat16)
        .reshape(frame_shape)
    )

    def masked_scores():
        raw = (
            jnp.einsum("fqhd,fkhd->fhqk", queries, key_rows, preferred_element_type=jnp.float32)
            * score_scale
        )
        return jnp.where(valid_keys[None, None, None, :], raw, NEG)

    scores = masked_scores()
    row_max = jnp.max(scores, axis=-1, keepdims=True)
    shifted = jnp.exp(scores - row_max)
    row_total = jnp.sum(shifted, axis=-1, keepdims=True)
    log_total = row_max + jnp.log(row_total)
    attn_weights = (shifted / row_total).astype(jnp.bfloat16)
    mixed = jnp.einsum("fhqk,fkhd->fqhd", attn_weights, values, preferred_element_type=jnp.float32)
    mixed_rows = mixed.reshape(row_count, model_width).astype(jnp.bfloat16)
    attn_out = jnp.dot(mixed_rows, w_proj, preferred_element_type=jnp.float32) + b_proj
    resid_one = token_vals + gate_attn * attn_out
    normed_two, inv_two = norm_rows(resid_one)
    mlp_in = (normed_two * (1.0 + scale_mlp) + shift_mlp).astype(jnp.bfloat16)
    hidden = jnp.dot(mlp_in, w_fc1, preferred_element_type=jnp.float32) + b_fc1
    gelu_vals, gelu_pull = jax.vjp(functools.partial(jax.nn.gelu, approximate=True), hidden)
    activated = gelu_vals.astype(jnp.bfloat16)
    branch = jnp.dot(activated, w_fc2, preferred_element_type=jnp.float32) + b_fc2
    block_out = (resid_one + gate_mlp * branch).astype(jnp.bfloat16)
    cotangent = out_grad.astype(jnp.float32) * live_rows
    d_gate_mlp = jnp.sum(cotangent * branch, axis=0)
    grad_branch = (cotangent * gate_mlp).astype(jnp.bfloat16)
    grad_act = jnp.dot(grad_branch, w_fc2.T, preferred_element_type=jnp.float32)
    grad_hidden = gelu_pull(grad_act)[0].astype(jnp.bfloat16)
    grad_mlp_in = jnp.dot(grad_hidden, w_fc1.T, preferred_element_type=jnp.float32)
    d_shift_mlp = jnp.sum(grad_mlp_in, axis=0)
    d_scale_mlp = jnp.sum(grad_mlp_in * normed_two, axis=0)
    grad_resid = cotangent + norm_back(grad_mlp_in * (1.0 + scale_mlp), normed_two, inv_two)
    d_gate_attn = jnp.sum(grad_resid * attn_out, axis=0)
    grad_attn = (grad_resid * gate_attn).astype(jnp.bfloat16)
    grad_mixed = (
        jnp.dot(grad_attn, w_proj.T, preferred_element_type=jnp.float32)
        .astype(jnp.bfloat16)
        .reshape(frame_shape)
    )
    probs_again = jnp.exp(masked_scores() - log_total)
    grad_weights = jnp.einsum(
        "fqhd,fkhd->fhqk", grad_mixed, values, preferred_element_type=jnp.float32
    )
    row_dot = jnp.sum(probs_again * grad_weights, axis=-1, keepdims=True)
    grad_scores = (probs_again * (grad_weights - row_dot)).astype(jnp.bfloat16)
    grad_query = (
        jnp.einsum("fhqk,fkhd->fqhd", grad_scores, key_rows, preferred_element_type=jnp.float32)
        * score_scale
    )
    grad_key = (
        jnp.einsum("fhqk,fqhd->fkhd", grad_scores, queries, preferred_element_type=jnp.float32)
        * score_scale
    )
    grad_value = jnp.einsum(
        "fhqk,fqhd->fkhd",
        probs_again.astype(jnp.bfloat16),
        grad_mixed,
        preferred_element_type=jnp.float32,
    )
    grad_qkv = jnp.concatenate(
        [
            grad_query.reshape(row_count, model_width),
            grad_key.reshape(row_count, model_width),
            grad_value.reshape(row_count, model_width),
        ],
        axis=1,
    ).astype(jnp.bfloat16)
    grad_attn_in = jnp.dot(grad_qkv, w_qkv.T, preferred_element_type=jnp.float32)
    d_shift_attn = jnp.sum(grad_attn_in, axis=0)
    d_scale_attn = jnp.sum(grad_attn_in * normed_one, axis=0)
    input_grad = (
        grad_resid + norm_back(grad_attn_in * (1.0 + scale_attn), normed_one, inv_one)
    ).astype(jnp.bfloat16)
    bias_qv = jnp.concatenate(
        [
            jnp.sum(grad_qkv[:, :model_width], axis=0, dtype=jnp.float32),
            jnp.sum(grad_qkv[:, 2 * model_width :], axis=0, dtype=jnp.float32),
        ]
    )
    bias_proj = jnp.sum(grad_attn, axis=0, dtype=jnp.float32)
    bias_fc1 = jnp.sum(grad_hidden, axis=0, dtype=jnp.float32)
    bias_fc2 = jnp.sum(grad_branch, axis=0, dtype=jnp.float32)
    d_mod_item = jnp.concatenate(
        [d_shift_attn, d_scale_attn, d_gate_attn, d_shift_mlp, d_scale_mlp, d_gate_mlp]
    )
    shares = jnp.concatenate(
        [
            jnp.pad(d_mod_item.reshape(32, 216), ((0, 0), (0, 40))).reshape(32, 2, 128),
            jnp.pad(bias_qv.reshape(32, 1, 72), ((0, 0), (0, 0), (0, 56))),
            jnp.pad(bias_proj.reshape(32, 1, 36), ((0, 0), (0, 0), (0, 92))),
            jnp.pad(bias_fc1.reshape(32, 144), ((0, 0), (0, 112))).reshape(32, 2, 128),
            jnp.pad(bias_fc2.reshape(32, 1, 36), ((0, 0), (0, 0), (0, 92))),
            jnp.zeros((32, 1, 128), jnp.float32),
        ],
        axis=1,
    )
    wide = lambda array: array.astype(jnp.float32)
    act_own = activated.T.reshape(16, 2, 144, row_count).transpose(1, 0, 2, 3)
    mlp_own = mlp_in.T.reshape(8, 144, row_count)
    ghid_own = grad_hidden.reshape(row_count, 2, 2304).transpose(1, 0, 2)
    two_own = jnp.stack([attn_in.T, mixed_rows.T]).reshape(16, 144, row_count)
    gqkv_own = jnp.stack(
        [grad_qkv[:, :2304], jnp.concatenate([grad_qkv[:, 2304:], grad_attn], axis=1)]
    )
    operands = []
    for array in (act_own, grad_branch, mlp_own, ghid_own, two_own, gqkv_own):
        operands += [array, wide(array)]
    sum_qkv, sum_proj, sum_fc1, sum_fc2 = reduce_grads(operands)
    packs, sums = tail(shares, w_ada, w_t2, pre_time, condition, time_feats, onehot)
    packs = packs.reshape(8, PACK)
    grad_cond, grad_pre = packs[:, 0:1152], packs[:, 1152:2304]
    act_cond, act_time = packs[:, 2304:3456], packs[:, 3456:4608]
    d_mod, feats_all = packs[:, 4608:4824], packs[:, 4864:5120]
    class_rows = packs[:, 5120 : 5120 + table.shape[0]]
    own_time = lax.dynamic_slice_in_dim(act_time, dp_place * 36, 36, 1)
    own_feats = lax.dynamic_slice_in_dim(feats_all, dp_place * 8, 8, 1)
    return (
        block_out,
        input_grad,
        sum_qkv,
        sums[2, 0:72],
        sum_proj,
        sums[3, 0:36],
        sum_fc1,
        sums[4:6].reshape(256)[0:144],
        sum_fc2,
        sums[6, 0:36],
        hdot_t(act_cond, d_mod),
        jnp.sum(d_mod, axis=0),
        hdot_t(own_feats, grad_pre),
        own_block(jnp.sum(grad_pre, axis=0), dp_place, dp_count),
        hdot_t(own_time, grad_cond),
        own_block(jnp.sum(grad_cond, axis=0), dp_place, dp_count),
        hdot_t(class_rows, grad_cond),
    )


def solution(mesh):
    placed = (
        P(("group", "dp"), None),
        P(("group", "dp"), None),
        P("group"),
        P("group"),
        P("group"),
        P(),
        P(),
        P(),
        P(),
        P(),
        P(),
        P(),
        P(),
        P(None, "dp"),
        P("dp"),
        P(),
        P(),
        P(),
        P(),
        P(),
    )
    return jax.shard_map(
        on_device,
        mesh=mesh,
        in_specs=placed,
        out_specs=(
            P(("group", "dp"), None),
            P(("group", "dp"), None),
            P("dp", None),
            P("dp"),
            P("dp", None),
            P("dp"),
            P("dp", None),
            P("dp"),
            P("dp", None),
            P("dp"),
            P(None, "dp"),
            P("dp"),
            P("dp", None),
            P("dp"),
            P("dp", None),
            P("dp"),
            P(),
        ),
        check_vma=False,
    )
```

```python
import functools
import math

import jax
import jax.numpy as jnp
from jax import lax
from jax.experimental import pallas as pl
from jax.experimental.pallas import tpu as pltpu
from jax.sharding import PartitionSpec as P

HEADS = 16
SLOTS = 256
ITEM_FRAMES = 16


EPS = 1e-06
NEG = -1e30


def hdot(left_op, right_op):
    return jnp.dot(
        left_op, right_op, precision=lax.Precision.HIGHEST, preferred_element_type=jnp.float32
    )


def hdot_t(left_op, right_op):
    return lax.dot_general(
        left_op,
        right_op,
        (((0,), (0,)), ((), ())),
        precision=lax.Precision.HIGHEST,
        preferred_element_type=jnp.float32,
    )


def weight_term(left_op, right_op):
    return lax.dot_general(
        left_op, right_op, (((0,), (0,)), ((), ())), preferred_element_type=jnp.float32
    )


def norm_rows(matrix):
    row_mean = jnp.mean(matrix, axis=-1, keepdims=True)
    centered = matrix - row_mean
    inv_std = lax.rsqrt(jnp.mean(centered * centered, axis=-1, keepdims=True) + EPS)
    return (centered * inv_std, inv_std)


def norm_back(grad_in, normed, inv_std):
    return inv_std * (
        grad_in
        - jnp.mean(grad_in, axis=-1, keepdims=True)
        - normed * jnp.mean(grad_in * normed, axis=-1, keepdims=True)
    )


def silu_back(pre_vals, grad_in):
    sigmoid = jax.nn.sigmoid(pre_vals)
    return grad_in * sigmoid * (1.0 + pre_vals * (1.0 - sigmoid))


def time_embed(step_ids, width_half):
    frequency = jnp.exp(
        jnp.arange(width_half, dtype=jnp.float32) * (-math.log(10000.0) / width_half)
    )
    angles = step_ids.astype(jnp.float32)[:, None] * frequency[None, :]
    return jnp.concatenate([jnp.cos(angles), jnp.sin(angles)], axis=1)


def own_block(vector, dp_place, dp_count):
    block_rows = vector.shape[0] // dp_count
    return lax.dynamic_slice_in_dim(vector, dp_place * block_rows, block_rows, 0)


def split_three(values):
    high = values.astype(jnp.bfloat16)
    rest = values - high.astype(jnp.float32)
    middle = rest.astype(jnp.bfloat16)
    low = (rest - middle.astype(jnp.float32)).astype(jnp.bfloat16)
    return jnp.concatenate([high, middle, low], axis=0)


def exact_dot(values, weights, contract=0):
    rows = values.shape[0]
    thrice = lax.dot_general(
        split_three(values),
        weights,
        (((1,), (contract,)), ((), ())),
        preferred_element_type=jnp.float32,
    )
    return thrice[0:rows] + thrice[rows : 2 * rows] + thrice[2 * rows : 3 * rows]


def silu(values):
    return values / (1.0 + jnp.exp(-values))


def dot_nn(left, right):
    return jnp.dot(left, right, preferred_element_type=jnp.float32)


def dot_nt(left, right):
    return lax.dot_general(
        left, right, (((1,), (1,)), ((), ())), preferred_element_type=jnp.float32
    )


def dot_tn(left, right):
    return lax.dot_general(
        left, right, (((0,), (0,)), ((), ())), preferred_element_type=jnp.float32
    )


MESH = pl.DeviceIdType.MESH
ORDERS = ((("y", "z", "x"), ("z", "x", "y"), ("x", "y", "z")),) * 3
STREAMS = tuple(
    tuple((order, pairing) for pairing in (0, 1) for order in orders) for orders in ORDERS
)
BLOCKS = (32, 16, 8, 4, 2, 1)
LANDS_AT = (0, 32, 48, 56, 60, 62)
PIECE = 56
OWN = 72
CHUNK = 384
ROWS = 32
WINDOWS = ((0, 216, 3), (54, 72, 2), (72, 36, 2), (81, 144, 3), (117, 36, 2))


def coords():
    place = lax.axis_index("dp")
    return {
        "y": lax.axis_index("group"),
        "z": lax.div(place, 8),
        "x": lax.rem(lax.div(place, 2), 4),
        "core": lax.rem(place, 2),
    }


def device_at(at):
    return (at["y"], (at["z"] * 4 + at["x"]) * 2 + at["core"])


def dp_peer(hop):
    return (lax.axis_index("group"), lax.rem(lax.axis_index("dp") + hop, 32))


def sibling_of(at):
    return device_at({**at, "core": 1 - at["core"]})


def partner_of(at, axis, pairing):
    here = at[axis]
    if pairing == 0:
        there = here + 1 - 2 * lax.rem(here, 2)
    else:
        there = lax.rem(here + 3 + 2 * lax.rem(here, 2), 4)
    return device_at({**at, axis: there})


def slot_of(pairing, value):
    if pairing == 1:
        return value
    if isinstance(value, int):
        return (0, 2, 3, 1)[value]
    return lax.rem(value + lax.div(value + 1, 2), 4)


PACK = 4 * 1152 + 2 * 256 + 128


def backward_kernel(
    act_split,
    act_wide,
    act_flat,
    slope,
    gbr_own,
    gbr_wide,
    mlp_own,
    mlp_wide,
    two_own,
    two_wide,
    heads,
    bias_keys,
    cot,
    resid,
    attn_out,
    tokens,
    mods,
    b_fc2,
    pre_in,
    cond_in,
    feats,
    onehot,
    w_ada,
    w_t2,
    w_qkv,
    w_proj,
    w_fc1,
    w_fc2,
    out_qkv,
    out_proj,
    out_fc1,
    out_fc2,
    block_out,
    input_grad,
    packed,
    sums,
    parts,
    landed,
    lhs,
    rhs,
    stage_lhs,
    stage_rhs,
    leave,
    final,
    other,
    narrow,
    d_mod,
    bias_fc1,
    bias_qv,
    bias_proj,
    bias_fc2,
    flat,
    shares,
    got,
    conds,
    sums_all,
    out_rows,
    in_rows,
    wa,
    wb,
    slope_in,
    act_in,
    grad_t,
    branch,
    grad_resid,
    all_t,
    mixed_t,
    heads_in,
    rows_a,
    rows_b,
    rows_c,
    rows_d,
    send_sem,
    recv_sem,
    credit,
    swap_send,
    swap_recv,
    swap_credit,
    own_sem,
    ring_send,
    ring_recv,
    pair_send,
    pair_recv,
    load_sem,
    row_sem,
    head_sem,
    other_credit,
    out_sem,
    share_send,
    share_recv,
    cond_send,
    cond_recv,
    group_send,
    group_recv,
):
    at = coords()
    core = at["core"]
    sibling = sibling_of(at)
    barrier = pltpu.get_barrier_semaphore()
    place = lax.axis_index("dp")

    def group_peer(hop):
        return (lax.rem(at["y"] + hop, 4), place)

    def hello(hop, _):
        pl.semaphore_signal(barrier, inc=1, device_id=dp_peer(hop), device_id_type=MESH)
        return _

    lax.fori_loop(1, 32, hello, 0)
    for hop in (1, 2, 3):
        pl.semaphore_signal(barrier, inc=1, device_id=group_peer(hop), device_id_type=MESH)
    pl.semaphore_wait(barrier, 34)

    def swap(phase):
        if phase == 0:
            pairs = [
                (act_wide.at[:, 1 - core], stage_lhs),
                (gbr_wide, stage_rhs.at[0:1152]),
            ]
        elif phase == 1:
            pairs = [(mlp_wide, stage_lhs.at[0:8]), (leave, stage_rhs)]
        else:
            pairs = [(two_wide, stage_lhs), (leave, stage_rhs)]
        return [
            pltpu.make_async_remote_copy(
                src_ref=source,
                dst_ref=target,
                send_sem=swap_send.at[place],
                recv_sem=swap_recv.at[place],
                device_id=sibling,
                device_id_type=MESH,
            )
            for place, (source, target) in enumerate(pairs)
        ]

    def own_loads(phase):
        if phase == 0:
            pairs = [
                (act_split.at[:, core], lhs.at[:, :, 0:256]),
                (gbr_own, rhs.at[0:1152, 0:256]),
            ]
        elif phase == 1:
            pairs = [(mlp_own, lhs.at[0:8, :, 0:256])]
        else:
            pairs = [(two_own, lhs.at[:, :, 0:256])]
        return [
            pltpu.make_async_copy(source, target, own_sem.at[place])
            for place, (source, target) in enumerate(pairs)
        ]

    def swap_start(phase):
        if phase:
            pl.semaphore_wait(swap_credit, 1)
        for copy in swap(phase):
            copy.start()

    def swap_finish(phase):
        for copy in own_loads(phase):
            copy.start()
        for copy in swap(phase):
            copy.wait()

        def narrow_lhs(step, _):
            lhs[step, :, 256:512] = stage_lhs[step].astype(jnp.bfloat16)
            return _

        lax.fori_loop(0, 8 if phase == 1 else 16, narrow_lhs, 0)

        def narrow_rhs(step, _):
            rows = pl.ds(pl.multiple_of(step * 144, 144), 144)
            rhs[rows, 256:512] = stage_rhs[rows, :].astype(jnp.bfloat16)
            return _

        lax.fori_loop(0, 8 if phase == 0 else 16, narrow_rhs, 0)
        if phase < 2:
            pl.semaphore_signal(swap_credit, inc=1, device_id=sibling, device_id_type=MESH)
        for copy in own_loads(phase):
            copy.wait()

    def base_of(phase, stream, z_place, x_place, y_slot):
        order, pairing = STREAMS[phase][stream]
        slots = {"y": y_slot, "z": slot_of(pairing, z_place), "x": slot_of(pairing, x_place)}
        return (slots[order[0]] * 4 + slots[order[1]]) * 4 + slots[order[2]]

    def keep(phase, stream, chip, rows):
        half = phase % 2
        z_place, x_place = lax.div(chip, 4), lax.rem(chip, 4)
        for y_slot in range(4):
            block = base_of(phase, stream, z_place, x_place, y_slot)
            first = y_slot * PIECE
            for unit in range(3):
                low, high = max(first, OWN * unit), min(first + PIECE, OWN * unit + OWN)
                if low < high:
                    parts[half, stream, block, low - first : high - first, :] = rows[
                        low - OWN * unit : high - OWN * unit, unit * 128 : unit * 128 + 128
                    ]

    def halving(phase, stream, step):
        order, pairing = STREAMS[phase][stream]
        axis = order[step // 2]
        slots = [slot_of(pairing, at[name]) for name in order]
        base = 0
        for level in range(step // 2):
            base = base + slots[level] * (64 // 4 ** (level + 1))
        slot = slots[step // 2]
        side = lax.div(slot, 2) if step % 2 == 0 else slot
        away = 1 - side if step % 2 == 0 else slot + 1 - 2 * lax.rem(slot, 2)
        count = BLOCKS[step]
        kept, sent = base + side * count, base + away * count
        partner = partner_of(at, axis, pairing if step % 2 == 0 else 1 - pairing)
        source = parts.at[phase % 2, stream]
        if phase == 0 and step >= 3:
            origin = slots[0] * 16 + lax.div(slots[1], 2) * 8
            kept, sent = kept - origin, sent - origin
            source = narrow.at[stream]
        copy = pltpu.make_async_remote_copy(
            src_ref=source.at[pl.ds(sent, count)],
            dst_ref=landed.at[stream, pl.ds(LANDS_AT[step], count)],
            send_sem=send_sem.at[stream, step],
            recv_sem=recv_sem.at[stream, step],
            device_id=partner,
            device_id_type=MESH,
        )
        return copy, kept, partner

    def send(phase, stream, step):
        copy, _, _ = halving(phase, stream, step)
        if phase:
            pl.semaphore_wait(credit.at[stream, step], 1)
        copy.start()

    def receive(phase, step):
        for stream in range(6):
            copy, kept, partner = halving(phase, stream, step)
            copy.wait()
            half = phase % 2
            count = BLOCKS[step]
            late = phase == 0 and step >= 3
            if step < 5:

                def add(block, _):
                    arrived = landed[stream, LANDS_AT[step] + block]
                    if late:
                        narrow[stream, kept + block] += arrived
                    elif phase == 0 and step == 2:
                        narrow[stream, block] = parts[half, stream, kept + block] + arrived
                    else:
                        parts[half, stream, kept + block] += arrived
                    return _

                lax.fori_loop(0, count, add, 0, unroll=min(count, 4))
            else:
                mine = narrow[stream, kept] if late else parts[half, stream, kept]
                final[phase, at["y"], stream] = mine + landed[stream, LANDS_AT[step]]
            if phase < 2:
                pl.semaphore_signal(
                    credit.at[stream, step], inc=1, device_id=partner, device_id_type=MESH
                )
            if step < 5:
                send(phase, stream, step + 1)

    def products(phase):
        together, stacked = (3, 2) if phase == 2 else (2, 4)
        for group in range(6 // together):
            members = range(group * together, (group + 1) * together)
            if phase == 0:
                first = group * together // 2 * CHUNK
                width = together // 2 * CHUNK
                count = 16
            else:
                first = members[0] * CHUNK
                width = together * CHUNK
                count = 8
            shift = core * 8 if phase == 2 and members[0] >= 3 else 0

            def some(step, _):
                left = lhs[pl.ds(step * stacked + shift, stacked)]
                rows = dot_nt(
                    left.reshape(stacked * 144, 512), rhs[first : first + width, :]
                )
                for place in range(stacked):
                    at_row = place * 144
                    if phase == 0:
                        chip = step * stacked + place
                        for third in range(together // 2):
                            column = third * CHUNK
                            block = rows[at_row : at_row + 144, column : column + CHUNK]
                            stream = group * together // 2 + third
                            keep(phase, stream, chip, block[0:72])
                            keep(phase, stream + 3, chip, block[72:144])
                    else:
                        chip = (step * stacked + place) * 2
                        for place_at, stream in enumerate(members):
                            column = place_at * CHUNK
                            block = rows[at_row : at_row + 144, column : column + CHUNK]
                            keep(phase, stream, chip, block[0:72])
                            keep(phase, stream, chip + 1, block[72:144])
                return _

            lax.fori_loop(0, count // stacked, some, 0)
            for member in members:
                stream = member
                if phase == 0:
                    stream = group * together // 2 + (member - members[0]) // 2
                    stream += 3 * ((member - members[0]) % 2)
                send(phase, stream, 0)

    def ring(phase):
        mine = at["y"]
        copies = []
        for place, hop in enumerate((1, 3)):
            copies.append(
                pltpu.make_async_remote_copy(
                    src_ref=final.at[phase, mine],
                    dst_ref=final.at[phase, mine],
                    send_sem=ring_send.at[phase, place],
                    recv_sem=ring_recv.at[phase, place],
                    device_id=device_at({**at, "y": lax.rem(mine + hop, 4)}),
                    device_id_type=MESH,
                )
            )
        return copies

    def relay(phase):
        mine = at["y"]
        copies = []
        for place, hop in enumerate((1, 3)):
            origin = lax.rem(mine + 4 - hop, 4)
            half = pl.ds(place * 3, 3)
            copies.append(
                pltpu.make_async_remote_copy(
                    src_ref=final.at[phase, origin, half],
                    dst_ref=final.at[phase, origin, half],
                    send_sem=ring_send.at[phase, place + 2],
                    recv_sem=ring_recv.at[phase, place + 2],
                    device_id=device_at({**at, "y": lax.rem(mine + hop, 4)}),
                    device_id_type=MESH,
                )
            )
        return copies

    def across(phase):
        return pltpu.make_async_remote_copy(
            src_ref=final.at[phase],
            dst_ref=other,
            send_sem=pair_send.at[phase - 1],
            recv_sem=pair_recv.at[phase - 1],
            device_id=sibling,
            device_id_type=MESH,
        )

    def whole(get, stream):
        pairing = STREAMS[0][stream][1]
        order = sorted(range(4), key=lambda y_place: slot_of(pairing, y_place))
        return jnp.concatenate([get(y_place, stream) for y_place in order], axis=0)

    def write_rows(phase, low):
        for side in range(2):
            mine = side == (0 if low == 0 else 1)
            for stream in range(6):
                if mine:
                    rows = whole(lambda y_place, stream: final[phase, y_place, stream], stream)
                else:
                    rows = whole(lambda y_place, stream: other[y_place, stream], stream)
                for unit in range(3):
                    block = rows[OWN * unit + low : OWN * unit + low + 36]
                    column = side * 18 + stream * 3 + unit
                    if phase == 1:
                        out_fc1[:, column * 128 : column * 128 + 128] = block
                    elif column < 27:
                        out_qkv[:, column * 128 : column * 128 + 128] = block
                    else:
                        out_proj[:, (column - 27) * 128 : (column - 27) * 128 + 128] = block

    def write(phase):
        if phase == 0:
            for stream in range(6):
                rows = whole(lambda y_place, stream: final[0, y_place, stream], stream)
                half, third = stream // 3, stream % 3
                for unit in range(3):
                    column = third * 3 + unit
                    out_fc2[half * 72 : half * 72 + 72, column * 128 : column * 128 + 128] = rows[
                        OWN * unit : OWN * unit + 72
                    ]
            return

        @pl.when(core == 0)
        def _():
            write_rows(phase, 0)

        @pl.when(core == 1)
        def _():
            write_rows(phase, 36)

        if phase == 1:
            pl.semaphore_signal(other_credit, inc=1, device_id=sibling, device_id_type=MESH)

    def ring_start(phase):
        for copy in ring(phase):
            copy.start()

    def ring_relay(phase):
        for copy, onward in zip(ring(phase), relay(phase)):
            copy.wait()
            onward.start()

    def ring_finish(phase):
        for copy in relay(phase):
            copy.wait()
        if phase == 2:
            pl.semaphore_wait(other_credit, 1)
        if phase:
            across(phase).start()

    def clear(chip, _):
        z_place, x_place = lax.div(chip, 4), lax.rem(chip, 4)
        for half in range(2):
            for stream in range(6):
                block = base_of(half, stream, z_place, x_place, 3)
                parts[half, stream, block, 48:56, :] = jnp.zeros((8, 128), jnp.float32)
        return _

    ones = jnp.ones((8, 256), jnp.bfloat16)

    def mlp_loads(chunk):
        slot = lax.rem(chunk, 2)
        rows = pl.ds(pl.multiple_of(chunk * CHUNK, CHUNK), CHUNK)
        return [
            pltpu.make_async_copy(w_fc2.at[rows], wa.at[slot], load_sem.at[0, slot]),
            pltpu.make_async_copy(w_fc1.at[:, rows], wb.at[slot], load_sem.at[1, slot]),
            pltpu.make_async_copy(slope.at[rows], slope_in.at[slot], load_sem.at[2, slot]),
            pltpu.make_async_copy(act_flat.at[rows], act_in.at[slot], load_sem.at[3, slot]),
        ]

    def mlp_begin():
        for copy in mlp_loads(0):
            copy.start()

    def mlp_backward(low, high):
        if low == 0:
            rhs[0:1152, 256:512] = rhs[0:1152, 0:256]
            grad_t[...] = jnp.zeros((1152, 256), jnp.float32)
            branch[...] = jnp.zeros((256, 1152), jnp.float32)

        def chunk_step(chunk, carry):
            slot = lax.rem(chunk, 2)

            @pl.when(chunk < 11)
            def _():
                for copy in mlp_loads(chunk + 1):
                    copy.start()

            for copy in mlp_loads(chunk):
                copy.wait()
            grad_act = dot_nn(wa[slot], rhs[0:1152, 256:512])
            grad_hidden = (grad_act * slope_in[slot].astype(jnp.float32)).astype(jnp.bfloat16)
            side = lax.div(chunk, 6)
            rows = pl.ds(pl.multiple_of(lax.rem(chunk, 6) * CHUNK, CHUNK), CHUNK)

            @pl.when(side == core)
            def _():
                rhs[rows, 0:256] = grad_hidden

            @pl.when(side != core)
            def _():
                leave[rows, :] = grad_hidden.astype(jnp.float32)

            columns = pl.ds(pl.multiple_of(chunk * CHUNK, CHUNK), CHUNK)
            bias_fc1[:, columns] = dot_nt(ones, grad_hidden)[0:1]
            grad_t[...] += dot_nn(wb[slot], grad_hidden)
            branch[...] += dot_tn(act_in[slot], wa[slot])
            return carry

        lax.fori_loop(low, high, chunk_step, 0)

    def row_block(source, index):
        return source.at[pl.ds(pl.multiple_of(index * ROWS, ROWS), ROWS)]

    def norm(values):
        mean = jnp.mean(values, axis=-1, keepdims=True)
        centered = values - mean
        inverse = lax.rsqrt(jnp.mean(centered * centered, axis=-1, keepdims=True) + EPS)
        return centered * inverse, inverse

    def total(values):
        return jnp.sum(values, axis=0, keepdims=True)

    def middle_loads(index):
        slot = lax.rem(index, 2)
        return [
            pltpu.make_async_copy(row_block(source, index), target.at[slot], row_sem.at[place, slot])
            for place, (source, target) in enumerate(
                ((cot, rows_a), (resid, rows_b), (attn_out, rows_c))
            )
        ]

    def token_load(index):
        slot = lax.rem(index, 2)
        return pltpu.make_async_copy(
            row_block(tokens, index), rows_d.at[slot], row_sem.at[3, slot]
        )

    def proj_load(chunk):
        slot = lax.rem(chunk, 2)
        rows = pl.ds(pl.multiple_of(chunk * 288, 288), 288)
        return pltpu.make_async_copy(w_proj.at[rows], wa.at[slot, 0:288], load_sem.at[0, slot])

    def rows_out(kind, index):
        slot = lax.rem(index, 2)
        target = block_out if kind == 0 else input_grad
        buffer = out_rows if kind == 0 else in_rows
        return pltpu.make_async_copy(
            buffer.at[slot], row_block(target, index), out_sem.at[kind, slot]
        )

    def drain(kind):
        rows_out(kind, 256 // ROWS - 2).wait()
        rows_out(kind, 256 // ROWS - 1).wait()

    def middle_begin():
        for copy in middle_loads(0):
            copy.start()
        proj_load(0).start()
        d_mod[...] = jnp.zeros((8, 1152), jnp.float32)
        bias_proj[...] = jnp.zeros((1, 1152), jnp.float32)
        bias_fc2[...] = jnp.zeros((1, 1152), jnp.float32)
        grad_resid[...] = grad_t[...].T

    def middle_rows(low, high):
        scale_mlp, gate_mlp = mods[4:5], mods[5:6]
        gate_attn = mods[2:3]

        def rows_step(index, carry):
            rows = pl.ds(pl.multiple_of(index * ROWS, ROWS), ROWS)
            slot = lax.rem(index, 2)

            @pl.when(index < 256 // ROWS - 1)
            def _():
                for copy in middle_loads(index + 1):
                    copy.start()

            for copy in middle_loads(index):
                copy.wait()

            @pl.when(index >= 2)
            def _():
                rows_out(0, index - 2).wait()

            cotangent, stream_rows = rows_a[slot], rows_b[slot]
            branch_rows = branch[rows, :] + b_fc2[...]
            out_rows[slot] = (stream_rows + gate_mlp * branch_rows).astype(jnp.bfloat16)
            rows_out(0, index).start()
            d_mod[5:6, :] += total(cotangent * branch_rows)
            bias_fc2[...] += total(
                (cotangent * gate_mlp).astype(jnp.bfloat16).astype(jnp.float32)
            )
            normed, inverse = norm(stream_rows)
            grad_in = grad_resid[rows, :]
            d_mod[3:4, :] += total(grad_in)
            d_mod[4:5, :] += total(grad_in * normed)
            back = norm_back(grad_in * (1.0 + scale_mlp), normed, inverse)
            grads = cotangent + back
            grad_resid[rows, :] = grads
            d_mod[2:3, :] += total(grads * rows_c[slot])
            grad_attn = (grads * gate_attn).astype(jnp.bfloat16).astype(jnp.float32)
            bias_proj[...] += total(grad_attn)
            branch[rows, :] = grad_attn
            return carry

        lax.fori_loop(low, high, rows_step, 0)

    def middle_end():
        all_t[3456:4608, :] = branch[...].T.astype(jnp.bfloat16)

        def proj_step(chunk, carry):
            @pl.when(chunk < 3)
            def _():
                proj_load(chunk + 1).start()

            proj_load(chunk).wait()
            grads = dot_nn(wa[lax.rem(chunk, 2), 0:288], all_t[3456:4608, :])
            for head in range(4):
                padded = jnp.concatenate(
                    [grads[head * 72 : head * 72 + 72], jnp.zeros((8, 256), jnp.float32)], axis=0
                )
                mixed_t[chunk * 4 + head] = padded.astype(jnp.bfloat16)
            return carry

        lax.fori_loop(0, 4, proj_step, 0)

    def heads_load(pair_at):
        slot = lax.rem(pair_at, 2)
        return [
            pltpu.make_async_copy(
                heads.at[pl.ds(part * 16 + pair_at * 2, 2)],
                heads_in.at[slot, part],
                head_sem.at[part, slot],
            )
            for part in range(3)
        ]

    def attention_backward(low, high):
        scale = 1.0 / math.sqrt(72)

        def one_head(pair_at, side):
            slot = lax.rem(pair_at, 2)
            query, key, value = (heads_in[slot, part, side] for part in range(3))
            grad_mixed = mixed_t[pair_at * 2 + side]
            scores = dot_tn(key, query) * scale + jnp.concatenate([bias_keys[...]] * 2, axis=1)
            shifted = jnp.exp(scores - jnp.max(scores, axis=0, keepdims=True))
            weights = shifted / jnp.sum(shifted, axis=0, keepdims=True)
            grad_weights = dot_tn(value, grad_mixed)
            row_dot = jnp.sum(weights * grad_weights, axis=0, keepdims=True)
            grad_scores = (weights * (grad_weights - row_dot)).astype(jnp.bfloat16)
            return (
                dot_nn(key, grad_scores)[0:72] * scale,
                dot_nt(query, grad_scores)[0:72] * scale,
                dot_nt(grad_mixed, weights.astype(jnp.bfloat16))[0:72],
            )

        def two_heads(pair_at, carry):
            @pl.when(pair_at < 7)
            def _():
                for copy in heads_load(pair_at + 1):
                    copy.start()

            for copy in heads_load(pair_at):
                copy.wait()
            first, second = one_head(pair_at, 0), one_head(pair_at, 1)
            for part in range(3):
                rows = pl.ds(pl.multiple_of(part * 1152 + pair_at * 144, 16), 144)
                all_t[rows, :] = jnp.concatenate([first[part], second[part]], axis=0).astype(
                    jnp.bfloat16
                )
            return carry

        lax.fori_loop(low, high, two_heads, 0)

    def sides():
        def side(step, _):
            mine = pl.ds(pl.multiple_of(core * 2304 + step * 144, 16), 144)
            theirs = pl.ds(pl.multiple_of((1 - core) * 2304 + step * 144, 16), 144)
            rows = pl.ds(pl.multiple_of(step * 144, 144), 144)
            rhs[rows, 0:256] = all_t[mine, :]
            leave[rows, :] = all_t[theirs, :].astype(jnp.float32)
            return _

        lax.fori_loop(0, 16, side, 0)

    def qkv_load(chunk):
        slot = lax.rem(chunk, 2)
        columns = pl.ds(pl.multiple_of(chunk * CHUNK, CHUNK), CHUNK)
        return pltpu.make_async_copy(w_qkv.at[:, columns], wb.at[slot], load_sem.at[1, slot])

    def last_columns(low, high):
        if low == 0:
            grad_t[...] = jnp.zeros((1152, 256), jnp.float32)
            token_load(0).start()

        def qkv_step(chunk, carry):
            @pl.when(chunk < 8)
            def _():
                qkv_load(chunk + 1).start()

            qkv_load(chunk).wait()
            rows = pl.ds(pl.multiple_of(chunk * CHUNK, CHUNK), CHUNK)
            grads = all_t[rows, :]
            grad_t[...] += dot_nn(wb[lax.rem(chunk, 2)], grads)
            bias_qv[:, rows] = dot_nt(ones, grads)[0:1]
            return carry

        lax.fori_loop(low, high, qkv_step, 0)

    def ada_load():
        return pltpu.make_async_copy(w_ada, wb.at[0, :, 0:256], load_sem.at[1, 0])

    def last_rows():
        ada_load().start()
        branch[...] = grad_t[...].T
        scale_attn = mods[1:2]

        def last_step(index, carry):
            rows = pl.ds(pl.multiple_of(index * ROWS, ROWS), ROWS)
            slot = lax.rem(index, 2)

            @pl.when(index < 256 // ROWS - 1)
            def _():
                token_load(index + 1).start()

            token_load(index).wait()

            @pl.when(index >= 2)
            def _():
                rows_out(1, index - 2).wait()

            normed, inverse = norm(rows_d[slot].astype(jnp.float32))
            grad_in = branch[rows, :]
            d_mod[0:1, :] += total(grad_in)
            d_mod[1:2, :] += total(grad_in * normed)
            back = norm_back(grad_in * (1.0 + scale_attn), normed, inverse)
            in_rows[slot] = (grad_resid[rows, :] + back).astype(jnp.bfloat16)
            rows_out(1, index).start()
            return carry

        lax.fori_loop(0, 256 // ROWS, last_step, 0)

    def share_to(hop):
        return pltpu.make_async_remote_copy(
            src_ref=shares.at[lax.rem(place + hop, 32)],
            dst_ref=got.at[place],
            send_sem=share_send.at[hop],
            recv_sem=share_recv.at[hop],
            device_id=dp_peer(hop),
            device_id_type=MESH,
        )

    def cond_to(hop):
        return pltpu.make_async_remote_copy(
            src_ref=conds.at[place],
            dst_ref=conds.at[place],
            send_sem=cond_send.at[hop],
            recv_sem=cond_recv.at[hop],
            device_id=dp_peer(hop),
            device_id_type=MESH,
        )

    def group_copies(hop):
        return [
            pltpu.make_async_remote_copy(
                src_ref=buffer.at[at["y"]],
                dst_ref=buffer.at[at["y"]],
                send_sem=group_send.at[side, hop],
                recv_sem=group_recv.at[side, hop],
                device_id=group_peer(hop),
                device_id_type=MESH,
            )
            for side, buffer in enumerate((packed, sums_all))
        ]

    def each(make, act):
        def one(hop, _):
            act(make(hop))
            return _

        lax.fori_loop(1, 32, one, 0)

    def tail_share():
        vectors = [d_mod[row : row + 1] for row in range(6)]
        vectors += [bias_qv[0:1, 0:1152], bias_qv[0:1, 2304:3456]]
        vectors += [bias_proj[...], bias_fc1[0:1, :], bias_fc2[...]]
        row = 0
        for vector in vectors:
            for column in range(vector.shape[1] // 128):
                flat[row] = vector[:, column * 128 : column * 128 + 128]
                row += 1
        flat[126] = jnp.zeros((1, 128), jnp.float32)
        flat[127] = jnp.zeros((1, 128), jnp.float32)

        def window(peer, _):
            into = 0
            for first, width, count in WINDOWS:
                start = first + lax.div(peer * width, 128)
                for offset in range(count):
                    shares[peer, into] = flat[start + offset]
                    into += 1
            return _

        lax.fori_loop(0, 32, window, 0)
        got[place] = shares[place]
        each(share_to, lambda copy: copy.start())

    def tail_cond():
        each(share_to, lambda copy: copy.wait())
        first, second = got[0], got[16]
        for source in range(1, 16):
            first = first + got[source]
            second = second + got[16 + source]

        def piece(rows, entry):
            begin = sum(count for _, _, count in WINDOWS[:entry])
            _, width, count = WINDOWS[entry]
            joined = jnp.concatenate([rows[begin + step] for step in range(count)], axis=1)
            joined = jnp.concatenate([joined] * 8, axis=0)
            shift = lax.rem(place * width, 128)
            moved = pltpu.roll(joined, lax.rem(count * 128 - shift, count * 128), 1)
            return moved[0:1]

        d_mod_own = jnp.concatenate([piece(first, 0), piece(second, 0)], axis=0)[:, 0:256]
        ada_load().wait()
        conds[place] = exact_dot(d_mod_own[:, 0:216], wb[0, :, 0:216], 1)
        each(cond_to, lambda copy: copy.start())
        for chunk in range(2):
            t2_load(chunk).start()
        both = first + second
        sums_all[at["y"], 0:1] = piece(both, 1)[:, 0:128]
        sums_all[at["y"], 1:2] = piece(both, 2)[:, 0:128]
        wide = piece(both, 3)
        sums_all[at["y"], 2:3] = wide[:, 0:128]
        sums_all[at["y"], 3:4] = wide[:, 128:256]
        sums_all[at["y"], 4:5] = piece(both, 4)[:, 0:128]
        sums_all[at["y"], 5:8] = jnp.zeros((3, 128), jnp.float32)
        packed[at["y"], :, 2304:3456] = silu(cond_in[...])
        packed[at["y"], :, 3456:4608] = silu(pre_in[...])
        packed[at["y"], :, 4608:4864] = d_mod_own
        packed[at["y"], :, 4864:5120] = feats[...]
        packed[at["y"], :, 5120:5248] = onehot[...]

    def t2_load(chunk):
        rows = pl.ds(chunk * CHUNK, CHUNK)
        return pltpu.make_async_copy(w_t2.at[rows], wa.at[chunk % 2], load_sem.at[0, chunk % 2])

    def tail_group():
        each(cond_to, lambda copy: copy.wait())
        total_cond = conds[0]
        for source in range(1, 32):
            total_cond = total_cond + conds[source]
        grad_cond = silu_back(cond_in[...], total_cond)
        packed[at["y"], :, 0:1152] = grad_cond
        for chunk in range(3):
            t2_load(chunk).wait()
            columns = exact_dot(grad_cond, wa[chunk % 2], 1)
            if chunk == 0:
                t2_load(2).start()
            begin = chunk * CHUNK
            packed[at["y"], :, 1152 + begin : 1152 + begin + CHUNK] = silu_back(
                pre_in[:, begin : begin + CHUNK], columns
            )
        for hop in (1, 2, 3):
            for copy in group_copies(hop):
                copy.start()

    def tail_end():
        for hop in (1, 2, 3):
            for copy in group_copies(hop):
                copy.wait()
        sums[...] = sums_all[0] + sums_all[1] + sums_all[2] + sums_all[3]

    swap_start(0)
    mlp_begin()
    for copy in heads_load(0):
        copy.start()
    lax.fori_loop(0, 16, clear, 0)
    swap_finish(0)
    products(0)
    mlp_backward(0, 4)
    mlp_backward(4, 8)
    mlp_backward(8, 12)
    swap_start(1)
    middle_begin()
    middle_rows(0, 4)
    receive(0, 0)
    middle_rows(4, 8)
    middle_end()
    swap_finish(1)
    products(1)
    qkv_load(0).start()
    attention_backward(0, 4)
    receive(0, 1)
    attention_backward(4, 8)
    sides()
    swap_start(2)
    last_columns(0, 5)
    last_columns(5, 9)
    receive(1, 0)
    swap_finish(2)
    receive(0, 2)
    products(2)
    last_rows()
    tail_share()
    receive(1, 1)
    receive(0, 3)
    tail_cond()
    receive(2, 0)
    receive(1, 2)
    receive(0, 4)
    tail_group()
    receive(2, 1)
    receive(1, 3)
    receive(0, 5)
    ring_start(0)
    receive(2, 2)
    receive(1, 4)
    ring_relay(0)
    receive(2, 3)
    receive(1, 5)
    ring_start(1)
    ring_finish(0)
    write(0)
    tail_end()
    receive(2, 4)
    ring_relay(1)
    receive(2, 5)
    ring_start(2)
    ring_finish(1)
    across(1).wait()
    write(1)
    ring_relay(2)
    drain(0)
    drain(1)
    ring_finish(2)
    across(2).wait()
    write(2)


def backward(operands):
    dma = pltpu.SemaphoreType.DMA
    regular = pltpu.SemaphoreType.REGULAR
    vmem = pl.BlockSpec(memory_space=pltpu.VMEM)
    anywhere = pl.BlockSpec(memory_space=pl.ANY)
    full = jnp.float32
    small = jnp.bfloat16
    return pl.pallas_call(
        backward_kernel,
        out_shape=(
            jax.ShapeDtypeStruct((36, 3456), full),
            jax.ShapeDtypeStruct((36, 1152), full),
            jax.ShapeDtypeStruct((36, 4608), full),
            jax.ShapeDtypeStruct((144, 1152), full),
            jax.ShapeDtypeStruct((256, 1152), small),
            jax.ShapeDtypeStruct((256, 1152), small),
            jax.ShapeDtypeStruct((4, 2, PACK), full),
            jax.ShapeDtypeStruct((8, 128), full),
        ),
        in_specs=[anywhere] * 11 + [vmem] + [anywhere] * 4 + [vmem] * 6 + [anywhere] * 6,
        out_specs=(vmem,) * 4 + (anywhere,) * 2 + (vmem,) * 2,
        scratch_shapes=[
            pltpu.VMEM((2, 6, 64, PIECE, 128), full),
            pltpu.VMEM((6, 63, PIECE, 128), full),
            pltpu.VMEM((16, 144, 512), small),
            pltpu.VMEM((2304, 512), small),
            pltpu.VMEM((16, 144, 256), full),
            pltpu.VMEM((2304, 256), full),
            pltpu.VMEM((2304, 256), full),
            pltpu.VMEM((3, 4, 6, PIECE, 128), full),
            pltpu.VMEM((4, 6, PIECE, 128), full),
            pltpu.VMEM((6, 8, PIECE, 128), full),
            pltpu.VMEM((8, 1152), full),
            pltpu.VMEM((1, 4608), full),
            pltpu.VMEM((1, 3456), full),
            pltpu.VMEM((1, 1152), full),
            pltpu.VMEM((1, 1152), full),
            pltpu.VMEM((128, 1, 128), full),
            pltpu.VMEM((32, 12, 1, 128), full),
            pltpu.VMEM((32, 12, 1, 128), full),
            pltpu.VMEM((32, 2, 1152), full),
            pltpu.VMEM((4, 8, 128), full),
            pltpu.VMEM((2, ROWS, 1152), small),
            pltpu.VMEM((2, ROWS, 1152), small),
            pltpu.VMEM((2, CHUNK, 1152), small),
            pltpu.VMEM((2, 1152, CHUNK), small),
            pltpu.VMEM((2, CHUNK, 256), small),
            pltpu.VMEM((2, CHUNK, 256), small),
            pltpu.VMEM((1152, 256), full),
            pltpu.VMEM((256, 1152), full),
            pltpu.VMEM((256, 1152), full),
            pltpu.VMEM((4608, 256), small),
            pltpu.VMEM((16, 80, 256), small),
            pltpu.VMEM((2, 3, 2, 80, 256), small),
            pltpu.VMEM((2, ROWS, 1152), full),
            pltpu.VMEM((2, ROWS, 1152), full),
            pltpu.VMEM((2, ROWS, 1152), full),
            pltpu.VMEM((2, ROWS, 1152), small),
            dma((6, 6)),
            dma((6, 6)),
            regular((6, 6)),
            dma((2,)),
            dma((2,)),
            regular,
            dma((2,)),
            dma((3, 4)),
            dma((3, 4)),
            dma((2,)),
            dma((2,)),
            dma((4, 2)),
            dma((4, 2)),
            dma((3, 2)),
            regular,
            dma((2, 2)),
            dma((32,)),
            dma((32,)),
            dma((32,)),
            dma((32,)),
            dma((2, 4)),
            dma((2, 4)),
        ],
        compiler_params=pltpu.CompilerParams(
            collective_id=1, has_side_effects=True, vmem_limit_bytes=255 * 2**18
        ),
    )(*operands)


def front_kernel(
    feats, w_t1, b_t1, w_t2, b_t2, rows_table, w_ada, b_ada, pre_out, cond_out, mods, mine, send, recv
):
    place = lax.axis_index("dp")
    barrier = pltpu.get_barrier_semaphore()

    def hello(hop, _):
        pl.semaphore_signal(barrier, inc=1, device_id=dp_peer(hop), device_id_type=MESH)
        return _

    lax.fori_loop(1, 32, hello, 0)
    pre_time = exact_dot(feats[...], w_t1[...]) + b_t1[...]
    condition = exact_dot(silu(pre_time), w_t2[...]) + b_t2[...] + rows_table[...]
    mod_part = exact_dot(silu(condition), w_ada[...]) + b_ada[...]
    pre_out[...] = pre_time
    cond_out[...] = condition
    for item in range(2):
        mine[item, :, 0:216] = mod_part[item : item + 1]
        mine[item, :, 216:256] = jnp.zeros((1, 40), jnp.float32)
    mods[place] = mine[lax.div(place, 16)]
    pl.semaphore_wait(barrier, 31)

    def copy_to(hop):
        target = lax.rem(place + hop, 32)
        return pltpu.make_async_remote_copy(
            src_ref=mine.at[lax.div(target, 16)],
            dst_ref=mods.at[place],
            send_sem=send.at[hop],
            recv_sem=recv.at[hop],
            device_id=dp_peer(hop),
            device_id_type=MESH,
        )

    def begin(hop, _):
        copy_to(hop).start()
        return _

    def finish(hop, _):
        copy_to(hop).wait()
        return _

    lax.fori_loop(1, 32, begin, 0)
    lax.fori_loop(1, 32, finish, 0)


def front(feats, w_t1, b_t1, w_t2, b_t2, rows_table, w_ada, b_ada):
    vmem = pl.BlockSpec(memory_space=pltpu.VMEM)
    width = w_t2.shape[0]
    return pl.pallas_call(
        front_kernel,
        out_shape=(
            jax.ShapeDtypeStruct((2, width), jnp.float32),
            jax.ShapeDtypeStruct((2, width), jnp.float32),
            jax.ShapeDtypeStruct((32, 1, 256), jnp.float32),
        ),
        in_specs=[vmem] * 8,
        out_specs=(vmem, vmem, vmem),
        scratch_shapes=[
            pltpu.VMEM((2, 1, 256), jnp.float32),
            pltpu.SemaphoreType.DMA((32,)),
            pltpu.SemaphoreType.DMA((32,)),
        ],
        compiler_params=pltpu.CompilerParams(
            collective_id=2, has_side_effects=True, vmem_limit_bytes=32 * 2**20
        ),
    )(feats, w_t1, b_t1[None], w_t2, b_t2[None], rows_table, w_ada, b_ada[None])


def on_device(
    tokens,
    out_grad,
    timesteps,
    labels,
    grid_ids,
    w_qkv,
    b_qv,
    w_proj,
    b_proj,
    w_fc1,
    b_fc1,
    w_fc2,
    b_fc2,
    w_ada,
    b_ada,
    w_t1,
    b_t1,
    w_t2,
    b_t2,
    table,
):
    dp_count = lax.axis_size("dp")
    dp_place = lax.axis_index("dp")
    row_count, model_width = tokens.shape
    frame_count = row_count // SLOTS
    head_count = HEADS
    head_dim = model_width // head_count
    score_scale = 1.0 / math.sqrt(head_dim)
    frame_shape = (frame_count, SLOTS, head_count, head_dim)
    time_feats = time_embed(timesteps, w_t1.shape[0] // 2)
    onehot = (labels[:, None] == jnp.arange(128, dtype=jnp.int32)[None, :]).astype(jnp.float32)
    pre_time, condition, mods = front(
        time_feats, w_t1, b_t1, w_t2, b_t2, table[labels], w_ada, b_ada
    )
    item_mod = mods.reshape(32, 256)[:, :216].reshape(6 * model_width)
    own_item = dp_place * frame_count // ITEM_FRAMES
    shift_attn, scale_attn, gate_attn, shift_mlp, scale_mlp, gate_mlp = jnp.split(item_mod, 6)
    grid_value = lax.dynamic_index_in_dim(grid_ids, own_item, 0, keepdims=False)
    first_live = jnp.where(grid_value == 2, SLOTS // 16, 0)
    end_live = jnp.where(grid_value == 1, SLOTS - SLOTS // 16, SLOTS)
    slot_pos = jnp.arange(SLOTS, dtype=jnp.int32)
    valid_keys = (slot_pos >= first_live) & (slot_pos < end_live)
    live_rows = jnp.tile(valid_keys, frame_count).astype(jnp.float32)[:, None]
    token_vals = tokens.astype(jnp.float32)
    normed_one, inv_one = norm_rows(token_vals)
    attn_in = (normed_one * (1.0 + scale_attn) + shift_attn).astype(jnp.bfloat16)
    qkv_rows = jnp.dot(attn_in, w_qkv, preferred_element_type=jnp.float32)
    queries = (
        (qkv_rows[:, :model_width] + b_qv[:model_width]).astype(jnp.bfloat16).reshape(frame_shape)
    )
    key_rows = qkv_rows[:, model_width : 2 * model_width].astype(jnp.bfloat16).reshape(frame_shape)
    values = (
        (qkv_rows[:, 2 * model_width :] + b_qv[model_width:])
        .astype(jnp.bfloat16)
        .reshape(frame_shape)
    )

    def masked_scores():
        raw = (
            jnp.einsum("fqhd,fkhd->fhqk", queries, key_rows, preferred_element_type=jnp.float32)
            * score_scale
        )
        return jnp.where(valid_keys[None, None, None, :], raw, NEG)

    scores = masked_scores()
    row_max = jnp.max(scores, axis=-1, keepdims=True)
    shifted = jnp.exp(scores - row_max)
    row_total = jnp.sum(shifted, axis=-1, keepdims=True)
    log_total = row_max + jnp.log(row_total)
    attn_weights = (shifted / row_total).astype(jnp.bfloat16)
    mixed = jnp.einsum("fhqk,fkhd->fqhd", attn_weights, values, preferred_element_type=jnp.float32)
    mixed_rows = mixed.reshape(row_count, model_width).astype(jnp.bfloat16)
    attn_out = jnp.dot(mixed_rows, w_proj, preferred_element_type=jnp.float32) + b_proj
    resid_one = token_vals + gate_attn * attn_out
    normed_two, inv_two = norm_rows(resid_one)
    mlp_in = (normed_two * (1.0 + scale_mlp) + shift_mlp).astype(jnp.bfloat16)
    hidden = jnp.dot(mlp_in, w_fc1, preferred_element_type=jnp.float32) + b_fc1
    gelu_vals, gelu_pull = jax.vjp(functools.partial(jax.nn.gelu, approximate=True), hidden)
    activated = gelu_vals.astype(jnp.bfloat16)
    slope = gelu_pull(jnp.ones_like(hidden))[0].astype(jnp.bfloat16)
    cotangent = out_grad.astype(jnp.float32) * live_rows
    grad_branch = (cotangent * gate_mlp).astype(jnp.bfloat16)
    act_t = activated.T
    act_split = act_t.reshape(16, 2, 144, row_count)
    gbr_t = grad_branch.T
    mlp_t = mlp_in.T.reshape(8, 144, row_count)
    two_t = jnp.stack([attn_in.T, mixed_rows.T]).reshape(16, 144, row_count)
    heads = jnp.stack([queries, key_rows, values])[:, 0].transpose(0, 2, 3, 1)
    wide = lambda array: array.astype(jnp.float32)
    bias_keys = jnp.broadcast_to(
        jnp.where(valid_keys, 0.0, NEG).astype(jnp.float32)[:, None], (SLOTS, 128)
    )
    mod_rows = jnp.pad(item_mod.reshape(6, model_width), ((0, 2), (0, 0)))
    (
        sum_qkv,
        sum_proj,
        sum_fc1,
        sum_fc2,
        block_out,
        input_grad,
        packs,
        sums,
    ) = backward(
        [
            act_split,
            wide(act_split),
            act_t,
            slope.T,
            gbr_t,
            wide(gbr_t),
            mlp_t,
            wide(mlp_t),
            two_t,
            wide(two_t),
            jnp.pad(heads.reshape(48, head_dim, SLOTS), ((0, 0), (0, 8), (0, 0))),
            bias_keys,
            cotangent,
            resid_one,
            attn_out,
            tokens,
            mod_rows,
            b_fc2[None],
            pre_time,
            condition,
            time_feats,
            onehot,
            jnp.pad(w_ada, ((0, 0), (0, 40))),
            w_t2,
            w_qkv,
            w_proj,
            w_fc1,
            w_fc2,
        ]
    )
    packs = packs.reshape(8, PACK)
    grad_cond, grad_pre = packs[:, 0:1152], packs[:, 1152:2304]
    act_cond, act_time = packs[:, 2304:3456], packs[:, 3456:4608]
    d_mod, feats_all = packs[:, 4608:4824], packs[:, 4864:5120]
    class_rows = packs[:, 5120 : 5120 + table.shape[0]]
    own_time = lax.dynamic_slice_in_dim(act_time, dp_place * 36, 36, 1)
    own_feats = lax.dynamic_slice_in_dim(feats_all, dp_place * 8, 8, 1)
    return (
        block_out,
        input_grad,
        sum_qkv,
        sums[0, 0:72],
        sum_proj,
        sums[1, 0:36],
        sum_fc1,
        sums[2:4].reshape(256)[0:144],
        sum_fc2,
        sums[4, 0:36],
        hdot_t(act_cond, d_mod),
        jnp.sum(d_mod, axis=0),
        hdot_t(own_feats, grad_pre),
        own_block(jnp.sum(grad_pre, axis=0), dp_place, dp_count),
        hdot_t(own_time, grad_cond),
        own_block(jnp.sum(grad_cond, axis=0), dp_place, dp_count),
        hdot_t(class_rows, grad_cond),
    )


def solution(mesh):
    placed = (
        P(("group", "dp"), None),
        P(("group", "dp"), None),
        P("group"),
        P("group"),
        P("group"),
        P(),
        P(),
        P(),
        P(),
        P(),
        P(),
        P(),
        P(),
        P(None, "dp"),
        P("dp"),
        P(),
        P(),
        P(),
        P(),
        P(),
    )
    return jax.shard_map(
        on_device,
        mesh=mesh,
        in_specs=placed,
        out_specs=(
            P(("group", "dp"), None),
            P(("group", "dp"), None),
            P("dp", None),
            P("dp"),
            P("dp", None),
            P("dp"),
            P("dp", None),
            P("dp"),
            P("dp", None),
            P("dp"),
            P(None, "dp"),
            P("dp"),
            P("dp", None),
            P("dp"),
            P("dp", None),
            P("dp"),
            P(),
        ),
        check_vma=False,
    )
```

```python
import math

import jax
import jax.numpy as jnp
from jax import lax
from jax.experimental import pallas as pl
from jax.experimental.pallas import tpu as pltpu
from jax.sharding import PartitionSpec as P

SLOTS = 256
ITEM_FRAMES = 16


EPS = 1e-06
NEG = -1e30


def hdot_t(left_op, right_op):
    return lax.dot_general(
        left_op,
        right_op,
        (((0,), (0,)), ((), ())),
        precision=lax.Precision.HIGHEST,
        preferred_element_type=jnp.float32,
    )


def norm_back(grad_in, normed, inv_std):
    return inv_std * (
        grad_in
        - jnp.mean(grad_in, axis=-1, keepdims=True)
        - normed * jnp.mean(grad_in * normed, axis=-1, keepdims=True)
    )


def silu_back(pre_vals, grad_in):
    sigmoid = jax.nn.sigmoid(pre_vals)
    return grad_in * sigmoid * (1.0 + pre_vals * (1.0 - sigmoid))


def time_embed(step_ids, width_half):
    frequency = jnp.exp(
        jnp.arange(width_half, dtype=jnp.float32) * (-math.log(10000.0) / width_half)
    )
    angles = step_ids.astype(jnp.float32)[:, None] * frequency[None, :]
    return jnp.concatenate([jnp.cos(angles), jnp.sin(angles)], axis=1)


def own_block(vector, dp_place, dp_count):
    block_rows = vector.shape[0] // dp_count
    return lax.dynamic_slice_in_dim(vector, dp_place * block_rows, block_rows, 0)


def split_three(values):
    high = values.astype(jnp.bfloat16)
    rest = values - high.astype(jnp.float32)
    middle = rest.astype(jnp.bfloat16)
    low = (rest - middle.astype(jnp.float32)).astype(jnp.bfloat16)
    return jnp.concatenate([high, middle, low], axis=0)


def exact_dot(values, weights, contract=0):
    rows = values.shape[0]
    thrice = lax.dot_general(
        split_three(values),
        weights,
        (((1,), (contract,)), ((), ())),
        preferred_element_type=jnp.float32,
    )
    return thrice[0:rows] + thrice[rows : 2 * rows] + thrice[2 * rows : 3 * rows]


def silu(values):
    return values / (1.0 + jnp.exp(-values))


def dot_nn(left, right):
    return jnp.dot(left, right, preferred_element_type=jnp.float32)


def dot_nt(left, right):
    return lax.dot_general(
        left, right, (((1,), (1,)), ((), ())), preferred_element_type=jnp.float32
    )


def dot_tn(left, right):
    return lax.dot_general(
        left, right, (((0,), (0,)), ((), ())), preferred_element_type=jnp.float32
    )


MESH = pl.DeviceIdType.MESH
ORDERS = ((("y", "z", "x"), ("z", "x", "y"), ("x", "y", "z")),) * 3
STREAMS = tuple(
    tuple((order, pairing) for pairing in (0, 1) for order in orders) for orders in ORDERS
)
BLOCKS = (32, 16, 8, 4, 2, 1)
LANDS_AT = (0, 32, 48, 56, 60, 62)
PIECE = 56
OWN = 72
CHUNK = 384
ROWS = 32
WINDOWS = ((0, 216, 3), (54, 72, 2), (72, 36, 2), (81, 144, 3), (117, 36, 2))


def coords():
    place = lax.axis_index("dp")
    return {
        "y": lax.axis_index("group"),
        "z": lax.div(place, 8),
        "x": lax.rem(lax.div(place, 2), 4),
        "core": lax.rem(place, 2),
    }


def device_at(at):
    return (at["y"], (at["z"] * 4 + at["x"]) * 2 + at["core"])


def dp_peer(hop):
    return (lax.axis_index("group"), lax.rem(lax.axis_index("dp") + hop, 32))


def sibling_of(at):
    return device_at({**at, "core": 1 - at["core"]})


def partner_of(at, axis, pairing):
    here = at[axis]
    if pairing == 0:
        there = here + 1 - 2 * lax.rem(here, 2)
    else:
        there = lax.rem(here + 3 + 2 * lax.rem(here, 2), 4)
    return device_at({**at, axis: there})


def slot_of(pairing, value):
    if pairing == 1:
        return value
    if isinstance(value, int):
        return (0, 2, 3, 1)[value]
    return lax.rem(value + lax.div(value + 1, 2), 4)


PACK = 4 * 1152 + 2 * 256 + 128


def backward_kernel(
    lhs_zero,
    lhs_one,
    lhs_two,
    rhs_zero,
    act_flat,
    slope,
    heads,
    bias_keys,
    cot,
    resid,
    attn_out,
    tokens,
    mods,
    b_fc2,
    pre_in,
    cond_in,
    feats,
    onehot,
    w_ada,
    w_t2,
    w_qkv,
    w_proj,
    w_fc1,
    w_fc2,
    out_qkv,
    out_proj,
    out_fc1,
    out_fc2,
    block_out,
    input_grad,
    packed,
    sums,
    parts,
    landed,
    lhs,
    rhs,
    stage_rhs,
    leave,
    final,
    other,
    narrow,
    d_mod,
    bias_fc1,
    bias_qv,
    bias_proj,
    bias_fc2,
    flat,
    shares,
    got,
    conds,
    sums_all,
    out_rows,
    in_rows,
    wa,
    wb,
    slope_in,
    act_in,
    grad_t,
    branch,
    grad_resid,
    all_t,
    mixed_t,
    heads_in,
    rows_a,
    rows_b,
    rows_c,
    rows_d,
    send_sem,
    recv_sem,
    credit,
    swap_send,
    swap_recv,
    swap_credit,
    own_sem,
    ring_send,
    ring_recv,
    pair_send,
    pair_recv,
    load_sem,
    row_sem,
    head_sem,
    other_credit,
    out_sem,
    share_send,
    share_recv,
    cond_send,
    cond_recv,
    group_send,
    group_recv,
):
    at = coords()
    core = at["core"]
    sibling = sibling_of(at)
    barrier = pltpu.get_barrier_semaphore()
    place = lax.axis_index("dp")

    def group_peer(hop):
        return (lax.rem(at["y"] + hop, 4), place)

    def hello(hop, _):
        pl.semaphore_signal(barrier, inc=1, device_id=dp_peer(hop), device_id_type=MESH)
        return _

    lax.fori_loop(1, 32, hello, 0)
    for hop in (1, 2, 3):
        pl.semaphore_signal(barrier, inc=1, device_id=group_peer(hop), device_id_type=MESH)
    def swap():
        return pltpu.make_async_remote_copy(
            src_ref=leave,
            dst_ref=stage_rhs,
            send_sem=swap_send,
            recv_sem=swap_recv,
            device_id=sibling,
            device_id_type=MESH,
        )

    def lhs_load(phase):
        source = (lhs_zero, lhs_one, lhs_two)[phase]
        target = lhs.at[0:8] if phase == 1 else lhs
        return pltpu.make_async_copy(source, target, own_sem.at[0])

    def rhs_load():
        return pltpu.make_async_copy(rhs_zero, rhs.at[0:1152], own_sem.at[1])

    def swap_start(phase):
        lhs_load(phase).start()
        if phase == 2:
            pl.semaphore_wait(swap_credit, 1)
        swap().start()

    def swap_finish(phase):
        swap().wait()

        def narrow_rhs(step, _):
            rows = pl.ds(pl.multiple_of(step * 144, 144), 144)
            rhs[rows, 256:512] = stage_rhs[rows, :].astype(jnp.bfloat16)
            return _

        lax.fori_loop(0, 16, narrow_rhs, 0)
        if phase == 1:
            pl.semaphore_signal(swap_credit, inc=1, device_id=sibling, device_id_type=MESH)
        lhs_load(phase).wait()

    def base_of(phase, stream, z_place, x_place, y_slot):
        order, pairing = STREAMS[phase][stream]
        slots = {"y": y_slot, "z": slot_of(pairing, z_place), "x": slot_of(pairing, x_place)}
        return (slots[order[0]] * 4 + slots[order[1]]) * 4 + slots[order[2]]

    def keep(phase, stream, chip, rows):
        half = phase % 2
        z_place, x_place = lax.div(chip, 4), lax.rem(chip, 4)
        for y_slot in range(4):
            block = base_of(phase, stream, z_place, x_place, y_slot)
            first = y_slot * PIECE
            for unit in range(3):
                low, high = max(first, OWN * unit), min(first + PIECE, OWN * unit + OWN)
                if low < high:
                    parts[half, stream, block, low - first : high - first, :] = rows[
                        low - OWN * unit : high - OWN * unit, unit * 128 : unit * 128 + 128
                    ]

    def halving(phase, stream, step):
        order, pairing = STREAMS[phase][stream]
        axis = order[step // 2]
        slots = [slot_of(pairing, at[name]) for name in order]
        base = 0
        for level in range(step // 2):
            base = base + slots[level] * (64 // 4 ** (level + 1))
        slot = slots[step // 2]
        side = lax.div(slot, 2) if step % 2 == 0 else slot
        away = 1 - side if step % 2 == 0 else slot + 1 - 2 * lax.rem(slot, 2)
        count = BLOCKS[step]
        kept, sent = base + side * count, base + away * count
        partner = partner_of(at, axis, pairing if step % 2 == 0 else 1 - pairing)
        source = parts.at[phase % 2, stream]
        if phase == 0 and step >= 3:
            origin = slots[0] * 16 + lax.div(slots[1], 2) * 8
            kept, sent = kept - origin, sent - origin
            source = narrow.at[stream]
        copy = pltpu.make_async_remote_copy(
            src_ref=source.at[pl.ds(sent, count)],
            dst_ref=landed.at[stream, pl.ds(LANDS_AT[step], count)],
            send_sem=send_sem.at[stream, step],
            recv_sem=recv_sem.at[stream, step],
            device_id=partner,
            device_id_type=MESH,
        )
        return copy, kept, partner

    def send(phase, stream, step):
        copy, _, _ = halving(phase, stream, step)
        if phase:
            pl.semaphore_wait(credit.at[stream, step], 1)
        copy.start()

    def receive(phase, step):
        for stream in range(6):
            copy, kept, partner = halving(phase, stream, step)
            copy.wait()
            half = phase % 2
            count = BLOCKS[step]
            late = phase == 0 and step >= 3
            if step < 5:

                def add(block, _):
                    arrived = landed[stream, LANDS_AT[step] + block]
                    if late:
                        narrow[stream, kept + block] += arrived
                    elif phase == 0 and step == 2:
                        narrow[stream, block] = parts[half, stream, kept + block] + arrived
                    else:
                        parts[half, stream, kept + block] += arrived
                    return _

                lax.fori_loop(0, count, add, 0, unroll=min(count, 4))
            else:
                mine = narrow[stream, kept] if late else parts[half, stream, kept]
                final[phase, at["y"], stream] = mine + landed[stream, LANDS_AT[step]]
            if phase < 2:
                pl.semaphore_signal(
                    credit.at[stream, step], inc=1, device_id=partner, device_id_type=MESH
                )
            if step < 5:
                send(phase, stream, step + 1)

    def products(phase):
        together, stacked = (3, 2) if phase == 2 else (2, 4)
        for group in range(6 // together):
            members = range(group * together, (group + 1) * together)
            if phase == 0:
                first = group * together // 2 * CHUNK
                width = together // 2 * CHUNK
                count = 16
            else:
                first = members[0] * CHUNK
                width = together * CHUNK
                count = 8
            shift = core * 8 if phase == 2 and members[0] >= 3 else 0

            def some(step, _):
                left = lhs[pl.ds(step * stacked + shift, stacked)]
                rows = dot_nt(
                    left.reshape(stacked * 144, 512), rhs[first : first + width, :]
                )
                for place in range(stacked):
                    at_row = place * 144
                    if phase == 0:
                        chip = step * stacked + place
                        for third in range(together // 2):
                            column = third * CHUNK
                            block = rows[at_row : at_row + 144, column : column + CHUNK]
                            stream = group * together // 2 + third
                            keep(phase, stream, chip, block[0:72])
                            keep(phase, stream + 3, chip, block[72:144])
                    else:
                        chip = (step * stacked + place) * 2
                        for place_at, stream in enumerate(members):
                            column = place_at * CHUNK
                            block = rows[at_row : at_row + 144, column : column + CHUNK]
                            keep(phase, stream, chip, block[0:72])
                            keep(phase, stream, chip + 1, block[72:144])
                return _

            lax.fori_loop(0, count // stacked, some, 0)
            for member in members:
                stream = member
                if phase == 0:
                    stream = group * together // 2 + (member - members[0]) // 2
                    stream += 3 * ((member - members[0]) % 2)
                send(phase, stream, 0)

    def ring(phase):
        mine = at["y"]
        copies = []
        for place, hop in enumerate((1, 3)):
            copies.append(
                pltpu.make_async_remote_copy(
                    src_ref=final.at[phase, mine],
                    dst_ref=final.at[phase, mine],
                    send_sem=ring_send.at[phase, place],
                    recv_sem=ring_recv.at[phase, place],
                    device_id=device_at({**at, "y": lax.rem(mine + hop, 4)}),
                    device_id_type=MESH,
                )
            )
        return copies

    def relay(phase):
        mine = at["y"]
        copies = []
        for place, hop in enumerate((1, 3)):
            origin = lax.rem(mine + 4 - hop, 4)
            half = pl.ds(place * 3, 3)
            copies.append(
                pltpu.make_async_remote_copy(
                    src_ref=final.at[phase, origin, half],
                    dst_ref=final.at[phase, origin, half],
                    send_sem=ring_send.at[phase, place + 2],
                    recv_sem=ring_recv.at[phase, place + 2],
                    device_id=device_at({**at, "y": lax.rem(mine + hop, 4)}),
                    device_id_type=MESH,
                )
            )
        return copies

    def across(phase):
        return pltpu.make_async_remote_copy(
            src_ref=final.at[phase],
            dst_ref=other,
            send_sem=pair_send.at[phase - 1],
            recv_sem=pair_recv.at[phase - 1],
            device_id=sibling,
            device_id_type=MESH,
        )

    def whole(get, stream):
        pairing = STREAMS[0][stream][1]
        order = sorted(range(4), key=lambda y_place: slot_of(pairing, y_place))
        return jnp.concatenate([get(y_place, stream) for y_place in order], axis=0)

    def write_rows(phase, low):
        for side in range(2):
            mine = side == (0 if low == 0 else 1)
            for stream in range(6):
                if mine:
                    rows = whole(lambda y_place, stream: final[phase, y_place, stream], stream)
                else:
                    rows = whole(lambda y_place, stream: other[y_place, stream], stream)
                for unit in range(3):
                    block = rows[OWN * unit + low : OWN * unit + low + 36]
                    column = side * 18 + stream * 3 + unit
                    if phase == 1:
                        out_fc1[:, column * 128 : column * 128 + 128] = block
                    elif column < 27:
                        out_qkv[:, column * 128 : column * 128 + 128] = block
                    else:
                        out_proj[:, (column - 27) * 128 : (column - 27) * 128 + 128] = block

    def write(phase):
        if phase == 0:
            for stream in range(6):
                rows = whole(lambda y_place, stream: final[0, y_place, stream], stream)
                half, third = stream // 3, stream % 3
                for unit in range(3):
                    column = third * 3 + unit
                    out_fc2[half * 72 : half * 72 + 72, column * 128 : column * 128 + 128] = rows[
                        OWN * unit : OWN * unit + 72
                    ]
            return

        @pl.when(core == 0)
        def _():
            write_rows(phase, 0)

        @pl.when(core == 1)
        def _():
            write_rows(phase, 36)

        if phase == 1:
            pl.semaphore_signal(other_credit, inc=1, device_id=sibling, device_id_type=MESH)

    def ring_start(phase):
        for copy in ring(phase):
            copy.start()

    def ring_relay(phase):
        for copy, onward in zip(ring(phase), relay(phase)):
            copy.wait()
            onward.start()

    def ring_finish(phase):
        for copy in relay(phase):
            copy.wait()
        if phase == 2:
            pl.semaphore_wait(other_credit, 1)
        if phase:
            across(phase).start()

    def clear(chip, _):
        z_place, x_place = lax.div(chip, 4), lax.rem(chip, 4)
        for half in range(2):
            for stream in range(6):
                block = base_of(half, stream, z_place, x_place, 3)
                parts[half, stream, block, 48:56, :] = jnp.zeros((8, 128), jnp.float32)
        return _

    ones = jnp.ones((8, 256), jnp.bfloat16)

    def mlp_loads(chunk):
        slot = lax.rem(chunk, 2)
        rows = pl.ds(pl.multiple_of(chunk * CHUNK, CHUNK), CHUNK)
        return [
            pltpu.make_async_copy(w_fc2.at[rows], wa.at[slot], load_sem.at[0, slot]),
            pltpu.make_async_copy(w_fc1.at[:, rows], wb.at[slot], load_sem.at[1, slot]),
            pltpu.make_async_copy(slope.at[rows], slope_in.at[slot], load_sem.at[2, slot]),
        ]

    def branch_loads(chunk):
        slot = lax.rem(chunk, 2)
        rows = pl.ds(pl.multiple_of(chunk * CHUNK, CHUNK), CHUNK)
        return [
            pltpu.make_async_copy(w_fc2.at[rows], wa.at[slot], load_sem.at[0, slot]),
            pltpu.make_async_copy(act_flat.at[rows], act_in.at[slot], load_sem.at[3, slot]),
        ]

    def branch_begin():
        for copy in branch_loads(0):
            copy.start()

    def branch_forward(low, high):
        if low == 0:
            branch[...] = jnp.zeros((256, 1152), jnp.float32)

        def branch_step(chunk, carry):
            slot = lax.rem(chunk, 2)

            @pl.when(chunk < 11)
            def _():
                for copy in branch_loads(chunk + 1):
                    copy.start()

            for copy in branch_loads(chunk):
                copy.wait()
            branch[...] += dot_tn(act_in[slot], wa[slot])
            return carry

        lax.fori_loop(low, high, branch_step, 0)

    def mlp_begin():
        for copy in mlp_loads(0):
            copy.start()

    def mlp_backward(low, high):
        if low == 0:
            rhs[0:1152, 256:512] = rhs[0:1152, 0:256]
            grad_t[...] = jnp.zeros((1152, 256), jnp.float32)

        def chunk_step(chunk, carry):
            slot = lax.rem(chunk, 2)

            @pl.when(chunk < 11)
            def _():
                for copy in mlp_loads(chunk + 1):
                    copy.start()

            for copy in mlp_loads(chunk):
                copy.wait()
            grad_act = dot_nn(wa[slot], rhs[0:1152, 256:512])
            grad_hidden = (grad_act * slope_in[slot].astype(jnp.float32)).astype(jnp.bfloat16)
            side = lax.div(chunk, 6)
            rows = pl.ds(pl.multiple_of(lax.rem(chunk, 6) * CHUNK, CHUNK), CHUNK)

            @pl.when(side == core)
            def _():
                rhs[rows, 0:256] = grad_hidden

            @pl.when(side != core)
            def _():
                leave[rows, :] = grad_hidden.astype(jnp.float32)

            columns = pl.ds(pl.multiple_of(chunk * CHUNK, CHUNK), CHUNK)
            bias_fc1[:, columns] = dot_nt(ones, grad_hidden)[0:1]
            grad_t[...] += dot_nn(wb[slot], grad_hidden)
            return carry

        lax.fori_loop(low, high, chunk_step, 0)

    def row_block(source, index):
        return source.at[pl.ds(pl.multiple_of(index * ROWS, ROWS), ROWS)]

    def norm(values):
        mean = jnp.mean(values, axis=-1, keepdims=True)
        centered = values - mean
        inverse = lax.rsqrt(jnp.mean(centered * centered, axis=-1, keepdims=True) + EPS)
        return centered * inverse, inverse

    def total(values):
        return jnp.sum(values, axis=0, keepdims=True)

    def middle_loads(index):
        slot = lax.rem(index, 2)
        return [
            pltpu.make_async_copy(row_block(source, index), target.at[slot], row_sem.at[place, slot])
            for place, (source, target) in enumerate(
                ((cot, rows_a), (resid, rows_b), (attn_out, rows_c))
            )
        ]

    def token_load(index):
        slot = lax.rem(index, 2)
        return pltpu.make_async_copy(
            row_block(tokens, index), rows_d.at[slot], row_sem.at[3, slot]
        )

    def proj_load(chunk):
        slot = lax.rem(chunk, 2)
        rows = pl.ds(pl.multiple_of(chunk * 288, 288), 288)
        return pltpu.make_async_copy(w_proj.at[rows], wa.at[slot, 0:288], load_sem.at[0, slot])

    def rows_out(kind, index):
        slot = lax.rem(index, 2)
        target = block_out if kind == 0 else input_grad
        buffer = out_rows if kind == 0 else in_rows
        return pltpu.make_async_copy(
            buffer.at[slot], row_block(target, index), out_sem.at[kind, slot]
        )

    def drain(kind):
        rows_out(kind, 256 // ROWS - 2).wait()
        rows_out(kind, 256 // ROWS - 1).wait()

    def middle_begin():
        for copy in middle_loads(0):
            copy.start()
        proj_load(0).start()
        d_mod[...] = jnp.zeros((8, 1152), jnp.float32)
        bias_proj[...] = jnp.zeros((1, 1152), jnp.float32)
        bias_fc2[...] = jnp.zeros((1, 1152), jnp.float32)
        grad_resid[...] = grad_t[...].T

    def middle_rows(low, high):
        scale_mlp, gate_attn = mods[4:5], mods[2:3]

        def rows_step(index, carry):
            rows = pl.ds(pl.multiple_of(index * ROWS, ROWS), ROWS)
            slot = lax.rem(index, 2)

            @pl.when(index < 256 // ROWS - 1)
            def _():
                for copy in middle_loads(index + 1):
                    copy.start()

            for copy in middle_loads(index):
                copy.wait()

            cotangent, stream_rows = rows_a[slot], rows_b[slot]
            normed, inverse = norm(stream_rows)
            grad_in = grad_resid[rows, :]
            d_mod[3:4, :] += total(grad_in)
            d_mod[4:5, :] += total(grad_in * normed)
            back = norm_back(grad_in * (1.0 + scale_mlp), normed, inverse)
            grads = cotangent + back
            grad_resid[rows, :] = grads
            d_mod[2:3, :] += total(grads * rows_c[slot])
            grad_attn = (grads * gate_attn).astype(jnp.bfloat16).astype(jnp.float32)
            bias_proj[...] += total(grad_attn)
            branch[rows, :] = grad_attn
            return carry

        lax.fori_loop(low, high, rows_step, 0)

    def finish_begin():
        for copy in middle_loads(0)[0:2]:
            copy.start()

    def finish_rows():
        gate_mlp = mods[5:6]

        def finish_step(index, carry):
            rows = pl.ds(pl.multiple_of(index * ROWS, ROWS), ROWS)
            slot = lax.rem(index, 2)

            @pl.when(index < 256 // ROWS - 1)
            def _():
                for copy in middle_loads(index + 1)[0:2]:
                    copy.start()

            for copy in middle_loads(index)[0:2]:
                copy.wait()

            @pl.when(index >= 2)
            def _():
                rows_out(0, index - 2).wait()

            cotangent, stream_rows = rows_a[slot], rows_b[slot]
            branch_rows = branch[rows, :] + b_fc2[...].reshape(1, 1152)
            out_rows[slot] = (stream_rows + gate_mlp * branch_rows).astype(jnp.bfloat16)
            rows_out(0, index).start()
            d_mod[5:6, :] += total(cotangent * branch_rows)
            bias_fc2[...] += total(
                (cotangent * gate_mlp).astype(jnp.bfloat16).astype(jnp.float32)
            )
            return carry

        lax.fori_loop(0, 256 // ROWS, finish_step, 0)

    def middle_end():
        all_t[3456:4608, :] = branch[...].T.astype(jnp.bfloat16)

        def proj_step(chunk, carry):
            @pl.when(chunk < 3)
            def _():
                proj_load(chunk + 1).start()

            proj_load(chunk).wait()
            grads = dot_nn(wa[lax.rem(chunk, 2), 0:288], all_t[3456:4608, :])
            for head in range(4):
                padded = jnp.concatenate(
                    [grads[head * 72 : head * 72 + 72], jnp.zeros((8, 256), jnp.float32)], axis=0
                )
                mixed_t[chunk * 4 + head] = padded.astype(jnp.bfloat16)
            return carry

        lax.fori_loop(0, 4, proj_step, 0)

    def heads_load(pair_at):
        slot = lax.rem(pair_at, 2)
        return [
            pltpu.make_async_copy(
                heads.at[pl.ds(part * 16 + pair_at * 2, 2)],
                heads_in.at[slot, part],
                head_sem.at[part, slot],
            )
            for part in range(3)
        ]

    def attention_backward(low, high):
        scale = 1.0 / math.sqrt(72)

        def one_head(pair_at, side):
            slot = lax.rem(pair_at, 2)
            query, key, value = (heads_in[slot, part, side] for part in range(3))
            grad_mixed = mixed_t[pair_at * 2 + side]
            scores = dot_tn(key, query) * scale + jnp.concatenate([bias_keys[...]] * 2, axis=1)
            shifted = jnp.exp(scores - jnp.max(scores, axis=0, keepdims=True))
            weights = shifted / jnp.sum(shifted, axis=0, keepdims=True)
            grad_weights = dot_tn(value, grad_mixed)
            row_dot = jnp.sum(weights * grad_weights, axis=0, keepdims=True)
            grad_scores = (weights * (grad_weights - row_dot)).astype(jnp.bfloat16)
            return (
                dot_nn(key, grad_scores)[0:72] * scale,
                dot_nt(query, grad_scores)[0:72] * scale,
                dot_nt(grad_mixed, weights.astype(jnp.bfloat16))[0:72],
            )

        def two_heads(pair_at, carry):
            @pl.when(pair_at < 7)
            def _():
                for copy in heads_load(pair_at + 1):
                    copy.start()

            for copy in heads_load(pair_at):
                copy.wait()
            first, second = one_head(pair_at, 0), one_head(pair_at, 1)
            for part in range(3):
                rows = pl.ds(pl.multiple_of(part * 1152 + pair_at * 144, 16), 144)
                all_t[rows, :] = jnp.concatenate([first[part], second[part]], axis=0).astype(
                    jnp.bfloat16
                )
            return carry

        lax.fori_loop(low, high, two_heads, 0)

    def sides():
        def side(step, _):
            mine = pl.ds(pl.multiple_of(core * 2304 + step * 144, 16), 144)
            theirs = pl.ds(pl.multiple_of((1 - core) * 2304 + step * 144, 16), 144)
            rows = pl.ds(pl.multiple_of(step * 144, 144), 144)
            rhs[rows, 0:256] = all_t[mine, :]
            leave[rows, :] = all_t[theirs, :].astype(jnp.float32)
            return _

        lax.fori_loop(0, 16, side, 0)

    def qkv_load(chunk):
        slot = lax.rem(chunk, 2)
        columns = pl.ds(pl.multiple_of(chunk * CHUNK, CHUNK), CHUNK)
        return pltpu.make_async_copy(w_qkv.at[:, columns], wb.at[slot], load_sem.at[1, slot])

    def last_columns(low, high):
        if low == 0:
            grad_t[...] = jnp.zeros((1152, 256), jnp.float32)
            token_load(0).start()

        def qkv_step(chunk, carry):
            @pl.when(chunk < 8)
            def _():
                qkv_load(chunk + 1).start()

            qkv_load(chunk).wait()
            rows = pl.ds(pl.multiple_of(chunk * CHUNK, CHUNK), CHUNK)
            grads = all_t[rows, :]
            grad_t[...] += dot_nn(wb[lax.rem(chunk, 2)], grads)
            bias_qv[:, rows] = dot_nt(ones, grads)[0:1]
            return carry

        lax.fori_loop(low, high, qkv_step, 0)

    def ada_load():
        return pltpu.make_async_copy(w_ada, wa.at[0, 0:256], load_sem.at[0, 0])

    def last_rows():
        branch[...] = grad_t[...].T
        scale_attn = mods[1:2]

        def last_step(index, carry):
            rows = pl.ds(pl.multiple_of(index * ROWS, ROWS), ROWS)
            slot = lax.rem(index, 2)

            @pl.when(index < 256 // ROWS - 1)
            def _():
                token_load(index + 1).start()

            token_load(index).wait()

            @pl.when(index >= 2)
            def _():
                rows_out(1, index - 2).wait()

            normed, inverse = norm(rows_d[slot].astype(jnp.float32))
            grad_in = branch[rows, :]
            d_mod[0:1, :] += total(grad_in)
            d_mod[1:2, :] += total(grad_in * normed)
            back = norm_back(grad_in * (1.0 + scale_attn), normed, inverse)
            in_rows[slot] = (grad_resid[rows, :] + back).astype(jnp.bfloat16)
            rows_out(1, index).start()
            return carry

        lax.fori_loop(0, 256 // ROWS, last_step, 0)

    def share_to(hop):
        return pltpu.make_async_remote_copy(
            src_ref=shares.at[lax.rem(place + hop, 32)],
            dst_ref=got.at[place],
            send_sem=share_send.at[hop],
            recv_sem=share_recv.at[hop],
            device_id=dp_peer(hop),
            device_id_type=MESH,
        )

    def cond_to(hop):
        return pltpu.make_async_remote_copy(
            src_ref=conds.at[place],
            dst_ref=conds.at[place],
            send_sem=cond_send.at[hop],
            recv_sem=cond_recv.at[hop],
            device_id=dp_peer(hop),
            device_id_type=MESH,
        )

    def group_copies(hop):
        return [
            pltpu.make_async_remote_copy(
                src_ref=buffer.at[at["y"]],
                dst_ref=buffer.at[at["y"]],
                send_sem=group_send.at[side, hop],
                recv_sem=group_recv.at[side, hop],
                device_id=group_peer(hop),
                device_id_type=MESH,
            )
            for side, buffer in enumerate((packed, sums_all))
        ]

    def each(make, act):
        def one(hop, _):
            act(make(hop))
            return _

        lax.fori_loop(1, 32, one, 0)

    def tail_share():
        ada_load().start()
        vectors = [d_mod[row : row + 1] for row in range(6)]
        vectors += [bias_qv[0:1, 0:1152], bias_qv[0:1, 2304:3456]]
        vectors += [bias_proj[...], bias_fc1[0:1, :], bias_fc2[...]]
        row = 0
        for vector in vectors:
            for column in range(vector.shape[1] // 128):
                flat[row] = vector[:, column * 128 : column * 128 + 128]
                row += 1
        flat[126] = jnp.zeros((1, 128), jnp.float32)
        flat[127] = jnp.zeros((1, 128), jnp.float32)

        def window(peer, _):
            into = 0
            for first, width, count in WINDOWS:
                start = first + lax.div(peer * width, 128)
                for offset in range(count):
                    shares[peer, into] = flat[start + offset]
                    into += 1
            return _

        lax.fori_loop(0, 32, window, 0)
        got[place] = shares[place]
        each(share_to, lambda copy: copy.start())

    def tail_cond():
        each(share_to, lambda copy: copy.wait())
        first, second = got[0], got[16]
        for source in range(1, 16):
            first = first + got[source]
            second = second + got[16 + source]

        lanes = lax.broadcasted_iota(jnp.int32, (1, 256), 1)

        def piece(rows, entry):
            begin = sum(count for _, _, count in WINDOWS[:entry])
            _, width, count = WINDOWS[entry]
            joined = jnp.concatenate([rows[begin + step] for step in range(count)], axis=1)
            joined = jnp.concatenate([joined] * 8, axis=0)
            shift = lax.rem(place * width, 128)
            moved = pltpu.roll(joined, lax.rem(count * 128 - shift, count * 128), 1)
            return moved[0:1]

        d_mod_own = jnp.concatenate(
            [jnp.where(lanes < 216, piece(rows, 0)[:, 0:256], 0.0) for rows in (first, second)],
            axis=0,
        )
        ada_load().wait()
        conds[place] = exact_dot(d_mod_own, wa[0, 0:256])
        each(cond_to, lambda copy: copy.start())
        for chunk in range(2):
            t2_load(chunk).start()
        both = first + second
        sums_all[at["y"], 0:1] = piece(both, 1)[:, 0:128]
        sums_all[at["y"], 1:2] = piece(both, 2)[:, 0:128]
        wide = piece(both, 3)
        sums_all[at["y"], 2:3] = wide[:, 0:128]
        sums_all[at["y"], 3:4] = wide[:, 128:256]
        sums_all[at["y"], 4:5] = piece(both, 4)[:, 0:128]
        sums_all[at["y"], 5:8] = jnp.zeros((3, 128), jnp.float32)
        packed[at["y"], :, 2304:3456] = silu(cond_in[...])
        packed[at["y"], :, 3456:4608] = silu(pre_in[...])
        packed[at["y"], :, 4608:4864] = d_mod_own
        packed[at["y"], :, 4864:5120] = feats[...]
        packed[at["y"], :, 5120:5248] = onehot[...]

    def t2_load(chunk):
        rows = pl.ds(chunk * CHUNK, CHUNK)
        return pltpu.make_async_copy(w_t2.at[rows], wa.at[chunk % 2], load_sem.at[0, chunk % 2])

    def tail_group():
        each(cond_to, lambda copy: copy.wait())
        total_cond = conds[0]
        for source in range(1, 32):
            total_cond = total_cond + conds[source]
        grad_cond = silu_back(cond_in[...], total_cond)
        packed[at["y"], :, 0:1152] = grad_cond
        for chunk in range(3):
            t2_load(chunk).wait()
            columns = exact_dot(grad_cond, wa[chunk % 2], 1)
            if chunk == 0:
                t2_load(2).start()
            begin = chunk * CHUNK
            packed[at["y"], :, 1152 + begin : 1152 + begin + CHUNK] = silu_back(
                pre_in[:, begin : begin + CHUNK], columns
            )
        for hop in (1, 2, 3):
            for copy in group_copies(hop):
                copy.start()

    def tail_end():
        for hop in (1, 2, 3):
            for copy in group_copies(hop):
                copy.wait()
        sums[...] = sums_all[0] + sums_all[1] + sums_all[2] + sums_all[3]

    lhs_load(0).start()
    rhs_load().start()
    mlp_begin()
    for copy in heads_load(0):
        copy.start()
    lax.fori_loop(0, 16, clear, 0)
    lhs_load(0).wait()
    rhs_load().wait()
    pl.semaphore_wait(barrier, 34)
    products(0)
    mlp_backward(0, 4)
    mlp_backward(4, 8)
    mlp_backward(8, 12)
    swap_start(1)
    middle_begin()
    middle_rows(0, 4)
    receive(0, 0)
    middle_rows(4, 8)
    middle_end()
    swap_finish(1)
    products(1)
    qkv_load(0).start()
    attention_backward(0, 4)
    receive(0, 1)
    attention_backward(4, 8)
    sides()
    swap_start(2)
    last_columns(0, 5)
    last_columns(5, 9)
    receive(1, 0)
    swap_finish(2)
    receive(0, 2)
    products(2)
    branch_begin()
    finish_begin()
    last_rows()
    receive(1, 1)
    receive(0, 3)
    branch_forward(0, 6)
    branch_forward(6, 12)
    receive(1, 2)
    finish_rows()
    tail_share()
    receive(2, 0)
    receive(0, 4)
    tail_cond()
    receive(2, 1)
    receive(1, 3)
    receive(0, 5)
    ring_start(0)
    tail_group()
    receive(2, 2)
    receive(1, 4)
    ring_relay(0)
    receive(2, 3)
    receive(1, 5)
    ring_start(1)
    ring_finish(0)
    write(0)
    tail_end()
    receive(2, 4)
    ring_relay(1)
    receive(2, 5)
    ring_start(2)
    ring_finish(1)
    across(1).wait()
    write(1)
    ring_relay(2)
    drain(0)
    drain(1)
    ring_finish(2)
    across(2).wait()
    write(2)


def backward(operands):
    dma = pltpu.SemaphoreType.DMA
    regular = pltpu.SemaphoreType.REGULAR
    vmem = pl.BlockSpec(memory_space=pltpu.VMEM)
    anywhere = pl.BlockSpec(memory_space=pl.ANY)
    full = jnp.float32
    small = jnp.bfloat16
    return pl.pallas_call(
        backward_kernel,
        out_shape=(
            jax.ShapeDtypeStruct((36, 3456), full),
            jax.ShapeDtypeStruct((36, 1152), full),
            jax.ShapeDtypeStruct((36, 4608), full),
            jax.ShapeDtypeStruct((144, 1152), full),
            jax.ShapeDtypeStruct((256, 1152), small),
            jax.ShapeDtypeStruct((256, 1152), small),
            jax.ShapeDtypeStruct((4, 2, PACK), full),
            jax.ShapeDtypeStruct((8, 128), full),
        ),
        in_specs=[anywhere] * 7 + [vmem] + [anywhere] * 4 + [vmem] * 6 + [anywhere] * 6,
        out_specs=(vmem,) * 4 + (anywhere,) * 2 + (vmem,) * 2,
        scratch_shapes=[
            pltpu.VMEM((2, 6, 64, PIECE, 128), full),
            pltpu.VMEM((6, 63, PIECE, 128), full),
            pltpu.VMEM((16, 144, 512), small),
            pltpu.VMEM((2304, 512), small),
            pltpu.VMEM((2304, 256), full),
            pltpu.VMEM((2304, 256), full),
            pltpu.VMEM((3, 4, 6, PIECE, 128), full),
            pltpu.VMEM((4, 6, PIECE, 128), full),
            pltpu.VMEM((6, 8, PIECE, 128), full),
            pltpu.VMEM((8, 1152), full),
            pltpu.VMEM((1, 4608), full),
            pltpu.VMEM((1, 3456), full),
            pltpu.VMEM((1, 1152), full),
            pltpu.VMEM((1, 1152), full),
            pltpu.VMEM((128, 1, 128), full),
            pltpu.VMEM((32, 12, 1, 128), full),
            pltpu.VMEM((32, 12, 1, 128), full),
            pltpu.VMEM((32, 2, 1152), full),
            pltpu.VMEM((4, 8, 128), full),
            pltpu.VMEM((2, ROWS, 1152), small),
            pltpu.VMEM((2, ROWS, 1152), small),
            pltpu.VMEM((2, CHUNK, 1152), small),
            pltpu.VMEM((2, 1152, CHUNK), small),
            pltpu.VMEM((2, CHUNK, 256), small),
            pltpu.VMEM((2, CHUNK, 256), small),
            pltpu.VMEM((1152, 256), full),
            pltpu.VMEM((256, 1152), full),
            pltpu.VMEM((256, 1152), full),
            pltpu.VMEM((4608, 256), small),
            pltpu.VMEM((16, 80, 256), small),
            pltpu.VMEM((2, 3, 2, 80, 256), small),
            pltpu.VMEM((2, ROWS, 1152), full),
            pltpu.VMEM((2, ROWS, 1152), full),
            pltpu.VMEM((2, ROWS, 1152), full),
            pltpu.VMEM((2, ROWS, 1152), small),
            dma((6, 6)),
            dma((6, 6)),
            regular((6, 6)),
            dma,
            dma,
            regular,
            dma((2,)),
            dma((3, 4)),
            dma((3, 4)),
            dma((2,)),
            dma((2,)),
            dma((4, 2)),
            dma((4, 2)),
            dma((3, 2)),
            regular,
            dma((2, 2)),
            dma((32,)),
            dma((32,)),
            dma((32,)),
            dma((32,)),
            dma((2, 4)),
            dma((2, 4)),
        ],
        compiler_params=pltpu.CompilerParams(
            collective_id=1, has_side_effects=True, vmem_limit_bytes=255 * 2**18
        ),
    )(*operands)


def as_row(ref):
    return ref[...].reshape(1, ref.shape[0])


def forward_kernel(
    tokens,
    out_grad,
    feats,
    labels,
    grid_ids,
    table,
    w_t1,
    b_t1,
    w_t2,
    b_t2,
    w_ada,
    b_ada,
    w_qkv,
    b_qv,
    w_proj,
    b_proj,
    w_fc1,
    b_fc1,
    pre_out,
    cond_out,
    mods,
    lhs_two,
    lhs_one,
    lhs_zero,
    rhs_zero,
    act_out,
    slope_out,
    heads,
    cot,
    resid,
    attn_out,
    ada_wide,
    bias_keys,
    onehot,
    mine,
    gathered,
    flat,
    normed,
    qkv_t,
    w_q,
    w_p,
    w_f,
    w_1,
    w_2,
    keys_off,
    live_rows,
    send_a,
    send_b,
    send_c,
    send_d,
    send_e,
    got_a,
    got_b,
    got_c,
    got_d,
    got_e,
    send,
    recv,
    load_sem,
    pair_send,
    pair_recv,
    fc_sem,
):
    at = coords()
    core = at["core"]
    sibling = sibling_of(at)
    place = lax.axis_index("dp")
    loads = [
        pltpu.make_async_copy(source, target, load_sem.at[index])
        for index, (source, target) in enumerate(
            ((w_t1, w_1), (w_t2, w_2), (w_qkv, w_q), (w_proj, w_p))
        )
    ]
    for copy in loads:
        copy.start()

    def fc_load(part):
        columns = pl.ds(part * 1152, 1152)
        return pltpu.make_async_copy(w_fc1.at[:, columns], w_f.at[part % 2], fc_sem.at[part % 2])

    fc_load(0).start()
    fc_load(1).start()
    barrier = pltpu.get_barrier_semaphore()

    def hello(hop, _):
        pl.semaphore_signal(barrier, inc=1, device_id=dp_peer(hop), device_id_type=MESH)
        return _

    lax.fori_loop(1, 32, hello, 0)
    rows_table = jnp.concatenate(
        [table[pl.ds(labels[0], 1), :], table[pl.ds(labels[1], 1), :]], axis=0
    )
    loads[0].wait()
    pre_time = exact_dot(feats[...], w_1[...]) + as_row(b_t1)
    loads[1].wait()
    condition = exact_dot(silu(pre_time), w_2[...]) + as_row(b_t2) + rows_table
    mod_part = exact_dot(silu(condition), w_ada[...], 1) + as_row(b_ada)
    pre_out[...] = pre_time
    cond_out[...] = condition
    for item in range(2):
        mine[item, :, 0:216] = mod_part[item : item + 1]
        mine[item, :, 216:256] = jnp.zeros((1, 40), jnp.float32)
    gathered[place] = mine[lax.div(place, 16)]
    pl.semaphore_wait(barrier, 31)

    def copy_to(hop):
        target = lax.rem(place + hop, 32)
        return pltpu.make_async_remote_copy(
            src_ref=mine.at[lax.div(target, 16)],
            dst_ref=gathered.at[place],
            send_sem=send.at[hop],
            recv_sem=recv.at[hop],
            device_id=dp_peer(hop),
            device_id_type=MESH,
        )

    def begin(hop, _):
        copy_to(hop).start()
        return _

    def finish(hop, _):
        copy_to(hop).wait()
        return _

    def norm(values):
        mean = jnp.mean(values, axis=-1, keepdims=True)
        centered = values - mean
        inverse = lax.rsqrt(jnp.mean(centered * centered, axis=-1, keepdims=True) + EPS)
        return centered * inverse

    def row_range(index):
        return pl.ds(pl.multiple_of(index * 64, 64), 64)

    lax.fori_loop(1, 32, begin, 0)
    ada_rows = jnp.concatenate([w_ada[...].astype(jnp.float32), jnp.zeros((40, 1152))], axis=0)
    ada_wide[...] = ada_rows.astype(jnp.bfloat16)
    grid_value = grid_ids[lax.div(place, 16)]
    first_live = jnp.where(grid_value == 2, 16, 0)
    end_live = jnp.where(grid_value == 1, 240, 256)
    slots = lax.broadcasted_iota(jnp.int32, (256, 128), 0)
    live = (slots >= first_live) & (slots < end_live)
    keys_off[...] = jnp.where(live, 0.0, NEG)
    live_rows[...] = jnp.where(live, 1.0, 0.0)
    bias_keys[...] = keys_off[...]
    for item in range(2):
        classes = lax.broadcasted_iota(jnp.int32, (1, 128), 1)
        onehot[item : item + 1, :] = jnp.where(classes == labels[item], 1.0, 0.0)

    def first_norm(index, _):
        rows = row_range(index)
        normed[rows, :] = norm(tokens[rows, :].astype(jnp.float32))
        cot[rows, :] = out_grad[rows, :].astype(jnp.float32) * live_rows[rows, 0:1]
        return _

    lax.fori_loop(0, 4, first_norm, 0)

    def blank(row, _):
        flat[row] = jnp.zeros((1, 128), jnp.float32)
        return _

    lax.fori_loop(0, 56, blank, 0)
    lax.fori_loop(1, 32, finish, 0)
    for piece in range(32):
        row, shift = piece * 216 // 128, piece * 216 % 128
        wide = jnp.concatenate([gathered[piece], jnp.zeros((1, 128), jnp.float32)], axis=1)
        wide = pltpu.roll(jnp.concatenate([wide] * 8, axis=0), shift, 1)[0:1]
        for step in range(3):
            flat[row + step] += wide[:, step * 128 : step * 128 + 128]
    for row in range(6):
        for column in range(9):
            mods[row : row + 1, column * 128 : column * 128 + 128] = flat[row * 9 + column]
    mods[6:8, :] = jnp.zeros((2, 1152), jnp.float32)

    def to_sibling(index, source, target):
        return pltpu.make_async_remote_copy(
            src_ref=source,
            dst_ref=target,
            send_sem=pair_send.at[index],
            recv_sem=pair_recv.at[index],
            device_id=sibling,
            device_id_type=MESH,
        )

    def modulate(index, _):
        rows = row_range(index)
        normed[rows, :] = normed[rows, :] * (1.0 + mods[1:2]) + mods[0:1]
        return _

    lax.fori_loop(0, 4, modulate, 0)
    send_a[...] = normed[...].T
    pair_a = to_sibling(0, send_a, got_a)
    pair_a.start()
    for part in range(8):
        lhs_two[part, :, 0:256] = send_a[part * 144 : part * 144 + 144].astype(jnp.bfloat16)
    loads[2].wait()
    for part in range(3):
        block = dot_nn(
            normed[...].astype(jnp.bfloat16), w_q[:, part * 1152 : part * 1152 + 1152]
        )
        if part == 0:
            block = block + as_row(b_qv)[:, 0:1152]
        if part == 2:
            block = block + as_row(b_qv)[:, 1152:2304]
        qkv_t[part * 1152 : part * 1152 + 1152, :] = block.T

    def branch_grad(index, _):
        rows = row_range(index)
        normed[rows, :] = cot[rows, :] * mods[5:6]
        return _

    scale = 1.0 / math.sqrt(72)

    def one_head(head, _):
        parts = []
        for part in range(3):
            rows = pl.ds(pl.multiple_of(part * 1152 + head * 72, 8), 72)
            padded = jnp.concatenate([qkv_t[rows, :], jnp.zeros((8, 256), jnp.float32)], axis=0)
            parts.append(padded.astype(jnp.bfloat16))
            heads[head + part * 16] = parts[-1]
        query, key, value = parts
        scores = dot_tn(key, query) * scale + jnp.concatenate([keys_off[...]] * 2, axis=1)
        shifted = jnp.exp(scores - jnp.max(scores, axis=0, keepdims=True))
        weights = (shifted / jnp.sum(shifted, axis=0, keepdims=True)).astype(jnp.bfloat16)
        rows = pl.ds(pl.multiple_of(head * 72, 8), 72)
        send_b[rows, :] = dot_nn(value, weights)[0:72]
        return _

    lax.fori_loop(0, 16, one_head, 0, unroll=4)
    pair_b = to_sibling(1, send_b, got_b)
    pair_b.start()
    for part in range(8):
        lhs_two[part + 8, :, 0:256] = send_b[part * 144 : part * 144 + 144].astype(jnp.bfloat16)
    lax.fori_loop(0, 4, branch_grad, 0)
    send_c[...] = normed[...].T
    pair_c = to_sibling(2, send_c, got_c)
    pair_c.start()
    rhs_zero[:, 0:256] = send_c[...].astype(jnp.bfloat16)
    loads[3].wait()
    attn_out[...] = dot_tn(send_b[...].astype(jnp.bfloat16), w_p[...]) + as_row(b_proj)

    def second_norm(index, _):
        rows = row_range(index)
        stream = tokens[rows, :].astype(jnp.float32) + mods[2:3] * attn_out[rows, :]
        resid[rows, :] = stream
        normed[rows, :] = norm(stream) * (1.0 + mods[4:5]) + mods[3:4]
        return _

    lax.fori_loop(0, 4, second_norm, 0)
    send_d[...] = normed[...].T
    pair_d = to_sibling(3, send_d, got_d)
    pair_d.start()
    for part in range(8):
        lhs_one[part, :, 0:256] = send_d[part * 144 : part * 144 + 144].astype(jnp.bfloat16)
    pair_a.wait()
    for part in range(8):
        lhs_two[part, :, 256:512] = got_a[part * 144 : part * 144 + 144].astype(jnp.bfloat16)
    inner = math.sqrt(2.0 / math.pi)
    pair_e = []
    for part in range(4):
        fc_load(part).wait()
        columns = slice(part * 1152, part * 1152 + 1152)
        hidden = dot_nn(normed[...].astype(jnp.bfloat16), w_f[part % 2]) + as_row(b_fc1)[:, columns]
        qkv_t[0:1152, :] = hidden.T
        if part < 2:
            fc_load(part + 2).start()

        def gelu(index, _, part=part):
            rows = pl.ds(pl.multiple_of(index * 144, 144), 144)
            values = qkv_t[rows, :]
            square = values * values
            bend = jnp.tanh(inner * values * (1.0 + 0.044715 * square))
            half = 0.5 * (1.0 + bend)
            active = values * half
            steep = half + 0.5 * values * (1.0 - bend * bend) * inner * (
                1.0 + 3.0 * 0.044715 * square
            )
            into = pl.ds(pl.multiple_of(part * 1152 + index * 144, 144), 144)
            act_out[into, :] = active.astype(jnp.bfloat16)
            slope_out[into, :] = steep.astype(jnp.bfloat16)
            chip = part * 4 + lax.div(index, 2)

            @pl.when(lax.rem(index, 2) == core)
            def _():
                lhs_zero[chip, :, 0:256] = active.astype(jnp.bfloat16)

            @pl.when(lax.rem(index, 2) != core)
            def _():
                send_e[chip] = active

            return 0

        lax.fori_loop(0, 8, gelu, 0)
        some = pl.ds(part * 4, 4)
        pair_e.append(to_sibling(4 + part, send_e.at[some], got_e.at[some]))
        pair_e[-1].start()
        if part == 0:
            pair_b.wait()
            for chip in range(8):
                rows = got_b[chip * 144 : chip * 144 + 144]
                lhs_two[chip + 8, :, 256:512] = rows.astype(jnp.bfloat16)
        if part == 1:
            pair_c.wait()
            rhs_zero[:, 256:512] = got_c[...].astype(jnp.bfloat16)
        if part == 2:
            pair_d.wait()
            for chip in range(8):
                rows = got_d[chip * 144 : chip * 144 + 144]
                lhs_one[chip, :, 256:512] = rows.astype(jnp.bfloat16)
    for part in range(4):
        pair_e[part].wait()
        for chip in range(part * 4, part * 4 + 4):
            lhs_zero[chip, :, 256:512] = got_e[chip].astype(jnp.bfloat16)


def forward(operands):
    dma = pltpu.SemaphoreType.DMA
    vmem = pl.BlockSpec(memory_space=pltpu.VMEM)
    smem = pl.BlockSpec(memory_space=pltpu.SMEM)
    anywhere = pl.BlockSpec(memory_space=pl.ANY)
    full, small = jnp.float32, jnp.bfloat16
    out = jax.ShapeDtypeStruct
    return pl.pallas_call(
        forward_kernel,
        out_shape=(
            out((2, 1152), full),
            out((2, 1152), full),
            out((8, 1152), full),
            out((16, 144, 512), small),
            out((8, 144, 512), small),
            out((16, 144, 512), small),
            out((1152, 512), small),
            out((4608, 256), small),
            out((4608, 256), small),
            out((48, 80, 256), small),
            out((256, 1152), full),
            out((256, 1152), full),
            out((256, 1152), full),
            out((256, 1152), small),
            out((256, 128), full),
            out((2, 128), full),
        ),
        in_specs=[vmem] * 3
        + [smem, smem, vmem]
        + [anywhere, vmem] * 2
        + [vmem, vmem]
        + [anywhere, vmem] * 3,
        out_specs=(vmem,) * 16,
        scratch_shapes=[
            pltpu.VMEM((2, 1, 256), full),
            pltpu.VMEM((32, 1, 256), full),
            pltpu.VMEM((56, 1, 128), full),
            pltpu.VMEM((256, 1152), full),
            pltpu.VMEM((3456, 256), full),
            pltpu.VMEM((1152, 3456), small),
            pltpu.VMEM((1152, 1152), small),
            pltpu.VMEM((2, 1152, 1152), small),
            pltpu.VMEM((256, 1152), small),
            pltpu.VMEM((1152, 1152), small),
            pltpu.VMEM((256, 128), full),
            pltpu.VMEM((256, 128), full),
            pltpu.VMEM((1152, 256), full),
            pltpu.VMEM((1152, 256), full),
            pltpu.VMEM((1152, 256), full),
            pltpu.VMEM((1152, 256), full),
            pltpu.VMEM((16, 144, 256), full),
            pltpu.VMEM((1152, 256), full),
            pltpu.VMEM((1152, 256), full),
            pltpu.VMEM((1152, 256), full),
            pltpu.VMEM((1152, 256), full),
            pltpu.VMEM((16, 144, 256), full),
            dma((32,)),
            dma((32,)),
            dma((4,)),
            dma((8,)),
            dma((8,)),
            dma((2,)),
        ],
        compiler_params=pltpu.CompilerParams(
            collective_id=2, has_side_effects=True, vmem_limit_bytes=255 * 2**18
        ),
    )(*operands)


def on_device(
    tokens,
    out_grad,
    timesteps,
    labels,
    grid_ids,
    w_qkv,
    b_qv,
    w_proj,
    b_proj,
    w_fc1,
    b_fc1,
    w_fc2,
    b_fc2,
    w_ada,
    b_ada,
    w_t1,
    b_t1,
    w_t2,
    b_t2,
    table,
):
    dp_count = lax.axis_size("dp")
    dp_place = lax.axis_index("dp")
    model_width = tokens.shape[1]
    time_feats = time_embed(timesteps, w_t1.shape[0] // 2)
    (
        pre_time,
        condition,
        mods,
        lhs_two,
        lhs_one,
        lhs_zero,
        rhs_zero,
        act_t,
        slope_t,
        heads,
        cotangent,
        resid_one,
        attn_out,
        ada_wide,
        bias_keys,
        onehot,
    ) = forward(
        [
            tokens,
            out_grad,
            time_feats,
            labels,
            grid_ids,
            table,
            w_t1,
            b_t1,
            w_t2,
            b_t2,
            w_ada.T,
            b_ada,
            w_qkv,
            b_qv,
            w_proj,
            b_proj,
            w_fc1,
            b_fc1,
        ]
    )
    (
        sum_qkv,
        sum_proj,
        sum_fc1,
        sum_fc2,
        block_out,
        input_grad,
        packs,
        sums,
    ) = backward(
        [
            lhs_zero,
            lhs_one,
            lhs_two,
            rhs_zero,
            act_t,
            slope_t,
            heads,
            bias_keys,
            cotangent,
            resid_one,
            attn_out,
            tokens,
            mods,
            b_fc2,
            pre_time,
            condition,
            time_feats,
            onehot,
            ada_wide,
            w_t2,
            w_qkv,
            w_proj,
            w_fc1,
            w_fc2,
        ]
    )
    packs = packs.reshape(8, PACK)
    grad_cond, grad_pre = packs[:, 0:1152], packs[:, 1152:2304]
    act_cond, act_time = packs[:, 2304:3456], packs[:, 3456:4608]
    d_mod, feats_all = packs[:, 4608:4824], packs[:, 4864:5120]
    class_rows = packs[:, 5120 : 5120 + table.shape[0]]
    own_time = lax.dynamic_slice_in_dim(act_time, dp_place * 36, 36, 1)
    own_feats = lax.dynamic_slice_in_dim(feats_all, dp_place * 8, 8, 1)
    return (
        block_out,
        input_grad,
        sum_qkv,
        sums[0, 0:72],
        sum_proj,
        sums[1, 0:36],
        sum_fc1,
        sums[2:4].reshape(256)[0:144],
        sum_fc2,
        sums[4, 0:36],
        hdot_t(act_cond, d_mod),
        jnp.sum(d_mod, axis=0),
        hdot_t(own_feats, grad_pre),
        own_block(jnp.sum(grad_pre, axis=0), dp_place, dp_count),
        hdot_t(own_time, grad_cond),
        own_block(jnp.sum(grad_cond, axis=0), dp_place, dp_count),
        hdot_t(class_rows, grad_cond),
    )


def solution(mesh):
    placed = (
        P(("group", "dp"), None),
        P(("group", "dp"), None),
        P("group"),
        P("group"),
        P("group"),
        P(),
        P(),
        P(),
        P(),
        P(),
        P(),
        P(),
        P(),
        P(None, "dp"),
        P("dp"),
        P(),
        P(),
        P(),
        P(),
        P(),
    )
    return jax.shard_map(
        on_device,
        mesh=mesh,
        in_specs=placed,
        out_specs=(
            P(("group", "dp"), None),
            P(("group", "dp"), None),
            P("dp", None),
            P("dp"),
            P("dp", None),
            P("dp"),
            P("dp", None),
            P("dp"),
            P("dp", None),
            P("dp"),
            P(None, "dp"),
            P("dp"),
            P("dp", None),
            P("dp"),
            P("dp", None),
            P("dp"),
            P(),
        ),
        check_vma=False,
    )
```

```python
import math

import jax
import jax.numpy as jnp
from jax import lax
from jax.experimental import pallas as pl
from jax.experimental.pallas import tpu as pltpu
from jax.sharding import PartitionSpec as P

SLOTS = 256
ITEM_FRAMES = 16


EPS = 1e-06
NEG = -1e30


def norm_back(grad_in, normed, inv_std):
    return inv_std * (
        grad_in
        - jnp.mean(grad_in, axis=-1, keepdims=True)
        - normed * jnp.mean(grad_in * normed, axis=-1, keepdims=True)
    )


def silu_back(pre_vals, grad_in):
    sigmoid = jax.nn.sigmoid(pre_vals)
    return grad_in * sigmoid * (1.0 + pre_vals * (1.0 - sigmoid))


def time_embed(step_ids, width_half):
    frequency = jnp.exp(
        jnp.arange(width_half, dtype=jnp.float32) * (-math.log(10000.0) / width_half)
    )
    angles = step_ids.astype(jnp.float32)[:, None] * frequency[None, :]
    return jnp.concatenate([jnp.cos(angles), jnp.sin(angles)], axis=1)


def split_three(values):
    high = values.astype(jnp.bfloat16)
    rest = values - high.astype(jnp.float32)
    middle = rest.astype(jnp.bfloat16)
    low = (rest - middle.astype(jnp.float32)).astype(jnp.bfloat16)
    return jnp.concatenate([high, middle, low], axis=0)


def exact_dot(values, weights, contract=0):
    rows = values.shape[0]
    thrice = lax.dot_general(
        split_three(values),
        weights,
        (((1,), (contract,)), ((), ())),
        preferred_element_type=jnp.float32,
    )
    return thrice[0:rows] + thrice[rows : 2 * rows] + thrice[2 * rows : 3 * rows]


def silu(values):
    return values / (1.0 + jnp.exp(-values))


def dot_nn(left, right):
    return jnp.dot(left, right, preferred_element_type=jnp.float32)


def dot_nt(left, right):
    return lax.dot_general(
        left, right, (((1,), (1,)), ((), ())), preferred_element_type=jnp.float32
    )


def dot_tn(left, right):
    return lax.dot_general(
        left, right, (((0,), (0,)), ((), ())), preferred_element_type=jnp.float32
    )


MESH = pl.DeviceIdType.MESH
ORDERS = ((("y", "z", "x"), ("z", "x", "y"), ("x", "y", "z")),) * 3
STREAMS = tuple(
    tuple((order, pairing) for pairing in (0, 1) for order in orders) for orders in ORDERS
)
BLOCKS = (32, 16, 8, 4, 2, 1)
LANDS_AT = (0, 32, 48, 56, 60, 62)
PIECE = 56
OWN = 72
CHUNK = 384
ROWS = 32
WINDOWS = ((0, 216, 3), (54, 72, 2), (72, 36, 2), (81, 144, 3), (117, 36, 2))


def coords():
    place = lax.axis_index("dp")
    return {
        "y": lax.axis_index("group"),
        "z": lax.div(place, 8),
        "x": lax.rem(lax.div(place, 2), 4),
        "core": lax.rem(place, 2),
    }


def device_at(at):
    return (at["y"], (at["z"] * 4 + at["x"]) * 2 + at["core"])


def dp_peer(hop):
    return (lax.axis_index("group"), lax.rem(lax.axis_index("dp") + hop, 32))


def sibling_of(at):
    return device_at({**at, "core": 1 - at["core"]})


def partner_of(at, axis, pairing):
    here = at[axis]
    if pairing == 0:
        there = here + 1 - 2 * lax.rem(here, 2)
    else:
        there = lax.rem(here + 3 + 2 * lax.rem(here, 2), 4)
    return device_at({**at, axis: there})


def slot_of(pairing, value):
    if pairing == 1:
        return value
    if isinstance(value, int):
        return (0, 2, 3, 1)[value]
    return lax.rem(value + lax.div(value + 1, 2), 4)


PACK = 4 * 1152 + 2 * 256 + 128


def backward_kernel(
    lhs_zero,
    lhs_one,
    lhs_two,
    rhs_zero,
    act_flat,
    slope,
    heads,
    bias_keys,
    cot,
    resid,
    attn_out,
    tokens,
    mods,
    b_fc2,
    pre_in,
    cond_in,
    feats,
    onehot,
    w_ada,
    w_t2,
    w_qkv,
    w_proj,
    w_fc1,
    w_fc2,
    out_qkv,
    out_proj,
    out_fc1,
    out_fc2,
    block_out,
    input_grad,
    packed,
    sums,
    parts,
    landed,
    lhs,
    rhs,
    stage_rhs,
    leave,
    final,
    other,
    narrow,
    d_mod,
    bias_fc1,
    bias_qv,
    bias_proj,
    bias_fc2,
    flat,
    shares,
    got,
    conds,
    sums_all,
    out_rows,
    in_rows,
    wa,
    wb,
    slope_in,
    act_in,
    grad_t,
    branch,
    grad_resid,
    all_t,
    mixed_t,
    heads_in,
    rows_a,
    rows_b,
    rows_c,
    rows_d,
    send_sem,
    recv_sem,
    credit,
    swap_send,
    swap_recv,
    swap_credit,
    own_sem,
    ring_send,
    ring_recv,
    pair_send,
    pair_recv,
    load_sem,
    row_sem,
    head_sem,
    other_credit,
    out_sem,
    share_send,
    share_recv,
    cond_send,
    cond_recv,
    group_send,
    group_recv,
):
    at = coords()
    core = at["core"]
    sibling = sibling_of(at)
    barrier = pltpu.get_barrier_semaphore()
    place = lax.axis_index("dp")

    def group_peer(hop):
        return (lax.rem(at["y"] + hop, 4), place)

    def hello(hop, _):
        pl.semaphore_signal(barrier, inc=1, device_id=dp_peer(hop), device_id_type=MESH)
        return _

    lax.fori_loop(1, 32, hello, 0)
    for hop in (1, 2, 3):
        pl.semaphore_signal(barrier, inc=1, device_id=group_peer(hop), device_id_type=MESH)
    def swap():
        return pltpu.make_async_remote_copy(
            src_ref=leave,
            dst_ref=stage_rhs,
            send_sem=swap_send,
            recv_sem=swap_recv,
            device_id=sibling,
            device_id_type=MESH,
        )

    def lhs_load(phase):
        source = (lhs_zero, lhs_one, lhs_two)[phase]
        target = lhs.at[0:8] if phase == 1 else lhs
        return pltpu.make_async_copy(source, target, own_sem.at[0])

    def rhs_load():
        return pltpu.make_async_copy(rhs_zero, rhs.at[0:1152], own_sem.at[1])

    def swap_start(phase):
        lhs_load(phase).start()
        if phase == 2:
            pl.semaphore_wait(swap_credit, 1)
        swap().start()

    def swap_finish(phase):
        swap().wait()

        def narrow_rhs(step, _):
            rows = pl.ds(pl.multiple_of(step * 144, 144), 144)
            rhs[rows, 256:512] = stage_rhs[rows, :].astype(jnp.bfloat16)
            return _

        lax.fori_loop(0, 16, narrow_rhs, 0)
        if phase == 1:
            pl.semaphore_signal(swap_credit, inc=1, device_id=sibling, device_id_type=MESH)
        lhs_load(phase).wait()

    def base_of(phase, stream, z_place, x_place, y_slot):
        order, pairing = STREAMS[phase][stream]
        slots = {"y": y_slot, "z": slot_of(pairing, z_place), "x": slot_of(pairing, x_place)}
        return (slots[order[0]] * 4 + slots[order[1]]) * 4 + slots[order[2]]

    def keep(phase, stream, chip, rows):
        half = phase % 2
        z_place, x_place = lax.div(chip, 4), lax.rem(chip, 4)
        for y_slot in range(4):
            block = base_of(phase, stream, z_place, x_place, y_slot)
            first = y_slot * PIECE
            for unit in range(3):
                low, high = max(first, OWN * unit), min(first + PIECE, OWN * unit + OWN)
                if low < high:
                    parts[half, stream, block, low - first : high - first, :] = rows[
                        low - OWN * unit : high - OWN * unit, unit * 128 : unit * 128 + 128
                    ]

    def halving(phase, stream, step):
        order, pairing = STREAMS[phase][stream]
        axis = order[step // 2]
        slots = [slot_of(pairing, at[name]) for name in order]
        base = 0
        for level in range(step // 2):
            base = base + slots[level] * (64 // 4 ** (level + 1))
        slot = slots[step // 2]
        side = lax.div(slot, 2) if step % 2 == 0 else slot
        away = 1 - side if step % 2 == 0 else slot + 1 - 2 * lax.rem(slot, 2)
        count = BLOCKS[step]
        kept, sent = base + side * count, base + away * count
        partner = partner_of(at, axis, pairing if step % 2 == 0 else 1 - pairing)
        source = parts.at[phase % 2, stream]
        if phase == 0 and step >= 3:
            origin = slots[0] * 16 + lax.div(slots[1], 2) * 8
            kept, sent = kept - origin, sent - origin
            source = narrow.at[stream]
        copy = pltpu.make_async_remote_copy(
            src_ref=source.at[pl.ds(sent, count)],
            dst_ref=landed.at[stream, pl.ds(LANDS_AT[step], count)],
            send_sem=send_sem.at[stream, step],
            recv_sem=recv_sem.at[stream, step],
            device_id=partner,
            device_id_type=MESH,
        )
        return copy, kept, partner

    def send(phase, stream, step):
        copy, _, _ = halving(phase, stream, step)
        if phase:
            pl.semaphore_wait(credit.at[stream, step], 1)
        copy.start()

    def receive(phase, step):
        for stream in range(6):
            copy, kept, partner = halving(phase, stream, step)
            copy.wait()
            half = phase % 2
            count = BLOCKS[step]
            late = phase == 0 and step >= 3
            if step < 5:

                def add(block, _):
                    arrived = landed[stream, LANDS_AT[step] + block]
                    if late:
                        narrow[stream, kept + block] += arrived
                    elif phase == 0 and step == 2:
                        narrow[stream, block] = parts[half, stream, kept + block] + arrived
                    else:
                        parts[half, stream, kept + block] += arrived
                    return _

                lax.fori_loop(0, count, add, 0, unroll=min(count, 4))
            else:
                mine = narrow[stream, kept] if late else parts[half, stream, kept]
                final[phase, at["y"], stream] = mine + landed[stream, LANDS_AT[step]]
            if phase < 2:
                pl.semaphore_signal(
                    credit.at[stream, step], inc=1, device_id=partner, device_id_type=MESH
                )
            if step < 5:
                send(phase, stream, step + 1)

    def products(phase):
        together, stacked = (3, 2) if phase == 2 else (2, 4)
        for group in range(6 // together):
            members = range(group * together, (group + 1) * together)
            if phase == 0:
                first = group * together // 2 * CHUNK
                width = together // 2 * CHUNK
                count = 16
            else:
                first = members[0] * CHUNK
                width = together * CHUNK
                count = 8
            shift = core * 8 if phase == 2 and members[0] >= 3 else 0

            def some(step, _):
                left = lhs[pl.ds(step * stacked + shift, stacked)]
                rows = dot_nt(
                    left.reshape(stacked * 144, 512), rhs[first : first + width, :]
                )
                for place in range(stacked):
                    at_row = place * 144
                    if phase == 0:
                        chip = step * stacked + place
                        for third in range(together // 2):
                            column = third * CHUNK
                            block = rows[at_row : at_row + 144, column : column + CHUNK]
                            stream = group * together // 2 + third
                            keep(phase, stream, chip, block[0:72])
                            keep(phase, stream + 3, chip, block[72:144])
                    else:
                        chip = (step * stacked + place) * 2
                        for place_at, stream in enumerate(members):
                            column = place_at * CHUNK
                            block = rows[at_row : at_row + 144, column : column + CHUNK]
                            keep(phase, stream, chip, block[0:72])
                            keep(phase, stream, chip + 1, block[72:144])
                return _

            lax.fori_loop(0, count // stacked, some, 0)
            for member in members:
                stream = member
                if phase == 0:
                    stream = group * together // 2 + (member - members[0]) // 2
                    stream += 3 * ((member - members[0]) % 2)
                send(phase, stream, 0)

    def ring(phase):
        mine = at["y"]
        copies = []
        for place, hop in enumerate((1, 3)):
            copies.append(
                pltpu.make_async_remote_copy(
                    src_ref=final.at[phase, mine],
                    dst_ref=final.at[phase, mine],
                    send_sem=ring_send.at[phase, place],
                    recv_sem=ring_recv.at[phase, place],
                    device_id=device_at({**at, "y": lax.rem(mine + hop, 4)}),
                    device_id_type=MESH,
                )
            )
        return copies

    def relay(phase):
        mine = at["y"]
        copies = []
        for place, hop in enumerate((1, 3)):
            origin = lax.rem(mine + 4 - hop, 4)
            half = pl.ds(place * 3, 3)
            copies.append(
                pltpu.make_async_remote_copy(
                    src_ref=final.at[phase, origin, half],
                    dst_ref=final.at[phase, origin, half],
                    send_sem=ring_send.at[phase, place + 2],
                    recv_sem=ring_recv.at[phase, place + 2],
                    device_id=device_at({**at, "y": lax.rem(mine + hop, 4)}),
                    device_id_type=MESH,
                )
            )
        return copies

    def across(phase):
        return pltpu.make_async_remote_copy(
            src_ref=final.at[phase],
            dst_ref=other,
            send_sem=pair_send.at[phase - 1],
            recv_sem=pair_recv.at[phase - 1],
            device_id=sibling,
            device_id_type=MESH,
        )

    def whole(get, stream):
        pairing = STREAMS[0][stream][1]
        order = sorted(range(4), key=lambda y_place: slot_of(pairing, y_place))
        return jnp.concatenate([get(y_place, stream) for y_place in order], axis=0)

    def write_rows(phase, low):
        for side in range(2):
            mine = side == (0 if low == 0 else 1)
            for stream in range(6):
                if mine:
                    rows = whole(lambda y_place, stream: final[phase, y_place, stream], stream)
                else:
                    rows = whole(lambda y_place, stream: other[y_place, stream], stream)
                for unit in range(3):
                    block = rows[OWN * unit + low : OWN * unit + low + 36]
                    column = side * 18 + stream * 3 + unit
                    if phase == 1:
                        out_fc1[:, column * 128 : column * 128 + 128] = block
                    elif column < 27:
                        out_qkv[:, column * 128 : column * 128 + 128] = block
                    else:
                        out_proj[:, (column - 27) * 128 : (column - 27) * 128 + 128] = block

    def write(phase):
        if phase == 0:
            for stream in range(6):
                rows = whole(lambda y_place, stream: final[0, y_place, stream], stream)
                half, third = stream // 3, stream % 3
                for unit in range(3):
                    column = third * 3 + unit
                    out_fc2[half * 72 : half * 72 + 72, column * 128 : column * 128 + 128] = rows[
                        OWN * unit : OWN * unit + 72
                    ]
            return

        @pl.when(core == 0)
        def _():
            write_rows(phase, 0)

        @pl.when(core == 1)
        def _():
            write_rows(phase, 36)

        if phase == 1:
            pl.semaphore_signal(other_credit, inc=1, device_id=sibling, device_id_type=MESH)

    def ring_start(phase):
        for copy in ring(phase):
            copy.start()

    def ring_relay(phase):
        for copy, onward in zip(ring(phase), relay(phase)):
            copy.wait()
            onward.start()

    def ring_finish(phase):
        for copy in relay(phase):
            copy.wait()
        if phase == 2:
            pl.semaphore_wait(other_credit, 1)
        if phase:
            across(phase).start()

    def clear(chip, _):
        z_place, x_place = lax.div(chip, 4), lax.rem(chip, 4)
        for half in range(2):
            for stream in range(6):
                block = base_of(half, stream, z_place, x_place, 3)
                parts[half, stream, block, 48:56, :] = jnp.zeros((8, 128), jnp.float32)
        return _

    ones = jnp.ones((8, 256), jnp.bfloat16)

    def mlp_loads(chunk):
        slot = lax.rem(chunk, 2)
        rows = pl.ds(pl.multiple_of(chunk * CHUNK, CHUNK), CHUNK)
        return [
            pltpu.make_async_copy(w_fc2.at[rows], wa.at[slot], load_sem.at[0, slot]),
            pltpu.make_async_copy(w_fc1.at[:, rows], wb.at[slot], load_sem.at[1, slot]),
            pltpu.make_async_copy(slope.at[rows], slope_in.at[slot], load_sem.at[2, slot]),
        ]

    def branch_loads(chunk):
        slot = lax.rem(chunk, 2)
        rows = pl.ds(pl.multiple_of(chunk * CHUNK, CHUNK), CHUNK)
        return [
            pltpu.make_async_copy(w_fc2.at[rows], wa.at[slot], load_sem.at[0, slot]),
            pltpu.make_async_copy(act_flat.at[rows], act_in.at[slot], load_sem.at[3, slot]),
        ]

    def branch_begin():
        for copy in branch_loads(0):
            copy.start()

    def branch_forward(low, high):
        if low == 0:
            branch[...] = jnp.zeros((256, 1152), jnp.float32)

        def branch_step(chunk, carry):
            slot = lax.rem(chunk, 2)

            @pl.when(chunk < 11)
            def _():
                for copy in branch_loads(chunk + 1):
                    copy.start()

            for copy in branch_loads(chunk):
                copy.wait()
            branch[...] += dot_tn(act_in[slot], wa[slot])
            return carry

        lax.fori_loop(low, high, branch_step, 0)

    def mlp_begin():
        for copy in mlp_loads(0):
            copy.start()

    def mlp_backward(low, high):
        if low == 0:
            rhs[0:1152, 256:512] = rhs[0:1152, 0:256]
            grad_t[...] = jnp.zeros((1152, 256), jnp.float32)

        def chunk_step(chunk, carry):
            slot = lax.rem(chunk, 2)

            @pl.when(chunk < 11)
            def _():
                for copy in mlp_loads(chunk + 1):
                    copy.start()

            for copy in mlp_loads(chunk):
                copy.wait()
            grad_act = dot_nn(wa[slot], rhs[0:1152, 256:512])
            grad_hidden = (grad_act * slope_in[slot].astype(jnp.float32)).astype(jnp.bfloat16)
            side = lax.div(chunk, 6)
            rows = pl.ds(pl.multiple_of(lax.rem(chunk, 6) * CHUNK, CHUNK), CHUNK)

            @pl.when(side == core)
            def _():
                rhs[rows, 0:256] = grad_hidden

            @pl.when(side != core)
            def _():
                leave[rows, :] = grad_hidden.astype(jnp.float32)

            columns = pl.ds(pl.multiple_of(chunk * CHUNK, CHUNK), CHUNK)
            bias_fc1[:, columns] = dot_nt(ones, grad_hidden)[0:1]
            grad_t[...] += dot_nn(wb[slot], grad_hidden)
            return carry

        lax.fori_loop(low, high, chunk_step, 0)

    def row_block(source, index):
        return source.at[pl.ds(pl.multiple_of(index * ROWS, ROWS), ROWS)]

    def norm(values):
        mean = jnp.mean(values, axis=-1, keepdims=True)
        centered = values - mean
        inverse = lax.rsqrt(jnp.mean(centered * centered, axis=-1, keepdims=True) + EPS)
        return centered * inverse, inverse

    def total(values):
        return jnp.sum(values, axis=0, keepdims=True)

    def middle_loads(index):
        slot = lax.rem(index, 2)
        return [
            pltpu.make_async_copy(row_block(source, index), target.at[slot], row_sem.at[place, slot])
            for place, (source, target) in enumerate(
                ((cot, rows_a), (resid, rows_b), (attn_out, rows_c))
            )
        ]

    def token_load(index):
        slot = lax.rem(index, 2)
        return pltpu.make_async_copy(
            row_block(tokens, index), rows_d.at[slot], row_sem.at[3, slot]
        )

    def proj_load(chunk):
        slot = lax.rem(chunk, 2)
        rows = pl.ds(pl.multiple_of(chunk * 288, 288), 288)
        return pltpu.make_async_copy(w_proj.at[rows], wa.at[slot, 0:288], load_sem.at[0, slot])

    def rows_out(kind, index):
        slot = lax.rem(index, 2)
        target = block_out if kind == 0 else input_grad
        buffer = out_rows if kind == 0 else in_rows
        return pltpu.make_async_copy(
            buffer.at[slot], row_block(target, index), out_sem.at[kind, slot]
        )

    def drain(kind):
        rows_out(kind, 256 // ROWS - 2).wait()
        rows_out(kind, 256 // ROWS - 1).wait()

    def middle_begin():
        for copy in middle_loads(0):
            copy.start()
        proj_load(0).start()
        d_mod[...] = jnp.zeros((8, 1152), jnp.float32)
        bias_proj[...] = jnp.zeros((1, 1152), jnp.float32)
        bias_fc2[...] = jnp.zeros((1, 1152), jnp.float32)
        grad_resid[...] = grad_t[...].T

    def middle_rows(low, high):
        scale_mlp, gate_attn = mods[4:5], mods[2:3]

        def rows_step(index, carry):
            rows = pl.ds(pl.multiple_of(index * ROWS, ROWS), ROWS)
            slot = lax.rem(index, 2)

            @pl.when(index < 256 // ROWS - 1)
            def _():
                for copy in middle_loads(index + 1):
                    copy.start()

            for copy in middle_loads(index):
                copy.wait()

            cotangent, stream_rows = rows_a[slot], rows_b[slot]
            normed, inverse = norm(stream_rows)
            grad_in = grad_resid[rows, :]
            d_mod[3:4, :] += total(grad_in)
            d_mod[4:5, :] += total(grad_in * normed)
            back = norm_back(grad_in * (1.0 + scale_mlp), normed, inverse)
            grads = cotangent + back
            grad_resid[rows, :] = grads
            d_mod[2:3, :] += total(grads * rows_c[slot])
            grad_attn = (grads * gate_attn).astype(jnp.bfloat16).astype(jnp.float32)
            bias_proj[...] += total(grad_attn)
            branch[rows, :] = grad_attn
            return carry

        lax.fori_loop(low, high, rows_step, 0)

    def finish_begin():
        for copy in middle_loads(0)[0:2]:
            copy.start()

    def finish_rows():
        gate_mlp = mods[5:6]

        def finish_step(index, carry):
            rows = pl.ds(pl.multiple_of(index * ROWS, ROWS), ROWS)
            slot = lax.rem(index, 2)

            @pl.when(index < 256 // ROWS - 1)
            def _():
                for copy in middle_loads(index + 1)[0:2]:
                    copy.start()

            for copy in middle_loads(index)[0:2]:
                copy.wait()

            @pl.when(index >= 2)
            def _():
                rows_out(0, index - 2).wait()

            cotangent, stream_rows = rows_a[slot], rows_b[slot]
            branch_rows = branch[rows, :] + b_fc2[...].reshape(1, 1152)
            out_rows[slot] = (stream_rows + gate_mlp * branch_rows).astype(jnp.bfloat16)
            rows_out(0, index).start()
            d_mod[5:6, :] += total(cotangent * branch_rows)
            bias_fc2[...] += total(
                (cotangent * gate_mlp).astype(jnp.bfloat16).astype(jnp.float32)
            )
            return carry

        lax.fori_loop(0, 256 // ROWS, finish_step, 0)

    def middle_end():
        all_t[3456:4608, :] = branch[...].T.astype(jnp.bfloat16)

        def proj_step(chunk, carry):
            @pl.when(chunk < 3)
            def _():
                proj_load(chunk + 1).start()

            proj_load(chunk).wait()
            grads = dot_nn(wa[lax.rem(chunk, 2), 0:288], all_t[3456:4608, :])
            for head in range(4):
                padded = jnp.concatenate(
                    [grads[head * 72 : head * 72 + 72], jnp.zeros((8, 256), jnp.float32)], axis=0
                )
                mixed_t[chunk * 4 + head] = padded.astype(jnp.bfloat16)
            return carry

        lax.fori_loop(0, 4, proj_step, 0)

    def heads_load(pair_at):
        slot = lax.rem(pair_at, 2)
        return [
            pltpu.make_async_copy(
                heads.at[pl.ds(part * 16 + pair_at * 2, 2)],
                heads_in.at[slot, part],
                head_sem.at[part, slot],
            )
            for part in range(3)
        ]

    def attention_backward(low, high):
        scale = 1.0 / math.sqrt(72)

        def one_head(pair_at, side):
            slot = lax.rem(pair_at, 2)
            query, key, value = (heads_in[slot, part, side] for part in range(3))
            grad_mixed = mixed_t[pair_at * 2 + side]
            scores = dot_tn(key, query) * scale + jnp.concatenate([bias_keys[...]] * 2, axis=1)
            shifted = jnp.exp(scores - jnp.max(scores, axis=0, keepdims=True))
            weights = shifted / jnp.sum(shifted, axis=0, keepdims=True)
            grad_weights = dot_tn(value, grad_mixed)
            row_dot = jnp.sum(weights * grad_weights, axis=0, keepdims=True)
            grad_scores = (weights * (grad_weights - row_dot)).astype(jnp.bfloat16)
            return (
                dot_nn(key, grad_scores)[0:72] * scale,
                dot_nt(query, grad_scores)[0:72] * scale,
                dot_nt(grad_mixed, weights.astype(jnp.bfloat16))[0:72],
            )

        def two_heads(pair_at, carry):
            @pl.when(pair_at < 7)
            def _():
                for copy in heads_load(pair_at + 1):
                    copy.start()

            for copy in heads_load(pair_at):
                copy.wait()
            first, second = one_head(pair_at, 0), one_head(pair_at, 1)
            for part in range(3):
                rows = pl.ds(pl.multiple_of(part * 1152 + pair_at * 144, 16), 144)
                all_t[rows, :] = jnp.concatenate([first[part], second[part]], axis=0).astype(
                    jnp.bfloat16
                )
            return carry

        lax.fori_loop(low, high, two_heads, 0)

    def sides():
        def side(step, _):
            mine = pl.ds(pl.multiple_of(core * 2304 + step * 144, 16), 144)
            theirs = pl.ds(pl.multiple_of((1 - core) * 2304 + step * 144, 16), 144)
            rows = pl.ds(pl.multiple_of(step * 144, 144), 144)
            rhs[rows, 0:256] = all_t[mine, :]
            leave[rows, :] = all_t[theirs, :].astype(jnp.float32)
            return _

        lax.fori_loop(0, 16, side, 0)

    def qkv_load(chunk):
        slot = lax.rem(chunk, 2)
        columns = pl.ds(pl.multiple_of(chunk * CHUNK, CHUNK), CHUNK)
        return pltpu.make_async_copy(w_qkv.at[:, columns], wb.at[slot], load_sem.at[1, slot])

    def last_columns(low, high):
        if low == 0:
            grad_t[...] = jnp.zeros((1152, 256), jnp.float32)
            token_load(0).start()

        def qkv_step(chunk, carry):
            @pl.when(chunk < 8)
            def _():
                qkv_load(chunk + 1).start()

            qkv_load(chunk).wait()
            rows = pl.ds(pl.multiple_of(chunk * CHUNK, CHUNK), CHUNK)
            grads = all_t[rows, :]
            grad_t[...] += dot_nn(wb[lax.rem(chunk, 2)], grads)
            bias_qv[:, rows] = dot_nt(ones, grads)[0:1]
            return carry

        lax.fori_loop(low, high, qkv_step, 0)

    def ada_load():
        return pltpu.make_async_copy(w_ada, wa.at[0, 0:256], load_sem.at[0, 0])

    def last_rows():
        branch[...] = grad_t[...].T
        scale_attn = mods[1:2]

        def last_step(index, carry):
            rows = pl.ds(pl.multiple_of(index * ROWS, ROWS), ROWS)
            slot = lax.rem(index, 2)

            @pl.when(index < 256 // ROWS - 1)
            def _():
                token_load(index + 1).start()

            token_load(index).wait()

            @pl.when(index >= 2)
            def _():
                rows_out(1, index - 2).wait()

            normed, inverse = norm(rows_d[slot].astype(jnp.float32))
            grad_in = branch[rows, :]
            d_mod[0:1, :] += total(grad_in)
            d_mod[1:2, :] += total(grad_in * normed)
            back = norm_back(grad_in * (1.0 + scale_attn), normed, inverse)
            in_rows[slot] = (grad_resid[rows, :] + back).astype(jnp.bfloat16)
            rows_out(1, index).start()
            return carry

        lax.fori_loop(0, 256 // ROWS, last_step, 0)

    def share_to(hop):
        return pltpu.make_async_remote_copy(
            src_ref=shares.at[lax.rem(place + hop, 32)],
            dst_ref=got.at[place],
            send_sem=share_send.at[hop],
            recv_sem=share_recv.at[hop],
            device_id=dp_peer(hop),
            device_id_type=MESH,
        )

    def cond_to(hop):
        return pltpu.make_async_remote_copy(
            src_ref=conds.at[place],
            dst_ref=conds.at[place],
            send_sem=cond_send.at[hop],
            recv_sem=cond_recv.at[hop],
            device_id=dp_peer(hop),
            device_id_type=MESH,
        )

    def group_copies(hop):
        return [
            pltpu.make_async_remote_copy(
                src_ref=buffer.at[at["y"]],
                dst_ref=buffer.at[at["y"]],
                send_sem=group_send.at[side, hop],
                recv_sem=group_recv.at[side, hop],
                device_id=group_peer(hop),
                device_id_type=MESH,
            )
            for side, buffer in enumerate((packed, sums_all))
        ]

    def each(make, act):
        def one(hop, _):
            act(make(hop))
            return _

        lax.fori_loop(1, 32, one, 0)

    def tail_share():
        ada_load().start()
        vectors = [d_mod[row : row + 1] for row in range(6)]
        vectors += [bias_qv[0:1, 0:1152], bias_qv[0:1, 2304:3456]]
        vectors += [bias_proj[...], bias_fc1[0:1, :], bias_fc2[...]]
        row = 0
        for vector in vectors:
            for column in range(vector.shape[1] // 128):
                flat[row] = vector[:, column * 128 : column * 128 + 128]
                row += 1
        flat[126] = jnp.zeros((1, 128), jnp.float32)
        flat[127] = jnp.zeros((1, 128), jnp.float32)

        def window(peer, _):
            into = 0
            for first, width, count in WINDOWS:
                start = first + lax.div(peer * width, 128)
                for offset in range(count):
                    shares[peer, into] = flat[start + offset]
                    into += 1
            return _

        lax.fori_loop(0, 32, window, 0)
        got[place] = shares[place]
        each(share_to, lambda copy: copy.start())

    def tail_cond():
        each(share_to, lambda copy: copy.wait())
        first, second = got[0], got[16]
        for source in range(1, 16):
            first = first + got[source]
            second = second + got[16 + source]

        lanes = lax.broadcasted_iota(jnp.int32, (1, 256), 1)

        def piece(rows, entry):
            begin = sum(count for _, _, count in WINDOWS[:entry])
            _, width, count = WINDOWS[entry]
            joined = jnp.concatenate([rows[begin + step] for step in range(count)], axis=1)
            joined = jnp.concatenate([joined] * 8, axis=0)
            shift = lax.rem(place * width, 128)
            moved = pltpu.roll(joined, lax.rem(count * 128 - shift, count * 128), 1)
            return moved[0:1]

        d_mod_own = jnp.concatenate(
            [jnp.where(lanes < 216, piece(rows, 0)[:, 0:256], 0.0) for rows in (first, second)],
            axis=0,
        )
        ada_load().wait()
        conds[place] = exact_dot(d_mod_own, wa[0, 0:256])
        each(cond_to, lambda copy: copy.start())
        for chunk in range(2):
            t2_load(chunk).start()
        both = first + second
        sums_all[at["y"], 0:1] = piece(both, 1)[:, 0:128]
        sums_all[at["y"], 1:2] = piece(both, 2)[:, 0:128]
        wide = piece(both, 3)
        sums_all[at["y"], 2:3] = wide[:, 0:128]
        sums_all[at["y"], 3:4] = wide[:, 128:256]
        sums_all[at["y"], 4:5] = piece(both, 4)[:, 0:128]
        sums_all[at["y"], 5:8] = jnp.zeros((3, 128), jnp.float32)
        packed[at["y"], :, 2304:3456] = silu(cond_in[...])
        packed[at["y"], :, 3456:4608] = silu(pre_in[...])
        packed[at["y"], :, 4608:4864] = d_mod_own
        packed[at["y"], :, 4864:5120] = feats[...]
        packed[at["y"], :, 5120:5248] = onehot[...]

    def t2_load(chunk):
        rows = pl.ds(chunk * CHUNK, CHUNK)
        return pltpu.make_async_copy(w_t2.at[rows], wa.at[chunk % 2], load_sem.at[0, chunk % 2])

    def tail_group():
        each(cond_to, lambda copy: copy.wait())
        total_cond = conds[0]
        for source in range(1, 32):
            total_cond = total_cond + conds[source]
        grad_cond = silu_back(cond_in[...], total_cond)
        packed[at["y"], :, 0:1152] = grad_cond
        for chunk in range(3):
            t2_load(chunk).wait()
            columns = exact_dot(grad_cond, wa[chunk % 2], 1)
            if chunk == 0:
                t2_load(2).start()
            begin = chunk * CHUNK
            packed[at["y"], :, 1152 + begin : 1152 + begin + CHUNK] = silu_back(
                pre_in[:, begin : begin + CHUNK], columns
            )
        for hop in (1, 2, 3):
            for copy in group_copies(hop):
                copy.start()

    def tail_end():
        for hop in (1, 2, 3):
            for copy in group_copies(hop):
                copy.wait()
        sums[...] = sums_all[0] + sums_all[1] + sums_all[2] + sums_all[3]

    lhs_load(0).start()
    rhs_load().start()
    mlp_begin()
    for copy in heads_load(0):
        copy.start()
    lax.fori_loop(0, 16, clear, 0)
    lhs_load(0).wait()
    rhs_load().wait()
    pl.semaphore_wait(barrier, 34)
    products(0)
    mlp_backward(0, 4)
    mlp_backward(4, 8)
    mlp_backward(8, 12)
    swap_start(1)
    middle_begin()
    middle_rows(0, 4)
    receive(0, 0)
    middle_rows(4, 8)
    middle_end()
    swap_finish(1)
    products(1)
    qkv_load(0).start()
    attention_backward(0, 4)
    receive(0, 1)
    attention_backward(4, 8)
    sides()
    swap_start(2)
    last_columns(0, 5)
    last_columns(5, 9)
    receive(1, 0)
    swap_finish(2)
    receive(0, 2)
    products(2)
    branch_begin()
    finish_begin()
    last_rows()
    receive(1, 1)
    receive(0, 3)
    branch_forward(0, 6)
    branch_forward(6, 12)
    receive(1, 2)
    finish_rows()
    tail_share()
    receive(2, 0)
    receive(0, 4)
    tail_cond()
    receive(2, 1)
    receive(1, 3)
    receive(0, 5)
    ring_start(0)
    tail_group()
    receive(2, 2)
    receive(1, 4)
    ring_relay(0)
    receive(2, 3)
    receive(1, 5)
    ring_start(1)
    ring_finish(0)
    write(0)
    tail_end()
    receive(2, 4)
    ring_relay(1)
    receive(2, 5)
    ring_start(2)
    ring_finish(1)
    across(1).wait()
    write(1)
    ring_relay(2)
    drain(0)
    drain(1)
    ring_finish(2)
    across(2).wait()
    write(2)


def backward(operands):
    dma = pltpu.SemaphoreType.DMA
    regular = pltpu.SemaphoreType.REGULAR
    vmem = pl.BlockSpec(memory_space=pltpu.VMEM)
    anywhere = pl.BlockSpec(memory_space=pl.ANY)
    full = jnp.float32
    small = jnp.bfloat16
    return pl.pallas_call(
        backward_kernel,
        out_shape=(
            jax.ShapeDtypeStruct((36, 3456), full),
            jax.ShapeDtypeStruct((36, 1152), full),
            jax.ShapeDtypeStruct((36, 4608), full),
            jax.ShapeDtypeStruct((144, 1152), full),
            jax.ShapeDtypeStruct((256, 1152), small),
            jax.ShapeDtypeStruct((256, 1152), small),
            jax.ShapeDtypeStruct((4, 2, PACK), full),
            jax.ShapeDtypeStruct((8, 128), full),
        ),
        in_specs=[anywhere] * 7 + [vmem] + [anywhere] * 4 + [vmem] * 6 + [anywhere] * 6,
        out_specs=(vmem,) * 4 + (anywhere,) * 2 + (vmem,) * 2,
        scratch_shapes=[
            pltpu.VMEM((2, 6, 64, PIECE, 128), full),
            pltpu.VMEM((6, 63, PIECE, 128), full),
            pltpu.VMEM((16, 144, 512), small),
            pltpu.VMEM((2304, 512), small),
            pltpu.VMEM((2304, 256), full),
            pltpu.VMEM((2304, 256), full),
            pltpu.VMEM((3, 4, 6, PIECE, 128), full),
            pltpu.VMEM((4, 6, PIECE, 128), full),
            pltpu.VMEM((6, 8, PIECE, 128), full),
            pltpu.VMEM((8, 1152), full),
            pltpu.VMEM((1, 4608), full),
            pltpu.VMEM((1, 3456), full),
            pltpu.VMEM((1, 1152), full),
            pltpu.VMEM((1, 1152), full),
            pltpu.VMEM((128, 1, 128), full),
            pltpu.VMEM((32, 12, 1, 128), full),
            pltpu.VMEM((32, 12, 1, 128), full),
            pltpu.VMEM((32, 2, 1152), full),
            pltpu.VMEM((4, 8, 128), full),
            pltpu.VMEM((2, ROWS, 1152), small),
            pltpu.VMEM((2, ROWS, 1152), small),
            pltpu.VMEM((2, CHUNK, 1152), small),
            pltpu.VMEM((2, 1152, CHUNK), small),
            pltpu.VMEM((2, CHUNK, 256), small),
            pltpu.VMEM((2, CHUNK, 256), small),
            pltpu.VMEM((1152, 256), full),
            pltpu.VMEM((256, 1152), full),
            pltpu.VMEM((256, 1152), full),
            pltpu.VMEM((4608, 256), small),
            pltpu.VMEM((16, 80, 256), small),
            pltpu.VMEM((2, 3, 2, 80, 256), small),
            pltpu.VMEM((2, ROWS, 1152), full),
            pltpu.VMEM((2, ROWS, 1152), full),
            pltpu.VMEM((2, ROWS, 1152), full),
            pltpu.VMEM((2, ROWS, 1152), small),
            dma((6, 6)),
            dma((6, 6)),
            regular((6, 6)),
            dma,
            dma,
            regular,
            dma((2,)),
            dma((3, 4)),
            dma((3, 4)),
            dma((2,)),
            dma((2,)),
            dma((4, 2)),
            dma((4, 2)),
            dma((3, 2)),
            regular,
            dma((2, 2)),
            dma((32,)),
            dma((32,)),
            dma((32,)),
            dma((32,)),
            dma((2, 4)),
            dma((2, 4)),
        ],
        compiler_params=pltpu.CompilerParams(
            collective_id=1, has_side_effects=True, vmem_limit_bytes=255 * 2**18
        ),
    )(*operands)


def as_row(ref):
    return ref[...].reshape(1, ref.shape[0])


def forward_kernel(
    tokens,
    out_grad,
    feats,
    labels,
    grid_ids,
    table,
    w_t1,
    b_t1,
    w_t2,
    b_t2,
    w_ada,
    b_ada,
    w_qkv,
    b_qv,
    w_proj,
    b_proj,
    w_fc1,
    b_fc1,
    pre_out,
    cond_out,
    mods,
    lhs_two,
    lhs_one,
    lhs_zero,
    rhs_zero,
    act_out,
    slope_out,
    heads,
    cot,
    resid,
    attn_out,
    ada_wide,
    bias_keys,
    onehot,
    mine,
    gathered,
    flat,
    normed,
    qkv_t,
    w_q,
    w_p,
    w_f,
    w_1,
    w_2,
    keys_off,
    live_rows,
    send_a,
    send_b,
    send_c,
    send_d,
    send_e,
    got_a,
    got_b,
    got_c,
    got_d,
    got_e,
    send,
    recv,
    load_sem,
    pair_send,
    pair_recv,
    fc_sem,
):
    at = coords()
    core = at["core"]
    sibling = sibling_of(at)
    place = lax.axis_index("dp")
    loads = [
        pltpu.make_async_copy(source, target, load_sem.at[index])
        for index, (source, target) in enumerate(
            ((w_t1, w_1), (w_t2, w_2), (w_qkv, w_q), (w_proj, w_p))
        )
    ]
    for copy in loads:
        copy.start()

    def fc_load(part):
        columns = pl.ds(part * 1152, 1152)
        return pltpu.make_async_copy(w_fc1.at[:, columns], w_f.at[part % 2], fc_sem.at[part % 2])

    fc_load(0).start()
    fc_load(1).start()
    barrier = pltpu.get_barrier_semaphore()

    def hello(hop, _):
        pl.semaphore_signal(barrier, inc=1, device_id=dp_peer(hop), device_id_type=MESH)
        return _

    lax.fori_loop(1, 32, hello, 0)
    rows_table = jnp.concatenate(
        [table[pl.ds(labels[0], 1), :], table[pl.ds(labels[1], 1), :]], axis=0
    )
    loads[0].wait()
    pre_time = exact_dot(feats[...], w_1[...]) + as_row(b_t1)
    loads[1].wait()
    condition = exact_dot(silu(pre_time), w_2[...]) + as_row(b_t2) + rows_table
    mod_part = exact_dot(silu(condition), w_ada[...], 1) + as_row(b_ada)
    pre_out[...] = pre_time
    cond_out[...] = condition
    for item in range(2):
        mine[item, :, 0:216] = mod_part[item : item + 1]
        mine[item, :, 216:256] = jnp.zeros((1, 40), jnp.float32)
    gathered[place] = mine[lax.div(place, 16)]
    pl.semaphore_wait(barrier, 31)

    def copy_to(hop):
        target = lax.rem(place + hop, 32)
        return pltpu.make_async_remote_copy(
            src_ref=mine.at[lax.div(target, 16)],
            dst_ref=gathered.at[place],
            send_sem=send.at[hop],
            recv_sem=recv.at[hop],
            device_id=dp_peer(hop),
            device_id_type=MESH,
        )

    def begin(hop, _):
        copy_to(hop).start()
        return _

    def finish(hop, _):
        copy_to(hop).wait()
        return _

    def norm(values):
        mean = jnp.mean(values, axis=-1, keepdims=True)
        centered = values - mean
        inverse = lax.rsqrt(jnp.mean(centered * centered, axis=-1, keepdims=True) + EPS)
        return centered * inverse

    def row_range(index):
        return pl.ds(pl.multiple_of(index * 64, 64), 64)

    lax.fori_loop(1, 32, begin, 0)
    ada_rows = jnp.concatenate([w_ada[...].astype(jnp.float32), jnp.zeros((40, 1152))], axis=0)
    ada_wide[...] = ada_rows.astype(jnp.bfloat16)
    grid_value = grid_ids[lax.div(place, 16)]
    first_live = jnp.where(grid_value == 2, 16, 0)
    end_live = jnp.where(grid_value == 1, 240, 256)
    slots = lax.broadcasted_iota(jnp.int32, (256, 128), 0)
    live = (slots >= first_live) & (slots < end_live)
    keys_off[...] = jnp.where(live, 0.0, NEG)
    live_rows[...] = jnp.where(live, 1.0, 0.0)
    bias_keys[...] = keys_off[...]
    for item in range(2):
        classes = lax.broadcasted_iota(jnp.int32, (1, 128), 1)
        onehot[item : item + 1, :] = jnp.where(classes == labels[item], 1.0, 0.0)

    def first_norm(index, _):
        rows = row_range(index)
        normed[rows, :] = norm(tokens[rows, :].astype(jnp.float32))
        cot[rows, :] = out_grad[rows, :].astype(jnp.float32) * live_rows[rows, 0:1]
        return _

    lax.fori_loop(0, 4, first_norm, 0)

    def blank(row, _):
        flat[row] = jnp.zeros((1, 128), jnp.float32)
        return _

    lax.fori_loop(0, 56, blank, 0)
    lax.fori_loop(1, 32, finish, 0)
    for piece in range(32):
        row, shift = piece * 216 // 128, piece * 216 % 128
        wide = jnp.concatenate([gathered[piece], jnp.zeros((1, 128), jnp.float32)], axis=1)
        wide = pltpu.roll(jnp.concatenate([wide] * 8, axis=0), shift, 1)[0:1]
        for step in range(3):
            flat[row + step] += wide[:, step * 128 : step * 128 + 128]
    for row in range(6):
        for column in range(9):
            mods[row : row + 1, column * 128 : column * 128 + 128] = flat[row * 9 + column]
    mods[6:8, :] = jnp.zeros((2, 1152), jnp.float32)

    def to_sibling(index, source, target):
        return pltpu.make_async_remote_copy(
            src_ref=source,
            dst_ref=target,
            send_sem=pair_send.at[index],
            recv_sem=pair_recv.at[index],
            device_id=sibling,
            device_id_type=MESH,
        )

    def modulate(index, _):
        rows = row_range(index)
        normed[rows, :] = normed[rows, :] * (1.0 + mods[1:2]) + mods[0:1]
        return _

    lax.fori_loop(0, 4, modulate, 0)
    send_a[...] = normed[...].T
    pair_a = to_sibling(0, send_a, got_a)
    pair_a.start()
    for part in range(8):
        lhs_two[part, :, 0:256] = send_a[part * 144 : part * 144 + 144].astype(jnp.bfloat16)
    loads[2].wait()
    for part in range(3):
        block = dot_nn(
            normed[...].astype(jnp.bfloat16), w_q[:, part * 1152 : part * 1152 + 1152]
        )
        if part == 0:
            block = block + as_row(b_qv)[:, 0:1152]
        if part == 2:
            block = block + as_row(b_qv)[:, 1152:2304]
        qkv_t[part * 1152 : part * 1152 + 1152, :] = block.T

    def branch_grad(index, _):
        rows = row_range(index)
        normed[rows, :] = cot[rows, :] * mods[5:6]
        return _

    scale = 1.0 / math.sqrt(72)

    def one_head(head, _):
        parts = []
        for part in range(3):
            rows = pl.ds(pl.multiple_of(part * 1152 + head * 72, 8), 72)
            padded = jnp.concatenate([qkv_t[rows, :], jnp.zeros((8, 256), jnp.float32)], axis=0)
            parts.append(padded.astype(jnp.bfloat16))
            heads[head + part * 16] = parts[-1]
        query, key, value = parts
        scores = dot_tn(key, query) * scale + jnp.concatenate([keys_off[...]] * 2, axis=1)
        shifted = jnp.exp(scores - jnp.max(scores, axis=0, keepdims=True))
        weights = (shifted / jnp.sum(shifted, axis=0, keepdims=True)).astype(jnp.bfloat16)
        rows = pl.ds(pl.multiple_of(head * 72, 8), 72)
        send_b[rows, :] = dot_nn(value, weights)[0:72]
        return _

    lax.fori_loop(0, 16, one_head, 0, unroll=4)
    pair_b = to_sibling(1, send_b, got_b)
    pair_b.start()
    for part in range(8):
        lhs_two[part + 8, :, 0:256] = send_b[part * 144 : part * 144 + 144].astype(jnp.bfloat16)
    lax.fori_loop(0, 4, branch_grad, 0)
    send_c[...] = normed[...].T
    pair_c = to_sibling(2, send_c, got_c)
    pair_c.start()
    rhs_zero[:, 0:256] = send_c[...].astype(jnp.bfloat16)
    loads[3].wait()
    attn_out[...] = dot_tn(send_b[...].astype(jnp.bfloat16), w_p[...]) + as_row(b_proj)

    def second_norm(index, _):
        rows = row_range(index)
        stream = tokens[rows, :].astype(jnp.float32) + mods[2:3] * attn_out[rows, :]
        resid[rows, :] = stream
        normed[rows, :] = norm(stream) * (1.0 + mods[4:5]) + mods[3:4]
        return _

    lax.fori_loop(0, 4, second_norm, 0)
    send_d[...] = normed[...].T
    pair_d = to_sibling(3, send_d, got_d)
    pair_d.start()
    for part in range(8):
        lhs_one[part, :, 0:256] = send_d[part * 144 : part * 144 + 144].astype(jnp.bfloat16)
    pair_a.wait()
    for part in range(8):
        lhs_two[part, :, 256:512] = got_a[part * 144 : part * 144 + 144].astype(jnp.bfloat16)
    inner = math.sqrt(2.0 / math.pi)
    pair_e = []
    for part in range(4):
        fc_load(part).wait()
        columns = slice(part * 1152, part * 1152 + 1152)
        hidden = dot_nn(normed[...].astype(jnp.bfloat16), w_f[part % 2]) + as_row(b_fc1)[:, columns]
        qkv_t[0:1152, :] = hidden.T
        if part < 2:
            fc_load(part + 2).start()

        def gelu(index, _, part=part):
            rows = pl.ds(pl.multiple_of(index * 144, 144), 144)
            values = qkv_t[rows, :]
            square = values * values
            bend = jnp.tanh(inner * values * (1.0 + 0.044715 * square))
            half = 0.5 * (1.0 + bend)
            active = values * half
            steep = half + 0.5 * values * (1.0 - bend * bend) * inner * (
                1.0 + 3.0 * 0.044715 * square
            )
            into = pl.ds(pl.multiple_of(part * 1152 + index * 144, 144), 144)
            act_out[into, :] = active.astype(jnp.bfloat16)
            slope_out[into, :] = steep.astype(jnp.bfloat16)
            chip = part * 4 + lax.div(index, 2)

            @pl.when(lax.rem(index, 2) == core)
            def _():
                lhs_zero[chip, :, 0:256] = active.astype(jnp.bfloat16)

            @pl.when(lax.rem(index, 2) != core)
            def _():
                send_e[chip] = active

            return 0

        lax.fori_loop(0, 8, gelu, 0)
        some = pl.ds(part * 4, 4)
        pair_e.append(to_sibling(4 + part, send_e.at[some], got_e.at[some]))
        pair_e[-1].start()
        if part == 0:
            pair_b.wait()
            for chip in range(8):
                rows = got_b[chip * 144 : chip * 144 + 144]
                lhs_two[chip + 8, :, 256:512] = rows.astype(jnp.bfloat16)
        if part == 1:
            pair_c.wait()
            rhs_zero[:, 256:512] = got_c[...].astype(jnp.bfloat16)
        if part == 2:
            pair_d.wait()
            for chip in range(8):
                rows = got_d[chip * 144 : chip * 144 + 144]
                lhs_one[chip, :, 256:512] = rows.astype(jnp.bfloat16)
    for part in range(4):
        pair_e[part].wait()
        for chip in range(part * 4, part * 4 + 4):
            lhs_zero[chip, :, 256:512] = got_e[chip].astype(jnp.bfloat16)


def forward(operands):
    dma = pltpu.SemaphoreType.DMA
    vmem = pl.BlockSpec(memory_space=pltpu.VMEM)
    smem = pl.BlockSpec(memory_space=pltpu.SMEM)
    anywhere = pl.BlockSpec(memory_space=pl.ANY)
    full, small = jnp.float32, jnp.bfloat16
    out = jax.ShapeDtypeStruct
    return pl.pallas_call(
        forward_kernel,
        out_shape=(
            out((2, 1152), full),
            out((2, 1152), full),
            out((8, 1152), full),
            out((16, 144, 512), small),
            out((8, 144, 512), small),
            out((16, 144, 512), small),
            out((1152, 512), small),
            out((4608, 256), small),
            out((4608, 256), small),
            out((48, 80, 256), small),
            out((256, 1152), full),
            out((256, 1152), full),
            out((256, 1152), full),
            out((256, 1152), small),
            out((256, 128), full),
            out((2, 128), full),
        ),
        in_specs=[vmem] * 3
        + [smem, smem, vmem]
        + [anywhere, vmem] * 2
        + [vmem, vmem]
        + [anywhere, vmem] * 3,
        out_specs=(vmem,) * 16,
        scratch_shapes=[
            pltpu.VMEM((2, 1, 256), full),
            pltpu.VMEM((32, 1, 256), full),
            pltpu.VMEM((56, 1, 128), full),
            pltpu.VMEM((256, 1152), full),
            pltpu.VMEM((3456, 256), full),
            pltpu.VMEM((1152, 3456), small),
            pltpu.VMEM((1152, 1152), small),
            pltpu.VMEM((2, 1152, 1152), small),
            pltpu.VMEM((256, 1152), small),
            pltpu.VMEM((1152, 1152), small),
            pltpu.VMEM((256, 128), full),
            pltpu.VMEM((256, 128), full),
            pltpu.VMEM((1152, 256), full),
            pltpu.VMEM((1152, 256), full),
            pltpu.VMEM((1152, 256), full),
            pltpu.VMEM((1152, 256), full),
            pltpu.VMEM((16, 144, 256), full),
            pltpu.VMEM((1152, 256), full),
            pltpu.VMEM((1152, 256), full),
            pltpu.VMEM((1152, 256), full),
            pltpu.VMEM((1152, 256), full),
            pltpu.VMEM((16, 144, 256), full),
            dma((32,)),
            dma((32,)),
            dma((4,)),
            dma((8,)),
            dma((8,)),
            dma((2,)),
        ],
        compiler_params=pltpu.CompilerParams(
            collective_id=2, has_side_effects=True, vmem_limit_bytes=255 * 2**18
        ),
    )(*operands)


def split_parts(values):
    high = values.astype(jnp.bfloat16)
    rest = values - high.astype(jnp.float32)
    middle = rest.astype(jnp.bfloat16)
    low = (rest - middle.astype(jnp.float32)).astype(jnp.bfloat16)
    return high, middle, low


def outer_sum(left, right):
    left_high, left_middle, left_low = split_parts(left)
    right_high, right_middle, right_low = split_parts(right)
    lefts = [left_high, left_high, left_middle, left_middle, left_high, left_low]
    rights = [right_high, right_middle, right_high, right_middle, right_low, right_high]
    return dot_tn(jnp.concatenate(lefts, axis=0), jnp.concatenate(rights, axis=0))


def finish_kernel(
    packs,
    sums,
    in_qkv,
    in_proj,
    in_fc1,
    in_fc2,
    in_block,
    in_grad,
    out_qkv,
    out_proj,
    out_fc1,
    out_fc2,
    out_block,
    out_grad,
    d_ada,
    b_ada,
    d_t1,
    b_t1,
    d_t2,
    b_t2,
    d_table,
    b_qv,
    b_proj,
    b_fc1,
    b_fc2,
    copy_sem,
):
    place = lax.axis_index("dp")
    copies = [
        pltpu.make_async_copy(source, target, copy_sem.at[index])
        for index, (source, target) in enumerate(
            (
                (in_qkv, out_qkv),
                (in_proj, out_proj),
                (in_fc1, out_fc1),
                (in_fc2, out_fc2),
                (in_block, out_block),
                (in_grad, out_grad),
            )
        )
    ]
    for copy in copies:
        copy.start()

    def eight(begin, end):
        return jnp.concatenate([packs[group, :, begin:end] for group in range(4)], axis=0)

    def own(rows, width):
        count = rows.shape[1]
        return pltpu.roll(rows, lax.rem(count - place * width, count), 1)

    grad_cond, grad_pre = eight(0, 1152), eight(1152, 2304)
    d_mod = eight(4608, 4864)
    d_ada[...] = outer_sum(d_mod, eight(2304, 3456))[0:216]
    b_ada[...] = jnp.sum(d_mod, axis=0, keepdims=True)[:, 0:216].reshape(216)
    d_t1[...] = outer_sum(own(eight(4864, 5120), 8)[:, 0:128], grad_pre)[0:8]
    d_t2[...] = outer_sum(own(eight(3456, 4608), 36)[:, 0:128], grad_cond)[0:36]
    d_table[...] = outer_sum(eight(5120, 5248), grad_cond)[0:101]
    total_pre = jnp.concatenate([jnp.sum(grad_pre, axis=0, keepdims=True)] * 8, axis=0)
    total_cond = jnp.concatenate([jnp.sum(grad_cond, axis=0, keepdims=True)] * 8, axis=0)
    b_t1[...] = own(total_pre, 36)[0:1, 0:36].reshape(36)
    b_t2[...] = own(total_cond, 36)[0:1, 0:36].reshape(36)
    b_qv[...] = sums[0:1, 0:72].reshape(72)
    b_proj[...] = sums[1:2, 0:36].reshape(36)
    b_fc1[...] = jnp.concatenate([sums[2:3, :], sums[3:4, :]], axis=1)[:, 0:144].reshape(144)
    b_fc2[...] = sums[4:5, 0:36].reshape(36)
    for copy in copies:
        copy.wait()


def finish(operands):
    vmem = pl.BlockSpec(memory_space=pltpu.VMEM)
    anywhere = pl.BlockSpec(memory_space=pl.ANY)
    full, small = jnp.float32, jnp.bfloat16
    out = jax.ShapeDtypeStruct
    return pl.pallas_call(
        finish_kernel,
        out_shape=(
            out((36, 3456), full),
            out((36, 1152), full),
            out((36, 4608), full),
            out((144, 1152), full),
            out((256, 1152), small),
            out((256, 1152), small),
            out((216, 1152), full),
            out((216,), full),
            out((8, 1152), full),
            out((36,), full),
            out((36, 1152), full),
            out((36,), full),
            out((101, 1152), full),
            out((72,), full),
            out((36,), full),
            out((144,), full),
            out((36,), full),
        ),
        in_specs=[vmem, vmem] + [anywhere] * 6,
        out_specs=(anywhere,) * 6 + (vmem,) * 11,
        scratch_shapes=[pltpu.SemaphoreType.DMA((6,))],
        compiler_params=pltpu.CompilerParams(vmem_limit_bytes=255 * 2**18),
    )(*operands)


def on_device(
    tokens,
    out_grad,
    timesteps,
    labels,
    grid_ids,
    w_qkv,
    b_qv,
    w_proj,
    b_proj,
    w_fc1,
    b_fc1,
    w_fc2,
    b_fc2,
    w_ada,
    b_ada,
    w_t1,
    b_t1,
    w_t2,
    b_t2,
    table,
):
    dp_place = lax.axis_index("dp")
    model_width = tokens.shape[1]
    time_feats = time_embed(timesteps, w_t1.shape[0] // 2)
    (
        pre_time,
        condition,
        mods,
        lhs_two,
        lhs_one,
        lhs_zero,
        rhs_zero,
        act_t,
        slope_t,
        heads,
        cotangent,
        resid_one,
        attn_out,
        ada_wide,
        bias_keys,
        onehot,
    ) = forward(
        [
            tokens,
            out_grad,
            time_feats,
            labels,
            grid_ids,
            table,
            w_t1,
            b_t1,
            w_t2,
            b_t2,
            w_ada.T,
            b_ada,
            w_qkv,
            b_qv,
            w_proj,
            b_proj,
            w_fc1,
            b_fc1,
        ]
    )
    (
        sum_qkv,
        sum_proj,
        sum_fc1,
        sum_fc2,
        block_out,
        input_grad,
        packs,
        sums,
    ) = backward(
        [
            lhs_zero,
            lhs_one,
            lhs_two,
            rhs_zero,
            act_t,
            slope_t,
            heads,
            bias_keys,
            cotangent,
            resid_one,
            attn_out,
            tokens,
            mods,
            b_fc2,
            pre_time,
            condition,
            time_feats,
            onehot,
            ada_wide,
            w_t2,
            w_qkv,
            w_proj,
            w_fc1,
            w_fc2,
        ]
    )
    (
        sum_qkv,
        sum_proj,
        sum_fc1,
        sum_fc2,
        block_out,
        input_grad,
        d_ada,
        b_ada,
        d_t1,
        b_t1,
        d_t2,
        b_t2,
        d_table,
        d_qv,
        d_proj,
        d_fc1,
        d_fc2,
    ) = finish([packs, sums, sum_qkv, sum_proj, sum_fc1, sum_fc2, block_out, input_grad])
    return (
        block_out,
        input_grad,
        sum_qkv,
        d_qv,
        sum_proj,
        d_proj,
        sum_fc1,
        d_fc1,
        sum_fc2,
        d_fc2,
        d_ada.T,
        b_ada,
        d_t1,
        b_t1,
        d_t2,
        b_t2,
        d_table,
    )


def solution(mesh):
    placed = (
        P(("group", "dp"), None),
        P(("group", "dp"), None),
        P("group"),
        P("group"),
        P("group"),
        P(),
        P(),
        P(),
        P(),
        P(),
        P(),
        P(),
        P(),
        P(None, "dp"),
        P("dp"),
        P(),
        P(),
        P(),
        P(),
        P(),
    )
    return jax.shard_map(
        on_device,
        mesh=mesh,
        in_specs=placed,
        out_specs=(
            P(("group", "dp"), None),
            P(("group", "dp"), None),
            P("dp", None),
            P("dp"),
            P("dp", None),
            P("dp"),
            P("dp", None),
            P("dp"),
            P("dp", None),
            P("dp"),
            P(None, "dp"),
            P("dp"),
            P("dp", None),
            P("dp"),
            P("dp", None),
            P("dp"),
            P(),
        ),
        check_vma=False,
    )
```

```python
import math

import jax
import jax.numpy as jnp
from jax import lax
from jax.experimental import pallas as pl
from jax.experimental.pallas import tpu as pltpu
from jax.sharding import PartitionSpec as P

SLOTS = 256
ITEM_FRAMES = 16


EPS = 1e-06
NEG = -1e30


def norm_back(grad_in, normed, inv_std):
    return inv_std * (
        grad_in
        - jnp.mean(grad_in, axis=-1, keepdims=True)
        - normed * jnp.mean(grad_in * normed, axis=-1, keepdims=True)
    )


def silu_back(pre_vals, grad_in):
    sigmoid = jax.nn.sigmoid(pre_vals)
    return grad_in * sigmoid * (1.0 + pre_vals * (1.0 - sigmoid))


def time_embed(step_ids, width_half):
    frequency = jnp.exp(
        jnp.arange(width_half, dtype=jnp.float32) * (-math.log(10000.0) / width_half)
    )
    angles = step_ids.astype(jnp.float32)[:, None] * frequency[None, :]
    return jnp.concatenate([jnp.cos(angles), jnp.sin(angles)], axis=1)


def split_three(values):
    high = values.astype(jnp.bfloat16)
    rest = values - high.astype(jnp.float32)
    middle = rest.astype(jnp.bfloat16)
    low = (rest - middle.astype(jnp.float32)).astype(jnp.bfloat16)
    return jnp.concatenate([high, middle, low], axis=0)


def exact_dot(values, weights, contract=0):
    rows = values.shape[0]
    thrice = lax.dot_general(
        split_three(values),
        weights,
        (((1,), (contract,)), ((), ())),
        preferred_element_type=jnp.float32,
    )
    return thrice[0:rows] + thrice[rows : 2 * rows] + thrice[2 * rows : 3 * rows]


def silu(values):
    return values / (1.0 + jnp.exp(-values))


def dot_nn(left, right):
    return jnp.dot(left, right, preferred_element_type=jnp.float32)


def dot_nt(left, right):
    return lax.dot_general(
        left, right, (((1,), (1,)), ((), ())), preferred_element_type=jnp.float32
    )


def dot_tn(left, right):
    return lax.dot_general(
        left, right, (((0,), (0,)), ((), ())), preferred_element_type=jnp.float32
    )


MESH = pl.DeviceIdType.MESH
ORDERS = ((("y", "z", "x"), ("z", "x", "y"), ("x", "y", "z")),) * 3
STREAMS = tuple(
    tuple((order, pairing) for pairing in (0, 1) for order in orders) for orders in ORDERS
)
BLOCKS = (32, 16, 8, 4, 2, 1)
LANDS_AT = (0, 32, 48, 56, 60, 62)
PIECE = 56
OWN = 72
CHUNK = 384
ROWS = 32
WINDOWS = ((0, 216, 3), (54, 72, 2), (72, 36, 2), (81, 144, 3), (117, 36, 2))


def coords():
    place = lax.axis_index("dp")
    return {
        "y": lax.axis_index("group"),
        "z": lax.div(place, 8),
        "x": lax.rem(lax.div(place, 2), 4),
        "core": lax.rem(place, 2),
    }


def device_at(at):
    return (at["y"], (at["z"] * 4 + at["x"]) * 2 + at["core"])


def dp_peer(hop):
    return (lax.axis_index("group"), lax.rem(lax.axis_index("dp") + hop, 32))


def sibling_of(at):
    return device_at({**at, "core": 1 - at["core"]})


def partner_of(at, axis, pairing):
    here = at[axis]
    if pairing == 0:
        there = here + 1 - 2 * lax.rem(here, 2)
    else:
        there = lax.rem(here + 3 + 2 * lax.rem(here, 2), 4)
    return device_at({**at, axis: there})


def slot_of(pairing, value):
    if pairing == 1:
        return value
    if isinstance(value, int):
        return (0, 2, 3, 1)[value]
    return lax.rem(value + lax.div(value + 1, 2), 4)


PACK = 4 * 1152 + 2 * 256 + 128


def backward_kernel(
    lhs_zero,
    lhs_one,
    lhs_two,
    rhs_zero,
    act_flat,
    slope,
    heads,
    bias_keys,
    cot,
    resid,
    attn_out,
    tokens,
    mods,
    b_fc2,
    pre_in,
    cond_in,
    feats,
    onehot,
    w_ada,
    w_t2,
    w_qkv,
    w_proj,
    w_fc1,
    w_fc2,
    out_qkv,
    out_proj,
    out_fc1,
    out_fc2,
    block_out,
    input_grad,
    packed,
    sums,
    parts,
    landed,
    lhs,
    rhs,
    stage_rhs,
    leave,
    final,
    other,
    narrow,
    d_mod,
    bias_fc1,
    bias_qv,
    bias_proj,
    bias_fc2,
    flat,
    shares,
    got,
    conds,
    sums_all,
    out_rows,
    in_rows,
    wa,
    wb,
    slope_in,
    act_in,
    grad_t,
    branch,
    grad_resid,
    all_t,
    mixed_t,
    heads_in,
    rows_a,
    rows_b,
    rows_c,
    rows_d,
    send_sem,
    recv_sem,
    credit,
    swap_send,
    swap_recv,
    swap_credit,
    own_sem,
    ring_send,
    ring_recv,
    pair_send,
    pair_recv,
    load_sem,
    row_sem,
    head_sem,
    other_credit,
    out_sem,
    share_send,
    share_recv,
    cond_send,
    cond_recv,
    group_send,
    group_recv,
):
    at = coords()
    core = at["core"]
    sibling = sibling_of(at)
    barrier = pltpu.get_barrier_semaphore()
    place = lax.axis_index("dp")

    def group_peer(hop):
        return (lax.rem(at["y"] + hop, 4), place)

    def hello(hop, _):
        pl.semaphore_signal(barrier, inc=1, device_id=dp_peer(hop), device_id_type=MESH)
        return _

    lax.fori_loop(1, 32, hello, 0)
    for hop in (1, 2, 3):
        pl.semaphore_signal(barrier, inc=1, device_id=group_peer(hop), device_id_type=MESH)
    def swap():
        return pltpu.make_async_remote_copy(
            src_ref=leave,
            dst_ref=stage_rhs,
            send_sem=swap_send,
            recv_sem=swap_recv,
            device_id=sibling,
            device_id_type=MESH,
        )

    def lhs_load(phase):
        source = (lhs_zero, lhs_one, lhs_two)[phase]
        target = lhs.at[0:8] if phase == 1 else lhs
        return pltpu.make_async_copy(source, target, own_sem.at[0])

    def rhs_load():
        return pltpu.make_async_copy(rhs_zero, rhs.at[0:1152], own_sem.at[1])

    def swap_start(phase):
        lhs_load(phase).start()
        if phase == 2:
            pl.semaphore_wait(swap_credit, 1)
        swap().start()

    def swap_finish(phase):
        swap().wait()

        def narrow_rhs(step, _):
            rows = pl.ds(pl.multiple_of(step * 144, 144), 144)
            rhs[rows, 256:512] = stage_rhs[rows, :].astype(jnp.bfloat16)
            return _

        lax.fori_loop(0, 16, narrow_rhs, 0)
        if phase == 1:
            pl.semaphore_signal(swap_credit, inc=1, device_id=sibling, device_id_type=MESH)
        lhs_load(phase).wait()

    def base_of(phase, stream, z_place, x_place, y_slot):
        order, pairing = STREAMS[phase][stream]
        slots = {"y": y_slot, "z": slot_of(pairing, z_place), "x": slot_of(pairing, x_place)}
        return (slots[order[0]] * 4 + slots[order[1]]) * 4 + slots[order[2]]

    def keep(phase, stream, chip, rows):
        half = phase % 2
        z_place, x_place = lax.div(chip, 4), lax.rem(chip, 4)
        for y_slot in range(4):
            block = base_of(phase, stream, z_place, x_place, y_slot)
            first = y_slot * PIECE
            for unit in range(3):
                low, high = max(first, OWN * unit), min(first + PIECE, OWN * unit + OWN)
                if low < high:
                    parts[half, stream, block, low - first : high - first, :] = rows[
                        low - OWN * unit : high - OWN * unit, unit * 128 : unit * 128 + 128
                    ]

    def halving(phase, stream, step):
        order, pairing = STREAMS[phase][stream]
        axis = order[step // 2]
        slots = [slot_of(pairing, at[name]) for name in order]
        base = 0
        for level in range(step // 2):
            base = base + slots[level] * (64 // 4 ** (level + 1))
        slot = slots[step // 2]
        side = lax.div(slot, 2) if step % 2 == 0 else slot
        away = 1 - side if step % 2 == 0 else slot + 1 - 2 * lax.rem(slot, 2)
        count = BLOCKS[step]
        kept, sent = base + side * count, base + away * count
        partner = partner_of(at, axis, pairing if step % 2 == 0 else 1 - pairing)
        source = parts.at[phase % 2, stream]
        if phase == 0 and step >= 3:
            origin = slots[0] * 16 + lax.div(slots[1], 2) * 8
            kept, sent = kept - origin, sent - origin
            source = narrow.at[stream]
        copy = pltpu.make_async_remote_copy(
            src_ref=source.at[pl.ds(sent, count)],
            dst_ref=landed.at[stream, pl.ds(LANDS_AT[step], count)],
            send_sem=send_sem.at[stream, step],
            recv_sem=recv_sem.at[stream, step],
            device_id=partner,
            device_id_type=MESH,
        )
        return copy, kept, partner

    def send(phase, stream, step):
        copy, _, _ = halving(phase, stream, step)
        if phase:
            pl.semaphore_wait(credit.at[stream, step], 1)
        copy.start()

    def receive(phase, step):
        for stream in range(6):
            copy, kept, partner = halving(phase, stream, step)
            copy.wait()
            half = phase % 2
            count = BLOCKS[step]
            late = phase == 0 and step >= 3
            if step < 5:

                def add(block, _):
                    arrived = landed[stream, LANDS_AT[step] + block]
                    if late:
                        narrow[stream, kept + block] += arrived
                    elif phase == 0 and step == 2:
                        narrow[stream, block] = parts[half, stream, kept + block] + arrived
                    else:
                        parts[half, stream, kept + block] += arrived
                    return _

                lax.fori_loop(0, count, add, 0, unroll=min(count, 4))
            else:
                mine = narrow[stream, kept] if late else parts[half, stream, kept]
                final[phase, at["y"], stream] = mine + landed[stream, LANDS_AT[step]]
            if phase < 2:
                pl.semaphore_signal(
                    credit.at[stream, step], inc=1, device_id=partner, device_id_type=MESH
                )
            if step < 5:
                send(phase, stream, step + 1)

    def products(phase):
        together, stacked = (3, 2) if phase == 2 else (2, 4)
        for group in range(6 // together):
            members = range(group * together, (group + 1) * together)
            if phase == 0:
                first = group * together // 2 * CHUNK
                width = together // 2 * CHUNK
                count = 16
            else:
                first = members[0] * CHUNK
                width = together * CHUNK
                count = 8
            shift = core * 8 if phase == 2 and members[0] >= 3 else 0

            def some(step, _):
                left = lhs[pl.ds(step * stacked + shift, stacked)]
                rows = dot_nt(
                    left.reshape(stacked * 144, 512), rhs[first : first + width, :]
                )
                for place in range(stacked):
                    at_row = place * 144
                    if phase == 0:
                        chip = step * stacked + place
                        for third in range(together // 2):
                            column = third * CHUNK
                            block = rows[at_row : at_row + 144, column : column + CHUNK]
                            stream = group * together // 2 + third
                            keep(phase, stream, chip, block[0:72])
                            keep(phase, stream + 3, chip, block[72:144])
                    else:
                        chip = (step * stacked + place) * 2
                        for place_at, stream in enumerate(members):
                            column = place_at * CHUNK
                            block = rows[at_row : at_row + 144, column : column + CHUNK]
                            keep(phase, stream, chip, block[0:72])
                            keep(phase, stream, chip + 1, block[72:144])
                return _

            lax.fori_loop(0, count // stacked, some, 0)
            for member in members:
                stream = member
                if phase == 0:
                    stream = group * together // 2 + (member - members[0]) // 2
                    stream += 3 * ((member - members[0]) % 2)
                send(phase, stream, 0)

    def ring(phase):
        mine = at["y"]
        copies = []
        for place, hop in enumerate((1, 3)):
            copies.append(
                pltpu.make_async_remote_copy(
                    src_ref=final.at[phase, mine],
                    dst_ref=final.at[phase, mine],
                    send_sem=ring_send.at[phase, place],
                    recv_sem=ring_recv.at[phase, place],
                    device_id=device_at({**at, "y": lax.rem(mine + hop, 4)}),
                    device_id_type=MESH,
                )
            )
        return copies

    def relay(phase):
        mine = at["y"]
        copies = []
        for place, hop in enumerate((1, 3)):
            origin = lax.rem(mine + 4 - hop, 4)
            half = pl.ds(place * 3, 3)
            copies.append(
                pltpu.make_async_remote_copy(
                    src_ref=final.at[phase, origin, half],
                    dst_ref=final.at[phase, origin, half],
                    send_sem=ring_send.at[phase, place + 2],
                    recv_sem=ring_recv.at[phase, place + 2],
                    device_id=device_at({**at, "y": lax.rem(mine + hop, 4)}),
                    device_id_type=MESH,
                )
            )
        return copies

    def across(phase):
        return pltpu.make_async_remote_copy(
            src_ref=final.at[phase],
            dst_ref=other,
            send_sem=pair_send.at[phase - 1],
            recv_sem=pair_recv.at[phase - 1],
            device_id=sibling,
            device_id_type=MESH,
        )

    def whole(get, stream):
        pairing = STREAMS[0][stream][1]
        order = sorted(range(4), key=lambda y_place: slot_of(pairing, y_place))
        return jnp.concatenate([get(y_place, stream) for y_place in order], axis=0)

    def write_rows(phase, low):
        for side in range(2):
            mine = side == (0 if low == 0 else 1)
            for stream in range(6):
                if mine:
                    rows = whole(lambda y_place, stream: final[phase, y_place, stream], stream)
                else:
                    rows = whole(lambda y_place, stream: other[y_place, stream], stream)
                for unit in range(3):
                    block = rows[OWN * unit + low : OWN * unit + low + 36]
                    column = side * 18 + stream * 3 + unit
                    if phase == 1:
                        out_fc1[:, column * 128 : column * 128 + 128] = block
                    elif column < 27:
                        out_qkv[:, column * 128 : column * 128 + 128] = block
                    else:
                        out_proj[:, (column - 27) * 128 : (column - 27) * 128 + 128] = block

    def write(phase):
        if phase == 0:
            for stream in range(6):
                rows = whole(lambda y_place, stream: final[0, y_place, stream], stream)
                half, third = stream // 3, stream % 3
                for unit in range(3):
                    column = third * 3 + unit
                    out_fc2[half * 72 : half * 72 + 72, column * 128 : column * 128 + 128] = rows[
                        OWN * unit : OWN * unit + 72
                    ]
            return

        @pl.when(core == 0)
        def _():
            write_rows(phase, 0)

        @pl.when(core == 1)
        def _():
            write_rows(phase, 36)

        if phase == 1:
            pl.semaphore_signal(other_credit, inc=1, device_id=sibling, device_id_type=MESH)

    def ring_start(phase):
        for copy in ring(phase):
            copy.start()

    def ring_relay(phase):
        for copy, onward in zip(ring(phase), relay(phase)):
            copy.wait()
            onward.start()

    def ring_finish(phase):
        for copy in relay(phase):
            copy.wait()
        if phase == 2:
            pl.semaphore_wait(other_credit, 1)
        if phase:
            across(phase).start()

    def clear(chip, _):
        z_place, x_place = lax.div(chip, 4), lax.rem(chip, 4)
        for half in range(2):
            for stream in range(6):
                block = base_of(half, stream, z_place, x_place, 3)
                parts[half, stream, block, 48:56, :] = jnp.zeros((8, 128), jnp.float32)
        return _

    ones = jnp.ones((8, 256), jnp.bfloat16)

    def mlp_loads(chunk):
        slot = lax.rem(chunk, 2)
        rows = pl.ds(pl.multiple_of(chunk * CHUNK, CHUNK), CHUNK)
        return [
            pltpu.make_async_copy(w_fc2.at[rows], wa.at[slot], load_sem.at[0, slot]),
            pltpu.make_async_copy(w_fc1.at[:, rows], wb.at[slot], load_sem.at[1, slot]),
            pltpu.make_async_copy(slope.at[rows], slope_in.at[slot], load_sem.at[2, slot]),
        ]

    def branch_loads(chunk):
        slot = lax.rem(chunk, 2)
        rows = pl.ds(pl.multiple_of(chunk * CHUNK, CHUNK), CHUNK)
        return [
            pltpu.make_async_copy(w_fc2.at[rows], wa.at[slot], load_sem.at[0, slot]),
            pltpu.make_async_copy(act_flat.at[rows], act_in.at[slot], load_sem.at[3, slot]),
        ]

    def branch_begin():
        for copy in branch_loads(0):
            copy.start()

    def branch_forward(low, high):
        if low == 0:
            branch[...] = jnp.zeros((256, 1152), jnp.float32)

        def branch_step(chunk, carry):
            slot = lax.rem(chunk, 2)

            @pl.when(chunk < 11)
            def _():
                for copy in branch_loads(chunk + 1):
                    copy.start()

            for copy in branch_loads(chunk):
                copy.wait()
            branch[...] += dot_tn(act_in[slot], wa[slot])
            return carry

        lax.fori_loop(low, high, branch_step, 0)

    def mlp_begin():
        for copy in mlp_loads(0):
            copy.start()

    def mlp_backward(low, high):
        if low == 0:
            rhs[0:1152, 256:512] = rhs[0:1152, 0:256]
            grad_t[...] = jnp.zeros((1152, 256), jnp.float32)

        def chunk_step(chunk, carry):
            slot = lax.rem(chunk, 2)

            @pl.when(chunk < 11)
            def _():
                for copy in mlp_loads(chunk + 1):
                    copy.start()

            for copy in mlp_loads(chunk):
                copy.wait()
            grad_act = dot_nn(wa[slot], rhs[0:1152, 256:512])
            grad_hidden = (grad_act * slope_in[slot].astype(jnp.float32)).astype(jnp.bfloat16)
            side = lax.div(chunk, 6)
            rows = pl.ds(pl.multiple_of(lax.rem(chunk, 6) * CHUNK, CHUNK), CHUNK)

            @pl.when(side == core)
            def _():
                rhs[rows, 0:256] = grad_hidden

            @pl.when(side != core)
            def _():
                leave[rows, :] = grad_hidden.astype(jnp.float32)

            columns = pl.ds(pl.multiple_of(chunk * CHUNK, CHUNK), CHUNK)
            bias_fc1[:, columns] = dot_nt(ones, grad_hidden)[0:1]
            grad_t[...] += dot_nn(wb[slot], grad_hidden)
            return carry

        lax.fori_loop(low, high, chunk_step, 0)

    def row_block(source, index):
        return source.at[pl.ds(pl.multiple_of(index * ROWS, ROWS), ROWS)]

    def norm(values):
        mean = jnp.mean(values, axis=-1, keepdims=True)
        centered = values - mean
        inverse = lax.rsqrt(jnp.mean(centered * centered, axis=-1, keepdims=True) + EPS)
        return centered * inverse, inverse

    def total(values):
        return jnp.sum(values, axis=0, keepdims=True)

    def middle_loads(index):
        slot = lax.rem(index, 2)
        return [
            pltpu.make_async_copy(row_block(source, index), target.at[slot], row_sem.at[place, slot])
            for place, (source, target) in enumerate(
                ((cot, rows_a), (resid, rows_b), (attn_out, rows_c))
            )
        ]

    def token_load(index):
        slot = lax.rem(index, 2)
        return pltpu.make_async_copy(
            row_block(tokens, index), rows_d.at[slot], row_sem.at[3, slot]
        )

    def proj_load(chunk):
        slot = lax.rem(chunk, 2)
        rows = pl.ds(pl.multiple_of(chunk * 288, 288), 288)
        return pltpu.make_async_copy(w_proj.at[rows], wa.at[slot, 0:288], load_sem.at[0, slot])

    def rows_out(kind, index):
        slot = lax.rem(index, 2)
        target = block_out if kind == 0 else input_grad
        buffer = out_rows if kind == 0 else in_rows
        return pltpu.make_async_copy(
            buffer.at[slot], row_block(target, index), out_sem.at[kind, slot]
        )

    def drain(kind):
        rows_out(kind, 256 // ROWS - 2).wait()
        rows_out(kind, 256 // ROWS - 1).wait()

    def middle_begin():
        for copy in middle_loads(0):
            copy.start()
        proj_load(0).start()
        d_mod[...] = jnp.zeros((8, 1152), jnp.float32)
        bias_proj[...] = jnp.zeros((1, 1152), jnp.float32)
        bias_fc2[...] = jnp.zeros((1, 1152), jnp.float32)
        grad_resid[...] = grad_t[...].T

    def middle_rows(low, high):
        scale_mlp, gate_attn = mods[4:5], mods[2:3]

        def rows_step(index, carry):
            rows = pl.ds(pl.multiple_of(index * ROWS, ROWS), ROWS)
            slot = lax.rem(index, 2)

            @pl.when(index < 256 // ROWS - 1)
            def _():
                for copy in middle_loads(index + 1):
                    copy.start()

            for copy in middle_loads(index):
                copy.wait()

            cotangent, stream_rows = rows_a[slot], rows_b[slot]
            normed, inverse = norm(stream_rows)
            grad_in = grad_resid[rows, :]
            d_mod[3:4, :] += total(grad_in)
            d_mod[4:5, :] += total(grad_in * normed)
            back = norm_back(grad_in * (1.0 + scale_mlp), normed, inverse)
            grads = cotangent + back
            grad_resid[rows, :] = grads
            d_mod[2:3, :] += total(grads * rows_c[slot])
            grad_attn = (grads * gate_attn).astype(jnp.bfloat16).astype(jnp.float32)
            bias_proj[...] += total(grad_attn)
            branch[rows, :] = grad_attn
            return carry

        lax.fori_loop(low, high, rows_step, 0)

    def finish_begin():
        for copy in middle_loads(0)[0:2]:
            copy.start()

    def finish_rows():
        gate_mlp = mods[5:6]

        def finish_step(index, carry):
            rows = pl.ds(pl.multiple_of(index * ROWS, ROWS), ROWS)
            slot = lax.rem(index, 2)

            @pl.when(index < 256 // ROWS - 1)
            def _():
                for copy in middle_loads(index + 1)[0:2]:
                    copy.start()

            for copy in middle_loads(index)[0:2]:
                copy.wait()

            @pl.when(index >= 2)
            def _():
                rows_out(0, index - 2).wait()

            cotangent, stream_rows = rows_a[slot], rows_b[slot]
            branch_rows = branch[rows, :] + b_fc2[...].reshape(1, 1152)
            out_rows[slot] = (stream_rows + gate_mlp * branch_rows).astype(jnp.bfloat16)
            rows_out(0, index).start()
            d_mod[5:6, :] += total(cotangent * branch_rows)
            bias_fc2[...] += total(
                (cotangent * gate_mlp).astype(jnp.bfloat16).astype(jnp.float32)
            )
            return carry

        lax.fori_loop(0, 256 // ROWS, finish_step, 0)

    def middle_end():
        all_t[3456:4608, :] = branch[...].T.astype(jnp.bfloat16)

        def proj_step(chunk, carry):
            @pl.when(chunk < 3)
            def _():
                proj_load(chunk + 1).start()

            proj_load(chunk).wait()
            grads = dot_nn(wa[lax.rem(chunk, 2), 0:288], all_t[3456:4608, :])
            for head in range(4):
                padded = jnp.concatenate(
                    [grads[head * 72 : head * 72 + 72], jnp.zeros((8, 256), jnp.float32)], axis=0
                )
                mixed_t[chunk * 4 + head] = padded.astype(jnp.bfloat16)
            return carry

        lax.fori_loop(0, 4, proj_step, 0)

    def heads_load(pair_at):
        slot = lax.rem(pair_at, 2)
        return [
            pltpu.make_async_copy(
                heads.at[pl.ds(part * 16 + pair_at * 2, 2)],
                heads_in.at[slot, part],
                head_sem.at[part, slot],
            )
            for part in range(3)
        ]

    def attention_backward(low, high):
        scale = 1.0 / math.sqrt(72)

        def one_head(pair_at, side):
            slot = lax.rem(pair_at, 2)
            query, key, value = (heads_in[slot, part, side] for part in range(3))
            grad_mixed = mixed_t[pair_at * 2 + side]
            scores = dot_tn(key, query) * scale + jnp.concatenate([bias_keys[...]] * 2, axis=1)
            shifted = jnp.exp(scores - jnp.max(scores, axis=0, keepdims=True))
            weights = shifted / jnp.sum(shifted, axis=0, keepdims=True)
            grad_weights = dot_tn(value, grad_mixed)
            row_dot = jnp.sum(weights * grad_weights, axis=0, keepdims=True)
            grad_scores = (weights * (grad_weights - row_dot)).astype(jnp.bfloat16)
            return (
                dot_nn(key, grad_scores)[0:72] * scale,
                dot_nt(query, grad_scores)[0:72] * scale,
                dot_nt(grad_mixed, weights.astype(jnp.bfloat16))[0:72],
            )

        def two_heads(pair_at, carry):
            @pl.when(pair_at < 7)
            def _():
                for copy in heads_load(pair_at + 1):
                    copy.start()

            for copy in heads_load(pair_at):
                copy.wait()
            first, second = one_head(pair_at, 0), one_head(pair_at, 1)
            for part in range(3):
                rows = pl.ds(pl.multiple_of(part * 1152 + pair_at * 144, 16), 144)
                all_t[rows, :] = jnp.concatenate([first[part], second[part]], axis=0).astype(
                    jnp.bfloat16
                )
            return carry

        lax.fori_loop(low, high, two_heads, 0)

    def sides():
        def side(step, _):
            mine = pl.ds(pl.multiple_of(core * 2304 + step * 144, 16), 144)
            theirs = pl.ds(pl.multiple_of((1 - core) * 2304 + step * 144, 16), 144)
            rows = pl.ds(pl.multiple_of(step * 144, 144), 144)
            rhs[rows, 0:256] = all_t[mine, :]
            leave[rows, :] = all_t[theirs, :].astype(jnp.float32)
            return _

        lax.fori_loop(0, 16, side, 0)

    def qkv_load(chunk):
        slot = lax.rem(chunk, 2)
        columns = pl.ds(pl.multiple_of(chunk * CHUNK, CHUNK), CHUNK)
        return pltpu.make_async_copy(w_qkv.at[:, columns], wb.at[slot], load_sem.at[1, slot])

    def last_columns(low, high):
        if low == 0:
            grad_t[...] = jnp.zeros((1152, 256), jnp.float32)
            token_load(0).start()

        def qkv_step(chunk, carry):
            @pl.when(chunk < 8)
            def _():
                qkv_load(chunk + 1).start()

            qkv_load(chunk).wait()
            rows = pl.ds(pl.multiple_of(chunk * CHUNK, CHUNK), CHUNK)
            grads = all_t[rows, :]
            grad_t[...] += dot_nn(wb[lax.rem(chunk, 2)], grads)
            bias_qv[:, rows] = dot_nt(ones, grads)[0:1]
            return carry

        lax.fori_loop(low, high, qkv_step, 0)

    def ada_load():
        return pltpu.make_async_copy(w_ada, wa.at[0, 0:256], load_sem.at[0, 0])

    def last_rows():
        branch[...] = grad_t[...].T
        scale_attn = mods[1:2]

        def last_step(index, carry):
            rows = pl.ds(pl.multiple_of(index * ROWS, ROWS), ROWS)
            slot = lax.rem(index, 2)

            @pl.when(index < 256 // ROWS - 1)
            def _():
                token_load(index + 1).start()

            token_load(index).wait()

            @pl.when(index >= 2)
            def _():
                rows_out(1, index - 2).wait()

            normed, inverse = norm(rows_d[slot].astype(jnp.float32))
            grad_in = branch[rows, :]
            d_mod[0:1, :] += total(grad_in)
            d_mod[1:2, :] += total(grad_in * normed)
            back = norm_back(grad_in * (1.0 + scale_attn), normed, inverse)
            in_rows[slot] = (grad_resid[rows, :] + back).astype(jnp.bfloat16)
            rows_out(1, index).start()
            return carry

        lax.fori_loop(0, 256 // ROWS, last_step, 0)

    def share_to(hop):
        return pltpu.make_async_remote_copy(
            src_ref=shares.at[lax.rem(place + hop, 32)],
            dst_ref=got.at[place],
            send_sem=share_send.at[hop],
            recv_sem=share_recv.at[hop],
            device_id=dp_peer(hop),
            device_id_type=MESH,
        )

    def cond_to(hop):
        return pltpu.make_async_remote_copy(
            src_ref=conds.at[place],
            dst_ref=conds.at[place],
            send_sem=cond_send.at[hop],
            recv_sem=cond_recv.at[hop],
            device_id=dp_peer(hop),
            device_id_type=MESH,
        )

    def group_copies(hop):
        return [
            pltpu.make_async_remote_copy(
                src_ref=buffer.at[at["y"]],
                dst_ref=buffer.at[at["y"]],
                send_sem=group_send.at[side, hop],
                recv_sem=group_recv.at[side, hop],
                device_id=group_peer(hop),
                device_id_type=MESH,
            )
            for side, buffer in enumerate((packed, sums_all))
        ]

    def each(make, act):
        def one(hop, _):
            act(make(hop))
            return _

        lax.fori_loop(1, 32, one, 0)

    def tail_share():
        ada_load().start()
        vectors = [d_mod[row : row + 1] for row in range(6)]
        vectors += [bias_qv[0:1, 0:1152], bias_qv[0:1, 2304:3456]]
        vectors += [bias_proj[...], bias_fc1[0:1, :], bias_fc2[...]]
        row = 0
        for vector in vectors:
            for column in range(vector.shape[1] // 128):
                flat[row] = vector[:, column * 128 : column * 128 + 128]
                row += 1
        flat[126] = jnp.zeros((1, 128), jnp.float32)
        flat[127] = jnp.zeros((1, 128), jnp.float32)

        def window(peer, _):
            into = 0
            for first, width, count in WINDOWS:
                start = first + lax.div(peer * width, 128)
                for offset in range(count):
                    shares[peer, into] = flat[start + offset]
                    into += 1
            return _

        lax.fori_loop(0, 32, window, 0)
        got[place] = shares[place]
        each(share_to, lambda copy: copy.start())

    def tail_cond():
        each(share_to, lambda copy: copy.wait())
        first, second = got[0], got[16]
        for source in range(1, 16):
            first = first + got[source]
            second = second + got[16 + source]

        lanes = lax.broadcasted_iota(jnp.int32, (1, 256), 1)

        def piece(rows, entry):
            begin = sum(count for _, _, count in WINDOWS[:entry])
            _, width, count = WINDOWS[entry]
            joined = jnp.concatenate([rows[begin + step] for step in range(count)], axis=1)
            joined = jnp.concatenate([joined] * 8, axis=0)
            shift = lax.rem(place * width, 128)
            moved = pltpu.roll(joined, lax.rem(count * 128 - shift, count * 128), 1)
            return moved[0:1]

        d_mod_own = jnp.concatenate(
            [jnp.where(lanes < 216, piece(rows, 0)[:, 0:256], 0.0) for rows in (first, second)],
            axis=0,
        )
        ada_load().wait()
        conds[place] = exact_dot(d_mod_own, wa[0, 0:256])
        each(cond_to, lambda copy: copy.start())
        for chunk in range(2):
            t2_load(chunk).start()
        both = first + second
        sums_all[at["y"], 0:1] = piece(both, 1)[:, 0:128]
        sums_all[at["y"], 1:2] = piece(both, 2)[:, 0:128]
        wide = piece(both, 3)
        sums_all[at["y"], 2:3] = wide[:, 0:128]
        sums_all[at["y"], 3:4] = wide[:, 128:256]
        sums_all[at["y"], 4:5] = piece(both, 4)[:, 0:128]
        sums_all[at["y"], 5:8] = jnp.zeros((3, 128), jnp.float32)
        packed[at["y"], :, 2304:3456] = silu(cond_in[...])
        packed[at["y"], :, 3456:4608] = silu(pre_in[...])
        packed[at["y"], :, 4608:4864] = d_mod_own
        packed[at["y"], :, 4864:5120] = feats[...]
        packed[at["y"], :, 5120:5248] = onehot[...]

    def t2_load(chunk):
        rows = pl.ds(chunk * CHUNK, CHUNK)
        return pltpu.make_async_copy(w_t2.at[rows], wa.at[chunk % 2], load_sem.at[0, chunk % 2])

    def tail_group():
        each(cond_to, lambda copy: copy.wait())
        total_cond = conds[0]
        for source in range(1, 32):
            total_cond = total_cond + conds[source]
        grad_cond = silu_back(cond_in[...], total_cond)
        packed[at["y"], :, 0:1152] = grad_cond
        for chunk in range(3):
            t2_load(chunk).wait()
            columns = exact_dot(grad_cond, wa[chunk % 2], 1)
            if chunk == 0:
                t2_load(2).start()
            begin = chunk * CHUNK
            packed[at["y"], :, 1152 + begin : 1152 + begin + CHUNK] = silu_back(
                pre_in[:, begin : begin + CHUNK], columns
            )
        for hop in (1, 2, 3):
            for copy in group_copies(hop):
                copy.start()

    def tail_end():
        for hop in (1, 2, 3):
            for copy in group_copies(hop):
                copy.wait()
        sums[...] = sums_all[0] + sums_all[1] + sums_all[2] + sums_all[3]

    lhs_load(0).start()
    rhs_load().start()
    mlp_begin()
    for copy in heads_load(0):
        copy.start()
    lax.fori_loop(0, 16, clear, 0)
    lhs_load(0).wait()
    rhs_load().wait()
    pl.semaphore_wait(barrier, 34)
    products(0)
    mlp_backward(0, 4)
    mlp_backward(4, 8)
    mlp_backward(8, 12)
    swap_start(1)
    middle_begin()
    middle_rows(0, 4)
    receive(0, 0)
    middle_rows(4, 8)
    middle_end()
    swap_finish(1)
    products(1)
    qkv_load(0).start()
    attention_backward(0, 4)
    receive(0, 1)
    attention_backward(4, 8)
    sides()
    swap_start(2)
    last_columns(0, 5)
    last_columns(5, 9)
    receive(1, 0)
    swap_finish(2)
    receive(0, 2)
    products(2)
    branch_begin()
    finish_begin()
    last_rows()
    receive(1, 1)
    receive(0, 3)
    branch_forward(0, 6)
    branch_forward(6, 12)
    receive(1, 2)
    finish_rows()
    tail_share()
    receive(2, 0)
    receive(0, 4)
    tail_cond()
    receive(2, 1)
    receive(1, 3)
    receive(0, 5)
    ring_start(0)
    tail_group()
    receive(2, 2)
    receive(1, 4)
    ring_relay(0)
    receive(2, 3)
    receive(1, 5)
    ring_start(1)
    ring_finish(0)
    write(0)
    tail_end()
    receive(2, 4)
    ring_relay(1)
    receive(2, 5)
    ring_start(2)
    ring_finish(1)
    across(1).wait()
    write(1)
    ring_relay(2)
    drain(0)
    drain(1)
    ring_finish(2)
    across(2).wait()
    write(2)


def backward(operands):
    dma = pltpu.SemaphoreType.DMA
    regular = pltpu.SemaphoreType.REGULAR
    vmem = pl.BlockSpec(memory_space=pltpu.VMEM)
    anywhere = pl.BlockSpec(memory_space=pl.ANY)
    full = jnp.float32
    small = jnp.bfloat16
    return pl.pallas_call(
        backward_kernel,
        out_shape=(
            jax.ShapeDtypeStruct((36, 3456), full),
            jax.ShapeDtypeStruct((36, 1152), full),
            jax.ShapeDtypeStruct((36, 4608), full),
            jax.ShapeDtypeStruct((144, 1152), full),
            jax.ShapeDtypeStruct((256, 1152), small),
            jax.ShapeDtypeStruct((256, 1152), small),
            jax.ShapeDtypeStruct((4, 2, PACK), full),
            jax.ShapeDtypeStruct((8, 128), full),
        ),
        in_specs=[anywhere] * 7 + [vmem] + [anywhere] * 4 + [vmem] * 6 + [anywhere] * 6,
        out_specs=(vmem,) * 4 + (anywhere,) * 2 + (vmem,) * 2,
        scratch_shapes=[
            pltpu.VMEM((2, 6, 64, PIECE, 128), full),
            pltpu.VMEM((6, 63, PIECE, 128), full),
            pltpu.VMEM((16, 144, 512), small),
            pltpu.VMEM((2304, 512), small),
            pltpu.VMEM((2304, 256), full),
            pltpu.VMEM((2304, 256), full),
            pltpu.VMEM((3, 4, 6, PIECE, 128), full),
            pltpu.VMEM((4, 6, PIECE, 128), full),
            pltpu.VMEM((6, 8, PIECE, 128), full),
            pltpu.VMEM((8, 1152), full),
            pltpu.VMEM((1, 4608), full),
            pltpu.VMEM((1, 3456), full),
            pltpu.VMEM((1, 1152), full),
            pltpu.VMEM((1, 1152), full),
            pltpu.VMEM((128, 1, 128), full),
            pltpu.VMEM((32, 12, 1, 128), full),
            pltpu.VMEM((32, 12, 1, 128), full),
            pltpu.VMEM((32, 2, 1152), full),
            pltpu.VMEM((4, 8, 128), full),
            pltpu.VMEM((2, ROWS, 1152), small),
            pltpu.VMEM((2, ROWS, 1152), small),
            pltpu.VMEM((2, CHUNK, 1152), small),
            pltpu.VMEM((2, 1152, CHUNK), small),
            pltpu.VMEM((2, CHUNK, 256), small),
            pltpu.VMEM((2, CHUNK, 256), small),
            pltpu.VMEM((1152, 256), full),
            pltpu.VMEM((256, 1152), full),
            pltpu.VMEM((256, 1152), full),
            pltpu.VMEM((4608, 256), small),
            pltpu.VMEM((16, 80, 256), small),
            pltpu.VMEM((2, 3, 2, 80, 256), small),
            pltpu.VMEM((2, ROWS, 1152), full),
            pltpu.VMEM((2, ROWS, 1152), full),
            pltpu.VMEM((2, ROWS, 1152), full),
            pltpu.VMEM((2, ROWS, 1152), small),
            dma((6, 6)),
            dma((6, 6)),
            regular((6, 6)),
            dma,
            dma,
            regular,
            dma((2,)),
            dma((3, 4)),
            dma((3, 4)),
            dma((2,)),
            dma((2,)),
            dma((4, 2)),
            dma((4, 2)),
            dma((3, 2)),
            regular,
            dma((2, 2)),
            dma((32,)),
            dma((32,)),
            dma((32,)),
            dma((32,)),
            dma((2, 4)),
            dma((2, 4)),
        ],
        compiler_params=pltpu.CompilerParams(
            collective_id=1, has_side_effects=True, vmem_limit_bytes=255 * 2**18
        ),
    )(*operands)


def as_row(ref):
    return ref[...].reshape(1, ref.shape[0])


def forward_kernel(
    tokens,
    out_grad,
    feats,
    labels,
    grid_ids,
    table,
    w_t1,
    b_t1,
    w_t2,
    b_t2,
    w_ada,
    b_ada,
    w_qkv,
    b_qv,
    w_proj,
    b_proj,
    w_fc1,
    b_fc1,
    pre_out,
    cond_out,
    mods,
    lhs_two_far,
    lhs_one_far,
    lhs_zero_far,
    rhs_zero_far,
    act_out_far,
    slope_out_far,
    heads_far,
    cot_far,
    resid_far,
    attn_out_far,
    ada_wide,
    bias_keys,
    onehot,
    lhs_two,
    lhs_one,
    lhs_zero,
    rhs_zero,
    act_out,
    slope_out,
    heads,
    cot,
    resid,
    attn_out,
    mine,
    gathered,
    flat,
    normed,
    qkv_t,
    w_q,
    w_p,
    w_f,
    w_1,
    w_2,
    keys_off,
    live_rows,
    send_a,
    send_b,
    send_c,
    send_d,
    send_e,
    got_a,
    got_b,
    got_c,
    got_d,
    got_e,
    send,
    recv,
    load_sem,
    pair_send,
    pair_recv,
    fc_sem,
    out_sem,
    part_sem,
):
    at = coords()
    core = at["core"]
    sibling = sibling_of(at)
    place = lax.axis_index("dp")
    loads = [
        pltpu.make_async_copy(source, target, load_sem.at[index])
        for index, (source, target) in enumerate(
            ((w_t1, w_1), (w_t2, w_2), (w_qkv, w_q), (w_proj, w_p))
        )
    ]
    for copy in loads:
        copy.start()

    def fc_load(part):
        columns = pl.ds(part * 1152, 1152)
        return pltpu.make_async_copy(w_fc1.at[:, columns], w_f.at[part % 2], fc_sem.at[part % 2])

    fc_load(0).start()
    fc_load(1).start()
    outs = [
        pltpu.make_async_copy(source, target, out_sem.at[index])
        for index, (source, target) in enumerate(
            (
                (cot, cot_far),
                (heads, heads_far),
                (attn_out, attn_out_far),
                (resid, resid_far),
                (lhs_two, lhs_two_far),
                (rhs_zero, rhs_zero_far),
                (lhs_one, lhs_one_far),
            )
        )
    ]

    def part_out(part):
        rows, chips = pl.ds(part * 1152, 1152), pl.ds(part * 4, 4)
        return [
            pltpu.make_async_copy(source, target, part_sem.at[index, part])
            for index, (source, target) in enumerate(
                (
                    (act_out.at[rows], act_out_far.at[rows]),
                    (slope_out.at[rows], slope_out_far.at[rows]),
                    (lhs_zero.at[chips], lhs_zero_far.at[chips]),
                )
            )
        ]

    barrier = pltpu.get_barrier_semaphore()

    def hello(hop, _):
        pl.semaphore_signal(barrier, inc=1, device_id=dp_peer(hop), device_id_type=MESH)
        return _

    lax.fori_loop(1, 32, hello, 0)
    rows_table = jnp.concatenate(
        [table[pl.ds(labels[0], 1), :], table[pl.ds(labels[1], 1), :]], axis=0
    )
    loads[0].wait()
    pre_time = exact_dot(feats[...], w_1[...]) + as_row(b_t1)
    loads[1].wait()
    condition = exact_dot(silu(pre_time), w_2[...]) + as_row(b_t2) + rows_table
    mod_part = exact_dot(silu(condition), w_ada[...], 1) + as_row(b_ada)
    pre_out[...] = pre_time
    cond_out[...] = condition
    for item in range(2):
        mine[item, :, 0:216] = mod_part[item : item + 1]
        mine[item, :, 216:256] = jnp.zeros((1, 40), jnp.float32)
    gathered[place] = mine[lax.div(place, 16)]
    pl.semaphore_wait(barrier, 31)

    def copy_to(hop):
        target = lax.rem(place + hop, 32)
        return pltpu.make_async_remote_copy(
            src_ref=mine.at[lax.div(target, 16)],
            dst_ref=gathered.at[place],
            send_sem=send.at[hop],
            recv_sem=recv.at[hop],
            device_id=dp_peer(hop),
            device_id_type=MESH,
        )

    def begin(hop, _):
        copy_to(hop).start()
        return _

    def finish(hop, _):
        copy_to(hop).wait()
        return _

    def norm(values):
        mean = jnp.mean(values, axis=-1, keepdims=True)
        centered = values - mean
        inverse = lax.rsqrt(jnp.mean(centered * centered, axis=-1, keepdims=True) + EPS)
        return centered * inverse

    def row_range(index):
        return pl.ds(pl.multiple_of(index * 64, 64), 64)

    lax.fori_loop(1, 32, begin, 0)
    ada_rows = jnp.concatenate([w_ada[...].astype(jnp.float32), jnp.zeros((40, 1152))], axis=0)
    ada_wide[...] = ada_rows.astype(jnp.bfloat16)
    grid_value = grid_ids[lax.div(place, 16)]
    first_live = jnp.where(grid_value == 2, 16, 0)
    end_live = jnp.where(grid_value == 1, 240, 256)
    slots = lax.broadcasted_iota(jnp.int32, (256, 128), 0)
    live = (slots >= first_live) & (slots < end_live)
    keys_off[...] = jnp.where(live, 0.0, NEG)
    live_rows[...] = jnp.where(live, 1.0, 0.0)
    bias_keys[...] = keys_off[...]
    for item in range(2):
        classes = lax.broadcasted_iota(jnp.int32, (1, 128), 1)
        onehot[item : item + 1, :] = jnp.where(classes == labels[item], 1.0, 0.0)

    def first_norm(index, _):
        rows = row_range(index)
        normed[rows, :] = norm(tokens[rows, :].astype(jnp.float32))
        cot[rows, :] = out_grad[rows, :].astype(jnp.float32) * live_rows[rows, 0:1]
        return _

    lax.fori_loop(0, 4, first_norm, 0)
    outs[0].start()

    def blank(row, _):
        flat[row] = jnp.zeros((1, 128), jnp.float32)
        return _

    lax.fori_loop(0, 56, blank, 0)
    lax.fori_loop(1, 32, finish, 0)
    for piece in range(32):
        row, shift = piece * 216 // 128, piece * 216 % 128
        wide = jnp.concatenate([gathered[piece], jnp.zeros((1, 128), jnp.float32)], axis=1)
        wide = pltpu.roll(jnp.concatenate([wide] * 8, axis=0), shift, 1)[0:1]
        for step in range(3):
            flat[row + step] += wide[:, step * 128 : step * 128 + 128]
    for row in range(6):
        for column in range(9):
            mods[row : row + 1, column * 128 : column * 128 + 128] = flat[row * 9 + column]
    mods[6:8, :] = jnp.zeros((2, 1152), jnp.float32)

    def to_sibling(index, source, target):
        return pltpu.make_async_remote_copy(
            src_ref=source,
            dst_ref=target,
            send_sem=pair_send.at[index],
            recv_sem=pair_recv.at[index],
            device_id=sibling,
            device_id_type=MESH,
        )

    def modulate(index, _):
        rows = row_range(index)
        normed[rows, :] = normed[rows, :] * (1.0 + mods[1:2]) + mods[0:1]
        return _

    lax.fori_loop(0, 4, modulate, 0)
    send_a[...] = normed[...].T
    pair_a = to_sibling(0, send_a, got_a)
    pair_a.start()
    for part in range(8):
        lhs_two[part, :, 0:256] = send_a[part * 144 : part * 144 + 144].astype(jnp.bfloat16)
    loads[2].wait()
    for part in range(3):
        block = dot_nn(
            normed[...].astype(jnp.bfloat16), w_q[:, part * 1152 : part * 1152 + 1152]
        )
        if part == 0:
            block = block + as_row(b_qv)[:, 0:1152]
        if part == 2:
            block = block + as_row(b_qv)[:, 1152:2304]
        qkv_t[part * 1152 : part * 1152 + 1152, :] = block.T

    def branch_grad(index, _):
        rows = row_range(index)
        normed[rows, :] = cot[rows, :] * mods[5:6]
        return _

    scale = 1.0 / math.sqrt(72)

    def one_head(head, _):
        parts = []
        for part in range(3):
            rows = pl.ds(pl.multiple_of(part * 1152 + head * 72, 8), 72)
            padded = jnp.concatenate([qkv_t[rows, :], jnp.zeros((8, 256), jnp.float32)], axis=0)
            parts.append(padded.astype(jnp.bfloat16))
            heads[head + part * 16] = parts[-1]
        query, key, value = parts
        scores = dot_tn(key, query) * scale + jnp.concatenate([keys_off[...]] * 2, axis=1)
        shifted = jnp.exp(scores - jnp.max(scores, axis=0, keepdims=True))
        weights = (shifted / jnp.sum(shifted, axis=0, keepdims=True)).astype(jnp.bfloat16)
        rows = pl.ds(pl.multiple_of(head * 72, 8), 72)
        send_b[rows, :] = dot_nn(value, weights)[0:72]
        return _

    lax.fori_loop(0, 16, one_head, 0, unroll=4)
    outs[1].start()
    pair_b = to_sibling(1, send_b, got_b)
    pair_b.start()
    for part in range(8):
        lhs_two[part + 8, :, 0:256] = send_b[part * 144 : part * 144 + 144].astype(jnp.bfloat16)
    lax.fori_loop(0, 4, branch_grad, 0)
    send_c[...] = normed[...].T
    pair_c = to_sibling(2, send_c, got_c)
    pair_c.start()
    rhs_zero[:, 0:256] = send_c[...].astype(jnp.bfloat16)
    loads[3].wait()
    attn_out[...] = dot_tn(send_b[...].astype(jnp.bfloat16), w_p[...]) + as_row(b_proj)

    def second_norm(index, _):
        rows = row_range(index)
        stream = tokens[rows, :].astype(jnp.float32) + mods[2:3] * attn_out[rows, :]
        resid[rows, :] = stream
        normed[rows, :] = norm(stream) * (1.0 + mods[4:5]) + mods[3:4]
        return _

    lax.fori_loop(0, 4, second_norm, 0)
    outs[2].start()
    outs[3].start()
    send_d[...] = normed[...].T
    pair_d = to_sibling(3, send_d, got_d)
    pair_d.start()
    for part in range(8):
        lhs_one[part, :, 0:256] = send_d[part * 144 : part * 144 + 144].astype(jnp.bfloat16)
    pair_a.wait()
    for part in range(8):
        lhs_two[part, :, 256:512] = got_a[part * 144 : part * 144 + 144].astype(jnp.bfloat16)
    inner = math.sqrt(2.0 / math.pi)
    pair_e = []
    for part in range(4):
        fc_load(part).wait()
        columns = slice(part * 1152, part * 1152 + 1152)
        hidden = dot_nn(normed[...].astype(jnp.bfloat16), w_f[part % 2]) + as_row(b_fc1)[:, columns]
        qkv_t[0:1152, :] = hidden.T
        if part < 2:
            fc_load(part + 2).start()

        def gelu(index, _, part=part):
            rows = pl.ds(pl.multiple_of(index * 144, 144), 144)
            values = qkv_t[rows, :]
            square = values * values
            bend = jnp.tanh(inner * values * (1.0 + 0.044715 * square))
            half = 0.5 * (1.0 + bend)
            active = values * half
            steep = half + 0.5 * values * (1.0 - bend * bend) * inner * (
                1.0 + 3.0 * 0.044715 * square
            )
            into = pl.ds(pl.multiple_of(part * 1152 + index * 144, 144), 144)
            act_out[into, :] = active.astype(jnp.bfloat16)
            slope_out[into, :] = steep.astype(jnp.bfloat16)
            chip = part * 4 + lax.div(index, 2)

            @pl.when(lax.rem(index, 2) == core)
            def _():
                lhs_zero[chip, :, 0:256] = active.astype(jnp.bfloat16)

            @pl.when(lax.rem(index, 2) != core)
            def _():
                send_e[chip] = active

            return 0

        lax.fori_loop(0, 8, gelu, 0)
        some = pl.ds(part * 4, 4)
        pair_e.append(to_sibling(4 + part, send_e.at[some], got_e.at[some]))
        pair_e[-1].start()
        part_out(part)[0].start()
        part_out(part)[1].start()
        if part == 0:
            pair_b.wait()
            for chip in range(8):
                rows = got_b[chip * 144 : chip * 144 + 144]
                lhs_two[chip + 8, :, 256:512] = rows.astype(jnp.bfloat16)
            outs[4].start()
        if part == 1:
            pair_c.wait()
            rhs_zero[:, 256:512] = got_c[...].astype(jnp.bfloat16)
            outs[5].start()
        if part == 2:
            pair_d.wait()
            for chip in range(8):
                rows = got_d[chip * 144 : chip * 144 + 144]
                lhs_one[chip, :, 256:512] = rows.astype(jnp.bfloat16)
            outs[6].start()
    for part in range(4):
        pair_e[part].wait()
        for chip in range(part * 4, part * 4 + 4):
            lhs_zero[chip, :, 256:512] = got_e[chip].astype(jnp.bfloat16)
        part_out(part)[2].start()
    for copy in outs:
        copy.wait()
    for part in range(4):
        for copy in part_out(part):
            copy.wait()


def forward(operands):
    dma = pltpu.SemaphoreType.DMA
    vmem = pl.BlockSpec(memory_space=pltpu.VMEM)
    smem = pl.BlockSpec(memory_space=pltpu.SMEM)
    anywhere = pl.BlockSpec(memory_space=pl.ANY)
    full, small = jnp.float32, jnp.bfloat16
    out = jax.ShapeDtypeStruct
    return pl.pallas_call(
        forward_kernel,
        out_shape=(
            out((2, 1152), full),
            out((2, 1152), full),
            out((8, 1152), full),
            out((16, 144, 512), small),
            out((8, 144, 512), small),
            out((16, 144, 512), small),
            out((1152, 512), small),
            out((4608, 256), small),
            out((4608, 256), small),
            out((48, 80, 256), small),
            out((256, 1152), full),
            out((256, 1152), full),
            out((256, 1152), full),
            out((256, 1152), small),
            out((256, 128), full),
            out((2, 128), full),
        ),
        in_specs=[vmem] * 3
        + [smem, smem, vmem]
        + [anywhere, vmem] * 2
        + [vmem, vmem]
        + [anywhere, vmem] * 3,
        out_specs=(vmem,) * 3 + (anywhere,) * 10 + (vmem,) * 3,
        scratch_shapes=[
            pltpu.VMEM((16, 144, 512), small),
            pltpu.VMEM((8, 144, 512), small),
            pltpu.VMEM((16, 144, 512), small),
            pltpu.VMEM((1152, 512), small),
            pltpu.VMEM((4608, 256), small),
            pltpu.VMEM((4608, 256), small),
            pltpu.VMEM((48, 80, 256), small),
            pltpu.VMEM((256, 1152), full),
            pltpu.VMEM((256, 1152), full),
            pltpu.VMEM((256, 1152), full),
            pltpu.VMEM((2, 1, 256), full),
            pltpu.VMEM((32, 1, 256), full),
            pltpu.VMEM((56, 1, 128), full),
            pltpu.VMEM((256, 1152), full),
            pltpu.VMEM((3456, 256), full),
            pltpu.VMEM((1152, 3456), small),
            pltpu.VMEM((1152, 1152), small),
            pltpu.VMEM((2, 1152, 1152), small),
            pltpu.VMEM((256, 1152), small),
            pltpu.VMEM((1152, 1152), small),
            pltpu.VMEM((256, 128), full),
            pltpu.VMEM((256, 128), full),
            pltpu.VMEM((1152, 256), full),
            pltpu.VMEM((1152, 256), full),
            pltpu.VMEM((1152, 256), full),
            pltpu.VMEM((1152, 256), full),
            pltpu.VMEM((16, 144, 256), full),
            pltpu.VMEM((1152, 256), full),
            pltpu.VMEM((1152, 256), full),
            pltpu.VMEM((1152, 256), full),
            pltpu.VMEM((1152, 256), full),
            pltpu.VMEM((16, 144, 256), full),
            dma((32,)),
            dma((32,)),
            dma((4,)),
            dma((8,)),
            dma((8,)),
            dma((2,)),
            dma((7,)),
            dma((3, 4)),
        ],
        compiler_params=pltpu.CompilerParams(
            collective_id=2, has_side_effects=True, vmem_limit_bytes=255 * 2**18
        ),
    )(*operands)


def split_parts(values):
    high = values.astype(jnp.bfloat16)
    rest = values - high.astype(jnp.float32)
    middle = rest.astype(jnp.bfloat16)
    low = (rest - middle.astype(jnp.float32)).astype(jnp.bfloat16)
    return high, middle, low


def outer_sum(left, right):
    left_high, left_middle, left_low = split_parts(left)
    right_high, right_middle, right_low = split_parts(right)
    lefts = [left_high, left_high, left_middle, left_middle, left_high, left_low]
    rights = [right_high, right_middle, right_high, right_middle, right_low, right_high]
    return dot_tn(jnp.concatenate(lefts, axis=0), jnp.concatenate(rights, axis=0))


def finish_kernel(
    packs,
    sums,
    in_qkv,
    in_proj,
    in_fc1,
    in_fc2,
    in_block,
    in_grad,
    out_qkv,
    out_proj,
    out_fc1,
    out_fc2,
    out_block,
    out_grad,
    d_ada,
    b_ada,
    d_t1,
    b_t1,
    d_t2,
    b_t2,
    d_table,
    b_qv,
    b_proj,
    b_fc1,
    b_fc2,
    copy_sem,
):
    place = lax.axis_index("dp")
    copies = [
        pltpu.make_async_copy(source, target, copy_sem.at[index])
        for index, (source, target) in enumerate(
            (
                (in_qkv, out_qkv),
                (in_proj, out_proj),
                (in_fc1, out_fc1),
                (in_fc2, out_fc2),
                (in_block, out_block),
                (in_grad, out_grad),
            )
        )
    ]
    for copy in copies:
        copy.start()

    def eight(begin, end):
        return jnp.concatenate([packs[group, :, begin:end] for group in range(4)], axis=0)

    def own(rows, width):
        count = rows.shape[1]
        return pltpu.roll(rows, lax.rem(count - place * width, count), 1)

    grad_cond, grad_pre = eight(0, 1152), eight(1152, 2304)
    d_mod = eight(4608, 4864)
    d_ada[...] = outer_sum(d_mod, eight(2304, 3456))[0:216]
    b_ada[...] = jnp.sum(d_mod, axis=0, keepdims=True)[:, 0:216].reshape(216)
    d_t1[...] = outer_sum(own(eight(4864, 5120), 8)[:, 0:128], grad_pre)[0:8]
    d_t2[...] = outer_sum(own(eight(3456, 4608), 36)[:, 0:128], grad_cond)[0:36]
    d_table[...] = outer_sum(eight(5120, 5248), grad_cond)[0:101]
    total_pre = jnp.concatenate([jnp.sum(grad_pre, axis=0, keepdims=True)] * 8, axis=0)
    total_cond = jnp.concatenate([jnp.sum(grad_cond, axis=0, keepdims=True)] * 8, axis=0)
    b_t1[...] = own(total_pre, 36)[0:1, 0:36].reshape(36)
    b_t2[...] = own(total_cond, 36)[0:1, 0:36].reshape(36)
    b_qv[...] = sums[0:1, 0:72].reshape(72)
    b_proj[...] = sums[1:2, 0:36].reshape(36)
    b_fc1[...] = jnp.concatenate([sums[2:3, :], sums[3:4, :]], axis=1)[:, 0:144].reshape(144)
    b_fc2[...] = sums[4:5, 0:36].reshape(36)
    for copy in copies:
        copy.wait()


def finish(operands):
    vmem = pl.BlockSpec(memory_space=pltpu.VMEM)
    anywhere = pl.BlockSpec(memory_space=pl.ANY)
    full, small = jnp.float32, jnp.bfloat16
    out = jax.ShapeDtypeStruct
    return pl.pallas_call(
        finish_kernel,
        out_shape=(
            out((36, 3456), full),
            out((36, 1152), full),
            out((36, 4608), full),
            out((144, 1152), full),
            out((256, 1152), small),
            out((256, 1152), small),
            out((216, 1152), full),
            out((216,), full),
            out((8, 1152), full),
            out((36,), full),
            out((36, 1152), full),
            out((36,), full),
            out((101, 1152), full),
            out((72,), full),
            out((36,), full),
            out((144,), full),
            out((36,), full),
        ),
        in_specs=[vmem] * 8,
        out_specs=(anywhere,) * 6 + (vmem,) * 11,
        scratch_shapes=[pltpu.SemaphoreType.DMA((6,))],
        compiler_params=pltpu.CompilerParams(vmem_limit_bytes=255 * 2**18),
    )(*operands)


def on_device(
    tokens,
    out_grad,
    timesteps,
    labels,
    grid_ids,
    w_qkv,
    b_qv,
    w_proj,
    b_proj,
    w_fc1,
    b_fc1,
    w_fc2,
    b_fc2,
    w_ada,
    b_ada,
    w_t1,
    b_t1,
    w_t2,
    b_t2,
    table,
):
    dp_place = lax.axis_index("dp")
    model_width = tokens.shape[1]
    time_feats = time_embed(timesteps, w_t1.shape[0] // 2)
    (
        pre_time,
        condition,
        mods,
        lhs_two,
        lhs_one,
        lhs_zero,
        rhs_zero,
        act_t,
        slope_t,
        heads,
        cotangent,
        resid_one,
        attn_out,
        ada_wide,
        bias_keys,
        onehot,
    ) = forward(
        [
            tokens,
            out_grad,
            time_feats,
            labels,
            grid_ids,
            table,
            w_t1,
            b_t1,
            w_t2,
            b_t2,
            w_ada.T,
            b_ada,
            w_qkv,
            b_qv,
            w_proj,
            b_proj,
            w_fc1,
            b_fc1,
        ]
    )
    (
        sum_qkv,
        sum_proj,
        sum_fc1,
        sum_fc2,
        block_out,
        input_grad,
        packs,
        sums,
    ) = backward(
        [
            lhs_zero,
            lhs_one,
            lhs_two,
            rhs_zero,
            act_t,
            slope_t,
            heads,
            bias_keys,
            cotangent,
            resid_one,
            attn_out,
            tokens,
            mods,
            b_fc2,
            pre_time,
            condition,
            time_feats,
            onehot,
            ada_wide,
            w_t2,
            w_qkv,
            w_proj,
            w_fc1,
            w_fc2,
        ]
    )
    (
        sum_qkv,
        sum_proj,
        sum_fc1,
        sum_fc2,
        block_out,
        input_grad,
        d_ada,
        b_ada,
        d_t1,
        b_t1,
        d_t2,
        b_t2,
        d_table,
        d_qv,
        d_proj,
        d_fc1,
        d_fc2,
    ) = finish([packs, sums, sum_qkv, sum_proj, sum_fc1, sum_fc2, block_out, input_grad])
    return (
        block_out,
        input_grad,
        sum_qkv,
        d_qv,
        sum_proj,
        d_proj,
        sum_fc1,
        d_fc1,
        sum_fc2,
        d_fc2,
        d_ada.T,
        b_ada,
        d_t1,
        b_t1,
        d_t2,
        b_t2,
        d_table,
    )


def solution(mesh):
    placed = (
        P(("group", "dp"), None),
        P(("group", "dp"), None),
        P("group"),
        P("group"),
        P("group"),
        P(),
        P(),
        P(),
        P(),
        P(),
        P(),
        P(),
        P(),
        P(None, "dp"),
        P("dp"),
        P(),
        P(),
        P(),
        P(),
        P(),
    )
    return jax.shard_map(
        on_device,
        mesh=mesh,
        in_specs=placed,
        out_specs=(
            P(("group", "dp"), None),
            P(("group", "dp"), None),
            P("dp", None),
            P("dp"),
            P("dp", None),
            P("dp"),
            P("dp", None),
            P("dp"),
            P("dp", None),
            P("dp"),
            P(None, "dp"),
            P("dp"),
            P("dp", None),
            P("dp"),
            P("dp", None),
            P("dp"),
            P(),
        ),
        check_vma=False,
    )
```

```python
import math

import jax
import jax.numpy as jnp
from jax import lax
from jax.experimental import pallas as pl
from jax.experimental.pallas import tpu as pltpu
from jax.sharding import PartitionSpec as P

SLOTS = 256
ITEM_FRAMES = 16


EPS = 1e-06
NEG = -1e30


def norm_back(grad_in, normed, inv_std):
    return inv_std * (
        grad_in
        - jnp.mean(grad_in, axis=-1, keepdims=True)
        - normed * jnp.mean(grad_in * normed, axis=-1, keepdims=True)
    )


def silu_back(pre_vals, grad_in):
    sigmoid = jax.nn.sigmoid(pre_vals)
    return grad_in * sigmoid * (1.0 + pre_vals * (1.0 - sigmoid))


def time_embed(step_ids, width_half):
    frequency = jnp.exp(
        jnp.arange(width_half, dtype=jnp.float32) * (-math.log(10000.0) / width_half)
    )
    angles = step_ids.astype(jnp.float32)[:, None] * frequency[None, :]
    return jnp.concatenate([jnp.cos(angles), jnp.sin(angles)], axis=1)


def split_three(values):
    high = values.astype(jnp.bfloat16)
    rest = values - high.astype(jnp.float32)
    middle = rest.astype(jnp.bfloat16)
    low = (rest - middle.astype(jnp.float32)).astype(jnp.bfloat16)
    return jnp.concatenate([high, middle, low], axis=0)


def exact_dot(values, weights, contract=0):
    rows = values.shape[0]
    thrice = lax.dot_general(
        split_three(values),
        weights,
        (((1,), (contract,)), ((), ())),
        preferred_element_type=jnp.float32,
    )
    return thrice[0:rows] + thrice[rows : 2 * rows] + thrice[2 * rows : 3 * rows]


def silu(values):
    return values / (1.0 + jnp.exp(-values))


def dot_nn(left, right):
    return jnp.dot(left, right, preferred_element_type=jnp.float32)


def dot_nt(left, right):
    return lax.dot_general(
        left, right, (((1,), (1,)), ((), ())), preferred_element_type=jnp.float32
    )


def dot_tn(left, right):
    return lax.dot_general(
        left, right, (((0,), (0,)), ((), ())), preferred_element_type=jnp.float32
    )


MESH = pl.DeviceIdType.MESH
ORDERS = ((("y", "z", "x"), ("z", "x", "y"), ("x", "y", "z")),) * 3
STREAMS = tuple(
    tuple((order, pairing) for pairing in (0, 1) for order in orders) for orders in ORDERS
)
BLOCKS = (32, 16, 8, 4, 2, 1)
LANDS_AT = (0, 32, 48, 56, 60, 62)
PIECE = 56
OWN = 72
CHUNK = 384
ROWS = 32
WINDOWS = ((0, 216, 3), (54, 72, 2), (72, 36, 2), (81, 144, 3), (117, 36, 2))


def coords():
    place = lax.axis_index("dp")
    return {
        "y": lax.axis_index("group"),
        "z": lax.div(place, 8),
        "x": lax.rem(lax.div(place, 2), 4),
        "core": lax.rem(place, 2),
    }


def device_at(at):
    return (at["y"], (at["z"] * 4 + at["x"]) * 2 + at["core"])


def dp_peer(hop):
    return (lax.axis_index("group"), lax.rem(lax.axis_index("dp") + hop, 32))


def sibling_of(at):
    return device_at({**at, "core": 1 - at["core"]})


def partner_of(at, axis, pairing):
    here = at[axis]
    if pairing == 0:
        there = here + 1 - 2 * lax.rem(here, 2)
    else:
        there = lax.rem(here + 3 + 2 * lax.rem(here, 2), 4)
    return device_at({**at, axis: there})


def slot_of(pairing, value):
    if pairing == 1:
        return value
    if isinstance(value, int):
        return (0, 2, 3, 1)[value]
    return lax.rem(value + lax.div(value + 1, 2), 4)


PACK = 4 * 1152 + 2 * 256 + 128


def backward_kernel(
    lhs_zero,
    lhs_one,
    lhs_two,
    rhs_zero,
    act_flat,
    slope,
    heads,
    bias_keys,
    cot,
    resid,
    attn_out,
    tokens,
    mods,
    b_fc2,
    pre_in,
    cond_in,
    feats,
    onehot,
    w_ada,
    w_t2,
    w_qkv,
    w_proj,
    w_fc1,
    w_fc2,
    out_qkv,
    out_proj,
    out_fc1,
    out_fc2,
    block_out,
    input_grad,
    packed,
    sums,
    parts,
    landed,
    lhs,
    rhs,
    stage_rhs,
    leave,
    final,
    other,
    narrow,
    d_mod,
    bias_fc1,
    bias_qv,
    bias_proj,
    bias_fc2,
    flat,
    shares,
    got,
    conds,
    sums_all,
    out_rows,
    in_rows,
    wa,
    wb,
    slope_in,
    act_in,
    grad_t,
    branch,
    grad_resid,
    all_t,
    mixed_t,
    heads_in,
    rows_a,
    rows_b,
    rows_c,
    rows_d,
    send_sem,
    recv_sem,
    credit,
    swap_send,
    swap_recv,
    swap_credit,
    own_sem,
    ring_send,
    ring_recv,
    pair_send,
    pair_recv,
    load_sem,
    row_sem,
    head_sem,
    other_credit,
    out_sem,
    share_send,
    share_recv,
    cond_send,
    cond_recv,
    group_send,
    group_recv,
):
    at = coords()
    core = at["core"]
    sibling = sibling_of(at)
    barrier = pltpu.get_barrier_semaphore()
    place = lax.axis_index("dp")

    def group_peer(hop):
        return (lax.rem(at["y"] + hop, 4), place)

    def swap():
        return pltpu.make_async_remote_copy(
            src_ref=leave,
            dst_ref=stage_rhs,
            send_sem=swap_send,
            recv_sem=swap_recv,
            device_id=sibling,
            device_id_type=MESH,
        )

    def lhs_load(phase):
        source = (lhs_zero, lhs_one, lhs_two)[phase]
        target = lhs.at[0:8] if phase == 1 else lhs
        return pltpu.make_async_copy(source, target, own_sem.at[0])

    def rhs_load():
        return pltpu.make_async_copy(rhs_zero, rhs.at[0:1152], own_sem.at[1])

    def swap_start(phase):
        lhs_load(phase).start()
        if phase == 2:
            pl.semaphore_wait(swap_credit, 1)
        swap().start()

    def swap_finish(phase):
        swap().wait()

        def narrow_rhs(step, _):
            rows = pl.ds(pl.multiple_of(step * 144, 144), 144)
            rhs[rows, 256:512] = stage_rhs[rows, :].astype(jnp.bfloat16)
            return _

        lax.fori_loop(0, 16, narrow_rhs, 0)
        if phase == 1:
            pl.semaphore_signal(swap_credit, inc=1, device_id=sibling, device_id_type=MESH)
        lhs_load(phase).wait()

    def base_of(phase, stream, z_place, x_place, y_slot):
        order, pairing = STREAMS[phase][stream]
        slots = {"y": y_slot, "z": slot_of(pairing, z_place), "x": slot_of(pairing, x_place)}
        return (slots[order[0]] * 4 + slots[order[1]]) * 4 + slots[order[2]]

    def keep(phase, stream, chip, rows):
        half = phase % 2
        z_place, x_place = lax.div(chip, 4), lax.rem(chip, 4)
        for y_slot in range(4):
            block = base_of(phase, stream, z_place, x_place, y_slot)
            first = y_slot * PIECE
            for unit in range(3):
                low, high = max(first, OWN * unit), min(first + PIECE, OWN * unit + OWN)
                if low < high:
                    parts[half, stream, block, low - first : high - first, :] = rows[
                        low - OWN * unit : high - OWN * unit, unit * 128 : unit * 128 + 128
                    ]
            if y_slot == 3:
                parts[half, stream, block, 48:56, :] = jnp.zeros((8, 128), jnp.float32)

    def halving(phase, stream, step):
        order, pairing = STREAMS[phase][stream]
        axis = order[step // 2]
        slots = [slot_of(pairing, at[name]) for name in order]
        base = 0
        for level in range(step // 2):
            base = base + slots[level] * (64 // 4 ** (level + 1))
        slot = slots[step // 2]
        side = lax.div(slot, 2) if step % 2 == 0 else slot
        away = 1 - side if step % 2 == 0 else slot + 1 - 2 * lax.rem(slot, 2)
        count = BLOCKS[step]
        kept, sent = base + side * count, base + away * count
        partner = partner_of(at, axis, pairing if step % 2 == 0 else 1 - pairing)
        source = parts.at[phase % 2, stream]
        if phase == 0 and step >= 3:
            origin = slots[0] * 16 + lax.div(slots[1], 2) * 8
            kept, sent = kept - origin, sent - origin
            source = narrow.at[stream]
        copy = pltpu.make_async_remote_copy(
            src_ref=source.at[pl.ds(sent, count)],
            dst_ref=landed.at[stream, pl.ds(LANDS_AT[step], count)],
            send_sem=send_sem.at[stream, step],
            recv_sem=recv_sem.at[stream, step],
            device_id=partner,
            device_id_type=MESH,
        )
        return copy, kept, partner

    def send(phase, stream, step):
        copy, _, _ = halving(phase, stream, step)
        if phase:
            pl.semaphore_wait(credit.at[stream, step], 1)
        copy.start()

    def receive(phase, step):
        for stream in range(6):
            copy, kept, partner = halving(phase, stream, step)
            copy.wait()
            half = phase % 2
            count = BLOCKS[step]
            late = phase == 0 and step >= 3
            if step < 5:

                def add(block, _):
                    arrived = landed[stream, LANDS_AT[step] + block]
                    if late:
                        narrow[stream, kept + block] += arrived
                    elif phase == 0 and step == 2:
                        narrow[stream, block] = parts[half, stream, kept + block] + arrived
                    else:
                        parts[half, stream, kept + block] += arrived
                    return _

                lax.fori_loop(0, count, add, 0, unroll=min(count, 4))
            else:
                mine = narrow[stream, kept] if late else parts[half, stream, kept]
                final[phase, at["y"], stream] = mine + landed[stream, LANDS_AT[step]]
            if phase < 2:
                pl.semaphore_signal(
                    credit.at[stream, step], inc=1, device_id=partner, device_id_type=MESH
                )
            if step < 5:
                send(phase, stream, step + 1)

    def products(phase):
        together, stacked = (3, 4) if phase == 2 else (2, 8)
        for group in range(6 // together):
            members = range(group * together, (group + 1) * together)
            if phase == 0:
                first = group * together // 2 * CHUNK
                width = together // 2 * CHUNK
                count = 16
            else:
                first = members[0] * CHUNK
                width = together * CHUNK
                count = 8
            shift = core * 8 if phase == 2 and members[0] >= 3 else 0

            def some(step, _):
                left = lhs[pl.ds(step * stacked + shift, stacked)]
                rows = dot_nt(
                    left.reshape(stacked * 144, 512), rhs[first : first + width, :]
                )
                for place in range(stacked):
                    at_row = place * 144
                    if phase == 0:
                        chip = step * stacked + place
                        for third in range(together // 2):
                            column = third * CHUNK
                            block = rows[at_row : at_row + 144, column : column + CHUNK]
                            stream = group * together // 2 + third
                            keep(phase, stream, chip, block[0:72])
                            keep(phase, stream + 3, chip, block[72:144])
                    else:
                        chip = (step * stacked + place) * 2
                        for place_at, stream in enumerate(members):
                            column = place_at * CHUNK
                            block = rows[at_row : at_row + 144, column : column + CHUNK]
                            keep(phase, stream, chip, block[0:72])
                            keep(phase, stream, chip + 1, block[72:144])
                return _

            lax.fori_loop(0, count // stacked, some, 0)
            for member in members:
                stream = member
                if phase == 0:
                    stream = group * together // 2 + (member - members[0]) // 2
                    stream += 3 * ((member - members[0]) % 2)
                send(phase, stream, 0)

    def ring(phase, late):
        mine = at["y"]
        copies = []
        for place, hop in enumerate((1, 3)):
            half = pl.ds(3 - place * 3 if late else place * 3, 3)
            copies.append(
                pltpu.make_async_remote_copy(
                    src_ref=final.at[phase, mine, half],
                    dst_ref=final.at[phase, mine, half],
                    send_sem=ring_send.at[phase, place + 4 * late],
                    recv_sem=ring_recv.at[phase, place + 4 * late],
                    device_id=device_at({**at, "y": lax.rem(mine + hop, 4)}),
                    device_id_type=MESH,
                )
            )
        return copies

    def relay(phase):
        mine = at["y"]
        copies = []
        for place, hop in enumerate((1, 3)):
            origin = lax.rem(mine + 4 - hop, 4)
            half = pl.ds(place * 3, 3)
            copies.append(
                pltpu.make_async_remote_copy(
                    src_ref=final.at[phase, origin, half],
                    dst_ref=final.at[phase, origin, half],
                    send_sem=ring_send.at[phase, place + 2],
                    recv_sem=ring_recv.at[phase, place + 2],
                    device_id=device_at({**at, "y": lax.rem(mine + hop, 4)}),
                    device_id_type=MESH,
                )
            )
        return copies

    def across(phase):
        return pltpu.make_async_remote_copy(
            src_ref=final.at[phase],
            dst_ref=other,
            send_sem=pair_send.at[phase - 1],
            recv_sem=pair_recv.at[phase - 1],
            device_id=sibling,
            device_id_type=MESH,
        )

    def whole(get, stream):
        pairing = STREAMS[0][stream][1]
        order = sorted(range(4), key=lambda y_place: slot_of(pairing, y_place))
        return jnp.concatenate([get(y_place, stream) for y_place in order], axis=0)

    def write_rows(phase, low):
        for side in range(2):
            mine = side == (0 if low == 0 else 1)
            for stream in range(6):
                if mine:
                    rows = whole(lambda y_place, stream: final[phase, y_place, stream], stream)
                else:
                    rows = whole(lambda y_place, stream: other[y_place, stream], stream)
                for unit in range(3):
                    block = rows[OWN * unit + low : OWN * unit + low + 36]
                    column = side * 18 + stream * 3 + unit
                    if phase == 1:
                        out_fc1[:, column * 128 : column * 128 + 128] = block
                    elif column < 27:
                        out_qkv[:, column * 128 : column * 128 + 128] = block
                    else:
                        out_proj[:, (column - 27) * 128 : (column - 27) * 128 + 128] = block

    def write(phase):
        if phase == 0:
            for stream in range(6):
                rows = whole(lambda y_place, stream: final[0, y_place, stream], stream)
                half, third = stream // 3, stream % 3
                for unit in range(3):
                    column = third * 3 + unit
                    out_fc2[half * 72 : half * 72 + 72, column * 128 : column * 128 + 128] = rows[
                        OWN * unit : OWN * unit + 72
                    ]
            return

        @pl.when(core == 0)
        def _():
            write_rows(phase, 0)

        @pl.when(core == 1)
        def _():
            write_rows(phase, 36)

        if phase == 1:
            pl.semaphore_signal(other_credit, inc=1, device_id=sibling, device_id_type=MESH)

    def ring_start(phase):
        for late in (0, 1):
            for copy in ring(phase, late):
                copy.start()

    def ring_relay(phase):
        for copy, onward in zip(ring(phase, 0), relay(phase)):
            copy.wait()
            onward.start()

    def ring_finish(phase):
        for copy in ring(phase, 1) + relay(phase):
            copy.wait()
        if phase == 2:
            pl.semaphore_wait(other_credit, 1)
        if phase:
            across(phase).start()

    ones = jnp.ones((8, 256), jnp.bfloat16)

    def mlp_loads(chunk):
        slot = lax.rem(chunk, 2)
        rows = pl.ds(pl.multiple_of(chunk * CHUNK, CHUNK), CHUNK)
        return [
            pltpu.make_async_copy(w_fc2.at[rows], wa.at[slot], load_sem.at[0, slot]),
            pltpu.make_async_copy(w_fc1.at[:, rows], wb.at[slot], load_sem.at[1, slot]),
            pltpu.make_async_copy(slope.at[rows], slope_in.at[slot], load_sem.at[2, slot]),
        ]

    def branch_loads(chunk):
        slot = lax.rem(chunk, 2)
        rows = pl.ds(pl.multiple_of(chunk * CHUNK, CHUNK), CHUNK)
        return [
            pltpu.make_async_copy(w_fc2.at[rows], wa.at[slot], load_sem.at[0, slot]),
            pltpu.make_async_copy(act_flat.at[rows], act_in.at[slot], load_sem.at[3, slot]),
        ]

    def branch_begin():
        for copy in branch_loads(0):
            copy.start()

    def branch_forward(low, high):
        if low == 0:
            branch[...] = jnp.zeros((256, 1152), jnp.float32)

        def branch_step(chunk, carry):
            slot = lax.rem(chunk, 2)

            @pl.when(chunk < 11)
            def _():
                for copy in branch_loads(chunk + 1):
                    copy.start()

            for copy in branch_loads(chunk):
                copy.wait()
            branch[...] += dot_tn(act_in[slot], wa[slot])
            return carry

        lax.fori_loop(low, high, branch_step, 0)

    def mlp_begin():
        for copy in mlp_loads(0):
            copy.start()

    def mlp_backward(low, high):
        if low == 0:
            rhs[0:1152, 256:512] = rhs[0:1152, 0:256]
            grad_t[...] = jnp.zeros((1152, 256), jnp.float32)

        def chunk_step(chunk, carry):
            slot = lax.rem(chunk, 2)

            @pl.when(chunk < 11)
            def _():
                for copy in mlp_loads(chunk + 1):
                    copy.start()

            for copy in mlp_loads(chunk):
                copy.wait()
            grad_act = dot_nn(wa[slot], rhs[0:1152, 256:512])
            grad_hidden = (grad_act * slope_in[slot].astype(jnp.float32)).astype(jnp.bfloat16)
            side = lax.div(chunk, 6)
            rows = pl.ds(pl.multiple_of(lax.rem(chunk, 6) * CHUNK, CHUNK), CHUNK)

            @pl.when(side == core)
            def _():
                rhs[rows, 0:256] = grad_hidden

            @pl.when(side != core)
            def _():
                leave[rows, :] = grad_hidden.astype(jnp.float32)

            columns = pl.ds(pl.multiple_of(chunk * CHUNK, CHUNK), CHUNK)
            bias_fc1[:, columns] = dot_nt(ones, grad_hidden)[0:1]
            grad_t[...] += dot_nn(wb[slot], grad_hidden)
            return carry

        lax.fori_loop(low, high, chunk_step, 0)

    def row_block(source, index):
        return source.at[pl.ds(pl.multiple_of(index * ROWS, ROWS), ROWS)]

    def norm(values):
        mean = jnp.mean(values, axis=-1, keepdims=True)
        centered = values - mean
        inverse = lax.rsqrt(jnp.mean(centered * centered, axis=-1, keepdims=True) + EPS)
        return centered * inverse, inverse

    def total(values):
        return jnp.sum(values, axis=0, keepdims=True)

    def middle_loads(index):
        slot = lax.rem(index, 2)
        return [
            pltpu.make_async_copy(row_block(source, index), target.at[slot], row_sem.at[place, slot])
            for place, (source, target) in enumerate(
                ((cot, rows_a), (resid, rows_b), (attn_out, rows_c))
            )
        ]

    def token_load(index):
        slot = lax.rem(index, 2)
        return pltpu.make_async_copy(
            row_block(tokens, index), rows_d.at[slot], row_sem.at[3, slot]
        )

    def proj_load(chunk):
        slot = lax.rem(chunk, 2)
        rows = pl.ds(pl.multiple_of(chunk * 288, 288), 288)
        return pltpu.make_async_copy(w_proj.at[rows], wa.at[slot, 0:288], load_sem.at[0, slot])

    def rows_out(kind, index):
        slot = lax.rem(index, 2)
        target = block_out if kind == 0 else input_grad
        buffer = out_rows if kind == 0 else in_rows
        return pltpu.make_async_copy(
            buffer.at[slot], row_block(target, index), out_sem.at[kind, slot]
        )

    def drain(kind):
        rows_out(kind, 256 // ROWS - 2).wait()
        rows_out(kind, 256 // ROWS - 1).wait()

    def middle_begin():
        for copy in middle_loads(0):
            copy.start()
        proj_load(0).start()
        d_mod[...] = jnp.zeros((8, 1152), jnp.float32)
        bias_proj[...] = jnp.zeros((1, 1152), jnp.float32)
        bias_fc2[...] = jnp.zeros((1, 1152), jnp.float32)
        grad_resid[...] = grad_t[...].T

    def middle_rows(low, high):
        scale_mlp, gate_attn = mods[4:5], mods[2:3]

        def rows_step(index, carry):
            rows = pl.ds(pl.multiple_of(index * ROWS, ROWS), ROWS)
            slot = lax.rem(index, 2)

            @pl.when(index < 256 // ROWS - 1)
            def _():
                for copy in middle_loads(index + 1):
                    copy.start()

            for copy in middle_loads(index):
                copy.wait()

            cotangent, stream_rows = rows_a[slot], rows_b[slot]
            normed, inverse = norm(stream_rows)
            grad_in = grad_resid[rows, :]
            d_mod[3:4, :] += total(grad_in)
            d_mod[4:5, :] += total(grad_in * normed)
            back = norm_back(grad_in * (1.0 + scale_mlp), normed, inverse)
            grads = cotangent + back
            grad_resid[rows, :] = grads
            d_mod[2:3, :] += total(grads * rows_c[slot])
            grad_attn = (grads * gate_attn).astype(jnp.bfloat16).astype(jnp.float32)
            bias_proj[...] += total(grad_attn)
            branch[rows, :] = grad_attn
            return carry

        lax.fori_loop(low, high, rows_step, 0)

    def finish_begin():
        for copy in middle_loads(0)[0:2]:
            copy.start()

    def finish_rows():
        gate_mlp = mods[5:6]

        def finish_step(index, carry):
            rows = pl.ds(pl.multiple_of(index * ROWS, ROWS), ROWS)
            slot = lax.rem(index, 2)

            @pl.when(index < 256 // ROWS - 1)
            def _():
                for copy in middle_loads(index + 1)[0:2]:
                    copy.start()

            for copy in middle_loads(index)[0:2]:
                copy.wait()

            @pl.when(index >= 2)
            def _():
                rows_out(0, index - 2).wait()

            cotangent, stream_rows = rows_a[slot], rows_b[slot]
            branch_rows = branch[rows, :] + b_fc2[...].reshape(1, 1152)
            out_rows[slot] = (stream_rows + gate_mlp * branch_rows).astype(jnp.bfloat16)
            rows_out(0, index).start()
            d_mod[5:6, :] += total(cotangent * branch_rows)
            bias_fc2[...] += total(
                (cotangent * gate_mlp).astype(jnp.bfloat16).astype(jnp.float32)
            )
            return carry

        lax.fori_loop(0, 256 // ROWS, finish_step, 0)

    def middle_end():
        all_t[3456:4608, :] = branch[...].T.astype(jnp.bfloat16)

        def proj_step(chunk, carry):
            @pl.when(chunk < 3)
            def _():
                proj_load(chunk + 1).start()

            proj_load(chunk).wait()
            grads = dot_nn(wa[lax.rem(chunk, 2), 0:288], all_t[3456:4608, :])
            for head in range(4):
                padded = jnp.concatenate(
                    [grads[head * 72 : head * 72 + 72], jnp.zeros((8, 256), jnp.float32)], axis=0
                )
                mixed_t[chunk * 4 + head] = padded.astype(jnp.bfloat16)
            return carry

        lax.fori_loop(0, 4, proj_step, 0)

    def heads_load(pair_at):
        slot = lax.rem(pair_at, 2)
        return [
            pltpu.make_async_copy(
                heads.at[pl.ds(part * 16 + pair_at * 2, 2)],
                heads_in.at[slot, part],
                head_sem.at[part, slot],
            )
            for part in range(3)
        ]

    def attention_backward(low, high):
        scale = 1.0 / math.sqrt(72)

        def one_head(pair_at, side):
            slot = lax.rem(pair_at, 2)
            query, key, value = (heads_in[slot, part, side] for part in range(3))
            grad_mixed = mixed_t[pair_at * 2 + side]
            scores = dot_tn(key, query) * scale + jnp.concatenate([bias_keys[...]] * 2, axis=1)
            shifted = jnp.exp(scores - jnp.max(scores, axis=0, keepdims=True))
            weights = shifted / jnp.sum(shifted, axis=0, keepdims=True)
            grad_weights = dot_tn(value, grad_mixed)
            row_dot = jnp.sum(weights * grad_weights, axis=0, keepdims=True)
            grad_scores = (weights * (grad_weights - row_dot)).astype(jnp.bfloat16)
            return (
                dot_nn(key, grad_scores)[0:72] * scale,
                dot_nt(query, grad_scores)[0:72] * scale,
                dot_nt(grad_mixed, weights.astype(jnp.bfloat16))[0:72],
            )

        def two_heads(pair_at, carry):
            @pl.when(pair_at < 7)
            def _():
                for copy in heads_load(pair_at + 1):
                    copy.start()

            for copy in heads_load(pair_at):
                copy.wait()
            first, second = one_head(pair_at, 0), one_head(pair_at, 1)
            for part in range(3):
                rows = pl.ds(pl.multiple_of(part * 1152 + pair_at * 144, 16), 144)
                all_t[rows, :] = jnp.concatenate([first[part], second[part]], axis=0).astype(
                    jnp.bfloat16
                )
            return carry

        lax.fori_loop(low, high, two_heads, 0)

    def sides():
        def side(step, _):
            mine = pl.ds(pl.multiple_of(core * 2304 + step * 144, 16), 144)
            theirs = pl.ds(pl.multiple_of((1 - core) * 2304 + step * 144, 16), 144)
            rows = pl.ds(pl.multiple_of(step * 144, 144), 144)
            rhs[rows, 0:256] = all_t[mine, :]
            leave[rows, :] = all_t[theirs, :].astype(jnp.float32)
            return _

        lax.fori_loop(0, 16, side, 0)

    def qkv_load(chunk):
        slot = lax.rem(chunk, 2)
        columns = pl.ds(pl.multiple_of(chunk * CHUNK, CHUNK), CHUNK)
        return pltpu.make_async_copy(w_qkv.at[:, columns], wb.at[slot], load_sem.at[1, slot])

    def last_columns(low, high):
        if low == 0:
            grad_t[...] = jnp.zeros((1152, 256), jnp.float32)
            token_load(0).start()

        def qkv_step(chunk, carry):
            @pl.when(chunk < 8)
            def _():
                qkv_load(chunk + 1).start()

            qkv_load(chunk).wait()
            rows = pl.ds(pl.multiple_of(chunk * CHUNK, CHUNK), CHUNK)
            grads = all_t[rows, :]
            grad_t[...] += dot_nn(wb[lax.rem(chunk, 2)], grads)
            bias_qv[:, rows] = dot_nt(ones, grads)[0:1]
            return carry

        lax.fori_loop(low, high, qkv_step, 0)

    def ada_load():
        return pltpu.make_async_copy(w_ada, wa.at[0, 0:256], load_sem.at[0, 0])

    def last_rows():
        branch[...] = grad_t[...].T
        scale_attn = mods[1:2]

        def last_step(index, carry):
            rows = pl.ds(pl.multiple_of(index * ROWS, ROWS), ROWS)
            slot = lax.rem(index, 2)

            @pl.when(index < 256 // ROWS - 1)
            def _():
                token_load(index + 1).start()

            token_load(index).wait()

            @pl.when(index >= 2)
            def _():
                rows_out(1, index - 2).wait()

            normed, inverse = norm(rows_d[slot].astype(jnp.float32))
            grad_in = branch[rows, :]
            d_mod[0:1, :] += total(grad_in)
            d_mod[1:2, :] += total(grad_in * normed)
            back = norm_back(grad_in * (1.0 + scale_attn), normed, inverse)
            in_rows[slot] = (grad_resid[rows, :] + back).astype(jnp.bfloat16)
            rows_out(1, index).start()
            return carry

        lax.fori_loop(0, 256 // ROWS, last_step, 0)

    def share_to(hop):
        return pltpu.make_async_remote_copy(
            src_ref=shares.at[lax.rem(place + hop, 32)],
            dst_ref=got.at[place],
            send_sem=share_send,
            recv_sem=share_recv,
            device_id=dp_peer(hop),
            device_id_type=MESH,
        )

    def cond_to(hop):
        return pltpu.make_async_remote_copy(
            src_ref=conds.at[place],
            dst_ref=conds.at[place],
            send_sem=cond_send,
            recv_sem=cond_recv,
            device_id=dp_peer(hop),
            device_id_type=MESH,
        )

    def group_copies(hop):
        return [
            pltpu.make_async_remote_copy(
                src_ref=buffer.at[at["y"]],
                dst_ref=buffer.at[at["y"]],
                send_sem=group_send.at[side, hop],
                recv_sem=group_recv.at[side, hop],
                device_id=group_peer(hop),
                device_id_type=MESH,
            )
            for side, buffer in enumerate((packed, sums_all))
        ]

    def each(make, act):
        def one(hop, _):
            act(make(hop))
            return _

        lax.fori_loop(1, 32, one, 0)

    def wait_all(source, target, sent, arrived):
        pltpu.make_async_remote_copy(
            src_ref=source.at[pl.ds(0, 31)],
            dst_ref=target.at[pl.ds(0, 31)],
            send_sem=sent,
            recv_sem=arrived,
            device_id=sibling,
            device_id_type=MESH,
        ).wait()

    def tail_share():
        ada_load().start()
        vectors = [d_mod[row : row + 1] for row in range(6)]
        vectors += [bias_qv[0:1, 0:1152], bias_qv[0:1, 2304:3456]]
        vectors += [bias_proj[...], bias_fc1[0:1, :], bias_fc2[...]]
        row = 0
        for vector in vectors:
            for column in range(vector.shape[1] // 128):
                flat[row] = vector[:, column * 128 : column * 128 + 128]
                row += 1
        flat[126] = jnp.zeros((1, 128), jnp.float32)
        flat[127] = jnp.zeros((1, 128), jnp.float32)

        def window(peer, _):
            into = 0
            for first, width, count in WINDOWS:
                start = first + lax.div(peer * width, 128)
                for offset in range(count):
                    shares[peer, into] = flat[start + offset]
                    into += 1
            return _

        lax.fori_loop(0, 32, window, 0)
        got[place] = shares[place]
        each(share_to, lambda copy: copy.start())

    def tail_cond():
        wait_all(shares, got, share_send, share_recv)
        first, second = got[0], got[16]
        for source in range(1, 16):
            first = first + got[source]
            second = second + got[16 + source]

        lanes = lax.broadcasted_iota(jnp.int32, (1, 256), 1)

        def piece(rows, entry):
            begin = sum(count for _, _, count in WINDOWS[:entry])
            _, width, count = WINDOWS[entry]
            joined = jnp.concatenate([rows[begin + step] for step in range(count)], axis=1)
            joined = jnp.concatenate([joined] * 8, axis=0)
            shift = lax.rem(place * width, 128)
            moved = pltpu.roll(joined, lax.rem(count * 128 - shift, count * 128), 1)
            return moved[0:1]

        d_mod_own = jnp.concatenate(
            [jnp.where(lanes < 216, piece(rows, 0)[:, 0:256], 0.0) for rows in (first, second)],
            axis=0,
        )
        ada_load().wait()
        conds[place] = exact_dot(d_mod_own, wa[0, 0:256])
        each(cond_to, lambda copy: copy.start())
        for chunk in range(2):
            t2_load(chunk).start()
        both = first + second
        sums_all[at["y"], 0:1] = piece(both, 1)[:, 0:128]
        sums_all[at["y"], 1:2] = piece(both, 2)[:, 0:128]
        wide = piece(both, 3)
        sums_all[at["y"], 2:3] = wide[:, 0:128]
        sums_all[at["y"], 3:4] = wide[:, 128:256]
        sums_all[at["y"], 4:5] = piece(both, 4)[:, 0:128]
        sums_all[at["y"], 5:8] = jnp.zeros((3, 128), jnp.float32)
        packed[at["y"], :, 2304:3456] = silu(cond_in[...])
        packed[at["y"], :, 3456:4608] = silu(pre_in[...])
        packed[at["y"], :, 4608:4864] = d_mod_own
        packed[at["y"], :, 4864:5120] = feats[...]
        packed[at["y"], :, 5120:5248] = onehot[...]

    def t2_load(chunk):
        rows = pl.ds(chunk * CHUNK, CHUNK)
        return pltpu.make_async_copy(w_t2.at[rows], wa.at[chunk % 2], load_sem.at[0, chunk % 2])

    def tail_group():
        wait_all(conds, conds, cond_send, cond_recv)
        total_cond = conds[0]
        for source in range(1, 32):
            total_cond = total_cond + conds[source]
        grad_cond = silu_back(cond_in[...], total_cond)
        packed[at["y"], :, 0:1152] = grad_cond
        for chunk in range(3):
            t2_load(chunk).wait()
            columns = exact_dot(grad_cond, wa[chunk % 2], 1)
            if chunk == 0:
                t2_load(2).start()
            begin = chunk * CHUNK
            packed[at["y"], :, 1152 + begin : 1152 + begin + CHUNK] = silu_back(
                pre_in[:, begin : begin + CHUNK], columns
            )
        for hop in (1, 2, 3):
            for copy in group_copies(hop):
                copy.start()

    def tail_end():
        for hop in (1, 2, 3):
            for copy in group_copies(hop):
                copy.wait()
        sums[...] = sums_all[0] + sums_all[1] + sums_all[2] + sums_all[3]

    lhs_load(0).start()
    rhs_load().start()
    mlp_begin()

    def hello(hop, _):
        pl.semaphore_signal(barrier, inc=1, device_id=dp_peer(hop), device_id_type=MESH)
        return _

    lax.fori_loop(1, 32, hello, 0)
    for hop in (1, 2, 3):
        pl.semaphore_signal(barrier, inc=1, device_id=group_peer(hop), device_id_type=MESH)
    for copy in heads_load(0):
        copy.start()
    lhs_load(0).wait()
    rhs_load().wait()
    pl.semaphore_wait(barrier, 34)
    products(0)
    mlp_backward(0, 4)
    mlp_backward(4, 8)
    mlp_backward(8, 12)
    swap_start(1)
    middle_begin()
    middle_rows(0, 4)
    receive(0, 0)
    swap_finish(1)
    products(1)
    middle_rows(4, 8)
    middle_end()
    qkv_load(0).start()
    attention_backward(0, 4)
    receive(0, 1)
    attention_backward(4, 8)
    sides()
    swap_start(2)
    last_columns(0, 5)
    last_columns(5, 9)
    receive(1, 0)
    swap_finish(2)
    receive(0, 2)
    products(2)
    branch_begin()
    finish_begin()
    last_rows()
    receive(1, 1)
    receive(0, 3)
    branch_forward(0, 6)
    branch_forward(6, 12)
    receive(1, 2)
    finish_rows()
    tail_share()
    receive(2, 0)
    receive(0, 4)
    tail_cond()
    receive(2, 1)
    receive(1, 3)
    receive(0, 5)
    ring_start(0)
    tail_group()
    receive(2, 2)
    receive(1, 4)
    ring_relay(0)
    receive(2, 3)
    receive(1, 5)
    ring_start(1)
    ring_finish(0)
    write(0)
    tail_end()
    receive(2, 4)
    ring_relay(1)
    receive(2, 5)
    ring_start(2)
    ring_finish(1)
    across(1).wait()
    write(1)
    ring_relay(2)
    drain(0)
    drain(1)
    ring_finish(2)
    across(2).wait()
    write(2)


def backward(operands):
    dma = pltpu.SemaphoreType.DMA
    regular = pltpu.SemaphoreType.REGULAR
    vmem = pl.BlockSpec(memory_space=pltpu.VMEM)
    anywhere = pl.BlockSpec(memory_space=pl.ANY)
    full = jnp.float32
    small = jnp.bfloat16
    return pl.pallas_call(
        backward_kernel,
        out_shape=(
            jax.ShapeDtypeStruct((36, 3456), full),
            jax.ShapeDtypeStruct((36, 1152), full),
            jax.ShapeDtypeStruct((36, 4608), full),
            jax.ShapeDtypeStruct((144, 1152), full),
            jax.ShapeDtypeStruct((256, 1152), small),
            jax.ShapeDtypeStruct((256, 1152), small),
            jax.ShapeDtypeStruct((4, 2, PACK), full),
            jax.ShapeDtypeStruct((8, 128), full),
        ),
        in_specs=[anywhere] * 7 + [vmem] + [anywhere] * 4 + [vmem] * 6 + [anywhere] * 6,
        out_specs=(vmem,) * 4 + (anywhere,) * 2 + (vmem,) * 2,
        scratch_shapes=[
            pltpu.VMEM((2, 6, 64, PIECE, 128), full),
            pltpu.VMEM((6, 63, PIECE, 128), full),
            pltpu.VMEM((16, 144, 512), small),
            pltpu.VMEM((2304, 512), small),
            pltpu.VMEM((2304, 256), full),
            pltpu.VMEM((2304, 256), full),
            pltpu.VMEM((3, 4, 6, PIECE, 128), full),
            pltpu.VMEM((4, 6, PIECE, 128), full),
            pltpu.VMEM((6, 8, PIECE, 128), full),
            pltpu.VMEM((8, 1152), full),
            pltpu.VMEM((1, 4608), full),
            pltpu.VMEM((1, 3456), full),
            pltpu.VMEM((1, 1152), full),
            pltpu.VMEM((1, 1152), full),
            pltpu.VMEM((128, 1, 128), full),
            pltpu.VMEM((32, 12, 1, 128), full),
            pltpu.VMEM((32, 12, 1, 128), full),
            pltpu.VMEM((32, 2, 1152), full),
            pltpu.VMEM((4, 8, 128), full),
            pltpu.VMEM((2, ROWS, 1152), small),
            pltpu.VMEM((2, ROWS, 1152), small),
            pltpu.VMEM((2, CHUNK, 1152), small),
            pltpu.VMEM((2, 1152, CHUNK), small),
            pltpu.VMEM((2, CHUNK, 256), small),
            pltpu.VMEM((2, CHUNK, 256), small),
            pltpu.VMEM((1152, 256), full),
            pltpu.VMEM((256, 1152), full),
            pltpu.VMEM((256, 1152), full),
            pltpu.VMEM((4608, 256), small),
            pltpu.VMEM((16, 80, 256), small),
            pltpu.VMEM((2, 3, 2, 80, 256), small),
            pltpu.VMEM((2, ROWS, 1152), full),
            pltpu.VMEM((2, ROWS, 1152), full),
            pltpu.VMEM((2, ROWS, 1152), full),
            pltpu.VMEM((2, ROWS, 1152), small),
            dma((6, 6)),
            dma((6, 6)),
            regular((6, 6)),
            dma,
            dma,
            regular,
            dma((2,)),
            dma((3, 6)),
            dma((3, 6)),
            dma((2,)),
            dma((2,)),
            dma((4, 2)),
            dma((4, 2)),
            dma((3, 2)),
            regular,
            dma((2, 2)),
            dma,
            dma,
            dma,
            dma,
            dma((2, 4)),
            dma((2, 4)),
        ],
        compiler_params=pltpu.CompilerParams(
            collective_id=1, has_side_effects=True, vmem_limit_bytes=255 * 2**18
        ),
    )(*operands)


def as_row(ref):
    return ref[...].reshape(1, ref.shape[0])


def forward_kernel(
    tokens,
    out_grad,
    feats,
    labels,
    grid_ids,
    table,
    w_t1,
    b_t1,
    w_t2,
    b_t2,
    w_ada,
    b_ada,
    w_qkv,
    b_qv,
    w_proj,
    b_proj,
    w_fc1,
    b_fc1,
    pre_out,
    cond_out,
    mods,
    lhs_two_far,
    lhs_one_far,
    lhs_zero_far,
    rhs_zero_far,
    act_out_far,
    slope_out_far,
    heads_far,
    cot_far,
    resid_far,
    attn_out_far,
    ada_wide,
    bias_keys,
    onehot,
    lhs_two,
    lhs_one,
    lhs_zero,
    rhs_zero,
    act_out,
    slope_out,
    heads,
    cot,
    resid,
    attn_out,
    mine,
    gathered,
    flat,
    normed,
    qkv_t,
    w_q,
    w_p,
    w_f,
    w_1,
    w_2,
    keys_off,
    live_rows,
    send_a,
    send_b,
    send_c,
    send_d,
    send_e,
    got_a,
    got_b,
    got_c,
    got_d,
    got_e,
    send,
    recv,
    load_sem,
    pair_send,
    pair_recv,
    fc_sem,
    out_sem,
    part_sem,
):
    at = coords()
    core = at["core"]
    sibling = sibling_of(at)
    place = lax.axis_index("dp")
    loads = [
        pltpu.make_async_copy(source, target, load_sem.at[index])
        for index, (source, target) in enumerate(
            ((w_t1, w_1), (w_t2, w_2), (w_qkv, w_q), (w_proj, w_p))
        )
    ]
    for copy in loads:
        copy.start()

    def fc_load(part):
        columns = pl.ds(part * 1152, 1152)
        return pltpu.make_async_copy(w_fc1.at[:, columns], w_f.at[part % 2], fc_sem.at[part % 2])

    fc_load(0).start()
    fc_load(1).start()
    outs = [
        pltpu.make_async_copy(source, target, out_sem.at[index])
        for index, (source, target) in enumerate(
            (
                (cot, cot_far),
                (heads, heads_far),
                (attn_out, attn_out_far),
                (resid, resid_far),
                (lhs_two, lhs_two_far),
                (rhs_zero, rhs_zero_far),
                (lhs_one, lhs_one_far),
            )
        )
    ]

    def part_out(part):
        rows, chips = pl.ds(part * 1152, 1152), pl.ds(part * 4, 4)
        return [
            pltpu.make_async_copy(source, target, part_sem.at[index, part])
            for index, (source, target) in enumerate(
                (
                    (act_out.at[rows], act_out_far.at[rows]),
                    (slope_out.at[rows], slope_out_far.at[rows]),
                    (lhs_zero.at[chips], lhs_zero_far.at[chips]),
                )
            )
        ]

    barrier = pltpu.get_barrier_semaphore()

    def hello(hop, _):
        pl.semaphore_signal(barrier, inc=1, device_id=dp_peer(hop), device_id_type=MESH)
        return _

    lax.fori_loop(1, 32, hello, 0)
    rows_table = jnp.concatenate(
        [table[pl.ds(labels[0], 1), :], table[pl.ds(labels[1], 1), :]], axis=0
    )
    loads[0].wait()
    pre_time = exact_dot(feats[...], w_1[...]) + as_row(b_t1)
    loads[1].wait()
    condition = exact_dot(silu(pre_time), w_2[...]) + as_row(b_t2) + rows_table
    mod_part = exact_dot(silu(condition), w_ada[...], 1) + as_row(b_ada)
    pre_out[...] = pre_time
    cond_out[...] = condition
    for item in range(2):
        mine[item, :, 0:216] = mod_part[item : item + 1]
        mine[item, :, 216:256] = jnp.zeros((1, 40), jnp.float32)
    gathered[place] = mine[lax.div(place, 16)]
    pl.semaphore_wait(barrier, 31)

    def copy_to(hop):
        target = lax.rem(place + hop, 32)
        return pltpu.make_async_remote_copy(
            src_ref=mine.at[lax.div(target, 16)],
            dst_ref=gathered.at[place],
            send_sem=send,
            recv_sem=recv,
            device_id=dp_peer(hop),
            device_id_type=MESH,
        )

    def begin(hop, _):
        copy_to(hop).start()
        return _

    def norm(values):
        mean = jnp.mean(values, axis=-1, keepdims=True)
        centered = values - mean
        inverse = lax.rsqrt(jnp.mean(centered * centered, axis=-1, keepdims=True) + EPS)
        return centered * inverse

    def row_range(index):
        return pl.ds(pl.multiple_of(index * 64, 64), 64)

    lax.fori_loop(1, 32, begin, 0)
    ada_rows = jnp.concatenate([w_ada[...].astype(jnp.float32), jnp.zeros((40, 1152))], axis=0)
    ada_wide[...] = ada_rows.astype(jnp.bfloat16)
    grid_value = grid_ids[lax.div(place, 16)]
    first_live = jnp.where(grid_value == 2, 16, 0)
    end_live = jnp.where(grid_value == 1, 240, 256)
    slots = lax.broadcasted_iota(jnp.int32, (256, 128), 0)
    live = (slots >= first_live) & (slots < end_live)
    keys_off[...] = jnp.where(live, 0.0, NEG)
    live_rows[...] = jnp.where(live, 1.0, 0.0)
    bias_keys[...] = keys_off[...]
    for item in range(2):
        classes = lax.broadcasted_iota(jnp.int32, (1, 128), 1)
        onehot[item : item + 1, :] = jnp.where(classes == labels[item], 1.0, 0.0)

    def first_norm(index, _):
        rows = row_range(index)
        normed[rows, :] = norm(tokens[rows, :].astype(jnp.float32))
        cot[rows, :] = out_grad[rows, :].astype(jnp.float32) * live_rows[rows, 0:1]
        return _

    lax.fori_loop(0, 4, first_norm, 0)
    outs[0].start()

    def blank(row, _):
        flat[row] = jnp.zeros((1, 128), jnp.float32)
        return _

    lax.fori_loop(0, 56, blank, 0)
    pltpu.make_async_remote_copy(
        src_ref=gathered.at[pl.ds(0, 31)],
        dst_ref=gathered.at[pl.ds(0, 31)],
        send_sem=send,
        recv_sem=recv,
        device_id=sibling,
        device_id_type=MESH,
    ).wait()
    for piece in range(32):
        row, shift = piece * 216 // 128, piece * 216 % 128
        wide = jnp.concatenate([gathered[piece], jnp.zeros((1, 128), jnp.float32)], axis=1)
        wide = pltpu.roll(jnp.concatenate([wide] * 8, axis=0), shift, 1)[0:1]
        for step in range(3):
            flat[row + step] += wide[:, step * 128 : step * 128 + 128]
    for row in range(6):
        for column in range(9):
            mods[row : row + 1, column * 128 : column * 128 + 128] = flat[row * 9 + column]
    mods[6:8, :] = jnp.zeros((2, 1152), jnp.float32)

    def to_sibling(index, source, target):
        return pltpu.make_async_remote_copy(
            src_ref=source,
            dst_ref=target,
            send_sem=pair_send.at[index],
            recv_sem=pair_recv.at[index],
            device_id=sibling,
            device_id_type=MESH,
        )

    def modulate(index, _):
        rows = row_range(index)
        normed[rows, :] = normed[rows, :] * (1.0 + mods[1:2]) + mods[0:1]
        return _

    lax.fori_loop(0, 4, modulate, 0)
    send_a[...] = normed[...].T
    pair_a = to_sibling(0, send_a, got_a)
    pair_a.start()
    for part in range(8):
        lhs_two[part, :, 0:256] = send_a[part * 144 : part * 144 + 144].astype(jnp.bfloat16)
    loads[2].wait()
    for part in range(3):
        block = dot_nn(
            normed[...].astype(jnp.bfloat16), w_q[:, part * 1152 : part * 1152 + 1152]
        )
        if part == 0:
            block = block + as_row(b_qv)[:, 0:1152]
        if part == 2:
            block = block + as_row(b_qv)[:, 1152:2304]
        qkv_t[part * 1152 : part * 1152 + 1152, :] = block.T

    def branch_grad(index, _):
        rows = row_range(index)
        normed[rows, :] = cot[rows, :] * mods[5:6]
        return _

    scale = 1.0 / math.sqrt(72)

    def one_head(head, _):
        parts = []
        for part in range(3):
            rows = pl.ds(pl.multiple_of(part * 1152 + head * 72, 8), 72)
            padded = jnp.concatenate([qkv_t[rows, :], jnp.zeros((8, 256), jnp.float32)], axis=0)
            parts.append(padded.astype(jnp.bfloat16))
            heads[head + part * 16] = parts[-1]
        query, key, value = parts
        scores = dot_tn(key, query) * scale + jnp.concatenate([keys_off[...]] * 2, axis=1)
        shifted = jnp.exp(scores - jnp.max(scores, axis=0, keepdims=True))
        weights = (shifted / jnp.sum(shifted, axis=0, keepdims=True)).astype(jnp.bfloat16)
        rows = pl.ds(pl.multiple_of(head * 72, 8), 72)
        send_b[rows, :] = dot_nn(value, weights)[0:72]
        return _

    lax.fori_loop(0, 16, one_head, 0, unroll=4)
    outs[1].start()
    pair_b = to_sibling(1, send_b, got_b)
    pair_b.start()
    for part in range(8):
        lhs_two[part + 8, :, 0:256] = send_b[part * 144 : part * 144 + 144].astype(jnp.bfloat16)
    lax.fori_loop(0, 4, branch_grad, 0)
    send_c[...] = normed[...].T
    pair_c = to_sibling(2, send_c, got_c)
    pair_c.start()
    rhs_zero[:, 0:256] = send_c[...].astype(jnp.bfloat16)
    loads[3].wait()
    attn_out[...] = dot_tn(send_b[...].astype(jnp.bfloat16), w_p[...]) + as_row(b_proj)

    def second_norm(index, _):
        rows = row_range(index)
        stream = tokens[rows, :].astype(jnp.float32) + mods[2:3] * attn_out[rows, :]
        resid[rows, :] = stream
        normed[rows, :] = norm(stream) * (1.0 + mods[4:5]) + mods[3:4]
        return _

    lax.fori_loop(0, 4, second_norm, 0)
    outs[2].start()
    outs[3].start()
    send_d[...] = normed[...].T
    pair_d = to_sibling(3, send_d, got_d)
    pair_d.start()
    for part in range(8):
        lhs_one[part, :, 0:256] = send_d[part * 144 : part * 144 + 144].astype(jnp.bfloat16)
    pair_a.wait()
    for part in range(8):
        lhs_two[part, :, 256:512] = got_a[part * 144 : part * 144 + 144].astype(jnp.bfloat16)
    inner = math.sqrt(2.0 / math.pi)
    pair_e = []
    for part in range(4):
        fc_load(part).wait()
        columns = slice(part * 1152, part * 1152 + 1152)
        hidden = dot_nn(normed[...].astype(jnp.bfloat16), w_f[part % 2]) + as_row(b_fc1)[:, columns]
        qkv_t[0:1152, :] = hidden.T
        if part < 2:
            fc_load(part + 2).start()

        def gelu(index, _, part=part):
            rows = pl.ds(pl.multiple_of(index * 144, 144), 144)
            values = qkv_t[rows, :]
            square = values * values
            bend = jnp.tanh(inner * values * (1.0 + 0.044715 * square))
            half = 0.5 * (1.0 + bend)
            active = values * half
            steep = half + 0.5 * values * (1.0 - bend * bend) * inner * (
                1.0 + 3.0 * 0.044715 * square
            )
            into = pl.ds(pl.multiple_of(part * 1152 + index * 144, 144), 144)
            act_out[into, :] = active.astype(jnp.bfloat16)
            slope_out[into, :] = steep.astype(jnp.bfloat16)
            chip = part * 4 + lax.div(index, 2)

            @pl.when(lax.rem(index, 2) == core)
            def _():
                lhs_zero[chip, :, 0:256] = active.astype(jnp.bfloat16)

            @pl.when(lax.rem(index, 2) != core)
            def _():
                send_e[chip] = active

            return 0

        lax.fori_loop(0, 8, gelu, 0)
        some = pl.ds(part * 4, 4)
        pair_e.append(to_sibling(4 + part, send_e.at[some], got_e.at[some]))
        pair_e[-1].start()
        part_out(part)[0].start()
        part_out(part)[1].start()
        if part == 0:
            pair_b.wait()
            for chip in range(8):
                rows = got_b[chip * 144 : chip * 144 + 144]
                lhs_two[chip + 8, :, 256:512] = rows.astype(jnp.bfloat16)
            outs[4].start()
        if part == 1:
            pair_c.wait()
            rhs_zero[:, 256:512] = got_c[...].astype(jnp.bfloat16)
            outs[5].start()
        if part == 2:
            pair_d.wait()
            for chip in range(8):
                rows = got_d[chip * 144 : chip * 144 + 144]
                lhs_one[chip, :, 256:512] = rows.astype(jnp.bfloat16)
            outs[6].start()
    for part in range(4):
        pair_e[part].wait()
        for chip in range(part * 4, part * 4 + 4):
            lhs_zero[chip, :, 256:512] = got_e[chip].astype(jnp.bfloat16)
        part_out(part)[2].start()
    for copy in outs:
        copy.wait()
    for part in range(4):
        for copy in part_out(part):
            copy.wait()


def forward(operands):
    dma = pltpu.SemaphoreType.DMA
    vmem = pl.BlockSpec(memory_space=pltpu.VMEM)
    smem = pl.BlockSpec(memory_space=pltpu.SMEM)
    anywhere = pl.BlockSpec(memory_space=pl.ANY)
    full, small = jnp.float32, jnp.bfloat16
    out = jax.ShapeDtypeStruct
    return pl.pallas_call(
        forward_kernel,
        out_shape=(
            out((2, 1152), full),
            out((2, 1152), full),
            out((8, 1152), full),
            out((16, 144, 512), small),
            out((8, 144, 512), small),
            out((16, 144, 512), small),
            out((1152, 512), small),
            out((4608, 256), small),
            out((4608, 256), small),
            out((48, 80, 256), small),
            out((256, 1152), full),
            out((256, 1152), full),
            out((256, 1152), full),
            out((256, 1152), small),
            out((256, 128), full),
            out((2, 128), full),
        ),
        in_specs=[vmem] * 3
        + [smem, smem, vmem]
        + [anywhere, vmem] * 2
        + [vmem, vmem]
        + [anywhere, vmem] * 3,
        out_specs=(vmem,) * 3 + (anywhere,) * 10 + (vmem,) * 3,
        scratch_shapes=[
            pltpu.VMEM((16, 144, 512), small),
            pltpu.VMEM((8, 144, 512), small),
            pltpu.VMEM((16, 144, 512), small),
            pltpu.VMEM((1152, 512), small),
            pltpu.VMEM((4608, 256), small),
            pltpu.VMEM((4608, 256), small),
            pltpu.VMEM((48, 80, 256), small),
            pltpu.VMEM((256, 1152), full),
            pltpu.VMEM((256, 1152), full),
            pltpu.VMEM((256, 1152), full),
            pltpu.VMEM((2, 1, 256), full),
            pltpu.VMEM((32, 1, 256), full),
            pltpu.VMEM((56, 1, 128), full),
            pltpu.VMEM((256, 1152), full),
            pltpu.VMEM((3456, 256), full),
            pltpu.VMEM((1152, 3456), small),
            pltpu.VMEM((1152, 1152), small),
            pltpu.VMEM((2, 1152, 1152), small),
            pltpu.VMEM((256, 1152), small),
            pltpu.VMEM((1152, 1152), small),
            pltpu.VMEM((256, 128), full),
            pltpu.VMEM((256, 128), full),
            pltpu.VMEM((1152, 256), full),
            pltpu.VMEM((1152, 256), full),
            pltpu.VMEM((1152, 256), full),
            pltpu.VMEM((1152, 256), full),
            pltpu.VMEM((16, 144, 256), full),
            pltpu.VMEM((1152, 256), full),
            pltpu.VMEM((1152, 256), full),
            pltpu.VMEM((1152, 256), full),
            pltpu.VMEM((1152, 256), full),
            pltpu.VMEM((16, 144, 256), full),
            dma,
            dma,
            dma((4,)),
            dma((8,)),
            dma((8,)),
            dma((2,)),
            dma((7,)),
            dma((3, 4)),
        ],
        compiler_params=pltpu.CompilerParams(
            collective_id=2, has_side_effects=True, vmem_limit_bytes=255 * 2**18
        ),
    )(*operands)


def split_parts(values):
    high = values.astype(jnp.bfloat16)
    rest = values - high.astype(jnp.float32)
    middle = rest.astype(jnp.bfloat16)
    low = (rest - middle.astype(jnp.float32)).astype(jnp.bfloat16)
    return high, middle, low


def outer_sum(left, right):
    left_high, left_middle, left_low = split_parts(left)
    right_high, right_middle, right_low = split_parts(right)
    lefts = [left_high, left_high, left_middle, left_middle, left_high, left_low]
    rights = [right_high, right_middle, right_high, right_middle, right_low, right_high]
    return dot_tn(jnp.concatenate(lefts, axis=0), jnp.concatenate(rights, axis=0))


def finish_kernel(
    packs,
    sums,
    in_qkv,
    in_proj,
    in_fc1,
    in_fc2,
    in_block,
    in_grad,
    out_qkv,
    out_proj,
    out_fc1,
    out_fc2,
    out_block,
    out_grad,
    d_ada,
    b_ada,
    d_t1,
    b_t1,
    d_t2,
    b_t2,
    d_table,
    b_qv,
    b_proj,
    b_fc1,
    b_fc2,
    copy_sem,
):
    place = lax.axis_index("dp")
    copies = [
        pltpu.make_async_copy(source, target, copy_sem.at[index])
        for index, (source, target) in enumerate(
            (
                (in_qkv, out_qkv),
                (in_proj, out_proj),
                (in_fc1, out_fc1),
                (in_fc2, out_fc2),
                (in_block, out_block),
                (in_grad, out_grad),
            )
        )
    ]
    for copy in copies:
        copy.start()

    def eight(begin, end):
        return jnp.concatenate([packs[group, :, begin:end] for group in range(4)], axis=0)

    def own(rows, width):
        count = rows.shape[1]
        return pltpu.roll(rows, lax.rem(count - place * width, count), 1)

    grad_cond, grad_pre = eight(0, 1152), eight(1152, 2304)
    d_mod = eight(4608, 4864)
    d_ada[...] = outer_sum(d_mod, eight(2304, 3456))[0:216]
    b_ada[...] = jnp.sum(d_mod, axis=0, keepdims=True)[:, 0:216].reshape(216)
    d_t1[...] = outer_sum(own(eight(4864, 5120), 8)[:, 0:128], grad_pre)[0:8]
    d_t2[...] = outer_sum(own(eight(3456, 4608), 36)[:, 0:128], grad_cond)[0:36]
    d_table[...] = outer_sum(eight(5120, 5248), grad_cond)[0:101]
    total_pre = jnp.concatenate([jnp.sum(grad_pre, axis=0, keepdims=True)] * 8, axis=0)
    total_cond = jnp.concatenate([jnp.sum(grad_cond, axis=0, keepdims=True)] * 8, axis=0)
    b_t1[...] = own(total_pre, 36)[0:1, 0:36].reshape(36)
    b_t2[...] = own(total_cond, 36)[0:1, 0:36].reshape(36)
    b_qv[...] = sums[0:1, 0:72].reshape(72)
    b_proj[...] = sums[1:2, 0:36].reshape(36)
    b_fc1[...] = jnp.concatenate([sums[2:3, :], sums[3:4, :]], axis=1)[:, 0:144].reshape(144)
    b_fc2[...] = sums[4:5, 0:36].reshape(36)
    for copy in copies:
        copy.wait()


def finish(operands):
    vmem = pl.BlockSpec(memory_space=pltpu.VMEM)
    anywhere = pl.BlockSpec(memory_space=pl.ANY)
    full, small = jnp.float32, jnp.bfloat16
    out = jax.ShapeDtypeStruct
    return pl.pallas_call(
        finish_kernel,
        out_shape=(
            out((36, 3456), full),
            out((36, 1152), full),
            out((36, 4608), full),
            out((144, 1152), full),
            out((256, 1152), small),
            out((256, 1152), small),
            out((216, 1152), full),
            out((216,), full),
            out((8, 1152), full),
            out((36,), full),
            out((36, 1152), full),
            out((36,), full),
            out((101, 1152), full),
            out((72,), full),
            out((36,), full),
            out((144,), full),
            out((36,), full),
        ),
        in_specs=[vmem] * 8,
        out_specs=(anywhere,) * 6 + (vmem,) * 11,
        scratch_shapes=[pltpu.SemaphoreType.DMA((6,))],
        compiler_params=pltpu.CompilerParams(vmem_limit_bytes=255 * 2**18),
    )(*operands)


def on_device(
    tokens,
    out_grad,
    timesteps,
    labels,
    grid_ids,
    w_qkv,
    b_qv,
    w_proj,
    b_proj,
    w_fc1,
    b_fc1,
    w_fc2,
    b_fc2,
    w_ada,
    b_ada,
    w_t1,
    b_t1,
    w_t2,
    b_t2,
    table,
):
    dp_place = lax.axis_index("dp")
    model_width = tokens.shape[1]
    time_feats = time_embed(timesteps, w_t1.shape[0] // 2)
    (
        pre_time,
        condition,
        mods,
        lhs_two,
        lhs_one,
        lhs_zero,
        rhs_zero,
        act_t,
        slope_t,
        heads,
        cotangent,
        resid_one,
        attn_out,
        ada_wide,
        bias_keys,
        onehot,
    ) = forward(
        [
            tokens,
            out_grad,
            time_feats,
            labels,
            grid_ids,
            table,
            w_t1,
            b_t1,
            w_t2,
            b_t2,
            w_ada.T,
            b_ada,
            w_qkv,
            b_qv,
            w_proj,
            b_proj,
            w_fc1,
            b_fc1,
        ]
    )
    (
        sum_qkv,
        sum_proj,
        sum_fc1,
        sum_fc2,
        block_out,
        input_grad,
        packs,
        sums,
    ) = backward(
        [
            lhs_zero,
            lhs_one,
            lhs_two,
            rhs_zero,
            act_t,
            slope_t,
            heads,
            bias_keys,
            cotangent,
            resid_one,
            attn_out,
            tokens,
            mods,
            b_fc2,
            pre_time,
            condition,
            time_feats,
            onehot,
            ada_wide,
            w_t2,
            w_qkv,
            w_proj,
            w_fc1,
            w_fc2,
        ]
    )
    (
        sum_qkv,
        sum_proj,
        sum_fc1,
        sum_fc2,
        block_out,
        input_grad,
        d_ada,
        b_ada,
        d_t1,
        b_t1,
        d_t2,
        b_t2,
        d_table,
        d_qv,
        d_proj,
        d_fc1,
        d_fc2,
    ) = finish([packs, sums, sum_qkv, sum_proj, sum_fc1, sum_fc2, block_out, input_grad])
    return (
        block_out,
        input_grad,
        sum_qkv,
        d_qv,
        sum_proj,
        d_proj,
        sum_fc1,
        d_fc1,
        sum_fc2,
        d_fc2,
        d_ada.T,
        b_ada,
        d_t1,
        b_t1,
        d_t2,
        b_t2,
        d_table,
    )


def solution(mesh):
    placed = (
        P(("group", "dp"), None),
        P(("group", "dp"), None),
        P("group"),
        P("group"),
        P("group"),
        P(),
        P(),
        P(),
        P(),
        P(),
        P(),
        P(),
        P(),
        P(None, "dp"),
        P("dp"),
        P(),
        P(),
        P(),
        P(),
        P(),
    )
    return jax.shard_map(
        on_device,
        mesh=mesh,
        in_specs=placed,
        out_specs=(
            P(("group", "dp"), None),
            P(("group", "dp"), None),
            P("dp", None),
            P("dp"),
            P("dp", None),
            P("dp"),
            P("dp", None),
            P("dp"),
            P("dp", None),
            P("dp"),
            P(None, "dp"),
            P("dp"),
            P("dp", None),
            P("dp"),
            P("dp", None),
            P("dp"),
            P(),
        ),
        check_vma=False,
    )
```

```python
import math

import jax
import jax.numpy as jnp
from jax import lax
from jax.experimental import pallas as pl
from jax.experimental.pallas import tpu as pltpu
from jax.sharding import PartitionSpec as P

SLOTS = 256
ITEM_FRAMES = 16


EPS = 1e-06
NEG = -1e30


def norm_back(grad_in, normed, inv_std):
    return inv_std * (
        grad_in
        - jnp.mean(grad_in, axis=-1, keepdims=True)
        - normed * jnp.mean(grad_in * normed, axis=-1, keepdims=True)
    )


def silu_back(pre_vals, grad_in):
    sigmoid = jax.nn.sigmoid(pre_vals)
    return grad_in * sigmoid * (1.0 + pre_vals * (1.0 - sigmoid))


def time_embed(step_ids, width_half):
    frequency = jnp.exp(
        jnp.arange(width_half, dtype=jnp.float32) * (-math.log(10000.0) / width_half)
    )
    angles = step_ids.astype(jnp.float32)[:, None] * frequency[None, :]
    return jnp.concatenate([jnp.cos(angles), jnp.sin(angles)], axis=1)


def split_three(values):
    high = values.astype(jnp.bfloat16)
    rest = values - high.astype(jnp.float32)
    middle = rest.astype(jnp.bfloat16)
    low = (rest - middle.astype(jnp.float32)).astype(jnp.bfloat16)
    return jnp.concatenate([high, middle, low], axis=0)


def exact_dot(values, weights, contract=0):
    rows = values.shape[0]
    thrice = lax.dot_general(
        split_three(values),
        weights,
        (((1,), (contract,)), ((), ())),
        preferred_element_type=jnp.float32,
    )
    return thrice[0:rows] + thrice[rows : 2 * rows] + thrice[2 * rows : 3 * rows]


def silu(values):
    return values / (1.0 + jnp.exp(-values))


def dot_nn(left, right):
    return jnp.dot(left, right, preferred_element_type=jnp.float32)


def dot_nt(left, right):
    return lax.dot_general(
        left, right, (((1,), (1,)), ((), ())), preferred_element_type=jnp.float32
    )


def dot_tn(left, right):
    return lax.dot_general(
        left, right, (((0,), (0,)), ((), ())), preferred_element_type=jnp.float32
    )


MESH = pl.DeviceIdType.MESH
ORDERS = ((("y", "z", "x"), ("z", "x", "y"), ("x", "y", "z")),) * 3
STREAMS = tuple(
    tuple((order, pairing) for pairing in (0, 1) for order in orders) for orders in ORDERS
)
BLOCKS = (32, 16, 8, 4, 2, 1)
LANDS_AT = (0, 32, 48, 56, 60, 62)
PIECE = 56
OWN = 72
CHUNK = 384
ROWS = 32
WINDOWS = ((0, 216, 3), (54, 72, 2), (72, 36, 2), (81, 144, 3), (117, 36, 2))


def coords():
    place = lax.axis_index("dp")
    return {
        "y": lax.axis_index("group"),
        "z": lax.div(place, 8),
        "x": lax.rem(lax.div(place, 2), 4),
        "core": lax.rem(place, 2),
    }


def device_at(at):
    return (at["y"], (at["z"] * 4 + at["x"]) * 2 + at["core"])


def dp_peer(hop):
    return (lax.axis_index("group"), lax.rem(lax.axis_index("dp") + hop, 32))


def sibling_of(at):
    return device_at({**at, "core": 1 - at["core"]})


def partner_of(at, axis, pairing):
    here = at[axis]
    if pairing == 0:
        there = here + 1 - 2 * lax.rem(here, 2)
    else:
        there = lax.rem(here + 3 + 2 * lax.rem(here, 2), 4)
    return device_at({**at, axis: there})


def slot_of(pairing, value):
    if pairing == 1:
        return value
    if isinstance(value, int):
        return (0, 2, 3, 1)[value]
    return lax.rem(value + lax.div(value + 1, 2), 4)


PACK = 4 * 1152 + 2 * 256 + 128


def backward_kernel(
    lhs_zero,
    lhs_one,
    lhs_two,
    rhs_zero,
    act_flat,
    slope,
    heads,
    bias_keys,
    cot,
    resid,
    attn_out,
    tokens,
    mods,
    b_fc2,
    pre_in,
    cond_in,
    feats,
    onehot,
    w_ada,
    w_t2,
    w_qkv,
    w_proj,
    w_fc1,
    w_fc2,
    out_qkv,
    out_proj,
    out_fc1,
    out_fc2,
    block_out,
    input_grad,
    packed,
    sums,
    parts,
    landed,
    lhs,
    rhs,
    stage_rhs,
    leave,
    final,
    other,
    narrow,
    d_mod,
    bias_fc1,
    bias_qv,
    bias_proj,
    bias_fc2,
    flat,
    shares,
    got,
    conds,
    sums_all,
    out_rows,
    in_rows,
    wa,
    wb,
    slope_in,
    act_in,
    grad_t,
    branch,
    grad_resid,
    all_t,
    mixed_t,
    heads_in,
    rows_a,
    rows_b,
    rows_c,
    rows_d,
    send_sem,
    recv_sem,
    credit,
    swap_send,
    swap_recv,
    swap_credit,
    own_sem,
    ring_send,
    ring_recv,
    pair_send,
    pair_recv,
    load_sem,
    row_sem,
    head_sem,
    other_credit,
    out_sem,
    share_send,
    share_recv,
    cond_send,
    cond_recv,
    group_send,
    group_recv,
):
    at = coords()
    core = at["core"]
    sibling = sibling_of(at)
    barrier = pltpu.get_barrier_semaphore()
    place = lax.axis_index("dp")

    def group_peer(hop):
        return (lax.rem(at["y"] + hop, 4), place)

    def swap():
        return pltpu.make_async_remote_copy(
            src_ref=leave,
            dst_ref=stage_rhs,
            send_sem=swap_send,
            recv_sem=swap_recv,
            device_id=sibling,
            device_id_type=MESH,
        )

    def lhs_load(phase):
        source = (lhs_zero, lhs_one, lhs_two)[phase]
        target = lhs.at[0:8] if phase == 1 else lhs
        return pltpu.make_async_copy(source, target, own_sem.at[0])

    def rhs_load():
        return pltpu.make_async_copy(rhs_zero, rhs.at[0:1152], own_sem.at[1])

    def swap_start(phase):
        lhs_load(phase).start()
        if phase == 2:
            pl.semaphore_wait(swap_credit, 1)
        swap().start()

    def swap_finish(phase):
        swap().wait()

        def narrow_rhs(step, _):
            rows = pl.ds(pl.multiple_of(step * 144, 144), 144)
            rhs[rows, 256:512] = stage_rhs[rows, :].astype(jnp.bfloat16)
            return _

        lax.fori_loop(0, 16, narrow_rhs, 0)
        if phase == 1:
            pl.semaphore_signal(swap_credit, inc=1, device_id=sibling, device_id_type=MESH)
        lhs_load(phase).wait()

    def base_of(phase, stream, z_place, x_place, y_slot):
        order, pairing = STREAMS[phase][stream]
        slots = {"y": y_slot, "z": slot_of(pairing, z_place), "x": slot_of(pairing, x_place)}
        return (slots[order[0]] * 4 + slots[order[1]]) * 4 + slots[order[2]]

    def keep(phase, stream, chip, rows):
        half = phase % 2
        z_place, x_place = lax.div(chip, 4), lax.rem(chip, 4)
        for y_slot in range(4):
            block = base_of(phase, stream, z_place, x_place, y_slot)
            first = y_slot * PIECE
            for unit in range(3):
                low, high = max(first, OWN * unit), min(first + PIECE, OWN * unit + OWN)
                if low < high:
                    parts[half, stream, block, low - first : high - first, :] = rows[
                        low - OWN * unit : high - OWN * unit, unit * 128 : unit * 128 + 128
                    ]
            if y_slot == 3:
                parts[half, stream, block, 48:56, :] = jnp.zeros((8, 128), jnp.float32)

    def halving(phase, stream, step):
        order, pairing = STREAMS[phase][stream]
        axis = order[step // 2]
        slots = [slot_of(pairing, at[name]) for name in order]
        base = 0
        for level in range(step // 2):
            base = base + slots[level] * (64 // 4 ** (level + 1))
        slot = slots[step // 2]
        side = lax.div(slot, 2) if step % 2 == 0 else slot
        away = 1 - side if step % 2 == 0 else slot + 1 - 2 * lax.rem(slot, 2)
        count = BLOCKS[step]
        kept, sent = base + side * count, base + away * count
        partner = partner_of(at, axis, pairing if step % 2 == 0 else 1 - pairing)
        source = parts.at[phase % 2, stream]
        if phase == 0 and step >= 3:
            origin = slots[0] * 16 + lax.div(slots[1], 2) * 8
            kept, sent = kept - origin, sent - origin
            source = narrow.at[stream]
        copy = pltpu.make_async_remote_copy(
            src_ref=source.at[pl.ds(sent, count)],
            dst_ref=landed.at[stream, pl.ds(LANDS_AT[step], count)],
            send_sem=send_sem.at[stream, step],
            recv_sem=recv_sem.at[stream, step],
            device_id=partner,
            device_id_type=MESH,
        )
        return copy, kept, partner

    def send(phase, stream, step):
        copy, _, _ = halving(phase, stream, step)
        if phase:
            pl.semaphore_wait(credit.at[stream, step], 1)
        copy.start()

    def receive(phase, step):
        for stream in range(6):
            copy, kept, partner = halving(phase, stream, step)
            copy.wait()
            half = phase % 2
            count = BLOCKS[step]
            late = phase == 0 and step >= 3
            if step < 5:

                def add(block, _):
                    arrived = landed[stream, LANDS_AT[step] + block]
                    if late:
                        narrow[stream, kept + block] += arrived
                    elif phase == 0 and step == 2:
                        narrow[stream, block] = parts[half, stream, kept + block] + arrived
                    else:
                        parts[half, stream, kept + block] += arrived
                    return _

                lax.fori_loop(0, count, add, 0, unroll=min(count, 4))
            else:
                mine = narrow[stream, kept] if late else parts[half, stream, kept]
                final[phase, at["y"], stream] = mine + landed[stream, LANDS_AT[step]]
            if phase < 2:
                pl.semaphore_signal(
                    credit.at[stream, step], inc=1, device_id=partner, device_id_type=MESH
                )
            if step < 5:
                send(phase, stream, step + 1)

    def products(phase):
        together, stacked = (3, 4) if phase == 2 else (2, 8)
        for group in range(6 // together):
            members = range(group * together, (group + 1) * together)
            if phase == 0:
                first = group * together // 2 * CHUNK
                width = together // 2 * CHUNK
                count = 16
            else:
                first = members[0] * CHUNK
                width = together * CHUNK
                count = 8
            shift = core * 8 if phase == 2 and members[0] >= 3 else 0

            def some(step, _):
                left = lhs[pl.ds(step * stacked + shift, stacked)]
                rows = dot_nt(
                    left.reshape(stacked * 144, 512), rhs[first : first + width, :]
                )
                for place in range(stacked):
                    at_row = place * 144
                    if phase == 0:
                        chip = step * stacked + place
                        for third in range(together // 2):
                            column = third * CHUNK
                            block = rows[at_row : at_row + 144, column : column + CHUNK]
                            stream = group * together // 2 + third
                            keep(phase, stream, chip, block[0:72])
                            keep(phase, stream + 3, chip, block[72:144])
                    else:
                        chip = (step * stacked + place) * 2
                        for place_at, stream in enumerate(members):
                            column = place_at * CHUNK
                            block = rows[at_row : at_row + 144, column : column + CHUNK]
                            keep(phase, stream, chip, block[0:72])
                            keep(phase, stream, chip + 1, block[72:144])
                return _

            lax.fori_loop(0, count // stacked, some, 0)
            for member in members:
                stream = member
                if phase == 0:
                    stream = group * together // 2 + (member - members[0]) // 2
                    stream += 3 * ((member - members[0]) % 2)
                send(phase, stream, 0)

    def ring(phase, late):
        mine = at["y"]
        copies = []
        for place, hop in enumerate((1, 3)):
            half = pl.ds(3 - place * 3 if late else place * 3, 3)
            copies.append(
                pltpu.make_async_remote_copy(
                    src_ref=final.at[phase, mine, half],
                    dst_ref=final.at[phase, mine, half],
                    send_sem=ring_send.at[phase, place + 4 * late],
                    recv_sem=ring_recv.at[phase, place + 4 * late],
                    device_id=device_at({**at, "y": lax.rem(mine + hop, 4)}),
                    device_id_type=MESH,
                )
            )
        return copies

    def relay(phase):
        mine = at["y"]
        copies = []
        for place, hop in enumerate((1, 3)):
            origin = lax.rem(mine + 4 - hop, 4)
            half = pl.ds(place * 3, 3)
            copies.append(
                pltpu.make_async_remote_copy(
                    src_ref=final.at[phase, origin, half],
                    dst_ref=final.at[phase, origin, half],
                    send_sem=ring_send.at[phase, place + 2],
                    recv_sem=ring_recv.at[phase, place + 2],
                    device_id=device_at({**at, "y": lax.rem(mine + hop, 4)}),
                    device_id_type=MESH,
                )
            )
        return copies

    def across(phase):
        return pltpu.make_async_remote_copy(
            src_ref=final.at[phase],
            dst_ref=other,
            send_sem=pair_send.at[phase - 1],
            recv_sem=pair_recv.at[phase - 1],
            device_id=sibling,
            device_id_type=MESH,
        )

    def whole(get, stream):
        pairing = STREAMS[0][stream][1]
        order = sorted(range(4), key=lambda y_place: slot_of(pairing, y_place))
        return jnp.concatenate([get(y_place, stream) for y_place in order], axis=0)

    def write_rows(phase, low):
        for side in range(2):
            mine = side == (0 if low == 0 else 1)
            for stream in range(6):
                if mine:
                    rows = whole(lambda y_place, stream: final[phase, y_place, stream], stream)
                else:
                    rows = whole(lambda y_place, stream: other[y_place, stream], stream)
                for unit in range(3):
                    block = rows[OWN * unit + low : OWN * unit + low + 36]
                    column = side * 18 + stream * 3 + unit
                    if phase == 1:
                        out_fc1[:, column * 128 : column * 128 + 128] = block
                    elif column < 27:
                        out_qkv[:, column * 128 : column * 128 + 128] = block
                    else:
                        out_proj[:, (column - 27) * 128 : (column - 27) * 128 + 128] = block

    def write(phase):
        if phase == 0:
            for stream in range(6):
                rows = whole(lambda y_place, stream: final[0, y_place, stream], stream)
                half, third = stream // 3, stream % 3
                for unit in range(3):
                    column = third * 3 + unit
                    out_fc2[half * 72 : half * 72 + 72, column * 128 : column * 128 + 128] = rows[
                        OWN * unit : OWN * unit + 72
                    ]
            return

        @pl.when(core == 0)
        def _():
            write_rows(phase, 0)

        @pl.when(core == 1)
        def _():
            write_rows(phase, 36)

        if phase == 1:
            pl.semaphore_signal(other_credit, inc=1, device_id=sibling, device_id_type=MESH)

    def ring_start(phase):
        for late in (0, 1):
            for copy in ring(phase, late):
                copy.start()

    def ring_relay(phase):
        for copy, onward in zip(ring(phase, 0), relay(phase)):
            copy.wait()
            onward.start()

    def ring_finish(phase):
        for copy in ring(phase, 1) + relay(phase):
            copy.wait()
        if phase == 2:
            pl.semaphore_wait(other_credit, 1)
        if phase:
            across(phase).start()

    ones = jnp.ones((8, 256), jnp.bfloat16)

    def mlp_loads(chunk):
        slot = lax.rem(chunk, 2)
        rows = pl.ds(pl.multiple_of(chunk * CHUNK, CHUNK), CHUNK)
        return [
            pltpu.make_async_copy(w_fc2.at[rows], wa.at[slot], load_sem.at[0, slot]),
            pltpu.make_async_copy(w_fc1.at[:, rows], wb.at[slot], load_sem.at[1, slot]),
            pltpu.make_async_copy(slope.at[rows], slope_in.at[slot], load_sem.at[2, slot]),
        ]

    def branch_loads(chunk):
        slot = lax.rem(chunk, 2)
        rows = pl.ds(pl.multiple_of(chunk * CHUNK, CHUNK), CHUNK)
        return [
            pltpu.make_async_copy(w_fc2.at[rows], wa.at[slot], load_sem.at[0, slot]),
            pltpu.make_async_copy(act_flat.at[rows], act_in.at[slot], load_sem.at[3, slot]),
        ]

    def branch_begin():
        for copy in branch_loads(0):
            copy.start()

    def branch_forward(low, high):
        if low == 0:
            branch[...] = jnp.zeros((256, 1152), jnp.float32)

        def branch_step(chunk, carry):
            slot = lax.rem(chunk, 2)

            @pl.when(chunk < 11)
            def _():
                for copy in branch_loads(chunk + 1):
                    copy.start()

            for copy in branch_loads(chunk):
                copy.wait()
            branch[...] += dot_tn(act_in[slot], wa[slot])
            return carry

        lax.fori_loop(low, high, branch_step, 0)

    def mlp_begin():
        for copy in mlp_loads(0):
            copy.start()

    def mlp_backward(low, high):
        if low == 0:
            rhs[0:1152, 256:512] = rhs[0:1152, 0:256]
            grad_t[...] = jnp.zeros((1152, 256), jnp.float32)

        def chunk_step(chunk, carry):
            slot = lax.rem(chunk, 2)

            @pl.when(chunk < 11)
            def _():
                for copy in mlp_loads(chunk + 1):
                    copy.start()

            for copy in mlp_loads(chunk):
                copy.wait()
            grad_act = dot_nn(wa[slot], rhs[0:1152, 256:512])
            grad_hidden = (grad_act * slope_in[slot].astype(jnp.float32)).astype(jnp.bfloat16)
            side = lax.div(chunk, 6)
            rows = pl.ds(pl.multiple_of(lax.rem(chunk, 6) * CHUNK, CHUNK), CHUNK)

            @pl.when(side == core)
            def _():
                rhs[rows, 0:256] = grad_hidden

            @pl.when(side != core)
            def _():
                leave[rows, :] = grad_hidden.astype(jnp.float32)

            columns = pl.ds(pl.multiple_of(chunk * CHUNK, CHUNK), CHUNK)
            bias_fc1[:, columns] = dot_nt(ones, grad_hidden)[0:1]
            grad_t[...] += dot_nn(wb[slot], grad_hidden)
            return carry

        lax.fori_loop(low, high, chunk_step, 0)

    def row_block(source, index):
        return source.at[pl.ds(pl.multiple_of(index * ROWS, ROWS), ROWS)]

    def norm(values):
        mean = jnp.mean(values, axis=-1, keepdims=True)
        centered = values - mean
        inverse = lax.rsqrt(jnp.mean(centered * centered, axis=-1, keepdims=True) + EPS)
        return centered * inverse, inverse

    def total(values):
        return jnp.sum(values, axis=0, keepdims=True)

    def middle_loads(index):
        slot = lax.rem(index, 2)
        return [
            pltpu.make_async_copy(row_block(source, index), target.at[slot], row_sem.at[place, slot])
            for place, (source, target) in enumerate(
                ((cot, rows_a), (resid, rows_b), (attn_out, rows_c))
            )
        ]

    def token_load(index):
        slot = lax.rem(index, 2)
        return pltpu.make_async_copy(
            row_block(tokens, index), rows_d.at[slot], row_sem.at[3, slot]
        )

    def proj_load(chunk):
        slot = lax.rem(chunk, 2)
        rows = pl.ds(pl.multiple_of(chunk * 288, 288), 288)
        return pltpu.make_async_copy(w_proj.at[rows], wa.at[slot, 0:288], load_sem.at[0, slot])

    def rows_out(kind, index):
        slot = lax.rem(index, 2)
        target = block_out if kind == 0 else input_grad
        buffer = out_rows if kind == 0 else in_rows
        return pltpu.make_async_copy(
            buffer.at[slot], row_block(target, index), out_sem.at[kind, slot]
        )

    def drain(kind):
        rows_out(kind, 256 // ROWS - 2).wait()
        rows_out(kind, 256 // ROWS - 1).wait()

    def middle_begin():
        for copy in middle_loads(0):
            copy.start()
        proj_load(0).start()
        d_mod[...] = jnp.zeros((8, 1152), jnp.float32)
        bias_proj[...] = jnp.zeros((1, 1152), jnp.float32)
        bias_fc2[...] = jnp.zeros((1, 1152), jnp.float32)
        grad_resid[...] = grad_t[...].T

    def middle_rows(low, high):
        scale_mlp, gate_attn = mods[4:5], mods[2:3]

        def rows_step(index, carry):
            rows = pl.ds(pl.multiple_of(index * ROWS, ROWS), ROWS)
            slot = lax.rem(index, 2)

            @pl.when(index < 256 // ROWS - 1)
            def _():
                for copy in middle_loads(index + 1):
                    copy.start()

            for copy in middle_loads(index):
                copy.wait()

            cotangent, stream_rows = rows_a[slot], rows_b[slot]
            normed, inverse = norm(stream_rows)
            grad_in = grad_resid[rows, :]
            d_mod[3:4, :] += total(grad_in)
            d_mod[4:5, :] += total(grad_in * normed)
            back = norm_back(grad_in * (1.0 + scale_mlp), normed, inverse)
            grads = cotangent + back
            grad_resid[rows, :] = grads
            d_mod[2:3, :] += total(grads * rows_c[slot])
            grad_attn = (grads * gate_attn).astype(jnp.bfloat16).astype(jnp.float32)
            bias_proj[...] += total(grad_attn)
            branch[rows, :] = grad_attn
            return carry

        lax.fori_loop(low, high, rows_step, 0)

    def finish_begin():
        for copy in middle_loads(0)[0:2]:
            copy.start()

    def finish_rows():
        gate_mlp = mods[5:6]

        def finish_step(index, carry):
            rows = pl.ds(pl.multiple_of(index * ROWS, ROWS), ROWS)
            slot = lax.rem(index, 2)

            @pl.when(index < 256 // ROWS - 1)
            def _():
                for copy in middle_loads(index + 1)[0:2]:
                    copy.start()

            for copy in middle_loads(index)[0:2]:
                copy.wait()

            @pl.when(index >= 2)
            def _():
                rows_out(0, index - 2).wait()

            cotangent, stream_rows = rows_a[slot], rows_b[slot]
            branch_rows = branch[rows, :] + b_fc2[...].reshape(1, 1152)
            out_rows[slot] = (stream_rows + gate_mlp * branch_rows).astype(jnp.bfloat16)
            rows_out(0, index).start()
            d_mod[5:6, :] += total(cotangent * branch_rows)
            bias_fc2[...] += total(
                (cotangent * gate_mlp).astype(jnp.bfloat16).astype(jnp.float32)
            )
            return carry

        lax.fori_loop(0, 256 // ROWS, finish_step, 0)

    def middle_end():
        all_t[3456:4608, :] = branch[...].T.astype(jnp.bfloat16)

        def proj_step(chunk, carry):
            @pl.when(chunk < 3)
            def _():
                proj_load(chunk + 1).start()

            proj_load(chunk).wait()
            grads = dot_nn(wa[lax.rem(chunk, 2), 0:288], all_t[3456:4608, :])
            for head in range(4):
                padded = jnp.concatenate(
                    [grads[head * 72 : head * 72 + 72], jnp.zeros((8, 256), jnp.float32)], axis=0
                )
                mixed_t[chunk * 4 + head] = padded.astype(jnp.bfloat16)
            return carry

        lax.fori_loop(0, 4, proj_step, 0)

    def heads_load(pair_at):
        slot = lax.rem(pair_at, 2)
        return [
            pltpu.make_async_copy(
                heads.at[pl.ds(part * 16 + pair_at * 2, 2)],
                heads_in.at[slot, part],
                head_sem.at[part, slot],
            )
            for part in range(3)
        ]

    def attention_backward(low, high):
        scale = 1.0 / math.sqrt(72)

        def one_head(pair_at, side):
            slot = lax.rem(pair_at, 2)
            query, key, value = (heads_in[slot, part, side] for part in range(3))
            grad_mixed = mixed_t[pair_at * 2 + side]
            scores = dot_tn(key, query) * scale + jnp.concatenate([bias_keys[...]] * 2, axis=1)
            shifted = jnp.exp(scores - jnp.max(scores, axis=0, keepdims=True))
            weights = shifted / jnp.sum(shifted, axis=0, keepdims=True)
            grad_weights = dot_tn(value, grad_mixed)
            row_dot = jnp.sum(weights * grad_weights, axis=0, keepdims=True)
            grad_scores = (weights * (grad_weights - row_dot)).astype(jnp.bfloat16)
            return (
                dot_nn(key, grad_scores)[0:72] * scale,
                dot_nt(query, grad_scores)[0:72] * scale,
                dot_nt(grad_mixed, weights.astype(jnp.bfloat16))[0:72],
            )

        def two_heads(pair_at, carry):
            @pl.when(pair_at < 7)
            def _():
                for copy in heads_load(pair_at + 1):
                    copy.start()

            for copy in heads_load(pair_at):
                copy.wait()
            first, second = one_head(pair_at, 0), one_head(pair_at, 1)
            for part in range(3):
                rows = pl.ds(pl.multiple_of(part * 1152 + pair_at * 144, 16), 144)
                all_t[rows, :] = jnp.concatenate([first[part], second[part]], axis=0).astype(
                    jnp.bfloat16
                )
            return carry

        lax.fori_loop(low, high, two_heads, 0)

    def sides():
        def side(step, _):
            mine = pl.ds(pl.multiple_of(core * 2304 + step * 144, 16), 144)
            theirs = pl.ds(pl.multiple_of((1 - core) * 2304 + step * 144, 16), 144)
            rows = pl.ds(pl.multiple_of(step * 144, 144), 144)
            rhs[rows, 0:256] = all_t[mine, :]
            leave[rows, :] = all_t[theirs, :].astype(jnp.float32)
            return _

        lax.fori_loop(0, 16, side, 0)

    def qkv_load(chunk):
        slot = lax.rem(chunk, 2)
        columns = pl.ds(pl.multiple_of(chunk * CHUNK, CHUNK), CHUNK)
        return pltpu.make_async_copy(w_qkv.at[:, columns], wb.at[slot], load_sem.at[1, slot])

    def last_columns(low, high):
        if low == 0:
            grad_t[...] = jnp.zeros((1152, 256), jnp.float32)
            token_load(0).start()

        def qkv_step(chunk, carry):
            @pl.when(chunk < 8)
            def _():
                qkv_load(chunk + 1).start()

            qkv_load(chunk).wait()
            rows = pl.ds(pl.multiple_of(chunk * CHUNK, CHUNK), CHUNK)
            grads = all_t[rows, :]
            grad_t[...] += dot_nn(wb[lax.rem(chunk, 2)], grads)
            bias_qv[:, rows] = dot_nt(ones, grads)[0:1]
            return carry

        lax.fori_loop(low, high, qkv_step, 0)

    def ada_load():
        return pltpu.make_async_copy(w_ada, wa.at[0, 0:256], load_sem.at[0, 0])

    def last_rows():
        branch[...] = grad_t[...].T
        scale_attn = mods[1:2]

        def last_step(index, carry):
            rows = pl.ds(pl.multiple_of(index * ROWS, ROWS), ROWS)
            slot = lax.rem(index, 2)

            @pl.when(index < 256 // ROWS - 1)
            def _():
                token_load(index + 1).start()

            token_load(index).wait()

            @pl.when(index >= 2)
            def _():
                rows_out(1, index - 2).wait()

            normed, inverse = norm(rows_d[slot].astype(jnp.float32))
            grad_in = branch[rows, :]
            d_mod[0:1, :] += total(grad_in)
            d_mod[1:2, :] += total(grad_in * normed)
            back = norm_back(grad_in * (1.0 + scale_attn), normed, inverse)
            in_rows[slot] = (grad_resid[rows, :] + back).astype(jnp.bfloat16)
            rows_out(1, index).start()
            return carry

        lax.fori_loop(0, 256 // ROWS, last_step, 0)

    def share_to(hop):
        return pltpu.make_async_remote_copy(
            src_ref=shares.at[lax.rem(place + hop, 32)],
            dst_ref=got.at[place],
            send_sem=share_send,
            recv_sem=share_recv,
            device_id=dp_peer(hop),
            device_id_type=MESH,
        )

    def cond_to(hop):
        return pltpu.make_async_remote_copy(
            src_ref=conds.at[place],
            dst_ref=conds.at[place],
            send_sem=cond_send,
            recv_sem=cond_recv,
            device_id=dp_peer(hop),
            device_id_type=MESH,
        )

    def group_copies(hop):
        return [
            pltpu.make_async_remote_copy(
                src_ref=buffer.at[at["y"]],
                dst_ref=buffer.at[at["y"]],
                send_sem=group_send.at[side, hop],
                recv_sem=group_recv.at[side, hop],
                device_id=group_peer(hop),
                device_id_type=MESH,
            )
            for side, buffer in enumerate((packed, sums_all))
        ]

    def each(make, act):
        def one(hop, _):
            act(make(hop))
            return _

        lax.fori_loop(1, 32, one, 0)

    def wait_all(source, target, sent, arrived):
        pltpu.make_async_remote_copy(
            src_ref=source.at[pl.ds(0, 31)],
            dst_ref=target.at[pl.ds(0, 31)],
            send_sem=sent,
            recv_sem=arrived,
            device_id=sibling,
            device_id_type=MESH,
        ).wait()

    def tail_share():
        ada_load().start()
        vectors = [d_mod[row : row + 1] for row in range(6)]
        vectors += [bias_qv[0:1, 0:1152], bias_qv[0:1, 2304:3456]]
        vectors += [bias_proj[...], bias_fc1[0:1, :], bias_fc2[...]]
        row = 0
        for vector in vectors:
            for column in range(vector.shape[1] // 128):
                flat[row] = vector[:, column * 128 : column * 128 + 128]
                row += 1
        flat[126] = jnp.zeros((1, 128), jnp.float32)
        flat[127] = jnp.zeros((1, 128), jnp.float32)

        def window(peer, _):
            into = 0
            for first, width, count in WINDOWS:
                start = first + lax.div(peer * width, 128)
                for offset in range(count):
                    shares[peer, into] = flat[start + offset]
                    into += 1
            return _

        lax.fori_loop(0, 32, window, 0)
        got[place] = shares[place]
        each(share_to, lambda copy: copy.start())

    def tail_cond():
        wait_all(shares, got, share_send, share_recv)
        first, second = got[0], got[16]
        for source in range(1, 16):
            first = first + got[source]
            second = second + got[16 + source]

        lanes = lax.broadcasted_iota(jnp.int32, (1, 256), 1)

        def piece(rows, entry):
            begin = sum(count for _, _, count in WINDOWS[:entry])
            _, width, count = WINDOWS[entry]
            joined = jnp.concatenate([rows[begin + step] for step in range(count)], axis=1)
            joined = jnp.concatenate([joined] * 8, axis=0)
            shift = lax.rem(place * width, 128)
            moved = pltpu.roll(joined, lax.rem(count * 128 - shift, count * 128), 1)
            return moved[0:1]

        d_mod_own = jnp.concatenate(
            [jnp.where(lanes < 216, piece(rows, 0)[:, 0:256], 0.0) for rows in (first, second)],
            axis=0,
        )
        ada_load().wait()
        conds[place] = exact_dot(d_mod_own, wa[0, 0:256])
        each(cond_to, lambda copy: copy.start())
        for chunk in range(2):
            t2_load(chunk).start()
        both = first + second
        sums_all[at["y"], 0:1] = piece(both, 1)[:, 0:128]
        sums_all[at["y"], 1:2] = piece(both, 2)[:, 0:128]
        wide = piece(both, 3)
        sums_all[at["y"], 2:3] = wide[:, 0:128]
        sums_all[at["y"], 3:4] = wide[:, 128:256]
        sums_all[at["y"], 4:5] = piece(both, 4)[:, 0:128]
        sums_all[at["y"], 5:8] = jnp.zeros((3, 128), jnp.float32)
        packed[at["y"], :, 2304:3456] = silu(cond_in[...])
        packed[at["y"], :, 3456:4608] = silu(pre_in[...])
        packed[at["y"], :, 4608:4864] = d_mod_own
        packed[at["y"], :, 4864:5120] = feats[...]
        packed[at["y"], :, 5120:5248] = onehot[...]

    def t2_load(chunk):
        rows = pl.ds(chunk * CHUNK, CHUNK)
        return pltpu.make_async_copy(w_t2.at[rows], wa.at[chunk % 2], load_sem.at[0, chunk % 2])

    def tail_group():
        wait_all(conds, conds, cond_send, cond_recv)
        total_cond = conds[0]
        for source in range(1, 32):
            total_cond = total_cond + conds[source]
        grad_cond = silu_back(cond_in[...], total_cond)
        packed[at["y"], :, 0:1152] = grad_cond
        for chunk in range(3):
            t2_load(chunk).wait()
            columns = exact_dot(grad_cond, wa[chunk % 2], 1)
            if chunk == 0:
                t2_load(2).start()
            begin = chunk * CHUNK
            packed[at["y"], :, 1152 + begin : 1152 + begin + CHUNK] = silu_back(
                pre_in[:, begin : begin + CHUNK], columns
            )
        for hop in (1, 2, 3):
            for copy in group_copies(hop):
                copy.start()

    def tail_end():
        for hop in (1, 2, 3):
            for copy in group_copies(hop):
                copy.wait()
        sums[...] = sums_all[0] + sums_all[1] + sums_all[2] + sums_all[3]

    lhs_load(0).start()
    rhs_load().start()
    mlp_begin()

    def hello(hop, _):
        pl.semaphore_signal(barrier, inc=1, device_id=dp_peer(hop), device_id_type=MESH)
        return _

    lax.fori_loop(1, 32, hello, 0)
    for hop in (1, 2, 3):
        pl.semaphore_signal(barrier, inc=1, device_id=group_peer(hop), device_id_type=MESH)
    for copy in heads_load(0):
        copy.start()
    lhs_load(0).wait()
    rhs_load().wait()
    pl.semaphore_wait(barrier, 34)
    products(0)
    mlp_backward(0, 4)
    mlp_backward(4, 8)
    mlp_backward(8, 12)
    swap_start(1)
    middle_begin()
    middle_rows(0, 4)
    receive(0, 0)
    swap_finish(1)
    products(1)
    middle_rows(4, 8)
    middle_end()
    qkv_load(0).start()
    attention_backward(0, 4)
    receive(0, 1)
    attention_backward(4, 8)
    sides()
    swap_start(2)
    last_columns(0, 5)
    last_columns(5, 9)
    receive(1, 0)
    swap_finish(2)
    receive(0, 2)
    products(2)
    branch_begin()
    finish_begin()
    last_rows()
    receive(1, 1)
    receive(0, 3)
    branch_forward(0, 6)
    branch_forward(6, 12)
    receive(1, 2)
    finish_rows()
    tail_share()
    receive(2, 0)
    receive(0, 4)
    tail_cond()
    receive(2, 1)
    receive(1, 3)
    receive(0, 5)
    ring_start(0)
    tail_group()
    receive(2, 2)
    receive(1, 4)
    ring_relay(0)
    receive(2, 3)
    receive(1, 5)
    ring_start(1)
    ring_finish(0)
    write(0)
    tail_end()
    receive(2, 4)
    ring_relay(1)
    receive(2, 5)
    ring_start(2)
    ring_finish(1)
    across(1).wait()
    write(1)
    ring_relay(2)
    drain(0)
    drain(1)
    ring_finish(2)
    across(2).wait()
    write(2)


def backward(operands):
    dma = pltpu.SemaphoreType.DMA
    regular = pltpu.SemaphoreType.REGULAR
    vmem = pl.BlockSpec(memory_space=pltpu.VMEM)
    anywhere = pl.BlockSpec(memory_space=pl.ANY)
    full = jnp.float32
    small = jnp.bfloat16
    return pl.pallas_call(
        backward_kernel,
        out_shape=(
            jax.ShapeDtypeStruct((36, 3456), full),
            jax.ShapeDtypeStruct((36, 1152), full),
            jax.ShapeDtypeStruct((36, 4608), full),
            jax.ShapeDtypeStruct((144, 1152), full),
            jax.ShapeDtypeStruct((256, 1152), small),
            jax.ShapeDtypeStruct((256, 1152), small),
            jax.ShapeDtypeStruct((4, 2, PACK), full),
            jax.ShapeDtypeStruct((8, 128), full),
        ),
        in_specs=[anywhere] * 7 + [vmem] + [anywhere] * 4 + [vmem] * 6 + [anywhere] * 6,
        out_specs=(vmem,) * 4 + (anywhere,) * 2 + (vmem,) * 2,
        scratch_shapes=[
            pltpu.VMEM((2, 6, 64, PIECE, 128), full),
            pltpu.VMEM((6, 63, PIECE, 128), full),
            pltpu.VMEM((16, 144, 512), small),
            pltpu.VMEM((2304, 512), small),
            pltpu.VMEM((2304, 256), full),
            pltpu.VMEM((2304, 256), full),
            pltpu.VMEM((3, 4, 6, PIECE, 128), full),
            pltpu.VMEM((4, 6, PIECE, 128), full),
            pltpu.VMEM((6, 8, PIECE, 128), full),
            pltpu.VMEM((8, 1152), full),
            pltpu.VMEM((1, 4608), full),
            pltpu.VMEM((1, 3456), full),
            pltpu.VMEM((1, 1152), full),
            pltpu.VMEM((1, 1152), full),
            pltpu.VMEM((128, 1, 128), full),
            pltpu.VMEM((32, 12, 1, 128), full),
            pltpu.VMEM((32, 12, 1, 128), full),
            pltpu.VMEM((32, 2, 1152), full),
            pltpu.VMEM((4, 8, 128), full),
            pltpu.VMEM((2, ROWS, 1152), small),
            pltpu.VMEM((2, ROWS, 1152), small),
            pltpu.VMEM((2, CHUNK, 1152), small),
            pltpu.VMEM((2, 1152, CHUNK), small),
            pltpu.VMEM((2, CHUNK, 256), small),
            pltpu.VMEM((2, CHUNK, 256), small),
            pltpu.VMEM((1152, 256), full),
            pltpu.VMEM((256, 1152), full),
            pltpu.VMEM((256, 1152), full),
            pltpu.VMEM((4608, 256), small),
            pltpu.VMEM((16, 80, 256), small),
            pltpu.VMEM((2, 3, 2, 80, 256), small),
            pltpu.VMEM((2, ROWS, 1152), full),
            pltpu.VMEM((2, ROWS, 1152), full),
            pltpu.VMEM((2, ROWS, 1152), full),
            pltpu.VMEM((2, ROWS, 1152), small),
            dma((6, 6)),
            dma((6, 6)),
            regular((6, 6)),
            dma,
            dma,
            regular,
            dma((2,)),
            dma((3, 6)),
            dma((3, 6)),
            dma((2,)),
            dma((2,)),
            dma((4, 2)),
            dma((4, 2)),
            dma((3, 2)),
            regular,
            dma((2, 2)),
            dma,
            dma,
            dma,
            dma,
            dma((2, 4)),
            dma((2, 4)),
        ],
        compiler_params=pltpu.CompilerParams(
            collective_id=1, has_side_effects=True, vmem_limit_bytes=255 * 2**18
        ),
    )(*operands)


def as_row(ref):
    return ref[...].reshape(1, ref.shape[0])


def forward_kernel(
    tokens,
    out_grad,
    feats,
    labels,
    grid_ids,
    table,
    w_t1,
    b_t1,
    w_t2,
    b_t2,
    w_ada,
    b_ada,
    w_qkv,
    b_qv,
    w_proj,
    b_proj,
    w_fc1,
    b_fc1,
    pre_out,
    cond_out,
    mods,
    lhs_two_far,
    lhs_one_far,
    lhs_zero_far,
    rhs_zero_far,
    act_out_far,
    slope_out_far,
    heads_far,
    cot_far,
    resid_far,
    attn_out_far,
    ada_wide,
    bias_keys,
    onehot,
    lhs_two,
    lhs_one,
    lhs_zero,
    rhs_zero,
    act_out,
    slope_out,
    heads,
    cot,
    resid,
    attn_out,
    mine,
    gathered,
    flat,
    normed,
    qkv_t,
    w_q,
    w_p,
    w_f,
    w_1,
    w_2,
    keys_off,
    live_rows,
    send_a,
    send_b,
    send_c,
    send_d,
    send_e,
    got_a,
    got_b,
    got_c,
    got_d,
    got_e,
    send,
    recv,
    load_sem,
    pair_send,
    pair_recv,
    fc_sem,
    out_sem,
    part_sem,
):
    at = coords()
    core = at["core"]
    sibling = sibling_of(at)
    place = lax.axis_index("dp")
    loads = [
        pltpu.make_async_copy(source, target, load_sem.at[index])
        for index, (source, target) in enumerate(
            ((w_t1, w_1), (w_t2, w_2), (w_qkv, w_q), (w_proj, w_p))
        )
    ]
    for copy in loads:
        copy.start()

    def fc_load(part):
        columns = pl.ds(part * 1152, 1152)
        return pltpu.make_async_copy(w_fc1.at[:, columns], w_f.at[part % 2], fc_sem.at[part % 2])

    fc_load(0).start()
    fc_load(1).start()
    outs = [
        pltpu.make_async_copy(source, target, out_sem.at[index])
        for index, (source, target) in enumerate(
            (
                (cot, cot_far),
                (heads, heads_far),
                (attn_out, attn_out_far),
                (resid, resid_far),
                (lhs_two, lhs_two_far),
                (rhs_zero, rhs_zero_far),
                (lhs_one, lhs_one_far),
            )
        )
    ]

    def part_out(part):
        rows, chips = pl.ds(part * 1152, 1152), pl.ds(part * 4, 4)
        return [
            pltpu.make_async_copy(source, target, part_sem.at[index, part])
            for index, (source, target) in enumerate(
                (
                    (act_out.at[rows], act_out_far.at[rows]),
                    (slope_out.at[rows], slope_out_far.at[rows]),
                    (lhs_zero.at[chips], lhs_zero_far.at[chips]),
                )
            )
        ]

    barrier = pltpu.get_barrier_semaphore()

    def hello(hop, _):
        pl.semaphore_signal(barrier, inc=1, device_id=dp_peer(hop), device_id_type=MESH)
        return _

    lax.fori_loop(1, 32, hello, 0)
    rows_table = jnp.concatenate(
        [table[pl.ds(labels[0], 1), :], table[pl.ds(labels[1], 1), :]], axis=0
    )
    loads[0].wait()
    pre_time = exact_dot(feats[...], w_1[...]) + as_row(b_t1)
    loads[1].wait()
    condition = exact_dot(silu(pre_time), w_2[...]) + as_row(b_t2) + rows_table
    mod_part = exact_dot(silu(condition), w_ada[...], 1) + as_row(b_ada)
    pre_out[...] = pre_time
    cond_out[...] = condition
    for item in range(2):
        mine[item, :, 0:216] = mod_part[item : item + 1]
        mine[item, :, 216:256] = jnp.zeros((1, 40), jnp.float32)
    gathered[place] = mine[lax.div(place, 16)]
    pl.semaphore_wait(barrier, 31)

    def copy_to(hop):
        target = lax.rem(place + hop, 32)
        return pltpu.make_async_remote_copy(
            src_ref=mine.at[lax.div(target, 16)],
            dst_ref=gathered.at[place],
            send_sem=send,
            recv_sem=recv,
            device_id=dp_peer(hop),
            device_id_type=MESH,
        )

    def begin(hop, _):
        copy_to(hop).start()
        return _

    def norm(values):
        mean = jnp.mean(values, axis=-1, keepdims=True)
        centered = values - mean
        inverse = lax.rsqrt(jnp.mean(centered * centered, axis=-1, keepdims=True) + EPS)
        return centered * inverse

    def row_range(index):
        return pl.ds(pl.multiple_of(index * 64, 64), 64)

    lax.fori_loop(1, 32, begin, 0)
    ada_rows = jnp.concatenate([w_ada[...].astype(jnp.float32), jnp.zeros((40, 1152))], axis=0)
    ada_wide[...] = ada_rows.astype(jnp.bfloat16)
    grid_value = grid_ids[lax.div(place, 16)]
    first_live = jnp.where(grid_value == 2, 16, 0)
    end_live = jnp.where(grid_value == 1, 240, 256)
    slots = lax.broadcasted_iota(jnp.int32, (256, 128), 0)
    live = (slots >= first_live) & (slots < end_live)
    keys_off[...] = jnp.where(live, 0.0, NEG)
    live_rows[...] = jnp.where(live, 1.0, 0.0)
    bias_keys[...] = keys_off[...]
    for item in range(2):
        classes = lax.broadcasted_iota(jnp.int32, (1, 128), 1)
        onehot[item : item + 1, :] = jnp.where(classes == labels[item], 1.0, 0.0)

    def first_norm(index, _):
        rows = row_range(index)
        normed[rows, :] = norm(tokens[rows, :].astype(jnp.float32))
        cot[rows, :] = out_grad[rows, :].astype(jnp.float32) * live_rows[rows, 0:1]
        return _

    lax.fori_loop(0, 4, first_norm, 0)
    outs[0].start()

    def blank(row, _):
        flat[row] = jnp.zeros((1, 128), jnp.float32)
        return _

    lax.fori_loop(0, 56, blank, 0)
    pltpu.make_async_remote_copy(
        src_ref=gathered.at[pl.ds(0, 31)],
        dst_ref=gathered.at[pl.ds(0, 31)],
        send_sem=send,
        recv_sem=recv,
        device_id=sibling,
        device_id_type=MESH,
    ).wait()
    for piece in range(32):
        row, shift = piece * 216 // 128, piece * 216 % 128
        wide = jnp.concatenate([gathered[piece], jnp.zeros((1, 128), jnp.float32)], axis=1)
        wide = pltpu.roll(jnp.concatenate([wide] * 8, axis=0), shift, 1)[0:1]
        for step in range(3):
            flat[row + step] += wide[:, step * 128 : step * 128 + 128]
    for row in range(6):
        for column in range(9):
            mods[row : row + 1, column * 128 : column * 128 + 128] = flat[row * 9 + column]
    mods[6:8, :] = jnp.zeros((2, 1152), jnp.float32)

    def to_sibling(index, source, target):
        return pltpu.make_async_remote_copy(
            src_ref=source,
            dst_ref=target,
            send_sem=pair_send.at[index],
            recv_sem=pair_recv.at[index],
            device_id=sibling,
            device_id_type=MESH,
        )

    def modulate(index, _):
        rows = row_range(index)
        normed[rows, :] = normed[rows, :] * (1.0 + mods[1:2]) + mods[0:1]
        return _

    lax.fori_loop(0, 4, modulate, 0)
    send_a[...] = normed[...].T
    pair_a = to_sibling(0, send_a, got_a)
    pair_a.start()
    for part in range(8):
        lhs_two[part, :, 0:256] = send_a[part * 144 : part * 144 + 144].astype(jnp.bfloat16)
    loads[2].wait()
    for part in range(3):
        block = dot_nn(
            normed[...].astype(jnp.bfloat16), w_q[:, part * 1152 : part * 1152 + 1152]
        )
        if part == 0:
            block = block + as_row(b_qv)[:, 0:1152]
        if part == 2:
            block = block + as_row(b_qv)[:, 1152:2304]
        qkv_t[part * 1152 : part * 1152 + 1152, :] = block.T

    def branch_grad(index, _):
        rows = row_range(index)
        normed[rows, :] = cot[rows, :] * mods[5:6]
        return _

    scale = 1.0 / math.sqrt(72)

    def one_head(head, _):
        parts = []
        for part in range(3):
            rows = pl.ds(pl.multiple_of(part * 1152 + head * 72, 8), 72)
            padded = jnp.concatenate([qkv_t[rows, :], jnp.zeros((8, 256), jnp.float32)], axis=0)
            parts.append(padded.astype(jnp.bfloat16))
            heads[head + part * 16] = parts[-1]
        query, key, value = parts
        scores = dot_tn(key, query) * scale + jnp.concatenate([keys_off[...]] * 2, axis=1)
        shifted = jnp.exp(scores - jnp.max(scores, axis=0, keepdims=True))
        weights = (shifted / jnp.sum(shifted, axis=0, keepdims=True)).astype(jnp.bfloat16)
        rows = pl.ds(pl.multiple_of(head * 72, 8), 72)
        send_b[rows, :] = dot_nn(value, weights)[0:72]
        return _

    lax.fori_loop(0, 16, one_head, 0, unroll=8)
    outs[1].start()
    pair_b = to_sibling(1, send_b, got_b)
    pair_b.start()
    for part in range(8):
        lhs_two[part + 8, :, 0:256] = send_b[part * 144 : part * 144 + 144].astype(jnp.bfloat16)
    lax.fori_loop(0, 4, branch_grad, 0)
    send_c[...] = normed[...].T
    pair_c = to_sibling(2, send_c, got_c)
    pair_c.start()
    rhs_zero[:, 0:256] = send_c[...].astype(jnp.bfloat16)
    loads[3].wait()
    attn_out[...] = dot_tn(send_b[...].astype(jnp.bfloat16), w_p[...]) + as_row(b_proj)

    def second_norm(index, _):
        rows = row_range(index)
        stream = tokens[rows, :].astype(jnp.float32) + mods[2:3] * attn_out[rows, :]
        resid[rows, :] = stream
        normed[rows, :] = norm(stream) * (1.0 + mods[4:5]) + mods[3:4]
        return _

    lax.fori_loop(0, 4, second_norm, 0)
    outs[2].start()
    outs[3].start()
    send_d[...] = normed[...].T
    pair_d = to_sibling(3, send_d, got_d)
    pair_d.start()
    for part in range(8):
        lhs_one[part, :, 0:256] = send_d[part * 144 : part * 144 + 144].astype(jnp.bfloat16)
    pair_a.wait()
    for part in range(8):
        lhs_two[part, :, 256:512] = got_a[part * 144 : part * 144 + 144].astype(jnp.bfloat16)
    inner = math.sqrt(2.0 / math.pi)
    pair_e = []
    for part in range(4):
        fc_load(part).wait()
        columns = slice(part * 1152, part * 1152 + 1152)
        hidden = dot_nn(normed[...].astype(jnp.bfloat16), w_f[part % 2]) + as_row(b_fc1)[:, columns]
        qkv_t[0:1152, :] = hidden.T
        if part < 2:
            fc_load(part + 2).start()

        def gelu(index, _, part=part):
            rows = pl.ds(pl.multiple_of(index * 144, 144), 144)
            values = qkv_t[rows, :]
            square = values * values
            bend = jnp.tanh(inner * values * (1.0 + 0.044715 * square))
            half = 0.5 * (1.0 + bend)
            active = values * half
            steep = half + 0.5 * values * (1.0 - bend * bend) * inner * (
                1.0 + 3.0 * 0.044715 * square
            )
            into = pl.ds(pl.multiple_of(part * 1152 + index * 144, 144), 144)
            act_out[into, :] = active.astype(jnp.bfloat16)
            slope_out[into, :] = steep.astype(jnp.bfloat16)
            chip = part * 4 + lax.div(index, 2)

            @pl.when(lax.rem(index, 2) == core)
            def _():
                lhs_zero[chip, :, 0:256] = active.astype(jnp.bfloat16)

            @pl.when(lax.rem(index, 2) != core)
            def _():
                send_e[chip] = active

            return 0

        lax.fori_loop(0, 8, gelu, 0)
        some = pl.ds(part * 4, 4)
        pair_e.append(to_sibling(4 + part, send_e.at[some], got_e.at[some]))
        pair_e[-1].start()
        part_out(part)[0].start()
        part_out(part)[1].start()
        if part == 0:
            pair_b.wait()
            for chip in range(8):
                rows = got_b[chip * 144 : chip * 144 + 144]
                lhs_two[chip + 8, :, 256:512] = rows.astype(jnp.bfloat16)
            outs[4].start()
        if part == 1:
            pair_c.wait()
            rhs_zero[:, 256:512] = got_c[...].astype(jnp.bfloat16)
            outs[5].start()
        if part == 2:
            pair_d.wait()
            for chip in range(8):
                rows = got_d[chip * 144 : chip * 144 + 144]
                lhs_one[chip, :, 256:512] = rows.astype(jnp.bfloat16)
            outs[6].start()
    for part in range(4):
        pair_e[part].wait()
        for chip in range(part * 4, part * 4 + 4):
            lhs_zero[chip, :, 256:512] = got_e[chip].astype(jnp.bfloat16)
        part_out(part)[2].start()
    for copy in outs:
        copy.wait()
    for part in range(4):
        for copy in part_out(part):
            copy.wait()


def forward(operands):
    dma = pltpu.SemaphoreType.DMA
    vmem = pl.BlockSpec(memory_space=pltpu.VMEM)
    smem = pl.BlockSpec(memory_space=pltpu.SMEM)
    anywhere = pl.BlockSpec(memory_space=pl.ANY)
    full, small = jnp.float32, jnp.bfloat16
    out = jax.ShapeDtypeStruct
    return pl.pallas_call(
        forward_kernel,
        out_shape=(
            out((2, 1152), full),
            out((2, 1152), full),
            out((8, 1152), full),
            out((16, 144, 512), small),
            out((8, 144, 512), small),
            out((16, 144, 512), small),
            out((1152, 512), small),
            out((4608, 256), small),
            out((4608, 256), small),
            out((48, 80, 256), small),
            out((256, 1152), full),
            out((256, 1152), full),
            out((256, 1152), full),
            out((256, 1152), small),
            out((256, 128), full),
            out((2, 128), full),
        ),
        in_specs=[vmem] * 3
        + [smem, smem, vmem]
        + [anywhere, vmem] * 2
        + [vmem, vmem]
        + [anywhere, vmem] * 3,
        out_specs=(vmem,) * 3 + (anywhere,) * 10 + (vmem,) * 3,
        scratch_shapes=[
            pltpu.VMEM((16, 144, 512), small),
            pltpu.VMEM((8, 144, 512), small),
            pltpu.VMEM((16, 144, 512), small),
            pltpu.VMEM((1152, 512), small),
            pltpu.VMEM((4608, 256), small),
            pltpu.VMEM((4608, 256), small),
            pltpu.VMEM((48, 80, 256), small),
            pltpu.VMEM((256, 1152), full),
            pltpu.VMEM((256, 1152), full),
            pltpu.VMEM((256, 1152), full),
            pltpu.VMEM((2, 1, 256), full),
            pltpu.VMEM((32, 1, 256), full),
            pltpu.VMEM((56, 1, 128), full),
            pltpu.VMEM((256, 1152), full),
            pltpu.VMEM((3456, 256), full),
            pltpu.VMEM((1152, 3456), small),
            pltpu.VMEM((1152, 1152), small),
            pltpu.VMEM((2, 1152, 1152), small),
            pltpu.VMEM((256, 1152), small),
            pltpu.VMEM((1152, 1152), small),
            pltpu.VMEM((256, 128), full),
            pltpu.VMEM((256, 128), full),
            pltpu.VMEM((1152, 256), full),
            pltpu.VMEM((1152, 256), full),
            pltpu.VMEM((1152, 256), full),
            pltpu.VMEM((1152, 256), full),
            pltpu.VMEM((16, 144, 256), full),
            pltpu.VMEM((1152, 256), full),
            pltpu.VMEM((1152, 256), full),
            pltpu.VMEM((1152, 256), full),
            pltpu.VMEM((1152, 256), full),
            pltpu.VMEM((16, 144, 256), full),
            dma,
            dma,
            dma((4,)),
            dma((8,)),
            dma((8,)),
            dma((2,)),
            dma((7,)),
            dma((3, 4)),
        ],
        compiler_params=pltpu.CompilerParams(
            collective_id=2, has_side_effects=True, vmem_limit_bytes=255 * 2**18
        ),
    )(*operands)


def split_parts(values):
    high = values.astype(jnp.bfloat16)
    rest = values - high.astype(jnp.float32)
    middle = rest.astype(jnp.bfloat16)
    low = (rest - middle.astype(jnp.float32)).astype(jnp.bfloat16)
    return high, middle, low


def outer_sum(left, right):
    left_high, left_middle, left_low = split_parts(left)
    right_high, right_middle, right_low = split_parts(right)
    lefts = [left_high, left_high, left_middle, left_middle, left_high, left_low]
    rights = [right_high, right_middle, right_high, right_middle, right_low, right_high]
    return dot_tn(jnp.concatenate(lefts, axis=0), jnp.concatenate(rights, axis=0))


def finish_kernel(
    packs,
    sums,
    in_qkv,
    in_proj,
    in_fc1,
    in_fc2,
    in_block,
    in_grad,
    out_qkv,
    out_proj,
    out_fc1,
    out_fc2,
    out_block,
    out_grad,
    d_ada,
    b_ada,
    d_t1,
    b_t1,
    d_t2,
    b_t2,
    d_table,
    b_qv,
    b_proj,
    b_fc1,
    b_fc2,
    copy_sem,
):
    place = lax.axis_index("dp")
    copies = [
        pltpu.make_async_copy(source, target, copy_sem.at[index])
        for index, (source, target) in enumerate(
            (
                (in_qkv, out_qkv),
                (in_proj, out_proj),
                (in_fc1, out_fc1),
                (in_fc2, out_fc2),
                (in_block, out_block),
                (in_grad, out_grad),
            )
        )
    ]
    for copy in copies:
        copy.start()

    def eight(begin, end):
        return jnp.concatenate([packs[group, :, begin:end] for group in range(4)], axis=0)

    def own(rows, width):
        count = rows.shape[1]
        return pltpu.roll(rows, lax.rem(count - place * width, count), 1)

    grad_cond, grad_pre = eight(0, 1152), eight(1152, 2304)
    d_mod = eight(4608, 4864)
    d_ada[...] = outer_sum(d_mod, eight(2304, 3456))[0:216]
    b_ada[...] = jnp.sum(d_mod, axis=0, keepdims=True)[:, 0:216].reshape(216)
    d_t1[...] = outer_sum(own(eight(4864, 5120), 8)[:, 0:128], grad_pre)[0:8]
    d_t2[...] = outer_sum(own(eight(3456, 4608), 36)[:, 0:128], grad_cond)[0:36]
    d_table[...] = outer_sum(eight(5120, 5248), grad_cond)[0:101]
    total_pre = jnp.concatenate([jnp.sum(grad_pre, axis=0, keepdims=True)] * 8, axis=0)
    total_cond = jnp.concatenate([jnp.sum(grad_cond, axis=0, keepdims=True)] * 8, axis=0)
    b_t1[...] = own(total_pre, 36)[0:1, 0:36].reshape(36)
    b_t2[...] = own(total_cond, 36)[0:1, 0:36].reshape(36)
    b_qv[...] = sums[0:1, 0:72].reshape(72)
    b_proj[...] = sums[1:2, 0:36].reshape(36)
    b_fc1[...] = jnp.concatenate([sums[2:3, :], sums[3:4, :]], axis=1)[:, 0:144].reshape(144)
    b_fc2[...] = sums[4:5, 0:36].reshape(36)
    for copy in copies:
        copy.wait()


def finish(operands):
    vmem = pl.BlockSpec(memory_space=pltpu.VMEM)
    anywhere = pl.BlockSpec(memory_space=pl.ANY)
    full, small = jnp.float32, jnp.bfloat16
    out = jax.ShapeDtypeStruct
    return pl.pallas_call(
        finish_kernel,
        out_shape=(
            out((36, 3456), full),
            out((36, 1152), full),
            out((36, 4608), full),
            out((144, 1152), full),
            out((256, 1152), small),
            out((256, 1152), small),
            out((216, 1152), full),
            out((216,), full),
            out((8, 1152), full),
            out((36,), full),
            out((36, 1152), full),
            out((36,), full),
            out((101, 1152), full),
            out((72,), full),
            out((36,), full),
            out((144,), full),
            out((36,), full),
        ),
        in_specs=[vmem] * 8,
        out_specs=(anywhere,) * 6 + (vmem,) * 11,
        scratch_shapes=[pltpu.SemaphoreType.DMA((6,))],
        compiler_params=pltpu.CompilerParams(vmem_limit_bytes=255 * 2**18),
    )(*operands)


def on_device(
    tokens,
    out_grad,
    timesteps,
    labels,
    grid_ids,
    w_qkv,
    b_qv,
    w_proj,
    b_proj,
    w_fc1,
    b_fc1,
    w_fc2,
    b_fc2,
    w_ada,
    b_ada,
    w_t1,
    b_t1,
    w_t2,
    b_t2,
    table,
):
    dp_place = lax.axis_index("dp")
    model_width = tokens.shape[1]
    time_feats = time_embed(timesteps, w_t1.shape[0] // 2)
    (
        pre_time,
        condition,
        mods,
        lhs_two,
        lhs_one,
        lhs_zero,
        rhs_zero,
        act_t,
        slope_t,
        heads,
        cotangent,
        resid_one,
        attn_out,
        ada_wide,
        bias_keys,
        onehot,
    ) = forward(
        [
            tokens,
            out_grad,
            time_feats,
            labels,
            grid_ids,
            table,
            w_t1,
            b_t1,
            w_t2,
            b_t2,
            w_ada.T,
            b_ada,
            w_qkv,
            b_qv,
            w_proj,
            b_proj,
            w_fc1,
            b_fc1,
        ]
    )
    (
        sum_qkv,
        sum_proj,
        sum_fc1,
        sum_fc2,
        block_out,
        input_grad,
        packs,
        sums,
    ) = backward(
        [
            lhs_zero,
            lhs_one,
            lhs_two,
            rhs_zero,
            act_t,
            slope_t,
            heads,
            bias_keys,
            cotangent,
            resid_one,
            attn_out,
            tokens,
            mods,
            b_fc2,
            pre_time,
            condition,
            time_feats,
            onehot,
            ada_wide,
            w_t2,
            w_qkv,
            w_proj,
            w_fc1,
            w_fc2,
        ]
    )
    (
        sum_qkv,
        sum_proj,
        sum_fc1,
        sum_fc2,
        block_out,
        input_grad,
        d_ada,
        b_ada,
        d_t1,
        b_t1,
        d_t2,
        b_t2,
        d_table,
        d_qv,
        d_proj,
        d_fc1,
        d_fc2,
    ) = finish([packs, sums, sum_qkv, sum_proj, sum_fc1, sum_fc2, block_out, input_grad])
    return (
        block_out,
        input_grad,
        sum_qkv,
        d_qv,
        sum_proj,
        d_proj,
        sum_fc1,
        d_fc1,
        sum_fc2,
        d_fc2,
        d_ada.T,
        b_ada,
        d_t1,
        b_t1,
        d_t2,
        b_t2,
        d_table,
    )


def solution(mesh):
    placed = (
        P(("group", "dp"), None),
        P(("group", "dp"), None),
        P("group"),
        P("group"),
        P("group"),
        P(),
        P(),
        P(),
        P(),
        P(),
        P(),
        P(),
        P(),
        P(None, "dp"),
        P("dp"),
        P(),
        P(),
        P(),
        P(),
        P(),
    )
    return jax.shard_map(
        on_device,
        mesh=mesh,
        in_specs=placed,
        out_specs=(
            P(("group", "dp"), None),
            P(("group", "dp"), None),
            P("dp", None),
            P("dp"),
            P("dp", None),
            P("dp"),
            P("dp", None),
            P("dp"),
            P("dp", None),
            P("dp"),
            P(None, "dp"),
            P("dp"),
            P("dp", None),
            P("dp"),
            P("dp", None),
            P("dp"),
            P(),
        ),
        check_vma=False,
    )
```
